128 devices in a mesh: dp: 32 (over y, x, z_lo), tensor: 2 (over core), group: 2 (over z_hi).
Axes of the slice: x: 4, y: 4, z: 4 (z_hi: 2, z_lo: 2; z = z_hi * 2 + z_lo), core: 2. Of those that a mesh axis runs over, the one named last changes fastest.
Arguments:
- ref_image: bfloat16 [4096, 768], P(('dp', 'tensor')), may hold values from -100 to 100
- ref_text: bfloat16 [4096, 768], P(('dp', 'tensor')), may hold values from -100 to 100
- learner_image: bfloat16 [4096, 1024], P(('dp', 'tensor')), may hold values from -100 to 100
- learner_text: bfloat16 [4096, 1024], P(('dp', 'tensor')), may hold values from -100 to 100
- patches: bfloat16 [4096, 16, 1024], P('dp', 'group', 'tensor'), may hold values from -6 to 6
- cotangent: bfloat16 [4096, 16, 1024], P('dp', 'group', 'tensor'), may hold values from -6 to 6
- w_up: bfloat16 [1024, 4096], P(None, 'tensor'), may hold values from -0.1875 to 0.1875
- w_down: bfloat16 [4096, 1024], P('tensor'), may hold values from -0.09375 to 0.09375
- counts: int32 [32], P('dp'), may hold values from 1 to 64, 1536 in all
- sel_index: int32 [2048], P('dp'), may hold values from 0 to 127, as said below
- sel_dest: int32 [2048, 1], P('dp'), may hold values from 0 to 31; in each aligned block of 64 rows (0 to 63, 64 to 127, ...) at most 4 rows name the same one
Outputs:
- learnability: float32 [4096], P(('dp', 'tensor'))
- routed_out: bfloat16 [4096, 16, 1024], P('dp', 'group', 'tensor')
- grad_up: float32 [1024, 4096], P(('dp', 'group'), 'tensor')
- grad_down_t: float32 [1024, 4096], P(('dp', 'group'), 'tensor')
The draws below stay inside these ranges and needn't reach their ends.
Inputs may be any that keep to these rules, and one draw needn't show every extreme that they name: `sel_index`: within each aligned block of 64 entries the positions are distinct. `sel_dest`: within each aligned block of 64 rows no shard is named more than 4 times.
All inputs are finite; a program needn't handle non-finite values. No bound on the sum of `counts` on one device may be relied on, other than what follows from the above.
Results may differ from the reference program's by a relative error of at most 0.012.
Values may be sent and summed in bfloat16 or wider, within the bound.
No kernel may reach another device: no remote copies, remote signals or barrier semaphores. Data moves between devices by JAX's collectives and lax.ppermute only.
A program may use at most 128 MiB of HBM per device.

```python
import math
import jax
import jax.numpy as jnp
import numpy as np
from jax import lax

DR = 768
DL = 1024
FF = 4096
PD = 128
PT = 16
SEL_DEV = 64
CAP = 4
PAIRS = 4096
ROUTED = 4096
N_DP = 32


def shared_parts(key, width, model):
    topic_ids = jax.random.randint(jax.random.fold_in(key, 11), (PAIRS,), 0, 64)
    topic_table = jnp.clip(jax.random.normal(jax.random.fold_in(key, 20 + model), (64, width), jnp.float32), -4.0, 4.0)
    content = jnp.clip(jax.random.normal(jax.random.fold_in(key, 30 + model), (PAIRS, width), jnp.float32), -4.0, 4.0)
    alignment = jax.random.uniform(jax.random.fold_in(key, 40 + model), (PAIRS, 1), jnp.float32)
    return (topic_table[topic_ids], content, alignment)


def blend(shared, private_noise, row_scale):
    topic_rows, content, alignment = shared
    mixed = topic_rows + jnp.sqrt(alignment) * content + jnp.sqrt(1.0 - alignment) * private_noise
    return (row_scale * mixed).astype(jnp.bfloat16)


def embedding(key, width, model, constant):
    shared = shared_parts(key, width, model)
    own_key = jax.random.fold_in(key, constant)
    noise_key = jax.random.fold_in(own_key, 1)
    scale_key = jax.random.fold_in(own_key, 2)
    private_noise = jnp.clip(jax.random.normal(noise_key, (PAIRS, width), jnp.float32), -4.0, 4.0)
    row_scale = jnp.exp(jax.random.uniform(scale_key, (PAIRS, 1), jnp.float32, 0.0, math.log(10.0)))
    return blend(shared, private_noise, row_scale)


def draw_ref_image(key, part):
    return embedding(key, DR, 0, 1)


def draw_ref_text(key, part):
    return embedding(key, DR, 0, 2)


def draw_learner_image(key, part):
    return embedding(key, DL, 1, 3)


def draw_learner_text(key, part):
    return embedding(key, DL, 1, 4)


def draw_sel_index(key, part):
    key = jax.random.fold_in(key, 7)
    keys = jax.random.split(key, N_DP)

    def one_block(block_key):
        order = jax.random.permutation(block_key, PD)[:SEL_DEV]
        return (order + (PD - 1 - order[0])) % PD
    return jax.vmap(one_block)(keys).reshape(-1).astype(jnp.int32)


def shard_levels(stream_key, shape, cuts, smallest, largest):
    loudness = 1.0
    for dim, shards_of in cuts:
        steps = jax.random.uniform(jax.random.fold_in(jax.random.fold_in(stream_key, 6), dim), (shards_of,), jnp.float32, smallest / len(cuts), largest / len(cuts))
        loudness = loudness * jnp.repeat(jnp.exp(steps), shape[dim] // shards_of).reshape((-1,) + (1,) * (len(shape) - 1 - dim))
    return loudness


def length_profile(count, total, bound, slope):
    loads = [(1 << 20) // math.isqrt(grade ** slope) + 1 for grade in range(2, count + 1)]
    spare, given = total - bound - (count - 1), [1] * (count - 1)
    while spare > 0:
        free = [i for i in range(count - 1) if given[i] < bound]
        pool, budget = sum([loads[i] for i in free]), spare
        for i in free:
            addition = min(bound - given[i], max(1, budget * loads[i] // pool), spare)
            given[i] = given[i] + addition
            spare = spare - addition
    return np.array([bound] + given)


def uneven_parts(rng, count, total, limit, slope):
    if count == 2:
        one = jax.random.randint(rng, (), max(1, total - limit), min(limit, total - 1) + 1)
        return jnp.stack([one, total - one])
    lengths = jnp.asarray(length_profile(count, total, limit, slope), jnp.int32)
    pairs = (count - 1) // 2
    giver, taker = lengths[1:1 + 2 * pairs:2], lengths[2:2 + 2 * pairs:2]
    slack = jnp.minimum(giver - 1, limit - taker)
    moved = jax.random.randint(jax.random.fold_in(rng, 1), (pairs,), 0, 1 << 20) % (slack + 1)
    lengths = lengths.at[1:1 + 2 * pairs:2].set(giver - moved).at[2:2 + 2 * pairs:2].set(taker + moved)
    return lengths[jax.random.permutation(jax.random.fold_in(rng, 2), count)]


def assign_block(key, own, number, rows, amount, top, limit, lean):
    sequence = jax.random.permutation(key, amount)
    crowded, common = portions_of(amount, rows * top, limit, lean, True), portions_of(amount, rows * top, limit, lean, False)
    places = jnp.arange(amount)

    def named(tallies, turn):
        used = int((tallies > 0).sum())
        fixed = max(1, used // 4)
        passed = fixed + (places - fixed + turn * (used - fixed)) % max(1, amount - fixed)
        return jnp.zeros((amount,), jnp.int32).at[sequence[jnp.where(places < fixed, places, passed)]].set(jnp.asarray(tallies, jnp.int32))

    tallies = jnp.where(number % 4 == 0, named(crowded, number // 4), named(common, number - number // 4 - 1))
    mixed = jax.random.permutation(jax.random.fold_in(own, 3), amount)
    source_of, sink = mixed[0:amount // 2 * 2:2], mixed[1:amount // 2 * 2:2]
    room = jnp.minimum(tallies[source_of] - 1, limit - tallies[sink]) // 2
    room = jnp.where((source_of == sequence[0]) | (sink == sequence[0]) | (tallies[sink] == 0), 0, jnp.maximum(room, 0))
    passed = jax.random.randint(jax.random.fold_in(own, 4), (amount // 2,), 0, 1 << 20) % (room + 1)
    tallies = tallies.at[source_of].add(-passed).at[sink].add(passed)
    labels = jnp.searchsorted(jnp.cumsum(tallies), jnp.arange(rows * top), side="right").astype(jnp.int32)
    table = labels.reshape(top, rows).T
    table = table[jax.random.permutation(jax.random.fold_in(own, 1), rows)]
    turn = jax.random.randint(jax.random.fold_in(own, 2), (rows, 1), 0, top)
    return jnp.take_along_axis(table, (jnp.arange(top)[None, :] + turn) % top, axis=1)


def portions_of(number_of, total, bound, lean, full):
    weights = [(1 << 20) // math.isqrt(grade ** lean) + 1 for grade in range(1, number_of + 1)]
    largest = bound if full else min(bound, max(-(-total // number_of), total * weights[0] // sum(weights)))
    least = 1 if total - largest >= number_of - 1 else 0
    given, rest = [largest] + [least] * (number_of - 1), total - largest - least * (number_of - 1)
    while rest > 0:
        free = [i for i in range(1, number_of) if given[i] < largest] or [i for i in range(1, number_of) if given[i] < bound]
        whole, budget = sum([weights[i] for i in free]), rest
        for i in free:
            addition = min(bound - given[i], max(1, budget * weights[i] // whole), rest)
            given[i] = given[i] + addition
            rest = rest - addition
    return np.array(given)


def scatter_about(key, shape, spread, bound, cuts=(), kind=jnp.bfloat16):
    entries = jax.random.normal(key, shape, jnp.float32) * spread
    if len(cuts) > 0:
        entries = shard_levels(key, shape, cuts, -0.22, 0.18) * entries
    return jnp.clip(entries, min=-bound, max=bound).astype(kind)


def setup_inputs(seed: int = 0) -> dict:
    splits = jax.random.split(jax.random.key(seed), 12)
    ref_image = draw_ref_image(jax.random.fold_in(splits[11], 71), 0)
    ref_text = draw_ref_text(jax.random.fold_in(splits[11], 71), 0)
    learner_image = draw_learner_image(jax.random.fold_in(splits[11], 71), 0)
    learner_text = draw_learner_text(jax.random.fold_in(splits[11], 71), 0)
    patches = scatter_about(splits[4], (PAIRS, PT, DL), 1.0, 6.0, ((0, 32), (1, 2), (2, 2)))
    cotangent = scatter_about(splits[5], (PAIRS, PT, DL), 1.0, 6.0, ((0, 32), (1, 2), (2, 2)))
    w_up = scatter_about(splits[6], (DL, FF), DL ** -0.5, 0.1875, ((1, 2),))
    w_down = scatter_about(splits[7], (FF, DL), FF ** -0.5, 0.09375, ((0, 2),))
    counts = uneven_parts(splits[8], N_DP, 3 * SEL_DEV * N_DP // 4, SEL_DEV, 2).astype(jnp.int32)
    sel_index = draw_sel_index(jax.random.fold_in(splits[11], 71), 0)
    sel_dest_keys = jax.random.split(jax.random.fold_in(splits[10], 1), (N_DP * SEL_DEV) // SEL_DEV)
    sel_dest_turns = jax.random.permutation(jax.random.fold_in(splits[10], 3), (N_DP * SEL_DEV) // SEL_DEV)
    sel_dest = jax.vmap(lambda own, number: assign_block(jax.random.fold_in(splits[10], 2), own, number, SEL_DEV, N_DP, 1, CAP, 2))(sel_dest_keys, sel_dest_turns).reshape((N_DP * SEL_DEV, 1))
    return {"ref_image": ref_image, "ref_text": ref_text, "learner_image": learner_image, "learner_text": learner_text, "patches": patches, "cotangent": cotangent, "w_up": w_up, "w_down": w_down, "counts": counts, "sel_index": sel_index, "sel_dest": sel_dest}


def unit_rows(block):
    wide = block.astype(jnp.float32)
    return (wide * lax.rsqrt(lax.optimization_barrier(jnp.sum(wide * wide, axis=1, keepdims=True)) + 1e-06)).astype(jnp.bfloat16)

def pair_losses(image, text, temp, bias):
    unit_img = unit_rows(image)
    unit_txt = unit_rows(text)
    scores = temp * jnp.dot(unit_img, unit_txt.T, preferred_element_type=jnp.float32) + bias
    count = scores.shape[0]
    same = jnp.arange(count, dtype=jnp.int32)[:, None] == jnp.arange(count, dtype=jnp.int32)[None, :]
    terms = jnp.where(same, jax.nn.softplus(-scores), jax.nn.softplus(scores))
    return 0.5 * (lax.optimization_barrier(jnp.sum(terms, axis=1)) + lax.optimization_barrier(jnp.sum(terms, axis=0)))

def reference(ref_image, ref_text, learner_image, learner_text, patches, cotangent, w_up, w_down, counts, sel_index, sel_dest):
    learnability = pair_losses(learner_image, learner_text, 10.0, -5.0) - pair_losses(ref_image, ref_text, 10.0, -5.0)
    chosen = sel_index.reshape(N_DP, SEL_DEV)
    target = sel_dest.reshape(N_DP, SEL_DEV)
    live = jnp.arange(SEL_DEV, dtype=jnp.int32)[None, :] < counts[:, None]
    hits = ((target[:, :, None] == jnp.arange(N_DP, dtype=jnp.int32)[None, None, :]) & live[:, :, None]).astype(jnp.int32)
    rank = lax.optimization_barrier(jnp.sum((jnp.cumsum(hits, axis=1) - hits) * hits, axis=2))
    source = jnp.arange(N_DP, dtype=jnp.int32)[:, None]
    pair_ids = (source * PD + chosen).astype(jnp.int32)
    weight = jnp.where(live, jax.nn.sigmoid(learnability[pair_ids]), 0.0).astype(jnp.float32)
    row_ids = jnp.where(live, target * (N_DP * CAP) + source * CAP + rank, ROUTED).astype(jnp.int32)

    def one_source(totals, item):
        ids, pair_weight = item
        block = patches[ids].reshape(SEL_DEV * PT, DL)
        scaled = (pair_weight[:, None, None] * cotangent[ids].astype(jnp.float32)).astype(jnp.bfloat16).reshape(SEL_DEV * PT, DL)
        pre = jnp.dot(block, w_up, preferred_element_type=jnp.float32)
        act_full, gelu_back = jax.vjp(jax.nn.gelu, pre)
        act = act_full.astype(jnp.bfloat16)
        out = (block.astype(jnp.float32) + jnp.dot(act, w_down, preferred_element_type=jnp.float32)).astype(jnp.bfloat16)
        back = jnp.dot(scaled, w_down.T, preferred_element_type=jnp.float32)
        grad_pre = gelu_back(back)[0].astype(jnp.bfloat16)
        grad_up = totals[0] + jnp.dot(block.T, grad_pre, preferred_element_type=jnp.float32)
        grad_down_t = totals[1] + jnp.dot(scaled.T, act, preferred_element_type=jnp.float32)
        return ((grad_up, grad_down_t), out.reshape(SEL_DEV, PT, DL))
    zeros = jnp.zeros((DL, FF), jnp.float32)
    (grad_up, grad_down_t), outs = lax.scan(one_source, (zeros, zeros), (pair_ids, weight))
    routed = jnp.zeros((ROUTED, PT, DL), jnp.bfloat16).at[row_ids.reshape(-1)].set(outs.reshape(-1, PT, DL), mode='drop')
    return (learnability, routed, grad_up, grad_down_t)
```

```python
import jax
import jax.numpy as jnp
from jax import lax
from jax.sharding import Mesh, PartitionSpec as P

ROW = ("x", "zl")
COL = ("y", "core")
DP = ("y", "x", "zl")
CHIPS = ("y", "x", "zl", "zh")
SWAP = [(0, 1), (1, 0)]


def unit_rows(block):
    wide = block.astype(jnp.float32)
    return (wide * lax.rsqrt(jnp.sum(wide * wide, axis=1, keepdims=True) + 1e-06)).astype(
        jnp.bfloat16
    )


def spread(block, axes, count):
    wide = jnp.broadcast_to(block[None], (count,) + block.shape)
    return lax.all_to_all(wide, axes, split_axis=0, concat_axis=0, tiled=True)


def shard_learnability(image, text, sign):
    rows = image.shape[0]
    unit_img = unit_rows(image)
    unit_txt = unit_rows(text)
    own = 10.0 * jnp.sum(unit_img.astype(jnp.float32) * unit_txt.astype(jnp.float32), axis=1) - 5.0
    far_img = spread(unit_img, ROW, 8).reshape(8 * rows, -1)
    far_txt = spread(unit_txt, COL, 8).reshape(8 * rows, -1)
    scores = (
        10.0 * jnp.einsum("rd,kd->rk", far_img, far_txt, preferred_element_type=jnp.float32) - 5.0
    )
    terms = jax.nn.softplus(scores)
    row_part = jnp.sum(terms, axis=1).reshape(8, rows)
    col_part = jnp.sum(terms, axis=0).reshape(4, 2 * rows)
    at = lax.axis_index("x") * 2 + lax.axis_index("zl")
    mine = (jnp.arange(8, dtype=jnp.int32) == at)[:, None]
    row_part = sign * (row_part - jnp.where(mine, 2.0 * own[None, :], 0.0))
    col_part = sign * col_part
    row_send = jnp.broadcast_to(row_part.reshape(8, 1, rows), (8, 4, rows)).reshape(32, rows)
    col_send = jnp.broadcast_to(col_part.reshape(4, 1, 2 * rows), (4, 4, 2 * rows)).reshape(
        16, 2 * rows
    )
    row_recv = lax.all_to_all(
        row_send, ("x", "zl", "core", "zh"), split_axis=0, concat_axis=0, tiled=True
    )
    col_recv = lax.all_to_all(col_send, ("y", "core", "zh"), split_axis=0, concat_axis=0, tiled=True)
    row_sum = jnp.sum(row_recv.reshape(8, 2, 2, rows), axis=(0, 2)).reshape(2 * rows)
    return 0.5 * (row_sum + jnp.sum(col_recv, axis=0))


def join_halves(half):
    other = lax.ppermute(half, "core", SWAP)
    low = lax.axis_index("core") == 0
    return jnp.concatenate([jnp.where(low, half, other), jnp.where(low, other, half)], axis=1)


def local(
    ref_image,
    ref_text,
    learner_image,
    learner_text,
    patches,
    cotangent,
    w_up,
    w_down,
    counts,
    sel_index,
    sel_dest,
):
    core = lax.axis_index("core")
    learner = lax.axis_index("zh") == 1
    pad = ((0, 0), (0, learner_image.shape[1] - ref_image.shape[1]))
    image = jnp.where(learner, learner_image, jnp.pad(ref_image, pad))
    text = jnp.where(learner, learner_text, jnp.pad(ref_text, pad))
    scores = shard_learnability(image, text, jnp.where(learner, 1.0, -1.0))
    rows = image.shape[0]
    learnability = lax.dynamic_slice_in_dim(scores, core * rows, rows)

    slots = sel_index.shape[0]
    patch_rows, half_width = patches.shape[1:]
    count = slots * patch_rows
    live = jnp.arange(slots, dtype=jnp.int32) < counts[0]
    target = sel_dest[:, 0]
    n_dp, cap = 32, 4
    hits = ((target[:, None] == jnp.arange(n_dp, dtype=jnp.int32)[None, :]) & live[:, None]).astype(
        jnp.int32
    )
    rank = jnp.sum((jnp.cumsum(hits, axis=0) - hits) * hits, axis=1)
    bucket = target * cap + rank
    placer = (
        (jnp.arange(n_dp * cap, dtype=jnp.int32)[:, None] == bucket[None, :]) & live[None, :]
    ).astype(jnp.bfloat16)

    half_x = patches[sel_index].reshape(count, half_width)
    half_cot = cotangent[sel_index].reshape(count, half_width)
    wide_x = join_halves(half_x)
    wide_cot = join_halves(half_cot)

    pre = jnp.dot(wide_x, w_up, preferred_element_type=jnp.float32)
    act_full, gelu_back = jax.vjp(jax.nn.gelu, pre)
    act = act_full.astype(jnp.bfloat16)
    part = jnp.dot(act, w_down, preferred_element_type=jnp.float32)
    low = core == 0
    keep = jnp.where(low, part[:, :half_width], part[:, half_width:])
    give = jnp.where(low, part[:, half_width:], part[:, :half_width])
    mixed = keep + lax.ppermute(give, "core", SWAP)
    out = (half_x.astype(jnp.float32) + mixed).astype(jnp.bfloat16)
    boxed = jnp.dot(
        placer, out.reshape(slots, -1), preferred_element_type=jnp.float32
    ).astype(jnp.bfloat16)
    boxed = boxed.reshape(n_dp, cap, patch_rows, half_width)
    routed = lax.all_to_all(boxed, DP, split_axis=0, concat_axis=0, tiled=True)
    routed = routed.reshape(n_dp * cap, patch_rows, half_width)

    back = jnp.einsum("md,fd->mf", wide_cot, w_down, preferred_element_type=jnp.float32)
    grad_pre = gelu_back(back)[0].astype(jnp.bfloat16)

    picked = sel_index[:, None] == jnp.arange(patches.shape[0], dtype=jnp.int32)[None, :]
    score_sel = jnp.sum(jnp.where(picked, scores[None, :], 0.0), axis=1)
    weight = jnp.where(live, jax.nn.sigmoid(score_sel), 0.0)
    weight = jnp.broadcast_to(weight[:, None], (slots, patch_rows)).reshape(count, 1)
    scaled_x = (weight * wide_x.astype(jnp.float32)).astype(jnp.bfloat16)
    scaled_cot = (weight * wide_cot.astype(jnp.float32)).astype(jnp.bfloat16)

    def summed(left, right):
        grad = jnp.einsum("md,mf->df", left, right, preferred_element_type=jnp.float32)
        grad = grad.astype(jnp.bfloat16).reshape(64, 16, grad.shape[1])
        parts = lax.all_to_all(grad, CHIPS, split_axis=0, concat_axis=0, tiled=True)
        return jnp.sum(parts.astype(jnp.float32), axis=0)

    grad_down_t = summed(scaled_cot, act)
    grad_up = summed(scaled_x, grad_pre)
    return (learnability, routed, grad_up, grad_down_t)


def solution(mesh):
    mesh = Mesh(mesh.devices.reshape(4, 4, 2, 2, 2), ("y", "x", "zl", "core", "zh"))
    pairs = P(("y", "x", "zl", "core"), None)
    patch = P(DP, "zh", "core")
    return jax.shard_map(
        local,
        mesh=mesh,
        in_specs=(
            pairs,
            pairs,
            pairs,
            pairs,
            patch,
            patch,
            P(None, "core"),
            P("core", None),
            P(DP),
            P(DP),
            P(DP, None),
        ),
        out_specs=(
            P(("y", "x", "zl", "core")),
            patch,
            P(CHIPS, "core"),
            P(CHIPS, "core"),
        ),
        check_vma=False,
    )
```

```python
import jax
import jax.numpy as jnp
from jax import lax
from jax.sharding import Mesh, PartitionSpec as P

ROW = ("x", "zl")
COL = ("y", "core")
DP = ("y", "x", "zl")
CHIPS = ("y", "x", "zl", "zh")
SWAP = [(0, 1), (1, 0)]


def unit_rows(block):
    wide = block.astype(jnp.float32)
    return (wide * lax.rsqrt(jnp.sum(wide * wide, axis=1, keepdims=True) + 1e-06)).astype(
        jnp.bfloat16
    )


def spread(block, axes, count):
    wide = jnp.broadcast_to(block[None], (count,) + block.shape)
    return lax.all_to_all(wide, axes, split_axis=0, concat_axis=0, tiled=True)


def shard_learnability(image, text, sign):
    rows = image.shape[0]
    unit_img = unit_rows(image)
    unit_txt = unit_rows(text)
    own = 10.0 * jnp.sum(unit_img.astype(jnp.float32) * unit_txt.astype(jnp.float32), axis=1) - 5.0
    far_img = spread(unit_img, ROW, 8).reshape(8 * rows, -1)
    far_txt = spread(unit_txt, COL, 8).reshape(8 * rows, -1)
    scores = (
        10.0 * jnp.einsum("rd,kd->rk", far_img, far_txt, preferred_element_type=jnp.float32) - 5.0
    )
    terms = jax.nn.softplus(scores)
    row_part = jnp.sum(terms, axis=1).reshape(8, rows)
    col_part = jnp.sum(terms, axis=0).reshape(4, 2 * rows)
    at = lax.axis_index("x") * 2 + lax.axis_index("zl")
    mine = (jnp.arange(8, dtype=jnp.int32) == at)[:, None]
    row_part = sign * (row_part - jnp.where(mine, 2.0 * own[None, :], 0.0))
    col_part = sign * col_part
    row_send = jnp.broadcast_to(row_part.reshape(8, 1, rows), (8, 4, rows)).reshape(32, rows)
    col_send = jnp.broadcast_to(col_part.reshape(4, 1, 2 * rows), (4, 4, 2 * rows)).reshape(
        16, 2 * rows
    )
    row_recv = lax.all_to_all(
        row_send, ("x", "zl", "core", "zh"), split_axis=0, concat_axis=0, tiled=True
    )
    col_recv = lax.all_to_all(col_send, ("y", "core", "zh"), split_axis=0, concat_axis=0, tiled=True)
    row_sum = jnp.sum(row_recv.reshape(8, 2, 2, rows), axis=(0, 2)).reshape(2 * rows)
    return 0.5 * (row_sum + jnp.sum(col_recv, axis=0))


def join_halves(half):
    other = lax.ppermute(half, "core", SWAP)
    low = lax.axis_index("core") == 0
    return jnp.concatenate([jnp.where(low, half, other), jnp.where(low, other, half)], axis=1)


ORDER = {"x": "xyz", "y": "yzx", "z": "zxy"}


def shift(block, axis, by):
    if axis == "z":
        at = [(z % 2) * 2 + z // 2 for z in range(4)]
        return lax.ppermute(block, ("zl", "zh"), [(at[z], at[(z + by) % 4]) for z in range(4)])
    return lax.ppermute(block, axis, [(k, (k + by) % 4) for k in range(4)])


def turned(left):
    wide = left.T.reshape(64, 16, left.shape[0])
    here = {
        "x": lax.axis_index("x"),
        "y": lax.axis_index("y"),
        "z": lax.axis_index("zh") * 2 + lax.axis_index("zl"),
    }
    steps = jnp.arange(4, dtype=jnp.int32)

    def ordered(start):
        at = {}
        for place, axis in enumerate(ORDER[start]):
            shape = [1, 1, 1]
            shape[place] = 4
            at[axis] = ((here[axis] + steps) % 4).reshape(shape)
        z = at["z"]
        index = ((at["y"] * 4 + at["x"]) * 2 + z % 2) * 2 + z // 2
        return wide[index.reshape(64)].reshape(4, 256, left.shape[0])

    return ordered


def products(left, right):
    return [
        jnp.dot(left[k], right, preferred_element_type=jnp.float32).astype(jnp.bfloat16)
        for k in range(4)
    ]


def summed(parts):
    for step in range(3):
        totals = []
        for blocks, start in zip(parts, "xyz"):
            axis = ORDER[start][step]
            total = blocks[0].astype(jnp.float32)
            for by in (2, 1, 3):
                total = total + shift(blocks[by], axis, by).astype(jnp.float32)
            totals.append(total)
        if step == 2:
            return totals
        parts = []
        for total in totals:
            rows = total.shape[0] // 4
            narrow = total.astype(jnp.bfloat16)
            parts.append([narrow[k * rows : (k + 1) * rows] for k in range(4)])


def local(
    ref_image,
    ref_text,
    learner_image,
    learner_text,
    patches,
    cotangent,
    w_up,
    w_down,
    counts,
    sel_index,
    sel_dest,
):
    core = lax.axis_index("core")
    learner = lax.axis_index("zh") == 1
    pad = ((0, 0), (0, learner_image.shape[1] - ref_image.shape[1]))
    image = jnp.where(learner, learner_image, jnp.pad(ref_image, pad))
    text = jnp.where(learner, learner_text, jnp.pad(ref_text, pad))
    scores = shard_learnability(image, text, jnp.where(learner, 1.0, -1.0))
    rows = image.shape[0]
    learnability = lax.dynamic_slice_in_dim(scores, core * rows, rows)

    slots = sel_index.shape[0]
    patch_rows, half_width = patches.shape[1:]
    count = slots * patch_rows
    live = jnp.arange(slots, dtype=jnp.int32) < counts[0]
    target = sel_dest[:, 0]
    n_dp, cap = 32, 4
    hits = ((target[:, None] == jnp.arange(n_dp, dtype=jnp.int32)[None, :]) & live[:, None]).astype(
        jnp.int32
    )
    rank = jnp.sum((jnp.cumsum(hits, axis=0) - hits) * hits, axis=1)
    bucket = target * cap + rank
    placer = (
        (jnp.arange(n_dp * cap, dtype=jnp.int32)[:, None] == bucket[None, :]) & live[None, :]
    ).astype(jnp.bfloat16)

    half_x = patches[sel_index].reshape(count, half_width)
    half_cot = cotangent[sel_index].reshape(count, half_width)
    wide_x = join_halves(half_x)
    wide_cot = join_halves(half_cot)

    pre = jnp.dot(wide_x, w_up, preferred_element_type=jnp.float32)
    act_full, gelu_back = jax.vjp(jax.nn.gelu, pre)
    act = act_full.astype(jnp.bfloat16)
    part = jnp.dot(act, w_down, preferred_element_type=jnp.float32)
    low = core == 0
    keep = jnp.where(low, part[:, :half_width], part[:, half_width:])
    give = jnp.where(low, part[:, half_width:], part[:, :half_width])
    mixed = keep + lax.ppermute(give, "core", SWAP)
    out = (half_x.astype(jnp.float32) + mixed).astype(jnp.bfloat16)
    boxed = jnp.dot(
        placer, out.reshape(slots, -1), preferred_element_type=jnp.float32
    ).astype(jnp.bfloat16)
    boxed = boxed.reshape(n_dp, cap, patch_rows, half_width)
    routed = lax.all_to_all(boxed, DP, split_axis=0, concat_axis=0, tiled=True)
    routed = routed.reshape(n_dp * cap, patch_rows, half_width)

    back = jnp.einsum("md,fd->mf", wide_cot, w_down, preferred_element_type=jnp.float32)
    grad_pre = gelu_back(back)[0].astype(jnp.bfloat16)

    picked = sel_index[:, None] == jnp.arange(patches.shape[0], dtype=jnp.int32)[None, :]
    score_sel = jnp.sum(jnp.where(picked, scores[None, :], 0.0), axis=1)
    weight = jnp.where(live, jax.nn.sigmoid(score_sel), 0.0)
    weight = jnp.broadcast_to(weight[:, None], (slots, patch_rows)).reshape(count, 1)
    scaled_x = (weight * wide_x.astype(jnp.float32)).astype(jnp.bfloat16)
    scaled_cot = (weight * wide_cot.astype(jnp.float32)).astype(jnp.bfloat16)

    left_down = turned(scaled_cot)
    left_up = turned(scaled_x)
    width = w_up.shape[1]
    cut_down, cut_up = 1408, 768
    first = products(left_down("x"), act[:, :cut_down])
    second = [
        jnp.concatenate(both, axis=1)
        for both in zip(
            products(left_down("y"), act[:, cut_down:]), products(left_up("y"), grad_pre[:, :cut_up])
        )
    ]
    third = products(left_up("z"), grad_pre[:, cut_up:])
    sums = summed([first, second, third])
    grad_down_t = jnp.concatenate([sums[0], sums[1][:, : width - cut_down]], axis=1)
    grad_up = jnp.concatenate([sums[1][:, width - cut_down :], sums[2]], axis=1)
    return (learnability, routed, grad_up, grad_down_t)


def solution(mesh):
    mesh = Mesh(mesh.devices.reshape(4, 4, 2, 2, 2), ("y", "x", "zl", "core", "zh"))
    pairs = P(("y", "x", "zl", "core"), None)
    patch = P(DP, "zh", "core")
    return jax.shard_map(
        local,
        mesh=mesh,
        in_specs=(
            pairs,
            pairs,
            pairs,
            pairs,
            patch,
            patch,
            P(None, "core"),
            P("core", None),
            P(DP),
            P(DP),
            P(DP, None),
        ),
        out_specs=(
            P(("y", "x", "zl", "core")),
            patch,
            P(CHIPS, "core"),
            P(CHIPS, "core"),
        ),
        check_vma=False,
    )
```

```python
import jax
import jax.numpy as jnp
from jax import lax
from jax.experimental import pallas as pl
from jax.experimental.pallas import tpu as pltpu
from jax.sharding import Mesh, PartitionSpec as P

DP = ("y", "x", "zl")
CHIPS = ("y", "x", "zl", "zh")
SWAP = [(0, 1), (1, 0)]


def unit(rows):
    wide = rows.astype(jnp.float32)
    norm = lax.rsqrt(jnp.sum(wide * wide, axis=1, keepdims=True) + 1e-06)
    return (wide * norm).astype(jnp.bfloat16)


def softplus(value):
    return jnp.maximum(value, 0.0) + jnp.log1p(jnp.exp(-jnp.abs(value)))


def loss_kernel(at, *refs):
    img_refs, txt_refs, out, img, txt = refs[:4], refs[4:8], refs[8], refs[9], refs[10]
    here_y, here_x, here_zl, here_core, learner = (at[k] for k in range(5))
    for k in range(4):
        img[pl.ds(128 * k, 128), :] = unit(img_refs[k][...])
        txt[pl.ds(128 * k, 128), :] = unit(txt_refs[k][...])
    contract = (((1,), (1,)), ((), ()))
    col_sum = jnp.zeros((1, 512), jnp.float32)
    row_sums = []
    for k in range(4):
        scores = (
            10.0
            * lax.dot_general(
                img[pl.ds(128 * k, 128), :], txt[...], contract, preferred_element_type=jnp.float32
            )
            - 5.0
        )
        if k == 0:
            row = lax.broadcasted_iota(jnp.int32, scores.shape, 0) - 64 * here_zl
            col = lax.broadcasted_iota(jnp.int32, scores.shape, 1) - 64 * here_core
            same = (row == col) & (row >= 0) & (row < 64)
            scores = jnp.where(same, -scores, scores)
        terms = softplus(scores)
        col_sum = col_sum + jnp.sum(terms, axis=0, keepdims=True)
        folded = terms[:, :128] + terms[:, 128:256] + terms[:, 256:384] + terms[:, 384:]
        row_sums.append(jnp.sum(folded.T, axis=0, keepdims=True))
    dest = lax.broadcasted_iota(jnp.int32, (128, 128), 0)
    lane = lax.broadcasted_iota(jnp.int32, (1, 128), 1)
    dest_y, dest_x, dest_zl = dest >> 5, (dest >> 3) & 3, (dest >> 2) & 1
    own_half = (lane >> 6) == here_core
    total = jnp.zeros((128, 128), jnp.float32)
    for k in range(4):
        straight = row_sums[k]
        crossed = pltpu.roll(straight, 64, 1)
        for zl in range(2):
            placed = jnp.where(own_half, jnp.where(here_core == zl, straight, crossed), 0.0)
            mine = (dest_y == here_y) & (dest_x == ((here_x + k) & 3)) & (dest_zl == zl)
            total = total + jnp.where(mine, placed, 0.0)
        mine = (dest_y == ((here_y + k) & 3)) & (dest_x == here_x) & (dest_zl == here_zl)
        total = total + jnp.where(mine, col_sum[:, 128 * k : 128 * (k + 1)], 0.0)
    out[...] = jnp.where(learner == 1, 0.5, -0.5) * total


def partial_losses(at, images, texts):
    whole = pl.BlockSpec(memory_space=pltpu.VMEM)
    return pl.pallas_call(
        loss_kernel,
        out_shape=jax.ShapeDtypeStruct((128, 128), jnp.float32),
        in_specs=[pl.BlockSpec(memory_space=pltpu.SMEM)] + [whole] * 8,
        out_specs=whole,
        scratch_shapes=[pltpu.VMEM((512, 1024), jnp.bfloat16)] * 2,
        compiler_params=pltpu.CompilerParams(vmem_limit_bytes=24 << 20),
        cost_estimate=pl.CostEstimate(
            flops=2 * 512 * 512 * 1024, bytes_accessed=2 << 20, transcendentals=2 * 512 * 512
        ),
    )(at, *images, *texts)


def weight_kernel(count, parts, index, learn, weight):
    score = jnp.sum(parts[...], axis=0, keepdims=True)
    learn[...] = jnp.broadcast_to(score, (8, 128))
    slots = index.shape[0]
    picked = index[...] == lax.broadcasted_iota(jnp.int32, (slots, 128), 1)
    chosen = jnp.sum(jnp.where(picked, score, 0.0), axis=1, keepdims=True)
    live = lax.broadcasted_iota(jnp.int32, (slots, 128), 0) < count[0]
    value = jnp.where(live, 1.0 / (1.0 + jnp.exp(-chosen)), 0.0)
    weight[...] = jnp.broadcast_to(value[:, None, :], (slots, 8, 128)).reshape(8 * slots, 128)


def weights(counts, parts, sel_index):
    whole = pl.BlockSpec(memory_space=pltpu.VMEM)
    slots = sel_index.shape[0]
    return pl.pallas_call(
        weight_kernel,
        out_shape=(
            jax.ShapeDtypeStruct((8, 128), jnp.float32),
            jax.ShapeDtypeStruct((8 * slots, 128), jnp.float32),
        ),
        in_specs=[pl.BlockSpec(memory_space=pltpu.SMEM), whole, whole],
        out_specs=(whole, whole),
    )(counts, parts, sel_index[:, None])


def swap(block, axis):
    other = lax.ppermute(block, axis, SWAP)
    low = lax.axis_index(axis) == 0
    return jnp.concatenate([jnp.where(low, block, other), jnp.where(low, other, block)], axis=0)


def around(block, axis):
    return [block] + [shift(block, axis, 4 - by) for by in (1, 2, 3)]


def join_halves(half):
    other = lax.ppermute(half, "core", SWAP)
    low = lax.axis_index("core") == 0
    return jnp.concatenate([jnp.where(low, half, other), jnp.where(low, other, half)], axis=1)


ORDER = {"x": "xyz", "y": "yzx", "z": "zxy"}


def shift(block, axis, by):
    if axis == "z":
        at = [(z % 2) * 2 + z // 2 for z in range(4)]
        return lax.ppermute(block, ("zl", "zh"), [(at[z], at[(z + by) % 4]) for z in range(4)])
    return lax.ppermute(block, axis, [(k, (k + by) % 4) for k in range(4)])


def turned(left):
    wide = left.T.reshape(64, 16, left.shape[0])
    here = {
        "x": lax.axis_index("x"),
        "y": lax.axis_index("y"),
        "z": lax.axis_index("zh") * 2 + lax.axis_index("zl"),
    }
    steps = jnp.arange(4, dtype=jnp.int32)

    def ordered(start):
        at = {}
        for place, axis in enumerate(ORDER[start]):
            shape = [1, 1, 1]
            shape[place] = 4
            at[axis] = ((here[axis] + steps) % 4).reshape(shape)
        z = at["z"]
        index = ((at["y"] * 4 + at["x"]) * 2 + z % 2) * 2 + z // 2
        return wide[index.reshape(64)].reshape(4, 256, left.shape[0])

    return ordered


def products(left, right):
    return [
        jnp.dot(left[k], right, preferred_element_type=jnp.float32).astype(jnp.bfloat16)
        for k in range(4)
    ]


def summed(parts):
    for step in range(3):
        totals = []
        for blocks, start in zip(parts, "xyz"):
            axis = ORDER[start][step]
            total = blocks[0].astype(jnp.float32)
            for by in (2, 1, 3):
                total = total + shift(blocks[by], axis, by).astype(jnp.float32)
            totals.append(total)
        if step == 2:
            return totals
        parts = []
        for total in totals:
            rows = total.shape[0] // 4
            narrow = total.astype(jnp.bfloat16)
            parts.append([narrow[k * rows : (k + 1) * rows] for k in range(4)])


def local(
    ref_image,
    ref_text,
    learner_image,
    learner_text,
    patches,
    cotangent,
    w_up,
    w_down,
    counts,
    sel_index,
    sel_dest,
):
    core = lax.axis_index("core")
    learner = lax.axis_index("zh") == 1
    pad = ((0, 0), (0, learner_image.shape[1] - ref_image.shape[1]))
    image = jnp.where(learner, learner_image, jnp.pad(ref_image, pad))
    text = jnp.where(learner, learner_text, jnp.pad(ref_text, pad))
    at = jnp.stack([lax.axis_index(name) for name in ("y", "x", "zl", "core", "zh")]).astype(
        jnp.int32
    )
    images = around(swap(image, "zl"), "x")
    texts = around(swap(text, "core"), "y")
    parts = partial_losses(at, images, texts)
    parts = lax.all_to_all(
        parts, ("y", "x", "zl", "core", "zh"), split_axis=0, concat_axis=0, tiled=True
    )
    scores, weight = weights(counts, parts, sel_index)
    rows = image.shape[0]
    learnability = lax.dynamic_slice_in_dim(scores[0], core * rows, rows)

    slots = sel_index.shape[0]
    patch_rows, half_width = patches.shape[1:]
    count = slots * patch_rows
    live = jnp.arange(slots, dtype=jnp.int32) < counts[0]
    target = sel_dest[:, 0]
    n_dp, cap = 32, 4
    hits = ((target[:, None] == jnp.arange(n_dp, dtype=jnp.int32)[None, :]) & live[:, None]).astype(
        jnp.int32
    )
    rank = jnp.sum((jnp.cumsum(hits, axis=0) - hits) * hits, axis=1)
    bucket = target * cap + rank
    placer = (
        (jnp.arange(n_dp * cap, dtype=jnp.int32)[:, None] == bucket[None, :]) & live[None, :]
    ).astype(jnp.bfloat16)

    half_x = patches[sel_index].reshape(count, half_width)
    half_cot = cotangent[sel_index].reshape(count, half_width)
    wide_x = join_halves(half_x)
    wide_cot = join_halves(half_cot)

    pre = jnp.dot(wide_x, w_up, preferred_element_type=jnp.float32)
    act_full, gelu_back = jax.vjp(jax.nn.gelu, pre)
    act = act_full.astype(jnp.bfloat16)
    part = jnp.dot(act, w_down, preferred_element_type=jnp.float32)
    low = core == 0
    keep = jnp.where(low, part[:, :half_width], part[:, half_width:])
    give = jnp.where(low, part[:, half_width:], part[:, :half_width])
    mixed = keep + lax.ppermute(give, "core", SWAP)
    out = (half_x.astype(jnp.float32) + mixed).astype(jnp.bfloat16)
    boxed = jnp.dot(
        placer, out.reshape(slots, -1), preferred_element_type=jnp.float32
    ).astype(jnp.bfloat16)
    boxed = boxed.reshape(n_dp, cap, patch_rows, half_width)
    routed = lax.all_to_all(boxed, DP, split_axis=0, concat_axis=0, tiled=True)
    routed = routed.reshape(n_dp * cap, patch_rows, half_width)

    back = jnp.einsum("md,fd->mf", wide_cot, w_down, preferred_element_type=jnp.float32)
    grad_pre = gelu_back(back)[0].astype(jnp.bfloat16)

    left_down = turned(wide_cot)
    left_up = turned(wide_x)
    act = (weight[:, :1] * act.astype(jnp.float32)).astype(jnp.bfloat16)
    grad_pre = (weight[:, :1] * grad_pre.astype(jnp.float32)).astype(jnp.bfloat16)
    width = w_up.shape[1]
    cut_down, cut_up = 1408, 768
    first = products(left_down("x"), act[:, :cut_down])
    second = [
        jnp.concatenate(both, axis=1)
        for both in zip(
            products(left_down("y"), act[:, cut_down:]), products(left_up("y"), grad_pre[:, :cut_up])
        )
    ]
    third = products(left_up("z"), grad_pre[:, cut_up:])
    sums = summed([first, second, third])
    grad_down_t = jnp.concatenate([sums[0], sums[1][:, : width - cut_down]], axis=1)
    grad_up = jnp.concatenate([sums[1][:, width - cut_down :], sums[2]], axis=1)
    return (learnability, routed, grad_up, grad_down_t)


def solution(mesh):
    mesh = Mesh(mesh.devices.reshape(4, 4, 2, 2, 2), ("y", "x", "zl", "core", "zh"))
    pairs = P(("y", "x", "zl", "core"), None)
    patch = P(DP, "zh", "core")
    return jax.shard_map(
        local,
        mesh=mesh,
        in_specs=(
            pairs,
            pairs,
            pairs,
            pairs,
            patch,
            patch,
            P(None, "core"),
            P("core", None),
            P(DP),
            P(DP),
            P(DP, None),
        ),
        out_specs=(
            P(("y", "x", "zl", "core")),
            patch,
            P(CHIPS, "core"),
            P(CHIPS, "core"),
        ),
        check_vma=False,
    )
```

```python
import functools

import jax
import jax.numpy as jnp
from jax import lax
from jax.experimental import pallas as pl
from jax.experimental.pallas import tpu as pltpu
from jax.sharding import Mesh, PartitionSpec as P

DP = ("y", "x", "zl")
CHIPS = ("y", "x", "zl", "zh")
SWAP = [(0, 1), (1, 0)]


def unit(rows):
    wide = rows.astype(jnp.float32)
    norm = lax.rsqrt(jnp.sum(wide * wide, axis=1, keepdims=True) + 1e-06)
    return (wide * norm).astype(jnp.bfloat16)


def softplus(value):
    return jnp.maximum(value, 0.0) + jnp.log1p(jnp.exp(-jnp.abs(value)))


def loss_kernel(at, *refs):
    img_refs, txt_refs, txt_other, (out, img, txt) = refs[:4], refs[4:8], refs[8], refs[-3:]
    here_y, here_x, here_zl, here_core, learner = (at[k] for k in range(5))
    for k in range(4):
        img[pl.ds(128 * k, 128), :] = unit(img_refs[k][...])
        own = pl.multiple_of(128 * k + 64 * here_core, 64)
        txt[pl.ds(own, 64), :] = unit(txt_refs[k][...])
        other = pl.multiple_of(128 * k + 64 * (1 - here_core), 64)
        txt[pl.ds(other, 64), :] = unit(txt_other[pl.ds(64 * k, 64), :])
    contract = (((1,), (1,)), ((), ()))
    col_sum = jnp.zeros((1, 512), jnp.float32)
    row_sums = []
    for k in range(4):
        scores = (
            10.0
            * lax.dot_general(
                img[pl.ds(128 * k, 128), :], txt[...], contract, preferred_element_type=jnp.float32
            )
            - 5.0
        )
        if k == 0:
            row = lax.broadcasted_iota(jnp.int32, scores.shape, 0) - 64 * here_zl
            col = lax.broadcasted_iota(jnp.int32, scores.shape, 1) - 64 * here_core
            same = (row == col) & (row >= 0) & (row < 64)
            scores = jnp.where(same, -scores, scores)
        terms = softplus(scores)
        col_sum = col_sum + jnp.sum(terms, axis=0, keepdims=True)
        folded = terms[:, :128] + terms[:, 128:256] + terms[:, 256:384] + terms[:, 384:]
        row_sums.append(jnp.sum(folded.T, axis=0, keepdims=True))
    dest = lax.broadcasted_iota(jnp.int32, (128, 128), 0)
    lane = lax.broadcasted_iota(jnp.int32, (1, 128), 1)
    dest_y, dest_x, dest_zl = dest >> 5, (dest >> 3) & 3, (dest >> 2) & 1
    own_half = (lane >> 6) == here_core
    total = jnp.zeros((128, 128), jnp.float32)
    for k in range(4):
        straight = row_sums[k]
        crossed = pltpu.roll(straight, 64, 1)
        for zl in range(2):
            placed = jnp.where(own_half, jnp.where(here_core == zl, straight, crossed), 0.0)
            mine = (dest_y == here_y) & (dest_x == ((here_x + k) & 3)) & (dest_zl == zl)
            total = total + jnp.where(mine, placed, 0.0)
        mine = (dest_y == ((here_y + k) & 3)) & (dest_x == here_x) & (dest_zl == here_zl)
        total = total + jnp.where(mine, col_sum[:, 128 * k : 128 * (k + 1)], 0.0)
    out[...] = jnp.where(learner == 1, 0.5, -0.5) * total


def partial_losses(at, images, texts, texts_other, ready):
    whole = pl.BlockSpec(memory_space=pltpu.VMEM)
    return pl.pallas_call(
        loss_kernel,
        out_shape=jax.ShapeDtypeStruct((128, 128), jnp.float32),
        in_specs=[pl.BlockSpec(memory_space=pltpu.SMEM)]
        + [whole] * 9
        + [pl.BlockSpec(memory_space=pl.ANY)] * len(ready),
        out_specs=whole,
        scratch_shapes=[pltpu.VMEM((512, 1024), jnp.bfloat16)] * 2,
        compiler_params=pltpu.CompilerParams(vmem_limit_bytes=24 << 20),
        cost_estimate=pl.CostEstimate(
            flops=2 * 512 * 512 * 1024, bytes_accessed=2 << 20, transcendentals=2 * 512 * 512
        ),
    )(at, *images, *texts, texts_other, *ready)


def weight_kernel(count, parts, index, *refs):
    learn, weight = refs[-2:]
    score = jnp.sum(parts[...], axis=0, keepdims=True)
    learn[...] = jnp.broadcast_to(score, (8, 128))
    slots = index.shape[0]
    picked = index[...] == lax.broadcasted_iota(jnp.int32, (slots, 128), 1)
    chosen = jnp.sum(jnp.where(picked, score, 0.0), axis=1, keepdims=True)
    live = lax.broadcasted_iota(jnp.int32, (slots, 128), 0) < count[0]
    value = jnp.where(live, 1.0 / (1.0 + jnp.exp(-chosen)), 0.0)
    weight[...] = jnp.broadcast_to(value[:, None, :], (slots, 8, 128)).reshape(8 * slots, 128)


def weights(counts, parts, sel_index, ready):
    whole = pl.BlockSpec(memory_space=pltpu.VMEM)
    slots = sel_index.shape[0]
    return pl.pallas_call(
        weight_kernel,
        out_shape=(
            jax.ShapeDtypeStruct((8, 128), jnp.float32),
            jax.ShapeDtypeStruct((8 * slots, 128), jnp.float32),
        ),
        in_specs=[pl.BlockSpec(memory_space=pltpu.SMEM), whole, whole]
        + [pl.BlockSpec(memory_space=pl.ANY)] * len(ready),
        out_specs=(whole, whole),
    )(counts, parts, sel_index[:, None], *ready)


def swap(block, axis):
    other = lax.ppermute(block, axis, SWAP)
    low = lax.axis_index(axis) == 0
    return jnp.concatenate([jnp.where(low, block, other), jnp.where(low, other, block)], axis=0)


def around(block, axis):
    return [block] + [shift(block, axis, 4 - by) for by in (1, 2, 3)]


def join_halves(half):
    other = lax.ppermute(half, "core", SWAP)
    low = lax.axis_index("core") == 0
    return jnp.concatenate([jnp.where(low, half, other), jnp.where(low, other, half)], axis=1)


ORDER = {"x": "xyz", "y": "yzx", "z": "zxy"}


def shift(block, axis, by):
    if axis == "z":
        at = [(z % 2) * 2 + z // 2 for z in range(4)]
        return lax.ppermute(block, ("zl", "zh"), [(at[z], at[(z + by) % 4]) for z in range(4)])
    return lax.ppermute(block, axis, [(k, (k + by) % 4) for k in range(4)])


def turned(left):
    wide = left.T.reshape(64, 16, left.shape[0])
    here = {
        "x": lax.axis_index("x"),
        "y": lax.axis_index("y"),
        "z": lax.axis_index("zh") * 2 + lax.axis_index("zl"),
    }
    steps = jnp.arange(4, dtype=jnp.int32)

    def ordered(start):
        at = {}
        for place, axis in enumerate(ORDER[start]):
            shape = [1, 1, 1]
            shape[place] = 4
            at[axis] = ((here[axis] + steps) % 4).reshape(shape)
        z = at["z"]
        index = ((at["y"] * 4 + at["x"]) * 2 + z % 2) * 2 + z // 2
        return wide[index.reshape(64)].reshape(4, 256, left.shape[0])

    return ordered


def product_kernel(pieces, weight, *refs):
    count = len(pieces)
    lefts, rights = refs[:count], refs[count : 2 * count]
    outs, scaled = refs[2 * count : 2 * count + 4], refs[-1]
    rows = weight[...]
    done = 0
    for left, right, (first, last) in zip(lefts, rights, pieces):
        for at in range(first, last, 128):
            part = right[:, at : at + 128].astype(jnp.float32) * rows
            scaled[:, done + at - first : done + at - first + 128] = part.astype(jnp.bfloat16)
        for k in range(4):
            for at in range(done, done + last - first, 256):
                end = min(at + 256, done + last - first)
                product = jnp.dot(
                    left[k], scaled[:, at:end], preferred_element_type=jnp.float32
                )
                outs[k][:, at:end] = product.astype(jnp.bfloat16)
        done += last - first


def products(weight, pieces):
    lefts, rights = [p[0] for p in pieces], [p[1] for p in pieces]
    cuts = tuple((p[2], p[3]) for p in pieces)
    width = sum(last - first for first, last in cuts)
    rows, depth = lefts[0].shape[1:]
    whole = pl.BlockSpec(memory_space=pltpu.VMEM)
    return pl.pallas_call(
        functools.partial(product_kernel, cuts),
        out_shape=[jax.ShapeDtypeStruct((rows, width), jnp.bfloat16)] * 4,
        in_specs=[whole] * (1 + 2 * len(pieces)),
        out_specs=[whole] * 4,
        scratch_shapes=[pltpu.VMEM((depth, width), jnp.bfloat16)],
        compiler_params=pltpu.CompilerParams(vmem_limit_bytes=32 << 20),
        cost_estimate=pl.CostEstimate(
            flops=8 * rows * depth * width, bytes_accessed=8 << 20, transcendentals=0
        ),
    )(weight, *lefts, *rights)


def sum_kernel(*refs):
    outs = refs[-4:]
    total = refs[0][...].astype(jnp.float32)
    for ref in refs[1:4]:
        total = total + ref[...].astype(jnp.float32)
    rows = outs[0].shape[0]
    for k in range(4):
        outs[k][...] = total[k * rows : (k + 1) * rows].astype(jnp.bfloat16)


def sum_blocks(blocks, ready):
    rows, width = blocks[0].shape
    whole = pl.BlockSpec(memory_space=pltpu.VMEM)
    return pl.pallas_call(
        sum_kernel,
        out_shape=[jax.ShapeDtypeStruct((rows // 4, width), jnp.bfloat16)] * 4,
        in_specs=[whole] * 4 + [pl.BlockSpec(memory_space=pl.ANY)] * len(ready),
        out_specs=[whole] * 4,
        compiler_params=pltpu.CompilerParams(vmem_limit_bytes=16 << 20),
    )(*blocks, *ready)


def last_kernel(cut_down, cut_up, *refs):
    down, up = refs[-2:]
    sums = []
    for part in range(3):
        total = refs[4 * part][...].astype(jnp.float32)
        for ref in refs[4 * part + 1 : 4 * part + 4]:
            total = total + ref[...].astype(jnp.float32)
        sums.append(total)
    rest = down.shape[1] - cut_down
    down[:, :cut_down] = sums[0]
    down[:, cut_down:] = sums[1][:, :rest]
    up[:, :cut_up] = sums[1][:, rest:]
    up[:, cut_up:] = sums[2]


def exchanged(blocks, axis):
    return [blocks[0]] + [shift(blocks[by], axis, by) for by in (1, 3, 2)]


def summed(parts, ready, cut_down, cut_up, width):
    for step in range(2):
        received = [
            exchanged(blocks, ORDER[start][step]) for blocks, start in zip(parts, "xyz")
        ]
        parts = [
            sum_blocks(blocks, ready if step == 0 and part == 2 else [])
            for part, blocks in enumerate(received)
        ]
    received = [exchanged(blocks, ORDER[start][2]) for blocks, start in zip(parts, "xyz")]
    whole = pl.BlockSpec(memory_space=pltpu.VMEM)
    return pl.pallas_call(
        functools.partial(last_kernel, cut_down, cut_up),
        out_shape=[jax.ShapeDtypeStruct((16, width), jnp.float32)] * 2,
        in_specs=[whole] * 12,
        out_specs=[whole] * 2,
    )(*[block for blocks in received for block in blocks])


def local(
    ref_image,
    ref_text,
    learner_image,
    learner_text,
    patches,
    cotangent,
    w_up,
    w_down,
    counts,
    sel_index,
    sel_dest,
):
    core = lax.axis_index("core")
    learner = lax.axis_index("zh") == 1
    pad = ((0, 0), (0, learner_image.shape[1] - ref_image.shape[1]))
    image = jnp.where(learner, learner_image, jnp.pad(ref_image, pad))
    text = jnp.where(learner, learner_text, jnp.pad(ref_text, pad))
    at = jnp.stack([lax.axis_index(name) for name in ("y", "x", "zl", "core", "zh")]).astype(
        jnp.int32
    )
    texts = around(text, "y")
    texts_other = lax.ppermute(jnp.concatenate(texts, axis=0), "core", SWAP)
    images = around(swap(image, "zl"), "x")

    slots = sel_index.shape[0]
    patch_rows, half_width = patches.shape[1:]
    count = slots * patch_rows
    live = jnp.arange(slots, dtype=jnp.int32) < counts[0]
    target = sel_dest[:, 0]
    n_dp, cap = 32, 4
    hits = ((target[:, None] == jnp.arange(n_dp, dtype=jnp.int32)[None, :]) & live[:, None]).astype(
        jnp.int32
    )
    rank = jnp.sum((jnp.cumsum(hits, axis=0) - hits) * hits, axis=1)
    bucket = target * cap + rank
    placer = (
        (jnp.arange(n_dp * cap, dtype=jnp.int32)[:, None] == bucket[None, :]) & live[None, :]
    ).astype(jnp.bfloat16)

    half_x = patches[sel_index].reshape(count, half_width)
    half_cot = cotangent[sel_index].reshape(count, half_width)
    wide_x = join_halves(half_x)
    wide_cot = join_halves(half_cot)

    pre = jnp.dot(wide_x, w_up, preferred_element_type=jnp.float32)
    act_full, gelu_back = jax.vjp(jax.nn.gelu, pre)
    act = act_full.astype(jnp.bfloat16)
    left_down, left_up = turned(wide_cot), turned(wide_x)
    left_down = {axis: left_down(axis) for axis in "xy"}
    left_up = {axis: left_up(axis) for axis in "yz"}
    parts = partial_losses(
        at, images, texts, texts_other, [act, *left_down.values(), *left_up.values()]
    )
    parts = lax.all_to_all(
        parts, ("y", "x", "zl", "core", "zh"), split_axis=0, concat_axis=0, tiled=True
    )
    part = jnp.dot(act, w_down, preferred_element_type=jnp.float32)
    low = core == 0
    keep = jnp.where(low, part[:, :half_width], part[:, half_width:])
    give = jnp.where(low, part[:, half_width:], part[:, :half_width])
    mixed = keep + lax.ppermute(give, "core", SWAP)
    out = (half_x.astype(jnp.float32) + mixed).astype(jnp.bfloat16)
    boxed = jnp.dot(
        placer, out.reshape(slots, -1), preferred_element_type=jnp.float32
    ).astype(jnp.bfloat16)
    boxed = boxed.reshape(n_dp, cap, patch_rows, half_width)
    back = jnp.einsum("md,fd->mf", wide_cot, w_down, preferred_element_type=jnp.float32)
    grad_pre = gelu_back(back)[0].astype(jnp.bfloat16)

    scores, weight = weights(counts, parts, sel_index, [boxed, grad_pre])
    rows = image.shape[0]
    learnability = lax.dynamic_slice_in_dim(scores[0], core * rows, rows)
    routed = lax.all_to_all(boxed, DP, split_axis=0, concat_axis=0, tiled=True)
    routed = routed.reshape(n_dp * cap, patch_rows, half_width)

    width = w_up.shape[1]
    cut_down, cut_up = 1408, 768
    blocks = [
        products(weight, [(left_down["x"], act, 0, cut_down)]),
        products(
            weight,
            [(left_down["y"], act, cut_down, width), (left_up["y"], grad_pre, 0, cut_up)],
        ),
        products(weight, [(left_up["z"], grad_pre, cut_up, width)]),
    ]
    grad_down_t, grad_up = summed(blocks, [routed], cut_down, cut_up, width)
    return (learnability, routed, grad_up, grad_down_t)


def solution(mesh):
    mesh = Mesh(mesh.devices.reshape(4, 4, 2, 2, 2), ("y", "x", "zl", "core", "zh"))
    pairs = P(("y", "x", "zl", "core"), None)
    patch = P(DP, "zh", "core")
    return jax.shard_map(
        local,
        mesh=mesh,
        in_specs=(
            pairs,
            pairs,
            pairs,
            pairs,
            patch,
            patch,
            P(None, "core"),
            P("core", None),
            P(DP),
            P(DP),
            P(DP, None),
        ),
        out_specs=(
            P(("y", "x", "zl", "core")),
            patch,
            P(CHIPS, "core"),
            P(CHIPS, "core"),
        ),
        check_vma=False,
    )
```

```python
import functools
import math

import jax
import jax.numpy as jnp
from jax import lax
from jax.experimental import pallas as pl
from jax.experimental.pallas import tpu as pltpu
from jax.sharding import Mesh, PartitionSpec as P

DP = ("y", "x", "zl")
CHIPS = ("y", "x", "zl", "zh")
SWAP = [(0, 1), (1, 0)]
ORDER = {"x": "xyz", "y": "yzx", "z": "zxy"}
WHOLE = pl.BlockSpec(memory_space=pltpu.VMEM)
SCALARS = pl.BlockSpec(memory_space=pltpu.SMEM)
UNREAD = pl.BlockSpec(memory_space=pl.ANY)
LIGHT = pl.CostEstimate(flops=1 << 20, bytes_accessed=1 << 16, transcendentals=0)


def unit(rows):
    wide = rows.astype(jnp.float32)
    norm = lax.rsqrt(jnp.sum(wide * wide, axis=1, keepdims=True) + 1e-06)
    return (wide * norm).astype(jnp.bfloat16)


def softplus(value):
    return jnp.maximum(value, 0.0) + jnp.log1p(jnp.exp(-jnp.abs(value)))


def loss_kernel(at, *refs):
    img_refs, txt_refs, txt_other, index = refs[:4], refs[4:8], refs[8], refs[9]
    out, index_out, img, txt = refs[-4:]
    index_out[...] = index[...]
    here_y, here_x, here_zl, here_core, learner = (at[k] for k in range(5))
    for k in range(4):
        img[pl.ds(128 * k, 128), :] = unit(img_refs[k][...])
        own = pl.multiple_of(128 * k + 64 * here_core, 64)
        txt[pl.ds(own, 64), :] = unit(txt_refs[k][...])
        other = pl.multiple_of(128 * k + 64 * (1 - here_core), 64)
        txt[pl.ds(other, 64), :] = unit(txt_other[pl.ds(64 * k, 64), :])
    contract = (((1,), (1,)), ((), ()))
    col_sum = jnp.zeros((1, 512), jnp.float32)
    row_sums = []
    for k in range(4):
        scores = (
            10.0
            * lax.dot_general(
                img[pl.ds(128 * k, 128), :], txt[...], contract, preferred_element_type=jnp.float32
            )
            - 5.0
        )
        if k == 0:
            row = lax.broadcasted_iota(jnp.int32, scores.shape, 0) - 64 * here_zl
            col = lax.broadcasted_iota(jnp.int32, scores.shape, 1) - 64 * here_core
            same = (row == col) & (row >= 0) & (row < 64)
            scores = jnp.where(same, -scores, scores)
        terms = softplus(scores)
        col_sum = col_sum + jnp.sum(terms, axis=0, keepdims=True)
        folded = terms[:, :128] + terms[:, 128:256] + terms[:, 256:384] + terms[:, 384:]
        row_sums.append(jnp.sum(folded.T, axis=0, keepdims=True))
    dest = lax.broadcasted_iota(jnp.int32, (128, 128), 0)
    lane = lax.broadcasted_iota(jnp.int32, (1, 128), 1)
    dest_y, dest_x, dest_zl = dest >> 5, (dest >> 3) & 3, (dest >> 2) & 1
    own_half = (lane >> 6) == here_core
    total = jnp.zeros((128, 128), jnp.float32)
    for k in range(4):
        straight = row_sums[k]
        crossed = pltpu.roll(straight, 64, 1)
        for zl in range(2):
            placed = jnp.where(own_half, jnp.where(here_core == zl, straight, crossed), 0.0)
            mine = (dest_y == here_y) & (dest_x == ((here_x + k) & 3)) & (dest_zl == zl)
            total = total + jnp.where(mine, placed, 0.0)
        mine = (dest_y == ((here_y + k) & 3)) & (dest_x == here_x) & (dest_zl == here_zl)
        total = total + jnp.where(mine, col_sum[:, 128 * k : 128 * (k + 1)], 0.0)
    out[...] = jnp.where(learner == 1, 0.5, -0.5) * total


def partial_losses(at, images, texts, texts_other, index, ready):
    return pl.pallas_call(
        loss_kernel,
        out_shape=(
            jax.ShapeDtypeStruct((128, 128), jnp.float32),
            jax.ShapeDtypeStruct(index.shape, jnp.int32),
        ),
        in_specs=[SCALARS] + [WHOLE] * 10 + [UNREAD] * len(ready),
        out_specs=(WHOLE, WHOLE),
        scratch_shapes=[pltpu.VMEM((512, 1024), jnp.bfloat16)] * 2,
        compiler_params=pltpu.CompilerParams(vmem_limit_bytes=12 << 20),
        cost_estimate=LIGHT,
    )(at, *images, *texts, texts_other, index, *ready)


def weight_kernel(count, parts, index, *refs):
    learn, weight = refs[-2:]
    score = jnp.sum(parts[...], axis=0, keepdims=True)
    learn[...] = jnp.broadcast_to(score, (8, 128))
    slots = index.shape[0]
    picked = index[...] == lax.broadcasted_iota(jnp.int32, (slots, 128), 1)
    chosen = jnp.sum(jnp.where(picked, score, 0.0), axis=1, keepdims=True)
    live = lax.broadcasted_iota(jnp.int32, (slots, 128), 0) < count[0]
    value = jnp.where(live, 1.0 / (1.0 + jnp.exp(-chosen)), 0.0)
    weight[...] = jnp.broadcast_to(value[:, None, :], (slots, 8, 128)).reshape(8 * slots, 128)


def weights(counts, parts, index, ready):
    slots = index.shape[0]
    return pl.pallas_call(
        weight_kernel,
        out_shape=(
            jax.ShapeDtypeStruct((8, 128), jnp.float32),
            jax.ShapeDtypeStruct((8 * slots, 128), jnp.float32),
        ),
        in_specs=[SCALARS, WHOLE, WHOLE] + [UNREAD] * len(ready),
        out_specs=(WHOLE, WHOLE),
        cost_estimate=LIGHT,
    )(counts, parts, index, *ready)


def pair_kernel(at, own, other, index, pair, index_out):
    pair[pl.ds(pl.multiple_of(64 * at[2], 64), 64), :] = own[...]
    pair[pl.ds(pl.multiple_of(64 * (1 - at[2]), 64), 64), :] = other[...]
    index_out[...] = index[...]


def pair_rows(at, own, other, index):
    rows, width = own.shape
    return pl.pallas_call(
        pair_kernel,
        out_shape=(
            jax.ShapeDtypeStruct((2 * rows, width), own.dtype),
            jax.ShapeDtypeStruct(index.shape, jnp.int32),
        ),
        in_specs=[SCALARS, WHOLE, WHOLE, WHOLE],
        out_specs=(WHOLE, WHOLE),
        cost_estimate=LIGHT,
    )(at, own, other, index)


def half(ref, axis, which, size):
    start = pl.multiple_of(which * size, size)
    return ref[pl.ds(start, size), :] if axis == 0 else ref[:, pl.ds(start, size)]


def up_kernel(at, mine, other, w_up, act, slope):
    size = mine.shape[1]
    pre = jnp.dot(mine[...], half(w_up, 0, at[3], size), preferred_element_type=jnp.float32)
    pre = pre + jnp.dot(
        other[...], half(w_up, 0, 1 - at[3], size), preferred_element_type=jnp.float32
    )
    scale = math.sqrt(2.0 / math.pi)
    square = pre * pre
    tanh = jnp.tanh(scale * pre * (1.0 + 0.044715 * square))
    gate = 0.5 * (1.0 + tanh)
    act[...] = (pre * gate).astype(jnp.bfloat16)
    bend = 0.5 * pre * (1.0 - tanh * tanh) * (scale * (1.0 + 3 * 0.044715 * square))
    slope[...] = (gate + bend).astype(jnp.bfloat16)


def up(at, mine, other, w_up):
    rows, size = mine.shape
    width, tile = w_up.shape[1], 512
    fixed = pl.BlockSpec((rows, size), lambda n: (0, 0))
    out = pl.BlockSpec((rows, tile), lambda n: (0, n))
    return pl.pallas_call(
        up_kernel,
        grid=(width // tile,),
        out_shape=[jax.ShapeDtypeStruct((rows, width), jnp.bfloat16)] * 2,
        in_specs=[SCALARS, fixed, fixed, pl.BlockSpec((2 * size, tile), lambda n: (0, n))],
        out_specs=[out, out],
        compiler_params=pltpu.CompilerParams(vmem_limit_bytes=16 << 20),
        cost_estimate=LIGHT,
    )(at, mine, other, w_up)


def back_kernel(at, mine, other, w_down, slope, out):
    size = mine.shape[1]
    contract = (((1,), (1,)), ((), ()))
    back = lax.dot_general(
        mine[...], half(w_down, 1, at[3], size), contract, preferred_element_type=jnp.float32
    )
    back = back + lax.dot_general(
        other[...], half(w_down, 1, 1 - at[3], size), contract, preferred_element_type=jnp.float32
    )
    out[...] = (back * slope[...].astype(jnp.float32)).astype(jnp.bfloat16)


def back(at, mine, other, w_down, slope):
    rows, size = mine.shape
    width, tile = w_down.shape[0], 512
    fixed = pl.BlockSpec((rows, size), lambda n: (0, 0))
    out = pl.BlockSpec((rows, tile), lambda n: (0, n))
    return pl.pallas_call(
        back_kernel,
        grid=(width // tile,),
        out_shape=jax.ShapeDtypeStruct((rows, width), jnp.bfloat16),
        in_specs=[SCALARS, fixed, fixed, pl.BlockSpec((tile, 2 * size), lambda n: (n, 0)), out],
        out_specs=out,
        compiler_params=pltpu.CompilerParams(vmem_limit_bytes=16 << 20),
        cost_estimate=LIGHT,
    )(at, mine, other, w_down, slope)


def turn_kernel(at, mine, other, out):
    blocks = out.shape[0] // 2
    out[pl.ds(at[3] * blocks, blocks)] = mine[...].T.reshape((blocks,) + out.shape[1:])
    out[pl.ds((1 - at[3]) * blocks, blocks)] = other[...].T.reshape((blocks,) + out.shape[1:])


def turn(at, mine, other):
    rows, size = mine.shape
    return pl.pallas_call(
        turn_kernel,
        out_shape=jax.ShapeDtypeStruct((2 * size // 16, 16, rows), mine.dtype),
        in_specs=[SCALARS, WHOLE, WHOLE],
        out_specs=WHOLE,
        compiler_params=pltpu.CompilerParams(vmem_limit_bytes=12 << 20),
        cost_estimate=LIGHT,
    )(at, mine, other)


def down_kernel(at, act, w_down, *refs):
    keep, give = refs[-2:]
    size = keep.shape[1]
    keep[...] = jnp.dot(
        act[...], half(w_down, 1, at[3], size), preferred_element_type=jnp.float32
    )
    give[...] = jnp.dot(
        act[...], half(w_down, 1, 1 - at[3], size), preferred_element_type=jnp.float32
    )


def down(at, act, w_down, ready):
    rows, size = act.shape[0], w_down.shape[1] // 2
    return pl.pallas_call(
        down_kernel,
        out_shape=[jax.ShapeDtypeStruct((rows, size), jnp.float32)] * 2,
        in_specs=[SCALARS, WHOLE, WHOLE] + [UNREAD] * len(ready),
        out_specs=[WHOLE, WHOLE],
        compiler_params=pltpu.CompilerParams(vmem_limit_bytes=20 << 20),
        cost_estimate=LIGHT,
    )(at, act, w_down, *ready)


def place_kernel(count, target_col, target_row, own, keep, got, *refs):
    out = refs[-1]
    slots, rows = target_col.shape[0], own.shape[0]
    each = rows // slots
    out_rows = (own[...].astype(jnp.float32) + keep[...] + got[...]).astype(jnp.bfloat16)
    slot = lax.broadcasted_iota(jnp.int32, (slots, slots), 0)
    before = lax.broadcasted_iota(jnp.int32, (slots, slots), 1)
    same = (target_row[...] == target_col[...]) & (before < slot)
    rank = jnp.sum(same.astype(jnp.int32), axis=1, keepdims=True)
    live = lax.broadcasted_iota(jnp.int32, (slots, 1), 0) < count[0]
    first = jnp.where(live, each * (4 * target_col[...] + rank), -each)
    lane = lax.broadcasted_iota(jnp.int32, (slots, rows), 1)
    mine = (lane // each) == lax.broadcasted_iota(jnp.int32, (slots, rows), 0)
    goes = jnp.sum(jnp.where(mine, first + lane % each, 0), axis=0, keepdims=True)
    step = 256
    for at in range(0, out.shape[0], step):
        here = lax.broadcasted_iota(jnp.int32, (step, rows), 0) + at == goes
        out[at : at + step, :] = jnp.dot(
            jnp.where(here, 1.0, 0.0).astype(jnp.bfloat16),
            out_rows,
            preferred_element_type=jnp.float32,
        ).astype(jnp.bfloat16)


def place(counts, target, own, keep, got, ready):
    rows, size = own.shape
    slots = target.shape[0]
    return pl.pallas_call(
        place_kernel,
        out_shape=jax.ShapeDtypeStruct((2 * rows, size), jnp.bfloat16),
        in_specs=[SCALARS] + [WHOLE] * 5 + [UNREAD] * len(ready),
        out_specs=WHOLE,
        compiler_params=pltpu.CompilerParams(vmem_limit_bytes=12 << 20),
        cost_estimate=LIGHT,
    )(counts, target, target.reshape(1, slots), own, keep, got, *ready)


def around(block, axis):
    return [block] + [shift(block, axis, 4 - by) for by in (1, 2, 3)]


def shift(block, axis, by):
    if axis == "z":
        at = [(z % 2) * 2 + z // 2 for z in range(4)]
        return lax.ppermute(block, ("zl", "zh"), [(at[z], at[(z + by) % 4]) for z in range(4)])
    return lax.ppermute(block, axis, [(k, (k + by) % 4) for k in range(4)])


def product_kernel(parts, at, weight, *refs):
    sides, outs = refs[:4], refs[4 : 4 + 4 * len(parts)]
    scaled, turned = refs[-2:]
    rows = weight[...]
    here = {"x": at[1], "y": at[0], "z": 2 * at[4] + at[2]}
    depth = turned.shape[0] // 4
    for part, (start, pieces) in enumerate(parts):
        done = 0
        for left, right, first, last in pieces:
            for k in range(64):
                spot = {
                    axis: (here[axis] + step) & 3
                    for axis, step in zip(ORDER[start], (k >> 4, (k >> 2) & 3, k & 3))
                }
                block = 16 * spot["y"] + 4 * spot["x"] + 2 * (spot["z"] & 1) + (spot["z"] >> 1)
                turned[16 * k : 16 * (k + 1), :] = sides[left][block]
            for col in range(first, last, 128):
                piece = sides[right][:, col : col + 128].astype(jnp.float32) * rows
                scaled[:, col - first : col - first + 128] = piece.astype(jnp.bfloat16)
            for k in range(4):
                for col in range(0, last - first, 256):
                    end = min(col + 256, last - first)
                    outs[4 * part + k][:, done + col : done + end] = jnp.dot(
                        turned[depth * k : depth * (k + 1), :],
                        scaled[:, col:end],
                        preferred_element_type=jnp.float32,
                    ).astype(jnp.bfloat16)
            done += last - first


def products(at, weight, sides, parts, ready=()):
    widths = [sum(last - first for _, _, first, last in pieces) for _, pieces in parts]
    depth = weight.shape[0]
    out = pl.pallas_call(
        functools.partial(product_kernel, parts),
        out_shape=[
            jax.ShapeDtypeStruct((256, width), jnp.bfloat16) for width in widths for _ in range(4)
        ],
        in_specs=[SCALARS] + [WHOLE] * 5,
        out_specs=[WHOLE] * (4 * len(parts)),
        scratch_shapes=[
            pltpu.VMEM((depth, max(widths)), jnp.bfloat16),
            pltpu.VMEM((1024, depth), jnp.bfloat16),
        ],
        compiler_params=pltpu.CompilerParams(vmem_limit_bytes=24 << 20),
        cost_estimate=LIGHT,
    )(at, weight, *sides)
    return [out[4 * k : 4 * k + 4] for k in range(len(parts))]


def sum_kernel(*refs):
    for part in range(3):
        blocks, outs = refs[4 * part : 4 * part + 4], refs[len(refs) - 12 + 4 * part :][:4]
        rows = outs[0].shape[0]
        for k in range(4):
            here = pl.ds(k * rows, rows)
            total = blocks[0][here, :].astype(jnp.float32)
            for ref in blocks[1:]:
                total = total + ref[here, :].astype(jnp.float32)
            outs[k][...] = total.astype(jnp.bfloat16)


def sum_blocks(parts):
    out = pl.pallas_call(
        sum_kernel,
        out_shape=[
            jax.ShapeDtypeStruct((blocks[0].shape[0] // 4, blocks[0].shape[1]), jnp.bfloat16)
            for blocks in parts
            for _ in range(4)
        ],
        in_specs=[WHOLE] * 12,
        out_specs=[WHOLE] * 12,
        compiler_params=pltpu.CompilerParams(vmem_limit_bytes=16 << 20),
        cost_estimate=LIGHT,
    )(*[block for blocks in parts for block in blocks])
    return [out[4 * k : 4 * k + 4] for k in range(3)]


def last_kernel(cut_down, cut_up, *refs):
    down, up = refs[-2:]
    sums = []
    for part in range(3):
        total = refs[4 * part][...].astype(jnp.float32)
        for ref in refs[4 * part + 1 : 4 * part + 4]:
            total = total + ref[...].astype(jnp.float32)
        sums.append(total)
    rest = down.shape[1] - cut_down
    down[:, :cut_down] = sums[0]
    down[:, cut_down:] = sums[1][:, :rest]
    up[:, :cut_up] = sums[1][:, rest:]
    up[:, cut_up:] = sums[2]


def last_sum(parts, ready, cut_down, cut_up, width):
    return pl.pallas_call(
        functools.partial(last_kernel, cut_down, cut_up),
        out_shape=[jax.ShapeDtypeStruct((16, width), jnp.float32)] * 2,
        in_specs=[WHOLE] * 12 + [UNREAD] * len(ready),
        out_specs=[WHOLE] * 2,
    )(*[block for blocks in parts for block in blocks], *ready)


def exchanged(parts, step):
    return [
        [blocks[0]] + [shift(blocks[by], ORDER[start][step], by) for by in (1, 3, 2)]
        for blocks, start in zip(parts, "xyz")
    ]


def local(
    ref_image,
    ref_text,
    learner_image,
    learner_text,
    patches,
    cotangent,
    w_up,
    w_down,
    counts,
    sel_index,
    sel_dest,
):
    core = lax.axis_index("core")
    learner = lax.axis_index("zh") == 1
    pad = ((0, 0), (0, learner_image.shape[1] - ref_image.shape[1]))
    image = jnp.where(learner, learner_image, jnp.pad(ref_image, pad))
    text = jnp.where(learner, learner_text, jnp.pad(ref_text, pad))
    at = jnp.stack([lax.axis_index(name) for name in ("y", "x", "zl", "core", "zh")]).astype(
        jnp.int32
    )
    slots = sel_index.shape[0]
    patch_rows, size = patches.shape[1:]
    count, width, rows = slots * patch_rows, w_up.shape[1], image.shape[0]
    index = sel_index[:, None]

    other_image = lax.ppermute(image, "zl", SWAP)
    texts = around(text, "y")
    texts_other = lax.ppermute(jnp.concatenate(texts, axis=0), "core", SWAP)
    pair, index = pair_rows(at, image, other_image, index)
    images = around(pair, "x")

    x_mine = patches[index[:, 0]].reshape(count, size)
    x_other = lax.ppermute(x_mine, "core", SWAP)
    act, slope = up(at, x_mine, x_other, w_up)

    parts, index = partial_losses(at, images, texts, texts_other, index, [act])
    parts = lax.all_to_all(
        parts, ("y", "x", "zl", "core", "zh"), split_axis=0, concat_axis=0, tiled=True
    )

    cot_mine = cotangent[index[:, 0]].reshape(count, size)
    cot_other = lax.ppermute(cot_mine, "core", SWAP)
    grad_pre = back(at, cot_mine, cot_other, w_down, slope)
    x_turned, cot_turned = turn(at, x_mine, x_other), turn(at, cot_mine, cot_other)

    scores, weight = weights(counts, parts, index, [grad_pre, x_turned, cot_turned])
    learnability = lax.dynamic_slice_in_dim(scores[0], core * rows, rows)

    cut_down, cut_up = 1408, 768
    sides = (cot_turned, x_turned, act, grad_pre)
    blocks = products(at, weight, sides, (("x", ((0, 2, 0, cut_down),)),))
    blocks += products(
        at,
        weight,
        sides,
        (
            ("y", ((0, 2, cut_down, width), (1, 3, 0, cut_up))),
            ("z", ((1, 3, cut_up, width),)),
        ),
    )
    keep, give = down(at, act, w_down, [blocks[-1][0]])
    got = lax.ppermute(give, "core", SWAP)
    blocks = sum_blocks(exchanged(blocks, 0))
    boxed = place(counts, sel_dest, x_mine, keep, got, [blocks[0][0]])
    boxed = boxed.reshape(32, 4, patch_rows, size)
    routed = lax.all_to_all(boxed, DP, split_axis=0, concat_axis=0, tiled=True)
    routed = routed.reshape(128, patch_rows, size)
    blocks = sum_blocks(exchanged(blocks, 1))
    grad_down_t, grad_up = last_sum(exchanged(blocks, 2), [routed], cut_down, cut_up, width)
    return (learnability, routed, grad_up, grad_down_t)


def solution(mesh):
    mesh = Mesh(mesh.devices.reshape(4, 4, 2, 2, 2), ("y", "x", "zl", "core", "zh"))
    pairs = P(("y", "x", "zl", "core"), None)
    patch = P(DP, "zh", "core")
    return jax.shard_map(
        local,
        mesh=mesh,
        in_specs=(
            pairs,
            pairs,
            pairs,
            pairs,
            patch,
            patch,
            P(None, "core"),
            P("core", None),
            P(DP),
            P(DP),
            P(DP, None),
        ),
        out_specs=(
            P(("y", "x", "zl", "core")),
            patch,
            P(CHIPS, "core"),
            P(CHIPS, "core"),
        ),
        check_vma=False,
    )
```

```python
import functools
import math

import jax
import jax.numpy as jnp
from jax import lax
from jax.experimental import pallas as pl
from jax.experimental.pallas import tpu as pltpu
from jax.sharding import Mesh, PartitionSpec as P

DP = ("y", "x", "zl")
CHIPS = ("y", "x", "zl", "zh")
SWAP = [(0, 1), (1, 0)]
ORDER = {"x": "xyz", "y": "yzx", "z": "zxy"}
WHOLE = pl.BlockSpec(memory_space=pltpu.VMEM)
SCALARS = pl.BlockSpec(memory_space=pltpu.SMEM)
UNREAD = pl.BlockSpec(memory_space=pl.ANY)
LIGHT = pl.CostEstimate(flops=1 << 20, bytes_accessed=1 << 16, transcendentals=0)


def unit(rows):
    wide = rows.astype(jnp.float32)
    norm = lax.rsqrt(jnp.sum(wide * wide, axis=1, keepdims=True) + 1e-06)
    return (wide * norm).astype(jnp.bfloat16)


def softplus(value):
    return jnp.maximum(value, 0.0) + jnp.log1p(jnp.exp(-jnp.abs(value)))


def loss_kernel(at, *refs):
    img_refs, txt_refs, txt_other, (out, img, txt) = refs[:4], refs[4:8], refs[8], refs[-3:]
    here_y, here_x, here_zl, here_core, learner = (at[k] for k in range(5))
    for k in range(4):
        img[pl.ds(128 * k, 128), :] = unit(img_refs[k][...])
        own = pl.multiple_of(128 * k + 64 * here_core, 64)
        txt[pl.ds(own, 64), :] = unit(txt_refs[k][...])
        other = pl.multiple_of(128 * k + 64 * (1 - here_core), 64)
        txt[pl.ds(other, 64), :] = unit(txt_other[pl.ds(64 * k, 64), :])
    contract = (((1,), (1,)), ((), ()))
    col_sum = jnp.zeros((1, 512), jnp.float32)
    row_sums = []
    for k in range(4):
        scores = (
            10.0
            * lax.dot_general(
                img[pl.ds(128 * k, 128), :], txt[...], contract, preferred_element_type=jnp.float32
            )
            - 5.0
        )
        if k == 0:
            row = lax.broadcasted_iota(jnp.int32, scores.shape, 0) - 64 * here_zl
            col = lax.broadcasted_iota(jnp.int32, scores.shape, 1) - 64 * here_core
            same = (row == col) & (row >= 0) & (row < 64)
            scores = jnp.where(same, -scores, scores)
        terms = softplus(scores)
        col_sum = col_sum + jnp.sum(terms, axis=0, keepdims=True)
        folded = terms[:, :128] + terms[:, 128:256] + terms[:, 256:384] + terms[:, 384:]
        row_sums.append(jnp.sum(folded.T, axis=0, keepdims=True))
    dest = lax.broadcasted_iota(jnp.int32, (128, 128), 0)
    lane = lax.broadcasted_iota(jnp.int32, (1, 128), 1)
    dest_y, dest_x, dest_zl = dest >> 5, (dest >> 3) & 3, (dest >> 2) & 1
    own_half = (lane >> 6) == here_core
    total = jnp.zeros((128, 128), jnp.float32)
    for k in range(4):
        straight = row_sums[k]
        crossed = pltpu.roll(straight, 64, 1)
        for zl in range(2):
            placed = jnp.where(own_half, jnp.where(here_core == zl, straight, crossed), 0.0)
            mine = (dest_y == here_y) & (dest_x == ((here_x + k) & 3)) & (dest_zl == zl)
            total = total + jnp.where(mine, placed, 0.0)
        mine = (dest_y == ((here_y + k) & 3)) & (dest_x == here_x) & (dest_zl == here_zl)
        total = total + jnp.where(mine, col_sum[:, 128 * k : 128 * (k + 1)], 0.0)
    out[...] = jnp.where(learner == 1, 0.5, -0.5) * total


def partial_losses(at, images, texts, texts_other, ready):
    return pl.pallas_call(
        loss_kernel,
        out_shape=jax.ShapeDtypeStruct((128, 128), jnp.float32),
        in_specs=[SCALARS] + [WHOLE] * 9 + [UNREAD] * len(ready),
        out_specs=WHOLE,
        scratch_shapes=[pltpu.VMEM((512, 1024), jnp.bfloat16)] * 2,
        compiler_params=pltpu.CompilerParams(vmem_limit_bytes=12 << 20),
        cost_estimate=LIGHT,
    )(at, *images, *texts, texts_other, *ready)


def weight_kernel(count, parts, index, *refs):
    learn, weight = refs[-2:]
    score = jnp.sum(parts[...], axis=0, keepdims=True)
    learn[...] = jnp.broadcast_to(score, (8, 128))
    slots = index.shape[0]
    picked = index[...] == lax.broadcasted_iota(jnp.int32, (slots, 128), 1)
    chosen = jnp.sum(jnp.where(picked, score, 0.0), axis=1, keepdims=True)
    live = lax.broadcasted_iota(jnp.int32, (slots, 128), 0) < count[0]
    value = jnp.where(live, 1.0 / (1.0 + jnp.exp(-chosen)), 0.0)
    weight[...] = jnp.broadcast_to(value[:, None, :], (slots, 8, 128)).reshape(8 * slots, 128)


def weights(counts, parts, index, ready):
    slots = index.shape[0]
    return pl.pallas_call(
        weight_kernel,
        out_shape=(
            jax.ShapeDtypeStruct((8, 128), jnp.float32),
            jax.ShapeDtypeStruct((8 * slots, 128), jnp.float32),
        ),
        in_specs=[SCALARS, WHOLE, WHOLE] + [UNREAD] * len(ready),
        out_specs=(WHOLE, WHOLE),
        cost_estimate=LIGHT,
    )(counts, parts, index, *ready)


def pair_kernel(at, own, other, index, pair, index_out):
    pair[pl.ds(pl.multiple_of(64 * at[2], 64), 64), :] = own[...]
    pair[pl.ds(pl.multiple_of(64 * (1 - at[2]), 64), 64), :] = other[...]
    index_out[...] = index[...]


def pair_rows(at, own, other, index):
    rows, width = own.shape
    return pl.pallas_call(
        pair_kernel,
        out_shape=(
            jax.ShapeDtypeStruct((2 * rows, width), own.dtype),
            jax.ShapeDtypeStruct(index.shape, jnp.int32),
        ),
        in_specs=[SCALARS, WHOLE, WHOLE, WHOLE],
        out_specs=(WHOLE, WHOLE),
        cost_estimate=LIGHT,
    )(at, own, other, index)


def half(ref, axis, which, size):
    start = pl.multiple_of(which * size, size)
    return ref[pl.ds(start, size), :] if axis == 0 else ref[:, pl.ds(start, size)]


def up_kernel(at, mine, other, w_up, act, slope):
    size = mine.shape[1]
    pre = jnp.dot(mine[...], half(w_up, 0, at[3], size), preferred_element_type=jnp.float32)
    pre = pre + jnp.dot(
        other[...], half(w_up, 0, 1 - at[3], size), preferred_element_type=jnp.float32
    )
    scale = math.sqrt(2.0 / math.pi)
    square = pre * pre
    tanh = jnp.tanh(scale * pre * (1.0 + 0.044715 * square))
    gate = 0.5 * (1.0 + tanh)
    act[...] = (pre * gate).astype(jnp.bfloat16)
    bend = 0.5 * pre * (1.0 - tanh * tanh) * (scale * (1.0 + 3 * 0.044715 * square))
    slope[...] = (gate + bend).astype(jnp.bfloat16)


def up(at, mine, other, w_up):
    rows, size = mine.shape
    width, tile = w_up.shape[1], 512
    fixed = pl.BlockSpec((rows, size), lambda n: (0, 0))
    out = pl.BlockSpec((rows, tile), lambda n: (0, n))
    return pl.pallas_call(
        up_kernel,
        grid=(width // tile,),
        out_shape=[jax.ShapeDtypeStruct((rows, width), jnp.bfloat16)] * 2,
        in_specs=[SCALARS, fixed, fixed, pl.BlockSpec((2 * size, tile), lambda n: (0, n))],
        out_specs=[out, out],
        compiler_params=pltpu.CompilerParams(vmem_limit_bytes=16 << 20),
        cost_estimate=LIGHT,
    )(at, mine, other, w_up)


def back_kernel(at, mine, other, w_down, slope, out):
    size = mine.shape[1]
    contract = (((1,), (1,)), ((), ()))
    back = lax.dot_general(
        mine[...], half(w_down, 1, at[3], size), contract, preferred_element_type=jnp.float32
    )
    back = back + lax.dot_general(
        other[...], half(w_down, 1, 1 - at[3], size), contract, preferred_element_type=jnp.float32
    )
    out[...] = (back * slope[...].astype(jnp.float32)).astype(jnp.bfloat16)


def back(at, mine, other, w_down, slope):
    rows, size = mine.shape
    width, tile = w_down.shape[0], 512
    fixed = pl.BlockSpec((rows, size), lambda n: (0, 0))
    out = pl.BlockSpec((rows, tile), lambda n: (0, n))
    return pl.pallas_call(
        back_kernel,
        grid=(width // tile,),
        out_shape=jax.ShapeDtypeStruct((rows, width), jnp.bfloat16),
        in_specs=[SCALARS, fixed, fixed, pl.BlockSpec((tile, 2 * size), lambda n: (n, 0)), out],
        out_specs=out,
        compiler_params=pltpu.CompilerParams(vmem_limit_bytes=16 << 20),
        cost_estimate=LIGHT,
    )(at, mine, other, w_down, slope)


def turn_kernel(starts, at, mine, other, *refs):
    outs, turned = refs[:-1], refs[-1]
    blocks = turned.shape[0] // 2
    turned[pl.ds(at[3] * blocks, blocks)] = mine[...].T.reshape((blocks,) + turned.shape[1:])
    turned[pl.ds((1 - at[3]) * blocks, blocks)] = other[...].T.reshape(
        (blocks,) + turned.shape[1:]
    )
    here = {"x": at[1], "y": at[0], "z": 2 * at[4] + at[2]}
    for start, out in zip(starts, outs):
        for k in range(2 * blocks):
            steps = (k >> 4, (k >> 2) & 3, k & 3)
            spot = {}
            for axis in "xyz":
                by = [steps[ORDER[one].index(axis)] for one in start]
                by = by[0] + at[3] * (by[-1] - by[0])
                spot[axis] = (here[axis] + by) & 3
            block = 16 * spot["y"] + 4 * spot["x"] + 2 * (spot["z"] & 1) + (spot["z"] >> 1)
            out[16 * k : 16 * (k + 1), :] = turned[block]


def turn(at, mine, other, starts):
    rows, size = mine.shape
    return pl.pallas_call(
        functools.partial(turn_kernel, starts),
        out_shape=[jax.ShapeDtypeStruct((2 * size, rows), mine.dtype)] * len(starts),
        in_specs=[SCALARS, WHOLE, WHOLE],
        out_specs=[WHOLE] * len(starts),
        scratch_shapes=[pltpu.VMEM((2 * size // 16, 16, rows), mine.dtype)],
        compiler_params=pltpu.CompilerParams(vmem_limit_bytes=12 << 20),
        cost_estimate=LIGHT,
    )(at, mine, other)


def down_kernel(at, act, w_down, *refs):
    keep, give = refs[-2:]
    size = keep.shape[1]
    keep[...] = jnp.dot(
        act[...], half(w_down, 1, at[3], size), preferred_element_type=jnp.float32
    )
    give[...] = jnp.dot(
        act[...], half(w_down, 1, 1 - at[3], size), preferred_element_type=jnp.float32
    )


def down(at, act, w_down, ready):
    rows, size = act.shape[0], w_down.shape[1] // 2
    return pl.pallas_call(
        down_kernel,
        out_shape=[jax.ShapeDtypeStruct((rows, size), jnp.float32)] * 2,
        in_specs=[SCALARS, WHOLE, WHOLE] + [UNREAD] * len(ready),
        out_specs=[WHOLE, WHOLE],
        compiler_params=pltpu.CompilerParams(vmem_limit_bytes=20 << 20),
        cost_estimate=LIGHT,
    )(at, act, w_down, *ready)


def place_kernel(count, target_col, target_row, own, keep, got, *refs):
    out = refs[-1]
    slots, rows = target_col.shape[0], own.shape[0]
    each = rows // slots
    out_rows = (own[...].astype(jnp.float32) + keep[...] + got[...]).astype(jnp.bfloat16)
    slot = lax.broadcasted_iota(jnp.int32, (slots, slots), 0)
    before = lax.broadcasted_iota(jnp.int32, (slots, slots), 1)
    same = (target_row[...] == target_col[...]) & (before < slot)
    rank = jnp.sum(same.astype(jnp.int32), axis=1, keepdims=True)
    live = lax.broadcasted_iota(jnp.int32, (slots, 1), 0) < count[0]
    first = jnp.where(live, each * (4 * target_col[...] + rank), -each)
    lane = lax.broadcasted_iota(jnp.int32, (slots, rows), 1)
    mine = (lane // each) == lax.broadcasted_iota(jnp.int32, (slots, rows), 0)
    goes = jnp.sum(jnp.where(mine, first + lane % each, 0), axis=0, keepdims=True)
    step = 256
    for at in range(0, out.shape[0], step):
        here = lax.broadcasted_iota(jnp.int32, (step, rows), 0) + at == goes
        out[at : at + step, :] = jnp.dot(
            jnp.where(here, 1.0, 0.0).astype(jnp.bfloat16),
            out_rows,
            preferred_element_type=jnp.float32,
        ).astype(jnp.bfloat16)


def place(counts, target, own, keep, got, ready):
    rows, size = own.shape
    slots = target.shape[0]
    return pl.pallas_call(
        place_kernel,
        out_shape=jax.ShapeDtypeStruct((2 * rows, size), jnp.bfloat16),
        in_specs=[SCALARS] + [WHOLE] * 5 + [UNREAD] * len(ready),
        out_specs=WHOLE,
        compiler_params=pltpu.CompilerParams(vmem_limit_bytes=12 << 20),
        cost_estimate=LIGHT,
    )(counts, target, target.reshape(1, slots), own, keep, got, *ready)


def around(block, axis):
    return [block] + [shift(block, axis, 4 - by) for by in (1, 2, 3)]


def shift(block, axis, by):
    if axis == "z":
        at = [(z % 2) * 2 + z // 2 for z in range(4)]
        return lax.ppermute(block, ("zl", "zh"), [(at[z], at[(z + by) % 4]) for z in range(4)])
    return lax.ppermute(block, axis, [(k, (k + by) % 4) for k in range(4)])


def number(spot, core):
    return 8 * (4 * spot["y"] + spot["x"]) + 4 * (spot["z"] % 2) + 2 * core + spot["z"] // 2


def shift_each(block, axes, by):
    route = []
    for chip in range(64):
        spot = {"x": chip % 4, "y": chip // 4 % 4, "z": chip // 16}
        for core in range(2):
            axis = axes[core]
            there = {**spot, axis: (spot[axis] + by) % 4}
            route.append((number(spot, core), number(there, core)))
    return lax.ppermute(block, ("y", "x", "zl", "core", "zh"), route)


def fetched(sources, targets, sems):
    copies = [
        pltpu.make_async_copy(source, target, sems.at[k])
        for k, (source, target) in enumerate(zip(sources, targets))
    ]
    for copy in copies:
        copy.start()
    return copies


def product_kernel(pieces, weight, *refs):
    lefts = 1 + max(piece[0] for piece in pieces)
    rights = 1 + max(piece[1] for piece in pieces)
    count = lefts + rights
    sources, outs, rest = refs[:count], refs[count : count + 4], refs[count + 4 :]
    held, scaled, sems = rest[:count], rest[count], rest[count + 1]
    copies = fetched(sources, held, sems)
    rows = weight[...]
    depth = outs[0].shape[0]
    done = 0
    seen = set()
    for left, right, first, last in pieces:
        for k in (lefts + right, left):
            if k not in seen:
                copies[k].wait()
                seen.add(k)
        for col in range(first, last, 128):
            piece = held[lefts + right][:, col : col + 128].astype(jnp.float32) * rows
            scaled[:, col - first : col - first + 128] = piece.astype(jnp.bfloat16)
        for k in range(4):
            for col in range(0, last - first, 256):
                end = min(col + 256, last - first)
                outs[k][:, done + col : done + end] = jnp.dot(
                    held[left][depth * k : depth * (k + 1), :],
                    scaled[:, col:end],
                    preferred_element_type=jnp.float32,
                ).astype(jnp.bfloat16)
        done += last - first


def products(weight, lefts, rights, pieces):
    width = sum(last - first for _, _, first, last in pieces)
    sides = [*lefts, *rights]
    depth = weight.shape[0]
    return pl.pallas_call(
        functools.partial(product_kernel, pieces),
        out_shape=[jax.ShapeDtypeStruct((256, width), jnp.bfloat16)] * 4,
        in_specs=[WHOLE] + [UNREAD] * len(sides),
        out_specs=[WHOLE] * 4,
        scratch_shapes=[pltpu.VMEM(side.shape, side.dtype) for side in sides]
        + [
            pltpu.VMEM((depth, max(piece[3] - piece[2] for piece in pieces)), jnp.bfloat16),
            pltpu.SemaphoreType.DMA((len(sides),)),
        ],
        compiler_params=pltpu.CompilerParams(vmem_limit_bytes=24 << 20),
        cost_estimate=LIGHT,
    )(weight, *sides)


def sum_kernel(*refs):
    sources, outs, held, sems = refs[:8], refs[8:16], refs[16:24], refs[24]
    copies = fetched(sources, held, sems)
    for part in range(2):
        blocks = held[4 * part : 4 * part + 4]
        for copy in copies[4 * part : 4 * part + 4]:
            copy.wait()
        rows = outs[4 * part].shape[0]
        for k in range(4):
            here = pl.ds(k * rows, rows)
            total = blocks[0][here, :].astype(jnp.float32)
            for ref in blocks[1:]:
                total = total + ref[here, :].astype(jnp.float32)
            outs[4 * part + k][...] = total.astype(jnp.bfloat16)


def sum_blocks(parts):
    blocks = [block for part in parts for block in part]
    out = pl.pallas_call(
        sum_kernel,
        out_shape=[
            jax.ShapeDtypeStruct((block.shape[0] // 4, block.shape[1]), jnp.bfloat16)
            for block in blocks
        ],
        in_specs=[UNREAD] * 8,
        out_specs=[WHOLE] * 8,
        scratch_shapes=[pltpu.VMEM(block.shape, block.dtype) for block in blocks]
        + [pltpu.SemaphoreType.DMA((8,))],
        compiler_params=pltpu.CompilerParams(vmem_limit_bytes=24 << 20),
        cost_estimate=LIGHT,
    )(*blocks)
    return [out[:4], out[4:]]


def last_kernel(*refs):
    down, up = refs[-2:]
    sums = []
    for part in range(2):
        total = refs[4 * part][...].astype(jnp.float32)
        for ref in refs[4 * part + 1 : 4 * part + 4]:
            total = total + ref[...].astype(jnp.float32)
        sums.append(total)
    width = down.shape[1]
    cut = sums[0].shape[1] - width
    down[...] = sums[0][:, :width]
    up[:, :cut] = sums[0][:, width:]
    up[:, cut:] = sums[1]


def last_sum(parts, ready, width):
    return pl.pallas_call(
        last_kernel,
        out_shape=[jax.ShapeDtypeStruct((16, width), jnp.float32)] * 2,
        in_specs=[WHOLE] * 8 + [UNREAD] * len(ready),
        out_specs=[WHOLE] * 2,
        cost_estimate=LIGHT,
    )(*[block for part in parts for block in part], *ready)


def exchanged(parts, step):
    first, second = parts
    axes = (ORDER["x"][step], ORDER["y"][step])
    return [
        [first[0]] + [shift_each(first[by], axes, by) for by in (1, 3, 2)],
        [second[0]] + [shift(second[by], ORDER["z"][step], by) for by in (1, 3, 2)],
    ]


def local(
    ref_image,
    ref_text,
    learner_image,
    learner_text,
    patches,
    cotangent,
    w_up,
    w_down,
    counts,
    sel_index,
    sel_dest,
):
    core = lax.axis_index("core")
    learner = lax.axis_index("zh") == 1
    pad = ((0, 0), (0, learner_image.shape[1] - ref_image.shape[1]))
    image = jnp.where(learner, learner_image, jnp.pad(ref_image, pad))
    text = jnp.where(learner, learner_text, jnp.pad(ref_text, pad))
    at = jnp.stack([lax.axis_index(name) for name in ("y", "x", "zl", "core", "zh")]).astype(
        jnp.int32
    )
    slots = sel_index.shape[0]
    patch_rows, size = patches.shape[1:]
    count, width, rows = slots * patch_rows, w_up.shape[1], image.shape[0]
    index = sel_index[:, None]

    other_image = lax.ppermute(image, "zl", SWAP)
    texts = around(text, "y")
    texts_other = lax.ppermute(jnp.concatenate(texts, axis=0), "core", SWAP)
    pair, index = pair_rows(at, image, other_image, index)
    images = around(pair, "x")

    x_mine = patches[index[:, 0]].reshape(count, size)
    x_other = lax.ppermute(x_mine, "core", SWAP)
    act, slope = up(at, x_mine, x_other, w_up)
    cot_mine = cotangent[index[:, 0]].reshape(count, size)
    cot_other = lax.ppermute(cot_mine, "core", SWAP)
    x_first, x_second = turn(at, x_mine, x_other, ("xy", "z"))

    parts = partial_losses(at, images, texts, texts_other, [act, x_first])
    parts = lax.all_to_all(
        parts, ("y", "x", "zl", "core", "zh"), split_axis=0, concat_axis=0, tiled=True
    )
    grad_pre = back(at, cot_mine, cot_other, w_down, slope)
    (cot_first,) = turn(at, cot_mine, cot_other, ("xy",))
    scores, weight = weights(counts, parts, index, [grad_pre, cot_first])
    learnability = lax.dynamic_slice_in_dim(scores[0], core * rows, rows)

    cut = 640
    blocks = [
        products(
            weight,
            [cot_first, x_first],
            [act, grad_pre],
            ((0, 0, 0, width), (1, 1, 0, cut)),
        ),
        products(weight, [x_second], [grad_pre], ((0, 0, cut, width),)),
    ]
    keep, give = down(at, act, w_down, [blocks[0][0], blocks[1][0]])
    got = lax.ppermute(give, "core", SWAP)
    blocks = sum_blocks(exchanged(blocks, 0))
    blocks = exchanged(blocks, 1)
    boxed = place(counts, sel_dest, x_mine, keep, got, [blocks[1][1]])
    boxed = boxed.reshape(32, 4, patch_rows, size)
    routed = lax.all_to_all(boxed, DP, split_axis=0, concat_axis=0, tiled=True)
    routed = routed.reshape(128, patch_rows, size)
    blocks = sum_blocks(blocks)
    grad_down_t, grad_up = last_sum(exchanged(blocks, 2), [routed], width)
    return (learnability, routed, grad_up, grad_down_t)


def solution(mesh):
    mesh = Mesh(mesh.devices.reshape(4, 4, 2, 2, 2), ("y", "x", "zl", "core", "zh"))
    pairs = P(("y", "x", "zl", "core"), None)
    patch = P(DP, "zh", "core")
    return jax.shard_map(
        local,
        mesh=mesh,
        in_specs=(
            pairs,
            pairs,
            pairs,
            pairs,
            patch,
            patch,
            P(None, "core"),
            P("core", None),
            P(DP),
            P(DP),
            P(DP, None),
        ),
        out_specs=(
            P(("y", "x", "zl", "core")),
            patch,
            P(CHIPS, "core"),
            P(CHIPS, "core"),
        ),
        check_vma=False,
    )
```

```python
import functools
import math

import jax
import jax.numpy as jnp
from jax import lax
from jax.experimental import pallas as pl
from jax.experimental.pallas import tpu as pltpu
from jax.sharding import Mesh, PartitionSpec as P

DP = ("y", "x", "zl")
CHIPS = ("y", "x", "zl", "zh")
SWAP = [(0, 1), (1, 0)]
ORDER = {"x": "xyz", "y": "yzx", "z": "zxy"}
WHOLE = pl.BlockSpec(memory_space=pltpu.VMEM)
SCALARS = pl.BlockSpec(memory_space=pltpu.SMEM)
UNREAD = pl.BlockSpec(memory_space=pl.ANY)
LIGHT = pl.CostEstimate(flops=1 << 20, bytes_accessed=1 << 16, transcendentals=0)


def unit(rows):
    wide = rows.astype(jnp.float32)
    norm = lax.rsqrt(jnp.sum(wide * wide, axis=1, keepdims=True) + 1e-06)
    return (wide * norm).astype(jnp.bfloat16)


def softplus(value):
    return jnp.maximum(value, 0.0) + jnp.log1p(jnp.exp(-jnp.abs(value)))


def loss_kernel(at, *refs):
    img_refs, txt_refs, txt_other, (out, img, txt) = refs[:4], refs[4:8], refs[8], refs[-3:]
    here_y, here_x, here_zl, here_core, learner = (at[k] for k in range(5))
    for k in range(4):
        img[pl.ds(128 * k, 128), :] = unit(img_refs[k][...])
        own = pl.multiple_of(128 * k + 64 * here_core, 64)
        txt[pl.ds(own, 64), :] = unit(txt_refs[k][...])
        other = pl.multiple_of(128 * k + 64 * (1 - here_core), 64)
        txt[pl.ds(other, 64), :] = unit(txt_other[pl.ds(64 * k, 64), :])
    contract = (((1,), (1,)), ((), ()))
    col_sum = jnp.zeros((1, 512), jnp.float32)
    row_sums = []
    for k in range(4):
        scores = (
            10.0
            * lax.dot_general(
                img[pl.ds(128 * k, 128), :], txt[...], contract, preferred_element_type=jnp.float32
            )
            - 5.0
        )
        if k == 0:
            row = lax.broadcasted_iota(jnp.int32, scores.shape, 0) - 64 * here_zl
            col = lax.broadcasted_iota(jnp.int32, scores.shape, 1) - 64 * here_core
            same = (row == col) & (row >= 0) & (row < 64)
            scores = jnp.where(same, -scores, scores)
        terms = softplus(scores)
        col_sum = col_sum + jnp.sum(terms, axis=0, keepdims=True)
        folded = terms[:, :128] + terms[:, 128:256] + terms[:, 256:384] + terms[:, 384:]
        row_sums.append(jnp.sum(folded.T, axis=0, keepdims=True))
    dest = lax.broadcasted_iota(jnp.int32, (128, 128), 0)
    lane = lax.broadcasted_iota(jnp.int32, (1, 128), 1)
    dest_y, dest_x, dest_zl = dest >> 5, (dest >> 3) & 3, (dest >> 2) & 1
    own_half = (lane >> 6) == here_core
    total = jnp.zeros((128, 128), jnp.float32)
    for k in range(4):
        straight = row_sums[k]
        crossed = pltpu.roll(straight, 64, 1)
        for zl in range(2):
            placed = jnp.where(own_half, jnp.where(here_core == zl, straight, crossed), 0.0)
            mine = (dest_y == here_y) & (dest_x == ((here_x + k) & 3)) & (dest_zl == zl)
            total = total + jnp.where(mine, placed, 0.0)
        mine = (dest_y == ((here_y + k) & 3)) & (dest_x == here_x) & (dest_zl == here_zl)
        total = total + jnp.where(mine, col_sum[:, 128 * k : 128 * (k + 1)], 0.0)
    out[...] = jnp.where(learner == 1, 0.5, -0.5) * total


def partial_losses(at, images, texts, texts_other, ready):
    return pl.pallas_call(
        loss_kernel,
        out_shape=jax.ShapeDtypeStruct((128, 128), jnp.float32),
        in_specs=[SCALARS] + [WHOLE] * 9 + [UNREAD] * len(ready),
        out_specs=WHOLE,
        scratch_shapes=[pltpu.VMEM((512, 1024), jnp.bfloat16)] * 2,
        compiler_params=pltpu.CompilerParams(vmem_limit_bytes=8 << 20),
        cost_estimate=LIGHT,
    )(at, *images, *texts, texts_other, *ready)


def weight_kernel(count, parts, index, *refs):
    learn, weight = refs[-2:]
    score = jnp.sum(parts[...], axis=0, keepdims=True)
    learn[...] = jnp.broadcast_to(score, (8, 128))
    slots = index.shape[0]
    picked = index[...] == lax.broadcasted_iota(jnp.int32, (slots, 128), 1)
    chosen = jnp.sum(jnp.where(picked, score, 0.0), axis=1, keepdims=True)
    live = lax.broadcasted_iota(jnp.int32, (slots, 128), 0) < count[0]
    value = jnp.where(live, 1.0 / (1.0 + jnp.exp(-chosen)), 0.0)
    weight[...] = jnp.broadcast_to(value[:, None, :], (slots, 8, 128)).reshape(8 * slots, 128)


def weights(counts, parts, index, ready):
    slots = index.shape[0]
    return pl.pallas_call(
        weight_kernel,
        out_shape=(
            jax.ShapeDtypeStruct((8, 128), jnp.float32),
            jax.ShapeDtypeStruct((8 * slots, 128), jnp.float32),
        ),
        in_specs=[SCALARS, WHOLE, WHOLE] + [UNREAD] * len(ready),
        out_specs=(WHOLE, WHOLE),
        compiler_params=pltpu.CompilerParams(vmem_limit_bytes=2 << 20),
        cost_estimate=LIGHT,
    )(counts, parts, index, *ready)


def pair_kernel(at, own, other, index, *refs):
    pair, index_out = refs[-2:]
    pair[pl.ds(pl.multiple_of(64 * at[2], 64), 64), :] = own[...]
    pair[pl.ds(pl.multiple_of(64 * (1 - at[2]), 64), 64), :] = other[...]
    index_out[...] = index[...]


def pair_rows(at, own, other, index, ready):
    rows, width = own.shape
    return pl.pallas_call(
        pair_kernel,
        out_shape=(
            jax.ShapeDtypeStruct((2 * rows, width), own.dtype),
            jax.ShapeDtypeStruct(index.shape, jnp.int32),
        ),
        in_specs=[SCALARS, WHOLE, WHOLE, WHOLE] + [UNREAD] * len(ready),
        out_specs=(WHOLE, WHOLE),
        compiler_params=pltpu.CompilerParams(vmem_limit_bytes=2 << 20),
        cost_estimate=LIGHT,
    )(at, own, other, index, *ready)


def half(ref, axis, which, size):
    start = pl.multiple_of(which * size, size)
    return ref[pl.ds(start, size), :] if axis == 0 else ref[:, pl.ds(start, size)]


def up_kernel(at, mine, other, w_up, act, slope):
    size = mine.shape[1]
    pre = jnp.dot(mine[...], half(w_up, 0, at[3], size), preferred_element_type=jnp.float32)
    pre = pre + jnp.dot(
        other[...], half(w_up, 0, 1 - at[3], size), preferred_element_type=jnp.float32
    )
    scale = math.sqrt(2.0 / math.pi)
    square = pre * pre
    tanh = jnp.tanh(scale * pre * (1.0 + 0.044715 * square))
    gate = 0.5 * (1.0 + tanh)
    act[...] = (pre * gate).astype(jnp.bfloat16)
    bend = 0.5 * pre * (1.0 - tanh * tanh) * (scale * (1.0 + 3 * 0.044715 * square))
    slope[...] = (gate + bend).astype(jnp.bfloat16)


def up(at, mine, other, w_up):
    rows, size = mine.shape
    width, tile = w_up.shape[1], 512
    fixed = pl.BlockSpec((rows, size), lambda n: (0, 0))
    out = pl.BlockSpec((rows, tile), lambda n: (0, n))
    return pl.pallas_call(
        up_kernel,
        grid=(width // tile,),
        out_shape=[jax.ShapeDtypeStruct((rows, width), jnp.bfloat16)] * 2,
        in_specs=[SCALARS, fixed, fixed, pl.BlockSpec((2 * size, tile), lambda n: (0, n))],
        out_specs=[out, out],
        compiler_params=pltpu.CompilerParams(vmem_limit_bytes=14 << 20),
        cost_estimate=LIGHT,
    )(at, mine, other, w_up)


def back_kernel(at, mine, other, w_down, slope, out):
    size = mine.shape[1]
    contract = (((1,), (1,)), ((), ()))
    back = lax.dot_general(
        mine[...], half(w_down, 1, at[3], size), contract, preferred_element_type=jnp.float32
    )
    back = back + lax.dot_general(
        other[...], half(w_down, 1, 1 - at[3], size), contract, preferred_element_type=jnp.float32
    )
    out[...] = (back * slope[...].astype(jnp.float32)).astype(jnp.bfloat16)


def back(at, mine, other, w_down, slope):
    rows, size = mine.shape
    width, tile = w_down.shape[0], 512
    fixed = pl.BlockSpec((rows, size), lambda n: (0, 0))
    out = pl.BlockSpec((rows, tile), lambda n: (0, n))
    return pl.pallas_call(
        back_kernel,
        grid=(width // tile,),
        out_shape=jax.ShapeDtypeStruct((rows, width), jnp.bfloat16),
        in_specs=[SCALARS, fixed, fixed, pl.BlockSpec((tile, 2 * size), lambda n: (n, 0)), out],
        out_specs=out,
        compiler_params=pltpu.CompilerParams(vmem_limit_bytes=12 << 20),
        cost_estimate=LIGHT,
    )(at, mine, other, w_down, slope)


def turn_kernel(starts, at, mine, other, *refs):
    outs, turned = refs[:-1], refs[-1]
    blocks = turned.shape[0] // 2
    turned[pl.ds(at[3] * blocks, blocks)] = mine[...].T.reshape((blocks,) + turned.shape[1:])
    turned[pl.ds((1 - at[3]) * blocks, blocks)] = other[...].T.reshape(
        (blocks,) + turned.shape[1:]
    )
    here = {"x": at[1], "y": at[0], "z": 2 * at[4] + at[2]}
    for start, out in zip(starts, outs):
        for k in range(2 * blocks):
            steps = (k >> 4, (k >> 2) & 3, k & 3)
            spot = {}
            for axis in "xyz":
                by = [steps[ORDER[one].index(axis)] for one in start]
                by = by[0] + at[3] * (by[-1] - by[0])
                spot[axis] = (here[axis] + by) & 3
            block = 16 * spot["y"] + 4 * spot["x"] + 2 * (spot["z"] & 1) + (spot["z"] >> 1)
            out[16 * k : 16 * (k + 1), :] = turned[block]


def turn(at, mine, other, starts):
    rows, size = mine.shape
    return pl.pallas_call(
        functools.partial(turn_kernel, starts),
        out_shape=[jax.ShapeDtypeStruct((2 * size, rows), mine.dtype)] * len(starts),
        in_specs=[SCALARS, WHOLE, WHOLE],
        out_specs=[WHOLE] * len(starts),
        scratch_shapes=[pltpu.VMEM((2 * size // 16, 16, rows), mine.dtype)],
        compiler_params=pltpu.CompilerParams(vmem_limit_bytes=8 << 20),
        cost_estimate=LIGHT,
    )(at, mine, other)


def down_kernel(at, act, w_down, *refs):
    keep, give = refs[-2:]
    size = keep.shape[1]
    keep[...] = jnp.dot(
        act[...], half(w_down, 1, at[3], size), preferred_element_type=jnp.float32
    )
    give[...] = jnp.dot(
        act[...], half(w_down, 1, 1 - at[3], size), preferred_element_type=jnp.float32
    )


def down(at, act, w_down, ready):
    rows, size = act.shape[0], w_down.shape[1] // 2
    return pl.pallas_call(
        down_kernel,
        out_shape=[jax.ShapeDtypeStruct((rows, size), jnp.float32)] * 2,
        in_specs=[SCALARS, WHOLE, WHOLE] + [UNREAD] * len(ready),
        out_specs=[WHOLE, WHOLE],
        compiler_params=pltpu.CompilerParams(vmem_limit_bytes=14 << 20),
        cost_estimate=LIGHT,
    )(at, act, w_down, *ready)


def place_kernel(count, target_col, target_row, own, keep, got, *refs):
    out = refs[-1]
    slots, rows = target_col.shape[0], own.shape[0]
    each = rows // slots
    out_rows = (own[...].astype(jnp.float32) + keep[...] + got[...]).astype(jnp.bfloat16)
    slot = lax.broadcasted_iota(jnp.int32, (slots, slots), 0)
    before = lax.broadcasted_iota(jnp.int32, (slots, slots), 1)
    same = (target_row[...] == target_col[...]) & (before < slot)
    rank = jnp.sum(same.astype(jnp.int32), axis=1, keepdims=True)
    live = lax.broadcasted_iota(jnp.int32, (slots, 1), 0) < count[0]
    first = jnp.where(live, each * (4 * target_col[...] + rank), -each)
    lane = lax.broadcasted_iota(jnp.int32, (slots, rows), 1)
    mine = (lane // each) == lax.broadcasted_iota(jnp.int32, (slots, rows), 0)
    goes = jnp.sum(jnp.where(mine, first + lane % each, 0), axis=0, keepdims=True)
    step = 256
    for at in range(0, out.shape[0], step):
        here = lax.broadcasted_iota(jnp.int32, (step, rows), 0) + at == goes
        out[at : at + step, :] = jnp.dot(
            jnp.where(here, 1.0, 0.0).astype(jnp.bfloat16),
            out_rows,
            preferred_element_type=jnp.float32,
        ).astype(jnp.bfloat16)


def place(counts, target, own, keep, got, ready):
    rows, size = own.shape
    slots = target.shape[0]
    return pl.pallas_call(
        place_kernel,
        out_shape=jax.ShapeDtypeStruct((2 * rows, size), jnp.bfloat16),
        in_specs=[SCALARS] + [WHOLE] * 5 + [UNREAD] * len(ready),
        out_specs=WHOLE,
        compiler_params=pltpu.CompilerParams(vmem_limit_bytes=8 << 20),
        cost_estimate=LIGHT,
    )(counts, target, target.reshape(1, slots), own, keep, got, *ready)


def around(block, axis):
    return [block] + [shift(block, axis, 4 - by) for by in (1, 2, 3)]


def shift(block, axis, by):
    if axis == "z":
        at = [(z % 2) * 2 + z // 2 for z in range(4)]
        return lax.ppermute(block, ("zl", "zh"), [(at[z], at[(z + by) % 4]) for z in range(4)])
    return lax.ppermute(block, axis, [(k, (k + by) % 4) for k in range(4)])


def number(spot, core):
    return 8 * (4 * spot["y"] + spot["x"]) + 4 * (spot["z"] % 2) + 2 * core + spot["z"] // 2


def shift_each(block, axes, by):
    route = []
    for chip in range(64):
        spot = {"x": chip % 4, "y": chip // 4 % 4, "z": chip // 16}
        for core in range(2):
            axis = axes[core]
            there = {**spot, axis: (spot[axis] + by) % 4}
            route.append((number(spot, core), number(there, core)))
    return lax.ppermute(block, ("y", "x", "zl", "core", "zh"), route)


def fetched(sources, targets, sems):
    copies = [
        pltpu.make_async_copy(source, target, sems.at[k])
        for k, (source, target) in enumerate(zip(sources, targets))
    ]
    for copy in copies:
        copy.start()
    return copies


def product_kernel(pieces, weight, *refs):
    lefts = 1 + max(piece[0] for piece in pieces)
    rights = 1 + max(piece[1] for piece in pieces)
    count = lefts + rights
    sources, outs, rest = refs[:count], refs[count : count + 4], refs[count + 4 :]
    held, scaled, sems = rest[:count], rest[count], rest[count + 1]
    copies = fetched(sources, held, sems)
    rows = weight[...]
    depth = outs[0].shape[0]
    done = 0
    seen = set()
    for left, right, first, last in pieces:
        for k in (lefts + right, left):
            if k not in seen:
                copies[k].wait()
                seen.add(k)
        for col in range(first, last, 128):
            piece = held[lefts + right][:, col : col + 128].astype(jnp.float32) * rows
            scaled[:, col - first : col - first + 128] = piece.astype(jnp.bfloat16)
        for k in range(4):
            for col in range(0, last - first, 256):
                end = min(col + 256, last - first)
                outs[k][:, done + col : done + end] = jnp.dot(
                    held[left][depth * k : depth * (k + 1), :],
                    scaled[:, col:end],
                    preferred_element_type=jnp.float32,
                ).astype(jnp.bfloat16)
        done += last - first


def products(weight, lefts, rights, pieces):
    width = sum(last - first for _, _, first, last in pieces)
    sides = [*lefts, *rights]
    depth = weight.shape[0]
    return pl.pallas_call(
        functools.partial(product_kernel, pieces),
        out_shape=[jax.ShapeDtypeStruct((256, width), jnp.bfloat16)] * 4,
        in_specs=[WHOLE] + [UNREAD] * len(sides),
        out_specs=[WHOLE] * 4,
        scratch_shapes=[pltpu.VMEM(side.shape, side.dtype) for side in sides]
        + [
            pltpu.VMEM((depth, max(piece[3] - piece[2] for piece in pieces)), jnp.bfloat16),
            pltpu.SemaphoreType.DMA((len(sides),)),
        ],
        compiler_params=pltpu.CompilerParams(vmem_limit_bytes=18 << 20),
        cost_estimate=LIGHT,
    )(weight, *sides)


def sum_kernel(*refs):
    sources, outs, held, sems = refs[:8], refs[-17:-9], refs[-9:-1], refs[-1]
    copies = fetched(sources, held, sems)
    for part in range(2):
        blocks = held[4 * part : 4 * part + 4]
        for copy in copies[4 * part : 4 * part + 4]:
            copy.wait()
        rows = outs[4 * part].shape[0]
        for k in range(4):
            here = pl.ds(k * rows, rows)
            total = blocks[0][here, :].astype(jnp.float32)
            for ref in blocks[1:]:
                total = total + ref[here, :].astype(jnp.float32)
            outs[4 * part + k][...] = total.astype(jnp.bfloat16)


def sum_blocks(parts, grant, ready=()):
    blocks = [block for part in parts for block in part]
    out = pl.pallas_call(
        sum_kernel,
        out_shape=[
            jax.ShapeDtypeStruct((block.shape[0] // 4, block.shape[1]), jnp.bfloat16)
            for block in blocks
        ],
        in_specs=[UNREAD] * (8 + len(ready)),
        out_specs=[WHOLE] * 8,
        scratch_shapes=[pltpu.VMEM(block.shape, block.dtype) for block in blocks]
        + [pltpu.SemaphoreType.DMA((8,))],
        compiler_params=pltpu.CompilerParams(vmem_limit_bytes=grant),
        cost_estimate=LIGHT,
    )(*blocks, *ready)
    return [out[:4], out[4:]]


def copy_kernel(source, out, sem):
    copy = pltpu.make_async_copy(source, out, sem)
    copy.start()
    copy.wait()


def copied(block):
    return pl.pallas_call(
        copy_kernel,
        out_shape=jax.ShapeDtypeStruct(block.shape, block.dtype),
        in_specs=[UNREAD],
        out_specs=UNREAD,
        scratch_shapes=[pltpu.SemaphoreType.DMA],
        compiler_params=pltpu.CompilerParams(vmem_limit_bytes=1 << 20),
        cost_estimate=LIGHT,
    )(block)


def last_kernel(*refs):
    down, up = refs[-2:]
    sums = []
    for part in range(2):
        total = refs[4 * part][...].astype(jnp.float32)
        for ref in refs[4 * part + 1 : 4 * part + 4]:
            total = total + ref[...].astype(jnp.float32)
        sums.append(total)
    width = down.shape[1]
    cut = sums[0].shape[1] - width
    down[...] = sums[0][:, :width]
    up[:, :cut] = sums[0][:, width:]
    up[:, cut:] = sums[1]


def last_sum(parts, ready, width):
    return pl.pallas_call(
        last_kernel,
        out_shape=[jax.ShapeDtypeStruct((16, width), jnp.float32)] * 2,
        in_specs=[WHOLE] * 8 + [UNREAD] * len(ready),
        out_specs=[WHOLE] * 2,
        compiler_params=pltpu.CompilerParams(vmem_limit_bytes=4 << 20),
        cost_estimate=LIGHT,
    )(*[block for part in parts for block in part], *ready)


def exchanged(parts, step):
    first, second = parts
    axes = (ORDER["x"][step], ORDER["y"][step])
    return [
        [first[0]] + [shift_each(first[by], axes, by) for by in (1, 3, 2)],
        [second[0]] + [shift(second[by], ORDER["z"][step], by) for by in (1, 3, 2)],
    ]


def local(
    ref_image,
    ref_text,
    learner_image,
    learner_text,
    patches,
    cotangent,
    w_up,
    w_down,
    counts,
    sel_index,
    sel_dest,
):
    core = lax.axis_index("core")
    learner = lax.axis_index("zh") == 1
    pad = ((0, 0), (0, learner_image.shape[1] - ref_image.shape[1]))
    image = jnp.where(learner, learner_image, jnp.pad(ref_image, pad))
    text = jnp.where(learner, learner_text, jnp.pad(ref_text, pad))
    at = jnp.stack([lax.axis_index(name) for name in ("y", "x", "zl", "core", "zh")]).astype(
        jnp.int32
    )
    slots = sel_index.shape[0]
    patch_rows, size = patches.shape[1:]
    count, width, rows = slots * patch_rows, w_up.shape[1], image.shape[0]
    index = sel_index[:, None]

    other_image = lax.ppermute(image, "zl", SWAP)
    texts = around(text, "y")
    texts_other = lax.ppermute(jnp.concatenate(texts, axis=0), "core", SWAP)
    pair, index = pair_rows(at, image, other_image, index, texts[1:])
    images = around(pair, "x")

    x_mine = patches[index[:, 0]].reshape(count, size)
    x_other = lax.ppermute(x_mine, "core", SWAP)
    act, slope = up(at, x_mine, x_other, w_up)
    cot_mine = cotangent[index[:, 0]].reshape(count, size)
    cot_other = lax.ppermute(cot_mine, "core", SWAP)
    x_first, x_second = turn(at, x_mine, x_other, ("xy", "z"))
    grad_pre = back(at, cot_mine, cot_other, w_down, slope)
    (cot_first,) = turn(at, cot_mine, cot_other, ("xy",))

    parts = partial_losses(at, images, texts, texts_other, [x_first, grad_pre, cot_first])
    parts = lax.all_to_all(
        parts, ("y", "x", "zl", "core", "zh"), split_axis=0, concat_axis=0, tiled=True
    )
    scores, weight = weights(counts, parts, index, [])
    learnability = lax.dynamic_slice_in_dim(scores[0], core * rows, rows)

    cut = 640
    blocks = [
        products(
            weight,
            [cot_first, x_first],
            [act, grad_pre],
            ((0, 0, 0, width), (1, 1, 0, cut)),
        ),
        products(weight, [x_second], [grad_pre], ((0, 0, cut, width),)),
    ]
    keep, give = down(at, act, w_down, [blocks[0][0], blocks[1][0]])
    got = lax.ppermute(give, "core", SWAP)
    blocks = exchanged(blocks, 0)
    boxed = place(counts, sel_dest, x_mine, keep, got, [blocks[1][2]])
    boxed = boxed.reshape(32, 4, patch_rows, size)
    routed = lax.all_to_all(boxed, DP, split_axis=0, concat_axis=0, tiled=True)
    blocks = sum_blocks(blocks, 18 << 20, [routed])
    routed = copied(routed.reshape(128, patch_rows, size))
    blocks = sum_blocks(exchanged(blocks, 1), 6 << 20)
    grad_down_t, grad_up = last_sum(exchanged(blocks, 2), [routed], width)
    return (learnability, routed, grad_up, grad_down_t)


def solution(mesh):
    mesh = Mesh(mesh.devices.reshape(4, 4, 2, 2, 2), ("y", "x", "zl", "core", "zh"))
    pairs = P(("y", "x", "zl", "core"), None)
    patch = P(DP, "zh", "core")
    return jax.shard_map(
        local,
        mesh=mesh,
        in_specs=(
            pairs,
            pairs,
            pairs,
            pairs,
            patch,
            patch,
            P(None, "core"),
            P("core", None),
            P(DP),
            P(DP),
            P(DP, None),
        ),
        out_specs=(
            P(("y", "x", "zl", "core")),
            patch,
            P(CHIPS, "core"),
            P(CHIPS, "core"),
        ),
        check_vma=False,
    )
```

```python
import functools
import math

import jax
import jax.numpy as jnp
from jax import lax
from jax.experimental import pallas as pl
from jax.experimental.pallas import tpu as pltpu
from jax.sharding import Mesh, PartitionSpec as P

DP = ("y", "x", "zl")
CHIPS = ("y", "x", "zl", "zh")
SWAP = [(0, 1), (1, 0)]
ORDER = {"x": "xyz", "y": "yzx", "z": "zxy"}
WHOLE = pl.BlockSpec(memory_space=pltpu.VMEM)
SCALARS = pl.BlockSpec(memory_space=pltpu.SMEM)
FAR = pl.BlockSpec(memory_space=pltpu.HBM)
UNREAD = pl.BlockSpec(memory_space=pl.ANY)
LIGHT = pl.CostEstimate(flops=1 << 20, bytes_accessed=1 << 16, transcendentals=0)


def unit(rows):
    wide = rows.astype(jnp.float32)
    norm = lax.rsqrt(jnp.sum(wide * wide, axis=1, keepdims=True) + 1e-06)
    return (wide * norm).astype(jnp.bfloat16)


def softplus(value):
    return jnp.maximum(value, 0.0) + jnp.log1p(jnp.exp(-jnp.abs(value)))


def loss_kernel(at, *refs):
    img_refs, txt_refs, txt_other, (out, img, txt) = refs[:4], refs[4:8], refs[8], refs[-3:]
    here_y, here_x, here_zl, here_core, learner = (at[k] for k in range(5))
    for k in range(4):
        img[pl.ds(128 * k, 128), :] = unit(img_refs[k][...])
        own = pl.multiple_of(128 * k + 64 * here_core, 64)
        txt[pl.ds(own, 64), :] = unit(txt_refs[k][...])
        other = pl.multiple_of(128 * k + 64 * (1 - here_core), 64)
        txt[pl.ds(other, 64), :] = unit(txt_other[pl.ds(64 * k, 64), :])
    contract = (((1,), (1,)), ((), ()))
    col_sum = jnp.zeros((1, 512), jnp.float32)
    row_sums = []
    for k in range(4):
        scores = (
            10.0
            * lax.dot_general(
                img[pl.ds(128 * k, 128), :], txt[...], contract, preferred_element_type=jnp.float32
            )
            - 5.0
        )
        if k == 0:
            row = lax.broadcasted_iota(jnp.int32, scores.shape, 0) - 64 * here_zl
            col = lax.broadcasted_iota(jnp.int32, scores.shape, 1) - 64 * here_core
            same = (row == col) & (row >= 0) & (row < 64)
            scores = jnp.where(same, -scores, scores)
        terms = softplus(scores)
        col_sum = col_sum + jnp.sum(terms, axis=0, keepdims=True)
        folded = terms[:, :128] + terms[:, 128:256] + terms[:, 256:384] + terms[:, 384:]
        row_sums.append(jnp.sum(folded.T, axis=0, keepdims=True))
    dest = lax.broadcasted_iota(jnp.int32, (128, 128), 0)
    lane = lax.broadcasted_iota(jnp.int32, (1, 128), 1)
    dest_y, dest_x, dest_zl = dest >> 5, (dest >> 3) & 3, (dest >> 2) & 1
    own_half = (lane >> 6) == here_core
    total = jnp.zeros((128, 128), jnp.float32)
    for k in range(4):
        straight = row_sums[k]
        crossed = pltpu.roll(straight, 64, 1)
        for zl in range(2):
            placed = jnp.where(own_half, jnp.where(here_core == zl, straight, crossed), 0.0)
            mine = (dest_y == here_y) & (dest_x == ((here_x + k) & 3)) & (dest_zl == zl)
            total = total + jnp.where(mine, placed, 0.0)
        mine = (dest_y == ((here_y + k) & 3)) & (dest_x == here_x) & (dest_zl == here_zl)
        total = total + jnp.where(mine, col_sum[:, 128 * k : 128 * (k + 1)], 0.0)
    out[...] = jnp.where(learner == 1, 0.5, -0.5) * total


def partial_losses(at, images, texts, texts_other, ready):
    return pl.pallas_call(
        loss_kernel,
        out_shape=jax.ShapeDtypeStruct((128, 128), jnp.float32),
        in_specs=[SCALARS] + [WHOLE] * 9 + [UNREAD] * len(ready),
        out_specs=WHOLE,
        scratch_shapes=[pltpu.VMEM((512, 1024), jnp.bfloat16)] * 2,
        compiler_params=pltpu.CompilerParams(vmem_limit_bytes=8 << 20),
        cost_estimate=LIGHT,
    )(at, *images, *texts, texts_other, *ready)


def weight_kernel(count, parts, index, *refs):
    learn, weight = refs[-2:]
    score = jnp.sum(parts[...], axis=0, keepdims=True)
    learn[...] = jnp.broadcast_to(score, (8, 128))
    slots = index.shape[0]
    picked = index[...] == lax.broadcasted_iota(jnp.int32, (slots, 128), 1)
    chosen = jnp.sum(jnp.where(picked, score, 0.0), axis=1, keepdims=True)
    live = lax.broadcasted_iota(jnp.int32, (slots, 128), 0) < count[0]
    value = jnp.where(live, 1.0 / (1.0 + jnp.exp(-chosen)), 0.0)
    weight[...] = jnp.broadcast_to(value[:, None, :], (slots, 8, 128)).reshape(8 * slots, 128)


def weights(counts, parts, index, ready):
    slots = index.shape[0]
    return pl.pallas_call(
        weight_kernel,
        out_shape=(
            jax.ShapeDtypeStruct((8, 128), jnp.float32),
            jax.ShapeDtypeStruct((8 * slots, 128), jnp.float32),
        ),
        in_specs=[SCALARS, WHOLE, WHOLE] + [UNREAD] * len(ready),
        out_specs=(WHOLE, WHOLE),
        compiler_params=pltpu.CompilerParams(vmem_limit_bytes=2 << 20),
        cost_estimate=LIGHT,
    )(counts, parts, index, *ready)


def pair_kernel(at, own, other, index, *refs):
    pair, index_out = refs[-2:]
    pair[pl.ds(pl.multiple_of(64 * at[2], 64), 64), :] = own[...]
    pair[pl.ds(pl.multiple_of(64 * (1 - at[2]), 64), 64), :] = other[...]
    index_out[...] = index[...]


def pair_rows(at, own, other, index, ready):
    rows, width = own.shape
    return pl.pallas_call(
        pair_kernel,
        out_shape=(
            jax.ShapeDtypeStruct((2 * rows, width), own.dtype),
            jax.ShapeDtypeStruct(index.shape, jnp.int32),
        ),
        in_specs=[SCALARS, WHOLE, WHOLE, WHOLE] + [UNREAD] * len(ready),
        out_specs=(WHOLE, WHOLE),
        compiler_params=pltpu.CompilerParams(vmem_limit_bytes=2 << 20),
        cost_estimate=LIGHT,
    )(at, own, other, index, *ready)


def half(ref, axis, which, size):
    start = pl.multiple_of(which * size, size)
    return ref[pl.ds(start, size), :] if axis == 0 else ref[:, pl.ds(start, size)]


def up_kernel(at, mine, other, w_up, act, slope, held, sems):
    size = mine.shape[1]
    steps, _, tile = held.shape
    columns = [pl.ds(n * tile, tile) for n in range(steps)]
    copies = fetched([w_up.at[:, cols] for cols in columns], [held.at[n] for n in range(steps)], sems)
    scale = math.sqrt(2.0 / math.pi)
    for n, cols in enumerate(columns):
        copies[n].wait()
        near, far = half(held.at[n], 0, at[3], size), half(held.at[n], 0, 1 - at[3], size)
        for row in range(0, mine.shape[0], 256):
            rows = pl.ds(row, 256)
            pre = jnp.dot(mine[rows, :], near, preferred_element_type=jnp.float32)
            pre = pre + jnp.dot(other[rows, :], far, preferred_element_type=jnp.float32)
            square = pre * pre
            tanh = jnp.tanh(pre * (scale + (scale * 0.044715) * square))
            gate = 0.5 + 0.5 * tanh
            act[rows, cols] = (pre * gate).astype(jnp.bfloat16)
            bend = pre * (0.5 - 0.5 * tanh * tanh) * (scale + (scale * 3 * 0.044715) * square)
            slope[rows, cols] = (gate + bend).astype(jnp.bfloat16)


def up(at, mine, other, w_up):
    rows, size = mine.shape
    width, tile = w_up.shape[1], 512
    return pl.pallas_call(
        up_kernel,
        out_shape=[jax.ShapeDtypeStruct((rows, width), jnp.bfloat16)] * 2,
        in_specs=[SCALARS, WHOLE, WHOLE, FAR],
        out_specs=[WHOLE, WHOLE],
        scratch_shapes=[
            pltpu.VMEM((width // tile, 2 * size, tile), w_up.dtype),
            pltpu.SemaphoreType.DMA((width // tile,)),
        ],
        compiler_params=pltpu.CompilerParams(vmem_limit_bytes=16 << 20),
        cost_estimate=LIGHT,
    )(at, mine, other, w_up)


def back_kernel(at, mine, other, w_down, slope, out, held, sems):
    size = mine.shape[1]
    steps, tile, _ = held.shape
    columns = [pl.ds(n * tile, tile) for n in range(steps)]
    copies = fetched([w_down.at[cols] for cols in columns], [held.at[n] for n in range(steps)], sems)
    contract = (((1,), (1,)), ((), ()))
    for n, cols in enumerate(columns):
        copies[n].wait()
        near, far = half(held.at[n], 1, at[3], size), half(held.at[n], 1, 1 - at[3], size)
        back = lax.dot_general(mine[...], near, contract, preferred_element_type=jnp.float32)
        back = back + lax.dot_general(other[...], far, contract, preferred_element_type=jnp.float32)
        out[:, cols] = (back * slope[:, cols].astype(jnp.float32)).astype(jnp.bfloat16)


def back(at, mine, other, w_down, slope):
    rows, size = mine.shape
    width, tile = w_down.shape[0], 512
    return pl.pallas_call(
        back_kernel,
        out_shape=jax.ShapeDtypeStruct((rows, width), jnp.bfloat16),
        in_specs=[SCALARS, WHOLE, WHOLE, FAR, WHOLE],
        out_specs=WHOLE,
        scratch_shapes=[
            pltpu.VMEM((width // tile, tile, 2 * size), w_down.dtype),
            pltpu.SemaphoreType.DMA((width // tile,)),
        ],
        compiler_params=pltpu.CompilerParams(vmem_limit_bytes=16 << 20),
        cost_estimate=LIGHT,
    )(at, mine, other, w_down, slope)


def turn_kernel(starts, at, mine, other, *refs):
    outs, turned = refs[:-1], refs[-1]
    blocks = turned.shape[0] // 2
    turned[pl.ds(at[3] * blocks, blocks)] = mine[...].T.reshape((blocks,) + turned.shape[1:])
    turned[pl.ds((1 - at[3]) * blocks, blocks)] = other[...].T.reshape(
        (blocks,) + turned.shape[1:]
    )
    here = {"x": at[1], "y": at[0], "z": 2 * at[4] + at[2]}
    for start, out in zip(starts, outs):
        for k in range(2 * blocks):
            steps = (k >> 4, (k >> 2) & 3, k & 3)
            spot = {}
            for axis in "xyz":
                by = [steps[ORDER[one].index(axis)] for one in start]
                by = by[0] + at[3] * (by[-1] - by[0])
                spot[axis] = (here[axis] + by) & 3
            block = 16 * spot["y"] + 4 * spot["x"] + 2 * (spot["z"] & 1) + (spot["z"] >> 1)
            out[16 * k : 16 * (k + 1), :] = turned[block]


def turn(at, mine, other, starts):
    rows, size = mine.shape
    return pl.pallas_call(
        functools.partial(turn_kernel, starts),
        out_shape=[jax.ShapeDtypeStruct((2 * size, rows), mine.dtype)] * len(starts),
        in_specs=[SCALARS, WHOLE, WHOLE],
        out_specs=[WHOLE] * len(starts),
        scratch_shapes=[pltpu.VMEM((2 * size // 16, 16, rows), mine.dtype)],
        compiler_params=pltpu.CompilerParams(vmem_limit_bytes=8 << 20),
        cost_estimate=LIGHT,
    )(at, mine, other)


def down_kernel(at, act, w_down, *refs):
    keep, give = refs[-2:]
    size = keep.shape[1]
    keep[...] = jnp.dot(
        act[...], half(w_down, 1, at[3], size), preferred_element_type=jnp.float32
    )
    give[...] = jnp.dot(
        act[...], half(w_down, 1, 1 - at[3], size), preferred_element_type=jnp.float32
    )


def down(at, act, w_down, ready):
    rows, size = act.shape[0], w_down.shape[1] // 2
    return pl.pallas_call(
        down_kernel,
        out_shape=[jax.ShapeDtypeStruct((rows, size), jnp.float32)] * 2,
        in_specs=[SCALARS, WHOLE, WHOLE] + [UNREAD] * len(ready),
        out_specs=[WHOLE, WHOLE],
        compiler_params=pltpu.CompilerParams(vmem_limit_bytes=14 << 20),
        cost_estimate=LIGHT,
    )(at, act, w_down, *ready)


def place_kernel(count, target_col, target_row, own, keep, got, *refs):
    out = refs[-1]
    slots, rows = target_col.shape[0], own.shape[0]
    each = rows // slots
    out_rows = (own[...].astype(jnp.float32) + keep[...] + got[...]).astype(jnp.bfloat16)
    slot = lax.broadcasted_iota(jnp.int32, (slots, slots), 0)
    before = lax.broadcasted_iota(jnp.int32, (slots, slots), 1)
    same = (target_row[...] == target_col[...]) & (before < slot)
    rank = jnp.sum(same.astype(jnp.int32), axis=1, keepdims=True)
    live = lax.broadcasted_iota(jnp.int32, (slots, 1), 0) < count[0]
    first = jnp.where(live, each * (4 * target_col[...] + rank), -each)
    lane = lax.broadcasted_iota(jnp.int32, (slots, rows), 1)
    mine = (lane // each) == lax.broadcasted_iota(jnp.int32, (slots, rows), 0)
    goes = jnp.sum(jnp.where(mine, first + lane % each, 0), axis=0, keepdims=True)
    step = 256
    for at in range(0, out.shape[0], step):
        here = lax.broadcasted_iota(jnp.int32, (step, rows), 0) + at == goes
        out[at : at + step, :] = jnp.dot(
            jnp.where(here, 1.0, 0.0).astype(jnp.bfloat16),
            out_rows,
            preferred_element_type=jnp.float32,
        ).astype(jnp.bfloat16)


def place(counts, target, own, keep, got, ready):
    rows, size = own.shape
    slots = target.shape[0]
    return pl.pallas_call(
        place_kernel,
        out_shape=jax.ShapeDtypeStruct((2 * rows, size), jnp.bfloat16),
        in_specs=[SCALARS] + [WHOLE] * 5 + [UNREAD] * len(ready),
        out_specs=WHOLE,
        compiler_params=pltpu.CompilerParams(vmem_limit_bytes=8 << 20),
        cost_estimate=LIGHT,
    )(counts, target, target.reshape(1, slots), own, keep, got, *ready)


def around(block, axis):
    return [block] + [shift(block, axis, 4 - by) for by in (1, 2, 3)]


def shift(block, axis, by):
    if axis == "z":
        at = [(z % 2) * 2 + z // 2 for z in range(4)]
        return lax.ppermute(block, ("zl", "zh"), [(at[z], at[(z + by) % 4]) for z in range(4)])
    return lax.ppermute(block, axis, [(k, (k + by) % 4) for k in range(4)])


def number(spot, core):
    return 8 * (4 * spot["y"] + spot["x"]) + 4 * (spot["z"] % 2) + 2 * core + spot["z"] // 2


def shift_each(block, axes, by):
    route = []
    for chip in range(64):
        spot = {"x": chip % 4, "y": chip // 4 % 4, "z": chip // 16}
        for core in range(2):
            axis = axes[core]
            there = {**spot, axis: (spot[axis] + by) % 4}
            route.append((number(spot, core), number(there, core)))
    return lax.ppermute(block, ("y", "x", "zl", "core", "zh"), route)


def fetched(sources, targets, sems):
    copies = [
        pltpu.make_async_copy(source, target, sems.at[k])
        for k, (source, target) in enumerate(zip(sources, targets))
    ]
    for copy in copies:
        copy.start()
    return copies


def product_kernel(pieces, weight, *refs):
    lefts = 1 + max(piece[0] for piece in pieces)
    rights = 1 + max(piece[1] for piece in pieces)
    count = lefts + rights
    sources, rest = refs[:count], refs[len(refs) - count - 6 :]
    outs, held, scaled, sems = rest[:4], rest[4 : 4 + count], rest[-2], rest[-1]
    copies = fetched(sources, held, sems)
    rows = weight[...]
    depth = outs[0].shape[0]
    done = 0
    seen = set()
    for left, right, first, last in pieces:
        for k in (lefts + right, left):
            if k not in seen:
                copies[k].wait()
                seen.add(k)
        for col in range(first, last, 128):
            piece = held[lefts + right][:, col : col + 128].astype(jnp.float32) * rows
            scaled[:, col - first : col - first + 128] = piece.astype(jnp.bfloat16)
        for k in range(4):
            for col in range(0, last - first, 256):
                end = min(col + 256, last - first)
                outs[k][:, done + col : done + end] = jnp.dot(
                    held[left][depth * k : depth * (k + 1), :],
                    scaled[:, col:end],
                    preferred_element_type=jnp.float32,
                ).astype(jnp.bfloat16)
        done += last - first


def products(weight, lefts, rights, pieces, ready=()):
    width = sum(last - first for _, _, first, last in pieces)
    sides = [*lefts, *rights]
    depth = weight.shape[0]
    return pl.pallas_call(
        functools.partial(product_kernel, pieces),
        out_shape=[jax.ShapeDtypeStruct((256, width), jnp.bfloat16)] * 4,
        in_specs=[WHOLE] + [FAR] * len(sides) + [UNREAD] * len(ready),
        out_specs=[WHOLE] * 4,
        scratch_shapes=[pltpu.VMEM(side.shape, side.dtype) for side in sides]
        + [
            pltpu.VMEM((depth, max(piece[3] - piece[2] for piece in pieces)), jnp.bfloat16),
            pltpu.SemaphoreType.DMA((len(sides),)),
        ],
        compiler_params=pltpu.CompilerParams(vmem_limit_bytes=18 << 20),
        cost_estimate=LIGHT,
    )(weight, *sides, *ready)


def sum_kernel(*refs):
    sources, outs, held, sems = refs[:8], refs[-17:-9], refs[-9:-1], refs[-1]
    copies = fetched(sources, held, sems)
    for part in range(2):
        blocks = held[4 * part : 4 * part + 4]
        for copy in copies[4 * part : 4 * part + 4]:
            copy.wait()
        rows = outs[4 * part].shape[0]
        for k in range(4):
            here = pl.ds(k * rows, rows)
            total = blocks[0][here, :].astype(jnp.float32)
            for ref in blocks[1:]:
                total = total + ref[here, :].astype(jnp.float32)
            outs[4 * part + k][...] = total.astype(jnp.bfloat16)


def sum_blocks(parts, grant, ready=()):
    blocks = [block for part in parts for block in part]
    out = pl.pallas_call(
        sum_kernel,
        out_shape=[
            jax.ShapeDtypeStruct((block.shape[0] // 4, block.shape[1]), jnp.bfloat16)
            for block in blocks
        ],
        in_specs=[UNREAD] * (8 + len(ready)),
        out_specs=[WHOLE] * 8,
        scratch_shapes=[pltpu.VMEM(block.shape, block.dtype) for block in blocks]
        + [pltpu.SemaphoreType.DMA((8,))],
        compiler_params=pltpu.CompilerParams(vmem_limit_bytes=grant),
        cost_estimate=LIGHT,
    )(*blocks, *ready)
    return [out[:4], out[4:]]


def copy_kernel(source, out, sem):
    copy = pltpu.make_async_copy(source, out, sem)
    copy.start()
    copy.wait()


def copied(block):
    return pl.pallas_call(
        copy_kernel,
        out_shape=jax.ShapeDtypeStruct(block.shape, block.dtype),
        in_specs=[UNREAD],
        out_specs=UNREAD,
        scratch_shapes=[pltpu.SemaphoreType.DMA],
        compiler_params=pltpu.CompilerParams(vmem_limit_bytes=1 << 20),
        cost_estimate=LIGHT,
    )(block)


def last_kernel(*refs):
    down, up = refs[-2:]
    sums = []
    for part in range(2):
        total = refs[4 * part][...].astype(jnp.float32)
        for ref in refs[4 * part + 1 : 4 * part + 4]:
            total = total + ref[...].astype(jnp.float32)
        sums.append(total)
    width = down.shape[1]
    cut = sums[0].shape[1] - width
    down[...] = sums[0][:, :width]
    up[:, :cut] = sums[0][:, width:]
    up[:, cut:] = sums[1]


def last_sum(parts, ready, width):
    return pl.pallas_call(
        last_kernel,
        out_shape=[jax.ShapeDtypeStruct((16, width), jnp.float32)] * 2,
        in_specs=[WHOLE] * 8 + [UNREAD] * len(ready),
        out_specs=[WHOLE] * 2,
        compiler_params=pltpu.CompilerParams(vmem_limit_bytes=4 << 20),
        cost_estimate=LIGHT,
    )(*[block for part in parts for block in part], *ready)


def exchanged(parts, step):
    first, second = parts
    axes = (ORDER["x"][step], ORDER["y"][step])
    return [
        [first[0]] + [shift_each(first[by], axes, by) for by in (1, 3, 2)],
        [second[0]] + [shift(second[by], ORDER["z"][step], by) for by in (1, 3, 2)],
    ]


def local(
    ref_image,
    ref_text,
    learner_image,
    learner_text,
    patches,
    cotangent,
    w_up,
    w_down,
    counts,
    sel_index,
    sel_dest,
):
    core = lax.axis_index("core")
    learner = lax.axis_index("zh") == 1
    pad = ((0, 0), (0, learner_image.shape[1] - ref_image.shape[1]))
    image = jnp.where(learner, learner_image, jnp.pad(ref_image, pad))
    text = jnp.where(learner, learner_text, jnp.pad(ref_text, pad))
    at = jnp.stack([lax.axis_index(name) for name in ("y", "x", "zl", "core", "zh")]).astype(
        jnp.int32
    )
    slots = sel_index.shape[0]
    patch_rows, size = patches.shape[1:]
    count, width, rows = slots * patch_rows, w_up.shape[1], image.shape[0]
    index = sel_index[:, None]

    other_image = lax.ppermute(image, "zl", SWAP)
    texts = around(text, "y")
    texts_other = lax.ppermute(jnp.concatenate(texts, axis=0), "core", SWAP)
    pair, index = pair_rows(at, image, other_image, index, texts[1:])
    images = around(pair, "x")

    x_mine = patches[sel_index].reshape(count, size)
    x_other = lax.ppermute(x_mine, "core", SWAP)
    act, slope = up(at, x_mine, x_other, w_up)
    cot_mine = cotangent[sel_index].reshape(count, size)
    cot_other = lax.ppermute(cot_mine, "core", SWAP)
    x_first, x_second = turn(at, x_mine, x_other, ("xy", "z"))
    grad_pre = back(at, cot_mine, cot_other, w_down, slope)
    (cot_first,) = turn(at, cot_mine, cot_other, ("xy",))

    parts = partial_losses(at, images, texts, texts_other, [x_first, grad_pre, cot_first])
    parts = lax.all_to_all(
        parts, ("y", "x", "zl", "core", "zh"), split_axis=0, concat_axis=0, tiled=True
    )
    scores, weight = weights(counts, parts, index, [])
    learnability = lax.dynamic_slice_in_dim(scores[0], core * rows, rows)

    cut = 640
    second = products(weight, [x_second], [grad_pre], ((0, 0, cut, width),))
    first = products(
        weight,
        [cot_first, x_first],
        [act, grad_pre],
        ((0, 0, 0, width), (1, 1, 0, cut)),
        second[:1],
    )
    blocks = exchanged([first, second], 0)
    keep, give = down(at, act, w_down, blocks[1][1:])
    got = lax.ppermute(give, "core", SWAP)
    boxed = place(counts, sel_dest, x_mine, keep, got, [])
    boxed = boxed.reshape(32, 4, patch_rows, size)
    routed = lax.all_to_all(boxed, DP, split_axis=0, concat_axis=0, tiled=True)
    routed = copied(routed.reshape(128, patch_rows, size))
    blocks = sum_blocks(blocks, 18 << 20)
    blocks = sum_blocks(exchanged(blocks, 1), 6 << 20)
    grad_down_t, grad_up = last_sum(exchanged(blocks, 2), [routed], width)
    return (learnability, routed, grad_up, grad_down_t)


def solution(mesh):
    mesh = Mesh(mesh.devices.reshape(4, 4, 2, 2, 2), ("y", "x", "zl", "core", "zh"))
    pairs = P(("y", "x", "zl", "core"), None)
    patch = P(DP, "zh", "core")
    return jax.shard_map(
        local,
        mesh=mesh,
        in_specs=(
            pairs,
            pairs,
            pairs,
            pairs,
            patch,
            patch,
            P(None, "core"),
            P("core", None),
            P(DP),
            P(DP),
            P(DP, None),
        ),
        out_specs=(
            P(("y", "x", "zl", "core")),
            patch,
            P(CHIPS, "core"),
            P(CHIPS, "core"),
        ),
        check_vma=False,
    )
```

```python
import functools
import math

import jax
import jax.numpy as jnp
from jax import lax
from jax.experimental import pallas as pl
from jax.experimental.pallas import tpu as pltpu
from jax.sharding import Mesh, PartitionSpec as P

DP = ("y", "x", "zl")
CHIPS = ("y", "x", "zl", "zh")
SWAP = [(0, 1), (1, 0)]
ORDER = {"x": "xyz", "y": "yzx", "z": "zxy"}
WHOLE = pl.BlockSpec(memory_space=pltpu.VMEM)
SCALARS = pl.BlockSpec(memory_space=pltpu.SMEM)
FAR = pl.BlockSpec(memory_space=pltpu.HBM)
UNREAD = pl.BlockSpec(memory_space=pl.ANY)
LIGHT = pl.CostEstimate(flops=1 << 20, bytes_accessed=1 << 16, transcendentals=0)


def unit(rows):
    wide = rows.astype(jnp.float32)
    norm = lax.rsqrt(jnp.sum(wide * wide, axis=1, keepdims=True) + 1e-06)
    return (wide * norm).astype(jnp.bfloat16)


def softplus(value):
    return jnp.maximum(value, 0.0) + jnp.log1p(jnp.exp(-jnp.abs(value)))


def loss_kernel(at, *refs):
    img_refs, txt_refs, txt_other, (out, img, txt) = refs[:4], refs[4:8], refs[8], refs[-3:]
    here_y, here_x, here_zl, here_core, learner = (at[k] for k in range(5))
    for k in range(4):
        img[pl.ds(128 * k, 128), :] = unit(img_refs[k][...])
        own = pl.multiple_of(128 * k + 64 * here_core, 64)
        txt[pl.ds(own, 64), :] = unit(txt_refs[k][...])
        other = pl.multiple_of(128 * k + 64 * (1 - here_core), 64)
        txt[pl.ds(other, 64), :] = unit(txt_other[pl.ds(64 * k, 64), :])
    contract = (((1,), (1,)), ((), ()))
    col_sum = jnp.zeros((1, 512), jnp.float32)
    row_sums = []
    for k in range(4):
        scores = (
            10.0
            * lax.dot_general(
                img[pl.ds(128 * k, 128), :], txt[...], contract, preferred_element_type=jnp.float32
            )
            - 5.0
        )
        if k == 0:
            row = lax.broadcasted_iota(jnp.int32, scores.shape, 0) - 64 * here_zl
            col = lax.broadcasted_iota(jnp.int32, scores.shape, 1) - 64 * here_core
            same = (row == col) & (row >= 0) & (row < 64)
            scores = jnp.where(same, -scores, scores)
        terms = softplus(scores)
        col_sum = col_sum + jnp.sum(terms, axis=0, keepdims=True)
        folded = terms[:, :128] + terms[:, 128:256] + terms[:, 256:384] + terms[:, 384:]
        row_sums.append(jnp.sum(folded.T, axis=0, keepdims=True))
    dest = lax.broadcasted_iota(jnp.int32, (128, 128), 0)
    lane = lax.broadcasted_iota(jnp.int32, (1, 128), 1)
    dest_y, dest_x, dest_zl = dest >> 5, (dest >> 3) & 3, (dest >> 2) & 1
    own_half = (lane >> 6) == here_core
    total = jnp.zeros((128, 128), jnp.float32)
    for k in range(4):
        straight = row_sums[k]
        crossed = pltpu.roll(straight, 64, 1)
        for zl in range(2):
            placed = jnp.where(own_half, jnp.where(here_core == zl, straight, crossed), 0.0)
            mine = (dest_y == here_y) & (dest_x == ((here_x + k) & 3)) & (dest_zl == zl)
            total = total + jnp.where(mine, placed, 0.0)
        mine = (dest_y == ((here_y + k) & 3)) & (dest_x == here_x) & (dest_zl == here_zl)
        total = total + jnp.where(mine, col_sum[:, 128 * k : 128 * (k + 1)], 0.0)
    out[...] = jnp.where(learner == 1, 0.5, -0.5) * total


def partial_losses(at, images, texts, texts_other, ready):
    return pl.pallas_call(
        loss_kernel,
        out_shape=jax.ShapeDtypeStruct((128, 128), jnp.float32),
        in_specs=[SCALARS] + [WHOLE] * 9 + [UNREAD] * len(ready),
        out_specs=WHOLE,
        scratch_shapes=[pltpu.VMEM((512, 1024), jnp.bfloat16)] * 2,
        compiler_params=pltpu.CompilerParams(vmem_limit_bytes=8 << 20),
        cost_estimate=LIGHT,
    )(at, *images, *texts, texts_other, *ready)


def listed(values, axis, shape):
    at = lax.broadcasted_iota(jnp.int32, shape, axis)
    out = jnp.zeros(shape, jnp.int32)
    for k in range(shape[axis]):
        out = jnp.where(at == k, values[k], out)
    return out


def weight_kernel(count, index, parts, learn, weight):
    score = jnp.sum(parts[...], axis=0, keepdims=True)
    learn[...] = jnp.broadcast_to(score, (8, 128))
    slots = index.shape[0]
    picked = listed(index, 0, (slots, 128)) == lax.broadcasted_iota(jnp.int32, (slots, 128), 1)
    chosen = jnp.sum(jnp.where(picked, score, 0.0), axis=1, keepdims=True)
    live = lax.broadcasted_iota(jnp.int32, (slots, 128), 0) < count[0]
    value = jnp.where(live, 1.0 / (1.0 + jnp.exp(-chosen)), 0.0)
    weight[...] = jnp.broadcast_to(value[:, None, :], (slots, 8, 128)).reshape(8 * slots, 128)


def weights(counts, index, parts):
    slots = index.shape[0]
    return pl.pallas_call(
        weight_kernel,
        out_shape=(
            jax.ShapeDtypeStruct((8, 128), jnp.float32),
            jax.ShapeDtypeStruct((8 * slots, 128), jnp.float32),
        ),
        in_specs=[SCALARS, SCALARS, WHOLE],
        out_specs=(WHOLE, WHOLE),
        compiler_params=pltpu.CompilerParams(vmem_limit_bytes=2 << 20),
        cost_estimate=LIGHT,
    )(counts, index, parts)


def choose_kernel(at, ref_image, ref_text, learner_image, learner_text, image, text):
    width = ref_image.shape[1]

    @pl.when(at[4] == 1)
    def _():
        image[...] = learner_image[...]
        text[...] = learner_text[...]

    @pl.when(at[4] == 0)
    def _():
        for source, out in ((ref_image, image), (ref_text, text)):
            out[:, :width] = source[...]
            out[:, width:] = jnp.zeros((out.shape[0], out.shape[1] - width), out.dtype)


def choose(at, ref_image, ref_text, learner_image, learner_text):
    shape = jax.ShapeDtypeStruct(learner_image.shape, learner_image.dtype)
    return pl.pallas_call(
        choose_kernel,
        out_shape=(shape, shape),
        in_specs=[SCALARS] + [WHOLE] * 4,
        out_specs=(WHOLE, WHOLE),
        compiler_params=pltpu.CompilerParams(vmem_limit_bytes=2 << 20),
        cost_estimate=LIGHT,
    )(at, ref_image, ref_text, learner_image, learner_text)


def pair_kernel(at, own, other, *refs):
    pair = refs[-1]
    pair[pl.ds(pl.multiple_of(64 * at[2], 64), 64), :] = own[...]
    pair[pl.ds(pl.multiple_of(64 * (1 - at[2]), 64), 64), :] = other[...]


def pair_rows(at, own, other, ready):
    rows, width = own.shape
    return pl.pallas_call(
        pair_kernel,
        out_shape=jax.ShapeDtypeStruct((2 * rows, width), own.dtype),
        in_specs=[SCALARS, WHOLE, WHOLE] + [UNREAD] * len(ready),
        out_specs=WHOLE,
        compiler_params=pltpu.CompilerParams(vmem_limit_bytes=2 << 20),
        cost_estimate=LIGHT,
    )(at, own, other, *ready)


def half(ref, axis, which, size):
    start = pl.multiple_of(which * size, size)
    return ref[pl.ds(start, size), :] if axis == 0 else ref[:, pl.ds(start, size)]


def up_kernel(at, mine, other, w_up, act, slope, held, sems):
    size = mine.shape[1]
    steps, _, tile = held.shape
    columns = [pl.ds(n * tile, tile) for n in range(steps)]
    copies = fetched([w_up.at[:, cols] for cols in columns], [held.at[n] for n in range(steps)], sems)
    scale = math.sqrt(2.0 / math.pi)
    for n, cols in enumerate(columns):
        copies[n].wait()
        near, far = half(held.at[n], 0, at[3], size), half(held.at[n], 0, 1 - at[3], size)
        for row in range(0, mine.shape[0], 256):
            rows = pl.ds(row, 256)
            pre = jnp.dot(mine[rows, :], near, preferred_element_type=jnp.float32)
            pre = pre + jnp.dot(other[rows, :], far, preferred_element_type=jnp.float32)
            square = pre * pre
            tanh = jnp.tanh(pre * (scale + (scale * 0.044715) * square))
            gate = 0.5 + 0.5 * tanh
            act[rows, cols] = (pre * gate).astype(jnp.bfloat16)
            bend = pre * (0.5 - 0.5 * tanh * tanh) * (scale + (scale * 3 * 0.044715) * square)
            slope[rows, cols] = (gate + bend).astype(jnp.bfloat16)


def up(at, mine, other, w_up):
    rows, size = mine.shape
    width, tile = w_up.shape[1], 512
    return pl.pallas_call(
        up_kernel,
        out_shape=[jax.ShapeDtypeStruct((rows, width), jnp.bfloat16)] * 2,
        in_specs=[SCALARS, WHOLE, WHOLE, FAR],
        out_specs=[WHOLE, WHOLE],
        scratch_shapes=[
            pltpu.VMEM((width // tile, 2 * size, tile), w_up.dtype),
            pltpu.SemaphoreType.DMA((width // tile,)),
        ],
        compiler_params=pltpu.CompilerParams(vmem_limit_bytes=16 << 20),
        cost_estimate=LIGHT,
    )(at, mine, other, w_up)


def back_kernel(at, mine, other, w_down, slope, out, held, sems):
    size = mine.shape[1]
    steps, tile, _ = held.shape
    columns = [pl.ds(n * tile, tile) for n in range(steps)]
    copies = fetched([w_down.at[cols] for cols in columns], [held.at[n] for n in range(steps)], sems)
    contract = (((1,), (1,)), ((), ()))
    for n, cols in enumerate(columns):
        copies[n].wait()
        near, far = half(held.at[n], 1, at[3], size), half(held.at[n], 1, 1 - at[3], size)
        back = lax.dot_general(mine[...], near, contract, preferred_element_type=jnp.float32)
        back = back + lax.dot_general(other[...], far, contract, preferred_element_type=jnp.float32)
        out[:, cols] = (back * slope[:, cols].astype(jnp.float32)).astype(jnp.bfloat16)


def back(at, mine, other, w_down, slope):
    rows, size = mine.shape
    width, tile = w_down.shape[0], 512
    return pl.pallas_call(
        back_kernel,
        out_shape=jax.ShapeDtypeStruct((rows, width), jnp.bfloat16),
        in_specs=[SCALARS, WHOLE, WHOLE, FAR, WHOLE],
        out_specs=WHOLE,
        scratch_shapes=[
            pltpu.VMEM((width // tile, tile, 2 * size), w_down.dtype),
            pltpu.SemaphoreType.DMA((width // tile,)),
        ],
        compiler_params=pltpu.CompilerParams(vmem_limit_bytes=16 << 20),
        cost_estimate=LIGHT,
    )(at, mine, other, w_down, slope)


def turn_kernel(starts, at, mine, other, *refs):
    outs, turned = refs[:-1], refs[-1]
    blocks = turned.shape[0] // 2
    turned[pl.ds(at[3] * blocks, blocks)] = mine[...].T.reshape((blocks,) + turned.shape[1:])
    turned[pl.ds((1 - at[3]) * blocks, blocks)] = other[...].T.reshape(
        (blocks,) + turned.shape[1:]
    )
    here = {"x": at[1], "y": at[0], "z": 2 * at[4] + at[2]}
    for start, out in zip(starts, outs):
        for k in range(2 * blocks):
            steps = (k >> 4, (k >> 2) & 3, k & 3)
            spot = {}
            for axis in "xyz":
                by = [steps[ORDER[one].index(axis)] for one in start]
                by = by[0] + at[3] * (by[-1] - by[0])
                spot[axis] = (here[axis] + by) & 3
            block = 16 * spot["y"] + 4 * spot["x"] + 2 * (spot["z"] & 1) + (spot["z"] >> 1)
            out[16 * k : 16 * (k + 1), :] = turned[block]


def turn(at, mine, other, starts):
    rows, size = mine.shape
    return pl.pallas_call(
        functools.partial(turn_kernel, starts),
        out_shape=[jax.ShapeDtypeStruct((2 * size, rows), mine.dtype)] * len(starts),
        in_specs=[SCALARS, WHOLE, WHOLE],
        out_specs=[WHOLE] * len(starts),
        scratch_shapes=[pltpu.VMEM((2 * size // 16, 16, rows), mine.dtype)],
        compiler_params=pltpu.CompilerParams(vmem_limit_bytes=8 << 20),
        cost_estimate=LIGHT,
    )(at, mine, other)


def down_kernel(at, act, w_down, *refs):
    keep, give = refs[-2:]
    size = keep.shape[1]
    keep[...] = jnp.dot(
        act[...], half(w_down, 1, at[3], size), preferred_element_type=jnp.float32
    )
    give[...] = jnp.dot(
        act[...], half(w_down, 1, 1 - at[3], size), preferred_element_type=jnp.float32
    )


def down(at, act, w_down, ready):
    rows, size = act.shape[0], w_down.shape[1] // 2
    return pl.pallas_call(
        down_kernel,
        out_shape=[jax.ShapeDtypeStruct((rows, size), jnp.float32)] * 2,
        in_specs=[SCALARS, WHOLE, WHOLE] + [UNREAD] * len(ready),
        out_specs=[WHOLE, WHOLE],
        compiler_params=pltpu.CompilerParams(vmem_limit_bytes=14 << 20),
        cost_estimate=LIGHT,
    )(at, act, w_down, *ready)


def place_kernel(count, target, own, keep, got, out):
    slots, rows = target.shape[0], own.shape[0]
    each = rows // slots
    out_rows = (own[...].astype(jnp.float32) + keep[...] + got[...]).astype(jnp.bfloat16)
    slot = lax.broadcasted_iota(jnp.int32, (slots, slots), 0)
    before = lax.broadcasted_iota(jnp.int32, (slots, slots), 1)
    to = listed(target, 0, (slots, slots))
    same = (listed(target, 1, (1, slots)) == to) & (before < slot)
    rank = jnp.sum(same.astype(jnp.int32), axis=1, keepdims=True)
    live = slot[:, :1] < count[0]
    first = jnp.where(live, each * (4 * to[:, :1] + rank), -each)
    lane = lax.broadcasted_iota(jnp.int32, (slots, rows), 1)
    mine = (lane // each) == lax.broadcasted_iota(jnp.int32, (slots, rows), 0)
    goes = jnp.sum(jnp.where(mine, first + lane % each, 0), axis=0, keepdims=True)
    step = 256
    for at in range(0, out.shape[0], step):
        here = lax.broadcasted_iota(jnp.int32, (step, rows), 0) + at == goes
        out[at : at + step, :] = jnp.dot(
            jnp.where(here, 1.0, 0.0).astype(jnp.bfloat16),
            out_rows,
            preferred_element_type=jnp.float32,
        ).astype(jnp.bfloat16)


def place(counts, target, own, keep, got):
    rows, size = own.shape
    return pl.pallas_call(
        place_kernel,
        out_shape=jax.ShapeDtypeStruct((2 * rows, size), jnp.bfloat16),
        in_specs=[SCALARS, SCALARS] + [WHOLE] * 3,
        out_specs=WHOLE,
        compiler_params=pltpu.CompilerParams(vmem_limit_bytes=8 << 20),
        cost_estimate=LIGHT,
    )(counts, target, own, keep, got)


def around(block, axis):
    return [block] + [shift(block, axis, 4 - by) for by in (1, 2, 3)]


def shift(block, axis, by):
    if axis == "z":
        at = [(z % 2) * 2 + z // 2 for z in range(4)]
        return lax.ppermute(block, ("zl", "zh"), [(at[z], at[(z + by) % 4]) for z in range(4)])
    return lax.ppermute(block, axis, [(k, (k + by) % 4) for k in range(4)])


def number(spot, core):
    return 8 * (4 * spot["y"] + spot["x"]) + 4 * (spot["z"] % 2) + 2 * core + spot["z"] // 2


def shift_each(block, axes, by):
    route = []
    for chip in range(64):
        spot = {"x": chip % 4, "y": chip // 4 % 4, "z": chip // 16}
        for core in range(2):
            axis = axes[core]
            there = {**spot, axis: (spot[axis] + by) % 4}
            route.append((number(spot, core), number(there, core)))
    return lax.ppermute(block, ("y", "x", "zl", "core", "zh"), route)


def fetched(sources, targets, sems):
    copies = [
        pltpu.make_async_copy(source, target, sems.at[k])
        for k, (source, target) in enumerate(zip(sources, targets))
    ]
    for copy in copies:
        copy.start()
    return copies


def product_kernel(pieces, weight, *refs):
    lefts = 1 + max(piece[0] for piece in pieces)
    rights = 1 + max(piece[1] for piece in pieces)
    count = lefts + rights
    sources, rest = refs[:count], refs[len(refs) - count - 6 :]
    outs, held, scaled, sems = rest[:4], rest[4 : 4 + count], rest[-2], rest[-1]
    copies = fetched(sources, held, sems)
    rows = weight[...]
    depth = outs[0].shape[0]
    done = 0
    seen = set()
    for left, right, first, last in pieces:
        for k in (lefts + right, left):
            if k not in seen:
                copies[k].wait()
                seen.add(k)
        for col in range(first, last, 128):
            piece = held[lefts + right][:, col : col + 128].astype(jnp.float32) * rows
            scaled[:, col - first : col - first + 128] = piece.astype(jnp.bfloat16)
        for k in range(4):
            for col in range(0, last - first, 256):
                end = min(col + 256, last - first)
                outs[k][:, done + col : done + end] = jnp.dot(
                    held[left][depth * k : depth * (k + 1), :],
                    scaled[:, col:end],
                    preferred_element_type=jnp.float32,
                ).astype(jnp.bfloat16)
        done += last - first


def products(weight, lefts, rights, pieces, ready=()):
    width = sum(last - first for _, _, first, last in pieces)
    sides = [*lefts, *rights]
    depth = weight.shape[0]
    return pl.pallas_call(
        functools.partial(product_kernel, pieces),
        out_shape=[jax.ShapeDtypeStruct((256, width), jnp.bfloat16)] * 4,
        in_specs=[WHOLE] + [FAR] * len(sides) + [UNREAD] * len(ready),
        out_specs=[WHOLE] * 4,
        scratch_shapes=[pltpu.VMEM(side.shape, side.dtype) for side in sides]
        + [
            pltpu.VMEM((depth, max(piece[3] - piece[2] for piece in pieces)), jnp.bfloat16),
            pltpu.SemaphoreType.DMA((len(sides),)),
        ],
        compiler_params=pltpu.CompilerParams(vmem_limit_bytes=18 << 20),
        cost_estimate=LIGHT,
    )(weight, *sides, *ready)


def sum_kernel(*refs):
    sources, outs, held, sems = refs[:8], refs[-17:-9], refs[-9:-1], refs[-1]
    copies = fetched(sources, held, sems)
    for part in range(2):
        blocks = held[4 * part : 4 * part + 4]
        for copy in copies[4 * part : 4 * part + 4]:
            copy.wait()
        rows = outs[4 * part].shape[0]
        for k in range(4):
            here = pl.ds(k * rows, rows)
            total = blocks[0][here, :].astype(jnp.float32)
            for ref in blocks[1:]:
                total = total + ref[here, :].astype(jnp.float32)
            outs[4 * part + k][...] = total.astype(jnp.bfloat16)


def sum_blocks(parts, grant, ready=()):
    blocks = [block for part in parts for block in part]
    out = pl.pallas_call(
        sum_kernel,
        out_shape=[
            jax.ShapeDtypeStruct((block.shape[0] // 4, block.shape[1]), jnp.bfloat16)
            for block in blocks
        ],
        in_specs=[UNREAD] * (8 + len(ready)),
        out_specs=[WHOLE] * 8,
        scratch_shapes=[pltpu.VMEM(block.shape, block.dtype) for block in blocks]
        + [pltpu.SemaphoreType.DMA((8,))],
        compiler_params=pltpu.CompilerParams(vmem_limit_bytes=grant),
        cost_estimate=LIGHT,
    )(*blocks, *ready)
    return [out[:4], out[4:]]


def copy_kernel(source, out, sem):
    copy = pltpu.make_async_copy(source, out, sem)
    copy.start()
    copy.wait()


def copied(block):
    return pl.pallas_call(
        copy_kernel,
        out_shape=jax.ShapeDtypeStruct(block.shape, block.dtype),
        in_specs=[UNREAD],
        out_specs=UNREAD,
        scratch_shapes=[pltpu.SemaphoreType.DMA],
        compiler_params=pltpu.CompilerParams(vmem_limit_bytes=1 << 20),
        cost_estimate=LIGHT,
    )(block)


def last_kernel(*refs):
    down, up = refs[-2:]
    sums = []
    for part in range(2):
        total = refs[4 * part][...].astype(jnp.float32)
        for ref in refs[4 * part + 1 : 4 * part + 4]:
            total = total + ref[...].astype(jnp.float32)
        sums.append(total)
    width = down.shape[1]
    cut = sums[0].shape[1] - width
    down[...] = sums[0][:, :width]
    up[:, :cut] = sums[0][:, width:]
    up[:, cut:] = sums[1]


def last_sum(parts, ready, width):
    return pl.pallas_call(
        last_kernel,
        out_shape=[jax.ShapeDtypeStruct((16, width), jnp.float32)] * 2,
        in_specs=[WHOLE] * 8 + [UNREAD] * len(ready),
        out_specs=[WHOLE] * 2,
        compiler_params=pltpu.CompilerParams(vmem_limit_bytes=4 << 20),
        cost_estimate=LIGHT,
    )(*[block for part in parts for block in part], *ready)


def exchanged(parts, step):
    first, second = parts
    axes = (ORDER["x"][step], ORDER["y"][step])
    return [
        [first[0]] + [shift_each(first[by], axes, by) for by in (1, 3, 2)],
        [second[0]] + [shift(second[by], ORDER["z"][step], by) for by in (1, 3, 2)],
    ]


def local(
    ref_image,
    ref_text,
    learner_image,
    learner_text,
    patches,
    cotangent,
    w_up,
    w_down,
    counts,
    sel_index,
    sel_dest,
):
    core = lax.axis_index("core")
    at = jnp.stack([lax.axis_index(name) for name in ("y", "x", "zl", "core", "zh")]).astype(
        jnp.int32
    )
    slots = sel_index.shape[0]
    patch_rows, size = patches.shape[1:]
    count, width, rows = slots * patch_rows, w_up.shape[1], ref_image.shape[0]

    image, text = choose(at, ref_image, ref_text, learner_image, learner_text)
    other_image = lax.ppermute(image, "zl", SWAP)
    texts = around(text, "y")
    texts_other = lax.ppermute(jnp.concatenate(texts, axis=0), "core", SWAP)
    x_mine = patches[sel_index].reshape(count, size)
    cot_mine = cotangent[sel_index].reshape(count, size)
    pair = pair_rows(at, image, other_image, [*texts[1:], x_mine, cot_mine])
    images = around(pair, "x")
    x_other = lax.ppermute(x_mine, "core", SWAP)
    cot_other = lax.ppermute(cot_mine, "core", SWAP)

    act, slope = up(at, x_mine, x_other, w_up)
    x_first, x_second = turn(at, x_mine, x_other, ("xy", "z"))
    grad_pre = back(at, cot_mine, cot_other, w_down, slope)
    (cot_first,) = turn(at, cot_mine, cot_other, ("xy",))

    parts = partial_losses(at, images, texts, texts_other, [x_first, grad_pre, cot_first])
    parts = lax.all_to_all(
        parts, ("y", "x", "zl", "core", "zh"), split_axis=0, concat_axis=0, tiled=True
    )
    scores, weight = weights(counts, sel_index, parts)
    learnability = lax.dynamic_slice_in_dim(scores[0], core * rows, rows)

    cut = 640
    second = products(weight, [x_second], [grad_pre], ((0, 0, cut, width),))
    first = products(
        weight,
        [cot_first, x_first],
        [act, grad_pre],
        ((0, 0, 0, width), (1, 1, 0, cut)),
        second[:1],
    )
    blocks = exchanged([first, second], 0)
    keep, give = down(at, act, w_down, [first[0], *blocks[1][1:]])
    got = lax.ppermute(give, "core", SWAP)
    boxed = place(counts, sel_dest.reshape(slots), x_mine, keep, got)
    boxed = boxed.reshape(32, 4, patch_rows, size)
    routed = lax.all_to_all(boxed, DP, split_axis=0, concat_axis=0, tiled=True)
    routed = copied(routed.reshape(128, patch_rows, size))
    blocks = sum_blocks(blocks, 18 << 20)
    blocks = sum_blocks(exchanged(blocks, 1), 6 << 20)
    grad_down_t, grad_up = last_sum(exchanged(blocks, 2), [routed], width)
    return (learnability, routed, grad_up, grad_down_t)


def solution(mesh):
    mesh = Mesh(mesh.devices.reshape(4, 4, 2, 2, 2), ("y", "x", "zl", "core", "zh"))
    pairs = P(("y", "x", "zl", "core"), None)
    patch = P(DP, "zh", "core")
    return jax.shard_map(
        local,
        mesh=mesh,
        in_specs=(
            pairs,
            pairs,
            pairs,
            pairs,
            patch,
            patch,
            P(None, "core"),
            P("core", None),
            P(DP),
            P(DP),
            P(DP, None),
        ),
        out_specs=(
            P(("y", "x", "zl", "core")),
            patch,
            P(CHIPS, "core"),
            P(CHIPS, "core"),
        ),
        check_vma=False,
    )
```

```python
import functools
import math

import jax
import jax.numpy as jnp
from jax import lax
from jax.experimental import pallas as pl
from jax.experimental.pallas import tpu as pltpu
from jax.sharding import Mesh, PartitionSpec as P

DP = ("y", "x", "zl")
CHIPS = ("y", "x", "zl", "zh")
SWAP = [(0, 1), (1, 0)]
ORDER = {"x": "xyz", "y": "yzx", "z": "zxy"}
WHOLE = pl.BlockSpec(memory_space=pltpu.VMEM)
SCALARS = pl.BlockSpec(memory_space=pltpu.SMEM)
UNREAD = pl.BlockSpec(memory_space=pl.ANY)
LIGHT = pl.CostEstimate(flops=1 << 20, bytes_accessed=1 << 16, transcendentals=0)


def unit(rows):
    wide = rows.astype(jnp.float32)
    norm = lax.rsqrt(jnp.sum(wide * wide, axis=1, keepdims=True) + 1e-06)
    return (wide * norm).astype(jnp.bfloat16)


def softplus(value):
    return jnp.maximum(value, 0.0) + jnp.log1p(jnp.exp(-jnp.abs(value)))


def loss_kernel(at, *refs):
    img_refs, txt_refs, txt_other, (out, img, txt) = refs[:4], refs[4:8], refs[8], refs[-3:]
    here_y, here_x, here_zl, here_core, learner = (at[k] for k in range(5))
    for k in range(4):
        img[pl.ds(128 * k, 128), :] = unit(img_refs[k][...])
        own = pl.multiple_of(128 * k + 64 * here_core, 64)
        txt[pl.ds(own, 64), :] = unit(txt_refs[k][...])
        other = pl.multiple_of(128 * k + 64 * (1 - here_core), 64)
        txt[pl.ds(other, 64), :] = unit(txt_other[pl.ds(64 * k, 64), :])
    contract = (((1,), (1,)), ((), ()))
    col_sum = jnp.zeros((1, 512), jnp.float32)
    row_sums = []
    for k in range(4):
        scores = (
            10.0
            * lax.dot_general(
                img[pl.ds(128 * k, 128), :], txt[...], contract, preferred_element_type=jnp.float32
            )
            - 5.0
        )
        if k == 0:
            row = lax.broadcasted_iota(jnp.int32, scores.shape, 0) - 64 * here_zl
            col = lax.broadcasted_iota(jnp.int32, scores.shape, 1) - 64 * here_core
            same = (row == col) & (row >= 0) & (row < 64)
            scores = jnp.where(same, -scores, scores)
        terms = softplus(scores)
        col_sum = col_sum + jnp.sum(terms, axis=0, keepdims=True)
        folded = terms[:, :128] + terms[:, 128:256] + terms[:, 256:384] + terms[:, 384:]
        row_sums.append(jnp.sum(folded.T, axis=0, keepdims=True))
    dest = lax.broadcasted_iota(jnp.int32, (128, 128), 0)
    lane = lax.broadcasted_iota(jnp.int32, (1, 128), 1)
    dest_y, dest_x, dest_zl = dest >> 5, (dest >> 3) & 3, (dest >> 2) & 1
    own_half = (lane >> 6) == here_core
    total = jnp.zeros((128, 128), jnp.float32)
    for k in range(4):
        straight = row_sums[k]
        crossed = pltpu.roll(straight, 64, 1)
        for zl in range(2):
            placed = jnp.where(own_half, jnp.where(here_core == zl, straight, crossed), 0.0)
            mine = (dest_y == here_y) & (dest_x == ((here_x + k) & 3)) & (dest_zl == zl)
            total = total + jnp.where(mine, placed, 0.0)
        mine = (dest_y == ((here_y + k) & 3)) & (dest_x == here_x) & (dest_zl == here_zl)
        total = total + jnp.where(mine, col_sum[:, 128 * k : 128 * (k + 1)], 0.0)
    out[...] = jnp.where(learner == 1, 0.5, -0.5) * total


def partial_losses(at, images, texts, texts_other, ready):
    return pl.pallas_call(
        loss_kernel,
        out_shape=jax.ShapeDtypeStruct((128, 128), jnp.float32),
        in_specs=[SCALARS] + [WHOLE] * 9 + [UNREAD] * len(ready),
        out_specs=WHOLE,
        scratch_shapes=[pltpu.VMEM((512, 1024), jnp.bfloat16)] * 2,
        compiler_params=pltpu.CompilerParams(vmem_limit_bytes=8 << 20),
        cost_estimate=LIGHT,
    )(at, *images, *texts, texts_other, *ready)


def listed(values, axis, shape):
    at = lax.broadcasted_iota(jnp.int32, shape, axis)
    out = jnp.zeros(shape, jnp.int32)
    for k in range(shape[axis]):
        out = jnp.where(at == k, values[k], out)
    return out


def weight_kernel(count, index, parts, *refs):
    learn, weight = refs[-2:]
    score = jnp.sum(parts[...], axis=0, keepdims=True)
    learn[...] = jnp.broadcast_to(score, (8, 128))
    slots = index.shape[0]
    picked = listed(index, 0, (slots, 128)) == lax.broadcasted_iota(jnp.int32, (slots, 128), 1)
    chosen = jnp.sum(jnp.where(picked, score, 0.0), axis=1, keepdims=True)
    live = lax.broadcasted_iota(jnp.int32, (slots, 128), 0) < count[0]
    value = jnp.where(live, 1.0 / (1.0 + jnp.exp(-chosen)), 0.0)
    weight[...] = jnp.broadcast_to(value[:, None, :], (slots, 8, 128)).reshape(8 * slots, 128)


def weights(counts, index, parts, ready):
    slots = index.shape[0]
    return pl.pallas_call(
        weight_kernel,
        out_shape=(
            jax.ShapeDtypeStruct((8, 128), jnp.float32),
            jax.ShapeDtypeStruct((8 * slots, 128), jnp.float32),
        ),
        in_specs=[SCALARS, SCALARS, WHOLE] + [UNREAD] * len(ready),
        out_specs=(WHOLE, WHOLE),
        compiler_params=pltpu.CompilerParams(vmem_limit_bytes=2 << 20),
        cost_estimate=LIGHT,
    )(counts, index, parts, *ready)


def pair_kernel(at, own, other, *refs):
    pair = refs[-1]
    pair[pl.ds(pl.multiple_of(64 * at[2], 64), 64), :] = own[...]
    pair[pl.ds(pl.multiple_of(64 * (1 - at[2]), 64), 64), :] = other[...]


def pair_rows(at, own, other, ready):
    rows, width = own.shape
    return pl.pallas_call(
        pair_kernel,
        out_shape=jax.ShapeDtypeStruct((2 * rows, width), own.dtype),
        in_specs=[SCALARS, WHOLE, WHOLE] + [UNREAD] * len(ready),
        out_specs=WHOLE,
        compiler_params=pltpu.CompilerParams(vmem_limit_bytes=2 << 20),
        cost_estimate=LIGHT,
    )(at, own, other, *ready)


def join_kernel(*refs):
    out = refs[-1]
    rows = refs[0].shape[0]
    for k, block in enumerate(refs[: out.shape[0] // rows]):
        out[k * rows : (k + 1) * rows, :] = block[...]


def join_rows(blocks, ready):
    rows, width = blocks[0].shape
    return pl.pallas_call(
        join_kernel,
        out_shape=jax.ShapeDtypeStruct((len(blocks) * rows, width), blocks[0].dtype),
        in_specs=[WHOLE] * len(blocks) + [UNREAD] * len(ready),
        out_specs=WHOLE,
        compiler_params=pltpu.CompilerParams(vmem_limit_bytes=2 << 20),
        cost_estimate=LIGHT,
    )(*blocks, *ready)


def half(ref, axis, which, size):
    start = pl.multiple_of(which * size, size)
    return ref[pl.ds(start, size), :] if axis == 0 else ref[:, pl.ds(start, size)]


def up_kernel(at, mine, other, w_up, act, slope, held, sems):
    size = mine.shape[1]
    steps, _, tile = held.shape
    columns = [pl.ds(n * tile, tile) for n in range(steps)]
    copies = fetched([w_up.at[:, cols] for cols in columns], [held.at[n] for n in range(steps)], sems)
    scale = math.sqrt(2.0 / math.pi)
    for n, cols in enumerate(columns):
        copies[n].wait()
        near, far = half(held.at[n], 0, at[3], size), half(held.at[n], 0, 1 - at[3], size)
        for row in range(0, mine.shape[0], 256):
            rows = pl.ds(row, 256)
            pre = jnp.dot(mine[rows, :], near, preferred_element_type=jnp.float32)
            pre = pre + jnp.dot(other[rows, :], far, preferred_element_type=jnp.float32)
            square = pre * pre
            tanh = jnp.tanh(pre * (scale + (scale * 0.044715) * square))
            gate = 0.5 + 0.5 * tanh
            act[rows, cols] = (pre * gate).astype(jnp.bfloat16)
            bend = pre * (0.5 - 0.5 * tanh * tanh) * (scale + (scale * 3 * 0.044715) * square)
            slope[rows, cols] = (gate + bend).astype(jnp.bfloat16)


def up(at, mine, other, w_up):
    rows, size = mine.shape
    width, tile = w_up.shape[1], 512
    return pl.pallas_call(
        up_kernel,
        out_shape=[jax.ShapeDtypeStruct((rows, width), jnp.bfloat16)] * 2,
        in_specs=[SCALARS, WHOLE, WHOLE, UNREAD],
        out_specs=[WHOLE, WHOLE],
        scratch_shapes=[
            pltpu.VMEM((width // tile, 2 * size, tile), w_up.dtype),
            pltpu.SemaphoreType.DMA((width // tile,)),
        ],
        compiler_params=pltpu.CompilerParams(vmem_limit_bytes=16 << 20),
        cost_estimate=LIGHT,
    )(at, mine, other, w_up)


def back_kernel(at, mine, other, w_down, slope, out, held, sems):
    size = mine.shape[1]
    steps, tile, _ = held.shape
    columns = [pl.ds(n * tile, tile) for n in range(steps)]
    copies = fetched([w_down.at[cols] for cols in columns], [held.at[n] for n in range(steps)], sems)
    contract = (((1,), (1,)), ((), ()))
    for n, cols in enumerate(columns):
        copies[n].wait()
        near, far = half(held.at[n], 1, at[3], size), half(held.at[n], 1, 1 - at[3], size)
        back = lax.dot_general(mine[...], near, contract, preferred_element_type=jnp.float32)
        back = back + lax.dot_general(other[...], far, contract, preferred_element_type=jnp.float32)
        out[:, cols] = (back * slope[:, cols].astype(jnp.float32)).astype(jnp.bfloat16)


def back(at, mine, other, w_down, slope):
    rows, size = mine.shape
    width, tile = w_down.shape[0], 512
    return pl.pallas_call(
        back_kernel,
        out_shape=jax.ShapeDtypeStruct((rows, width), jnp.bfloat16),
        in_specs=[SCALARS, WHOLE, WHOLE, UNREAD, WHOLE],
        out_specs=WHOLE,
        scratch_shapes=[
            pltpu.VMEM((width // tile, tile, 2 * size), w_down.dtype),
            pltpu.SemaphoreType.DMA((width // tile,)),
        ],
        compiler_params=pltpu.CompilerParams(vmem_limit_bytes=16 << 20),
        cost_estimate=LIGHT,
    )(at, mine, other, w_down, slope)


def turn_kernel(starts, at, mine, other, *refs):
    outs, turned = refs[:-1], refs[-1]
    blocks = turned.shape[0] // 2
    turned[pl.ds(at[3] * blocks, blocks)] = mine[...].T.reshape((blocks,) + turned.shape[1:])
    turned[pl.ds((1 - at[3]) * blocks, blocks)] = other[...].T.reshape(
        (blocks,) + turned.shape[1:]
    )
    here = {"x": at[1], "y": at[0], "z": 2 * at[4] + at[2]}
    for start, out in zip(starts, outs):
        for k in range(2 * blocks):
            steps = (k >> 4, (k >> 2) & 3, k & 3)
            spot = {}
            for axis in "xyz":
                by = [steps[ORDER[one].index(axis)] for one in start]
                by = by[0] + at[3] * (by[-1] - by[0])
                spot[axis] = (here[axis] + by) & 3
            block = 16 * spot["y"] + 4 * spot["x"] + 2 * (spot["z"] & 1) + (spot["z"] >> 1)
            out[16 * k : 16 * (k + 1), :] = turned[block]


def turn(at, mine, other, starts):
    rows, size = mine.shape
    return pl.pallas_call(
        functools.partial(turn_kernel, starts),
        out_shape=[jax.ShapeDtypeStruct((2 * size, rows), mine.dtype)] * len(starts),
        in_specs=[SCALARS, WHOLE, WHOLE],
        out_specs=[WHOLE] * len(starts),
        scratch_shapes=[pltpu.VMEM((2 * size // 16, 16, rows), mine.dtype)],
        compiler_params=pltpu.CompilerParams(vmem_limit_bytes=8 << 20),
        cost_estimate=LIGHT,
    )(at, mine, other)


def down_kernel(at, act, w_down, *refs):
    keep, give = refs[-2:]
    size = keep.shape[1]
    keep[...] = jnp.dot(
        act[...], half(w_down, 1, at[3], size), preferred_element_type=jnp.float32
    )
    give[...] = jnp.dot(
        act[...], half(w_down, 1, 1 - at[3], size), preferred_element_type=jnp.float32
    )


def down(at, act, w_down, ready):
    rows, size = act.shape[0], w_down.shape[1] // 2
    return pl.pallas_call(
        down_kernel,
        out_shape=[jax.ShapeDtypeStruct((rows, size), jnp.float32)] * 2,
        in_specs=[SCALARS, WHOLE, WHOLE] + [UNREAD] * len(ready),
        out_specs=[WHOLE, WHOLE],
        compiler_params=pltpu.CompilerParams(vmem_limit_bytes=14 << 20),
        cost_estimate=LIGHT,
    )(at, act, w_down, *ready)


def place_kernel(count, target, own, keep, got, *refs):
    out = refs[-1]
    slots, rows = target.shape[0], own.shape[0]
    each = rows // slots
    out_rows = (own[...].astype(jnp.float32) + keep[...] + got[...]).astype(jnp.bfloat16)
    slot = lax.broadcasted_iota(jnp.int32, (slots, slots), 0)
    before = lax.broadcasted_iota(jnp.int32, (slots, slots), 1)
    to = listed(target, 0, (slots, slots))
    same = (listed(target, 1, (1, slots)) == to) & (before < slot)
    rank = jnp.sum(same.astype(jnp.int32), axis=1, keepdims=True)
    live = slot[:, :1] < count[0]
    first = jnp.where(live, each * (4 * to[:, :1] + rank), -each)
    lane = lax.broadcasted_iota(jnp.int32, (slots, rows), 1)
    mine = (lane // each) == lax.broadcasted_iota(jnp.int32, (slots, rows), 0)
    goes = jnp.sum(jnp.where(mine, first + lane % each, 0), axis=0, keepdims=True)
    step = 256
    for at in range(0, out.shape[0], step):
        here = lax.broadcasted_iota(jnp.int32, (step, rows), 0) + at == goes
        out[at : at + step, :] = jnp.dot(
            jnp.where(here, 1.0, 0.0).astype(jnp.bfloat16),
            out_rows,
            preferred_element_type=jnp.float32,
        ).astype(jnp.bfloat16)


def place(counts, target, own, keep, got, ready):
    rows, size = own.shape
    return pl.pallas_call(
        place_kernel,
        out_shape=jax.ShapeDtypeStruct((2 * rows, size), jnp.bfloat16),
        in_specs=[SCALARS, SCALARS] + [WHOLE] * 3 + [UNREAD] * len(ready),
        out_specs=WHOLE,
        compiler_params=pltpu.CompilerParams(vmem_limit_bytes=8 << 20),
        cost_estimate=LIGHT,
    )(counts, target, own, keep, got, *ready)


def around(block, axis):
    return [block] + [shift(block, axis, 4 - by) for by in (1, 2, 3)]


def shift(block, axis, by):
    if axis == "z":
        at = [(z % 2) * 2 + z // 2 for z in range(4)]
        return lax.ppermute(block, ("zl", "zh"), [(at[z], at[(z + by) % 4]) for z in range(4)])
    return lax.ppermute(block, axis, [(k, (k + by) % 4) for k in range(4)])


def number(spot, core):
    return 8 * (4 * spot["y"] + spot["x"]) + 4 * (spot["z"] % 2) + 2 * core + spot["z"] // 2


def shift_each(block, axes, by):
    route = []
    for chip in range(64):
        spot = {"x": chip % 4, "y": chip // 4 % 4, "z": chip // 16}
        for core in range(2):
            axis = axes[core]
            there = {**spot, axis: (spot[axis] + by) % 4}
            route.append((number(spot, core), number(there, core)))
    return lax.ppermute(block, ("y", "x", "zl", "core", "zh"), route)


def fetched(sources, targets, sems):
    copies = [
        pltpu.make_async_copy(source, target, sems.at[k])
        for k, (source, target) in enumerate(zip(sources, targets))
    ]
    for copy in copies:
        copy.start()
    return copies


def product_kernel(pieces, weight, *refs):
    lefts = 1 + max(piece[0] for piece in pieces)
    rights = 1 + max(piece[1] for piece in pieces)
    count = lefts + rights
    sources, rest = refs[:count], refs[len(refs) - count - 6 :]
    outs, held, scaled, sems = rest[:4], rest[4 : 4 + count], rest[-2], rest[-1]
    copies = fetched(sources, held, sems)
    rows = weight[...]
    depth = outs[0].shape[0]
    done = 0
    seen = set()
    for left, right, first, last in pieces:
        for k in (lefts + right, left):
            if k not in seen:
                copies[k].wait()
                seen.add(k)
        for col in range(first, last, 128):
            piece = held[lefts + right][:, col : col + 128].astype(jnp.float32) * rows
            scaled[:, col - first : col - first + 128] = piece.astype(jnp.bfloat16)
        for k in range(4):
            for col in range(0, last - first, 256):
                end = min(col + 256, last - first)
                outs[k][:, done + col : done + end] = jnp.dot(
                    held[left][depth * k : depth * (k + 1), :],
                    scaled[:, col:end],
                    preferred_element_type=jnp.float32,
                ).astype(jnp.bfloat16)
        done += last - first


def products(weight, lefts, rights, pieces, ready=()):
    width = sum(last - first for _, _, first, last in pieces)
    sides = [*lefts, *rights]
    depth = weight.shape[0]
    return pl.pallas_call(
        functools.partial(product_kernel, pieces),
        out_shape=[jax.ShapeDtypeStruct((256, width), jnp.bfloat16)] * 4,
        in_specs=[WHOLE] + [UNREAD] * len(sides) + [UNREAD] * len(ready),
        out_specs=[WHOLE] * 4,
        scratch_shapes=[pltpu.VMEM(side.shape, side.dtype) for side in sides]
        + [
            pltpu.VMEM((depth, max(piece[3] - piece[2] for piece in pieces)), jnp.bfloat16),
            pltpu.SemaphoreType.DMA((len(sides),)),
        ],
        compiler_params=pltpu.CompilerParams(vmem_limit_bytes=56 << 20),
        cost_estimate=LIGHT,
    )(weight, *sides, *ready)


def sum_kernel(*refs):
    sources, outs, held, sems = refs[:8], refs[-17:-9], refs[-9:-1], refs[-1]
    copies = fetched(sources, held, sems)
    for part in range(2):
        blocks = held[4 * part : 4 * part + 4]
        for copy in copies[4 * part : 4 * part + 4]:
            copy.wait()
        rows = outs[4 * part].shape[0]
        for k in range(4):
            here = pl.ds(k * rows, rows)
            total = blocks[0][here, :].astype(jnp.float32)
            for ref in blocks[1:]:
                total = total + ref[here, :].astype(jnp.float32)
            outs[4 * part + k][...] = total.astype(jnp.bfloat16)


def sum_blocks(parts, grant, ready=()):
    blocks = [block for part in parts for block in part]
    out = pl.pallas_call(
        sum_kernel,
        out_shape=[
            jax.ShapeDtypeStruct((block.shape[0] // 4, block.shape[1]), jnp.bfloat16)
            for block in blocks
        ],
        in_specs=[UNREAD] * (8 + len(ready)),
        out_specs=[WHOLE] * 8,
        scratch_shapes=[pltpu.VMEM(block.shape, block.dtype) for block in blocks]
        + [pltpu.SemaphoreType.DMA((8,))],
        compiler_params=pltpu.CompilerParams(vmem_limit_bytes=grant),
        cost_estimate=LIGHT,
    )(*blocks, *ready)
    return [out[:4], out[4:]]


def copy_kernel(source, out, sem):
    copy = pltpu.make_async_copy(source, out, sem)
    copy.start()
    copy.wait()


def copied(block):
    return pl.pallas_call(
        copy_kernel,
        out_shape=jax.ShapeDtypeStruct(block.shape, block.dtype),
        in_specs=[UNREAD],
        out_specs=UNREAD,
        scratch_shapes=[pltpu.SemaphoreType.DMA],
        compiler_params=pltpu.CompilerParams(vmem_limit_bytes=1 << 20),
        cost_estimate=LIGHT,
    )(block)


def last_kernel(*refs):
    down, up = refs[-2:]
    sums = []
    for part in range(2):
        total = refs[4 * part][...].astype(jnp.float32)
        for ref in refs[4 * part + 1 : 4 * part + 4]:
            total = total + ref[...].astype(jnp.float32)
        sums.append(total)
    width = down.shape[1]
    cut = sums[0].shape[1] - width
    down[...] = sums[0][:, :width]
    up[:, :cut] = sums[0][:, width:]
    up[:, cut:] = sums[1]


def last_sum(parts, ready, width):
    return pl.pallas_call(
        last_kernel,
        out_shape=[jax.ShapeDtypeStruct((16, width), jnp.float32)] * 2,
        in_specs=[WHOLE] * 8 + [UNREAD] * len(ready),
        out_specs=[WHOLE] * 2,
        compiler_params=pltpu.CompilerParams(vmem_limit_bytes=4 << 20),
        cost_estimate=LIGHT,
    )(*[block for part in parts for block in part], *ready)


def exchanged(parts, step):
    first, second = parts
    axes = (ORDER["x"][step], ORDER["y"][step])
    return [
        [first[0]] + [shift_each(first[by], axes, by) for by in (1, 3, 2)],
        [second[0]] + [shift(second[by], ORDER["z"][step], by) for by in (1, 3, 2)],
    ]


def local(
    ref_image,
    ref_text,
    learner_image,
    learner_text,
    patches,
    cotangent,
    w_up,
    w_down,
    counts,
    sel_index,
    sel_dest,
):
    core = lax.axis_index("core")
    at = jnp.stack([lax.axis_index(name) for name in ("y", "x", "zl", "core", "zh")]).astype(
        jnp.int32
    )
    slots = sel_index.shape[0]
    patch_rows, size = patches.shape[1:]
    count, width, rows = slots * patch_rows, w_up.shape[1], ref_image.shape[0]

    learner = lax.axis_index("zh") == 1
    pad = ((0, 0), (0, learner_image.shape[1] - ref_image.shape[1]))
    image = jnp.where(learner, learner_image, jnp.pad(ref_image, pad))
    text = jnp.where(learner, learner_text, jnp.pad(ref_text, pad))
    other_image = lax.ppermute(image, "zl", SWAP)
    x_mine = patches[sel_index].reshape(count, size)
    cot_mine = cotangent[sel_index].reshape(count, size)
    x_other = lax.ppermute(x_mine, "core", SWAP)
    cot_other = lax.ppermute(cot_mine, "core", SWAP)
    texts = around(text, "y")
    joined = join_rows(texts, [other_image, x_other, cot_mine])
    texts_other = lax.ppermute(joined, "core", SWAP)
    pair = pair_rows(at, image, other_image, [joined])
    images = around(pair, "x")

    act, slope = up(at, x_mine, x_other, w_up)
    x_first, x_second = turn(at, x_mine, x_other, ("xy", "z"))
    grad_pre = back(at, cot_mine, cot_other, w_down, slope)
    (cot_first,) = turn(at, cot_mine, cot_other, ("xy",))

    parts = partial_losses(at, images, texts, texts_other, [x_first, grad_pre, cot_first])
    keep, give = down(at, act, w_down, [parts])
    got = lax.ppermute(give, "core", SWAP)
    parts = lax.all_to_all(
        parts, ("y", "x", "zl", "core", "zh"), split_axis=0, concat_axis=0, tiled=True
    )
    scores, weight = weights(counts, sel_index, parts, [got])
    learnability = lax.dynamic_slice_in_dim(scores[0], core * rows, rows)

    cut = 640
    second = products(weight, [x_second], [grad_pre], ((0, 0, cut, width),))
    first = products(
        weight,
        [cot_first, x_first],
        [act, grad_pre],
        ((0, 0, 0, width), (1, 1, 0, cut)),
        second[:1],
    )
    blocks = exchanged([first, second], 0)
    boxed = place(counts, sel_dest.reshape(slots), x_mine, keep, got, [first[0]])
    boxed = boxed.reshape(32, 4, patch_rows, size)
    routed = lax.all_to_all(boxed, DP, split_axis=0, concat_axis=0, tiled=True)
    routed = copied(routed.reshape(128, patch_rows, size))
    blocks = sum_blocks(blocks, 56 << 20)
    blocks = sum_blocks(exchanged(blocks, 1), 6 << 20)
    grad_down_t, grad_up = last_sum(exchanged(blocks, 2), [routed], width)
    return (learnability, routed, grad_up, grad_down_t)


def solution(mesh):
    mesh = Mesh(mesh.devices.reshape(4, 4, 2, 2, 2), ("y", "x", "zl", "core", "zh"))
    pairs = P(("y", "x", "zl", "core"), None)
    patch = P(DP, "zh", "core")
    return jax.shard_map(
        local,
        mesh=mesh,
        in_specs=(
            pairs,
            pairs,
            pairs,
            pairs,
            patch,
            patch,
            P(None, "core"),
            P("core", None),
            P(DP),
            P(DP),
            P(DP, None),
        ),
        out_specs=(
            P(("y", "x", "zl", "core")),
            patch,
            P(CHIPS, "core"),
            P(CHIPS, "core"),
        ),
        check_vma=False,
    )
```

```python
import functools
import math

import jax
import jax.numpy as jnp
from jax import lax
from jax.experimental import pallas as pl
from jax.experimental.pallas import tpu as pltpu
from jax.sharding import Mesh, PartitionSpec as P

DP = ("y", "x", "zl")
CHIPS = ("y", "x", "zl", "zh")
SWAP = [(0, 1), (1, 0)]
ORDER = {"x": "xyz", "y": "yzx", "z": "zxy"}
WHOLE = pl.BlockSpec(memory_space=pltpu.VMEM)
SCALARS = pl.BlockSpec(memory_space=pltpu.SMEM)
UNREAD = pl.BlockSpec(memory_space=pl.ANY)
LIGHT = pl.CostEstimate(flops=1 << 20, bytes_accessed=1 << 16, transcendentals=0)


def unit(rows):
    wide = rows.astype(jnp.float32)
    norm = lax.rsqrt(jnp.sum(wide * wide, axis=1, keepdims=True) + 1e-06)
    return (wide * norm).astype(jnp.bfloat16)


def softplus(value):
    return jnp.maximum(value, 0.0) + jnp.log1p(jnp.exp(-jnp.abs(value)))


def loss_kernel(at, *refs):
    img_refs, txt_refs, txt_other, (out, img, txt) = refs[:4], refs[4:8], refs[8], refs[-3:]
    here_y, here_x, here_zl, here_core, learner = (at[k] for k in range(5))
    for k in range(4):
        img[pl.ds(128 * k, 128), :] = unit(img_refs[k][...])
        own = pl.multiple_of(128 * k + 64 * here_core, 64)
        txt[pl.ds(own, 64), :] = unit(txt_refs[k][...])
        other = pl.multiple_of(128 * k + 64 * (1 - here_core), 64)
        txt[pl.ds(other, 64), :] = unit(txt_other[pl.ds(64 * k, 64), :])
    contract = (((1,), (1,)), ((), ()))
    col_sum = jnp.zeros((1, 512), jnp.float32)
    row_sums = []
    for k in range(4):
        scores = (
            10.0
            * lax.dot_general(
                img[pl.ds(128 * k, 128), :], txt[...], contract, preferred_element_type=jnp.float32
            )
            - 5.0
        )
        if k == 0:
            row = lax.broadcasted_iota(jnp.int32, scores.shape, 0) - 64 * here_zl
            col = lax.broadcasted_iota(jnp.int32, scores.shape, 1) - 64 * here_core
            same = (row == col) & (row >= 0) & (row < 64)
            scores = jnp.where(same, -scores, scores)
        terms = softplus(scores)
        col_sum = col_sum + jnp.sum(terms, axis=0, keepdims=True)
        folded = terms[:, :128] + terms[:, 128:256] + terms[:, 256:384] + terms[:, 384:]
        row_sums.append(jnp.sum(folded.T, axis=0, keepdims=True))
    dest = lax.broadcasted_iota(jnp.int32, (128, 128), 0)
    lane = lax.broadcasted_iota(jnp.int32, (1, 128), 1)
    dest_y, dest_x, dest_zl = dest >> 5, (dest >> 3) & 3, (dest >> 2) & 1
    own_half = (lane >> 6) == here_core
    total = jnp.zeros((128, 128), jnp.float32)
    for k in range(4):
        straight = row_sums[k]
        crossed = pltpu.roll(straight, 64, 1)
        for zl in range(2):
            placed = jnp.where(own_half, jnp.where(here_core == zl, straight, crossed), 0.0)
            mine = (dest_y == here_y) & (dest_x == ((here_x + k) & 3)) & (dest_zl == zl)
            total = total + jnp.where(mine, placed, 0.0)
        mine = (dest_y == ((here_y + k) & 3)) & (dest_x == here_x) & (dest_zl == here_zl)
        total = total + jnp.where(mine, col_sum[:, 128 * k : 128 * (k + 1)], 0.0)
    out[...] = jnp.where(learner == 1, 0.5, -0.5) * total


def partial_losses(at, images, texts, texts_other, ready):
    return pl.pallas_call(
        loss_kernel,
        out_shape=jax.ShapeDtypeStruct((128, 128), jnp.float32),
        in_specs=[SCALARS] + [WHOLE] * 9 + [UNREAD] * len(ready),
        out_specs=WHOLE,
        scratch_shapes=[pltpu.VMEM((512, 1024), jnp.bfloat16)] * 2,
        compiler_params=pltpu.CompilerParams(vmem_limit_bytes=8 << 20),
        cost_estimate=LIGHT,
    )(at, *images, *texts, texts_other, *ready)


def listed(values, axis, shape):
    at = lax.broadcasted_iota(jnp.int32, shape, axis)
    out = jnp.zeros(shape, jnp.int32)
    for k in range(shape[axis]):
        out = jnp.where(at == k, values[k], out)
    return out


def weight_kernel(count, index, parts, *refs):
    learn, weight = refs[-2:]
    score = jnp.sum(parts[...], axis=0, keepdims=True)
    learn[...] = jnp.broadcast_to(score, (8, 128))
    slots = index.shape[0]
    picked = listed(index, 0, (slots, 128)) == lax.broadcasted_iota(jnp.int32, (slots, 128), 1)
    chosen = jnp.sum(jnp.where(picked, score, 0.0), axis=1, keepdims=True)
    live = lax.broadcasted_iota(jnp.int32, (slots, 128), 0) < count[0]
    value = jnp.where(live, 1.0 / (1.0 + jnp.exp(-chosen)), 0.0)
    weight[...] = jnp.broadcast_to(value[:, None, :], (slots, 8, 128)).reshape(8 * slots, 128)


def weights(counts, index, parts, ready):
    slots = index.shape[0]
    return pl.pallas_call(
        weight_kernel,
        out_shape=(
            jax.ShapeDtypeStruct((8, 128), jnp.float32),
            jax.ShapeDtypeStruct((8 * slots, 128), jnp.float32),
        ),
        in_specs=[SCALARS, SCALARS, WHOLE] + [UNREAD] * len(ready),
        out_specs=(WHOLE, WHOLE),
        compiler_params=pltpu.CompilerParams(vmem_limit_bytes=2 << 20),
        cost_estimate=LIGHT,
    )(counts, index, parts, *ready)


def pair_kernel(at, own, other, *refs):
    pair = refs[-1]
    pair[pl.ds(pl.multiple_of(64 * at[2], 64), 64), :] = own[...]
    pair[pl.ds(pl.multiple_of(64 * (1 - at[2]), 64), 64), :] = other[...]


def pair_rows(at, own, other, ready):
    rows, width = own.shape
    return pl.pallas_call(
        pair_kernel,
        out_shape=jax.ShapeDtypeStruct((2 * rows, width), own.dtype),
        in_specs=[SCALARS, WHOLE, WHOLE] + [UNREAD] * len(ready),
        out_specs=WHOLE,
        compiler_params=pltpu.CompilerParams(vmem_limit_bytes=2 << 20),
        cost_estimate=LIGHT,
    )(at, own, other, *ready)


def join_kernel(*refs):
    out = refs[-1]
    rows = refs[0].shape[0]
    for k, block in enumerate(refs[: out.shape[0] // rows]):
        out[k * rows : (k + 1) * rows, :] = block[...]


def join_rows(blocks, ready):
    rows, width = blocks[0].shape
    return pl.pallas_call(
        join_kernel,
        out_shape=jax.ShapeDtypeStruct((len(blocks) * rows, width), blocks[0].dtype),
        in_specs=[WHOLE] * len(blocks) + [UNREAD] * len(ready),
        out_specs=WHOLE,
        compiler_params=pltpu.CompilerParams(vmem_limit_bytes=2 << 20),
        cost_estimate=LIGHT,
    )(*blocks, *ready)


def half(ref, axis, which, size):
    start = pl.multiple_of(which * size, size)
    return ref[pl.ds(start, size), :] if axis == 0 else ref[:, pl.ds(start, size)]


def up_kernel(at, mine, other, w_up, act, slope, held, sems):
    size = mine.shape[1]
    steps, _, tile = held.shape
    columns = [pl.ds(n * tile, tile) for n in range(steps)]
    copies = fetched([w_up.at[:, cols] for cols in columns], [held.at[n] for n in range(steps)], sems)
    scale = math.sqrt(2.0 / math.pi)
    for n, cols in enumerate(columns):
        copies[n].wait()
        near, far = half(held.at[n], 0, at[3], size), half(held.at[n], 0, 1 - at[3], size)
        for row in range(0, mine.shape[0], 256):
            rows = pl.ds(row, 256)
            pre = jnp.dot(mine[rows, :], near, preferred_element_type=jnp.float32)
            pre = pre + jnp.dot(other[rows, :], far, preferred_element_type=jnp.float32)
            square = pre * pre
            tanh = jnp.tanh(pre * (scale + (scale * 0.044715) * square))
            gate = 0.5 + 0.5 * tanh
            act[rows, cols] = (pre * gate).astype(jnp.bfloat16)
            bend = pre * (0.5 - 0.5 * tanh * tanh) * (scale + (scale * 3 * 0.044715) * square)
            slope[rows, cols] = (gate + bend).astype(jnp.bfloat16)


def up(at, mine, other, w_up):
    rows, size = mine.shape
    width, tile = w_up.shape[1], 512
    return pl.pallas_call(
        up_kernel,
        out_shape=[jax.ShapeDtypeStruct((rows, width), jnp.bfloat16)] * 2,
        in_specs=[SCALARS, WHOLE, WHOLE, UNREAD],
        out_specs=[WHOLE, WHOLE],
        scratch_shapes=[
            pltpu.VMEM((width // tile, 2 * size, tile), w_up.dtype),
            pltpu.SemaphoreType.DMA((width // tile,)),
        ],
        compiler_params=pltpu.CompilerParams(vmem_limit_bytes=16 << 20),
        cost_estimate=LIGHT,
    )(at, mine, other, w_up)


def back_kernel(at, mine, other, w_down, slope, *refs):
    out, held, sems = refs[-3:]
    size = mine.shape[1]
    steps, tile, _ = held.shape
    columns = [pl.ds(n * tile, tile) for n in range(steps)]
    copies = fetched([w_down.at[cols] for cols in columns], [held.at[n] for n in range(steps)], sems)
    contract = (((1,), (1,)), ((), ()))
    for n, cols in enumerate(columns):
        copies[n].wait()
        near, far = half(held.at[n], 1, at[3], size), half(held.at[n], 1, 1 - at[3], size)
        back = lax.dot_general(mine[...], near, contract, preferred_element_type=jnp.float32)
        back = back + lax.dot_general(other[...], far, contract, preferred_element_type=jnp.float32)
        out[:, cols] = (back * slope[:, cols].astype(jnp.float32)).astype(jnp.bfloat16)


def back(at, mine, other, w_down, slope, ready):
    rows, size = mine.shape
    width, tile = w_down.shape[0], 512
    return pl.pallas_call(
        back_kernel,
        out_shape=jax.ShapeDtypeStruct((rows, width), jnp.bfloat16),
        in_specs=[SCALARS, WHOLE, WHOLE, UNREAD, WHOLE] + [UNREAD] * len(ready),
        out_specs=WHOLE,
        scratch_shapes=[
            pltpu.VMEM((width // tile, tile, 2 * size), w_down.dtype),
            pltpu.SemaphoreType.DMA((width // tile,)),
        ],
        compiler_params=pltpu.CompilerParams(vmem_limit_bytes=16 << 20),
        cost_estimate=LIGHT,
    )(at, mine, other, w_down, slope, *ready)


def turn_kernel(starts, at, mine, other, *refs):
    outs, turned = refs[len(refs) - 1 - len(starts) : -1], refs[-1]
    blocks = turned.shape[0] // 2
    turned[pl.ds(at[3] * blocks, blocks)] = mine[...].T.reshape((blocks,) + turned.shape[1:])
    turned[pl.ds((1 - at[3]) * blocks, blocks)] = other[...].T.reshape(
        (blocks,) + turned.shape[1:]
    )
    here = {"x": at[1], "y": at[0], "z": 2 * at[4] + at[2]}
    for start, out in zip(starts, outs):
        for k in range(2 * blocks):
            steps = (k >> 4, (k >> 2) & 3, k & 3)
            spot = {}
            for axis in "xyz":
                by = [steps[ORDER[one].index(axis)] for one in start]
                by = by[0] + at[3] * (by[-1] - by[0])
                spot[axis] = (here[axis] + by) & 3
            block = 16 * spot["y"] + 4 * spot["x"] + 2 * (spot["z"] & 1) + (spot["z"] >> 1)
            out[16 * k : 16 * (k + 1), :] = turned[block]


def turn(at, mine, other, starts, ready):
    rows, size = mine.shape
    return pl.pallas_call(
        functools.partial(turn_kernel, starts),
        out_shape=[jax.ShapeDtypeStruct((2 * size, rows), mine.dtype)] * len(starts),
        in_specs=[SCALARS, WHOLE, WHOLE] + [UNREAD] * len(ready),
        out_specs=[WHOLE] * len(starts),
        scratch_shapes=[pltpu.VMEM((2 * size // 16, 16, rows), mine.dtype)],
        compiler_params=pltpu.CompilerParams(vmem_limit_bytes=8 << 20),
        cost_estimate=LIGHT,
    )(at, mine, other, *ready)


def down_kernel(at, act, w_down, *refs):
    keep, give = refs[-2:]
    size = keep.shape[1]
    keep[...] = jnp.dot(
        act[...], half(w_down, 1, at[3], size), preferred_element_type=jnp.float32
    )
    give[...] = jnp.dot(
        act[...], half(w_down, 1, 1 - at[3], size), preferred_element_type=jnp.float32
    )


def down(at, act, w_down, ready):
    rows, size = act.shape[0], w_down.shape[1] // 2
    return pl.pallas_call(
        down_kernel,
        out_shape=[jax.ShapeDtypeStruct((rows, size), jnp.float32)] * 2,
        in_specs=[SCALARS, WHOLE, WHOLE] + [UNREAD] * len(ready),
        out_specs=[WHOLE, WHOLE],
        compiler_params=pltpu.CompilerParams(vmem_limit_bytes=14 << 20),
        cost_estimate=LIGHT,
    )(at, act, w_down, *ready)


def place_kernel(count, target, own, keep, got, *refs):
    out = refs[-1]
    slots, rows = target.shape[0], own.shape[0]
    each = rows // slots
    out_rows = (own[...].astype(jnp.float32) + keep[...] + got[...]).astype(jnp.bfloat16)
    slot = lax.broadcasted_iota(jnp.int32, (slots, slots), 0)
    before = lax.broadcasted_iota(jnp.int32, (slots, slots), 1)
    to = listed(target, 0, (slots, slots))
    same = (listed(target, 1, (1, slots)) == to) & (before < slot)
    rank = jnp.sum(same.astype(jnp.int32), axis=1, keepdims=True)
    live = slot[:, :1] < count[0]
    first = jnp.where(live, each * (4 * to[:, :1] + rank), -each)
    lane = lax.broadcasted_iota(jnp.int32, (slots, rows), 1)
    mine = (lane // each) == lax.broadcasted_iota(jnp.int32, (slots, rows), 0)
    goes = jnp.sum(jnp.where(mine, first + lane % each, 0), axis=0, keepdims=True)
    step = 256
    for at in range(0, out.shape[0], step):
        here = lax.broadcasted_iota(jnp.int32, (step, rows), 0) + at == goes
        out[at : at + step, :] = jnp.dot(
            jnp.where(here, 1.0, 0.0).astype(jnp.bfloat16),
            out_rows,
            preferred_element_type=jnp.float32,
        ).astype(jnp.bfloat16)


def place(counts, target, own, keep, got, ready):
    rows, size = own.shape
    return pl.pallas_call(
        place_kernel,
        out_shape=jax.ShapeDtypeStruct((2 * rows, size), jnp.bfloat16),
        in_specs=[SCALARS, SCALARS] + [WHOLE] * 3 + [UNREAD] * len(ready),
        out_specs=WHOLE,
        compiler_params=pltpu.CompilerParams(vmem_limit_bytes=8 << 20),
        cost_estimate=LIGHT,
    )(counts, target, own, keep, got, *ready)


def around(block, axis):
    return [block] + [shift(block, axis, 4 - by) for by in (1, 2, 3)]


def shift(block, axis, by):
    if axis == "z":
        at = [(z % 2) * 2 + z // 2 for z in range(4)]
        return lax.ppermute(block, ("zl", "zh"), [(at[z], at[(z + by) % 4]) for z in range(4)])
    return lax.ppermute(block, axis, [(k, (k + by) % 4) for k in range(4)])


def number(spot, core):
    return 8 * (4 * spot["y"] + spot["x"]) + 4 * (spot["z"] % 2) + 2 * core + spot["z"] // 2


def shift_each(block, axes, by):
    route = []
    for chip in range(64):
        spot = {"x": chip % 4, "y": chip // 4 % 4, "z": chip // 16}
        for core in range(2):
            axis = axes[core]
            there = {**spot, axis: (spot[axis] + by) % 4}
            route.append((number(spot, core), number(there, core)))
    return lax.ppermute(block, ("y", "x", "zl", "core", "zh"), route)


def fetched(sources, targets, sems):
    copies = [
        pltpu.make_async_copy(source, target, sems.at[k])
        for k, (source, target) in enumerate(zip(sources, targets))
    ]
    for copy in copies:
        copy.start()
    return copies


def product_kernel(pieces, weight, *refs):
    lefts = 1 + max(piece[0] for piece in pieces)
    rights = 1 + max(piece[1] for piece in pieces)
    count = lefts + rights
    sources, rest = refs[:count], refs[len(refs) - count - 6 :]
    outs, held, scaled, sems = rest[:4], rest[4 : 4 + count], rest[-2], rest[-1]
    copies = fetched(sources, held, sems)
    rows = weight[...]
    depth = outs[0].shape[0]
    done = 0
    seen = set()
    for left, right, first, last in pieces:
        for k in (lefts + right, left):
            if k not in seen:
                copies[k].wait()
                seen.add(k)
        for col in range(first, last, 128):
            piece = held[lefts + right][:, col : col + 128].astype(jnp.float32) * rows
            scaled[:, col - first : col - first + 128] = piece.astype(jnp.bfloat16)
        for k in range(4):
            for col in range(0, last - first, 256):
                end = min(col + 256, last - first)
                outs[k][:, done + col : done + end] = jnp.dot(
                    held[left][depth * k : depth * (k + 1), :],
                    scaled[:, col:end],
                    preferred_element_type=jnp.float32,
                ).astype(jnp.bfloat16)
        done += last - first


def products(weight, lefts, rights, pieces, ready=()):
    width = sum(last - first for _, _, first, last in pieces)
    sides = [*lefts, *rights]
    depth = weight.shape[0]
    return pl.pallas_call(
        functools.partial(product_kernel, pieces),
        out_shape=[jax.ShapeDtypeStruct((256, width), jnp.bfloat16)] * 4,
        in_specs=[WHOLE] + [UNREAD] * len(sides) + [UNREAD] * len(ready),
        out_specs=[WHOLE] * 4,
        scratch_shapes=[pltpu.VMEM(side.shape, side.dtype) for side in sides]
        + [
            pltpu.VMEM((depth, max(piece[3] - piece[2] for piece in pieces)), jnp.bfloat16),
            pltpu.SemaphoreType.DMA((len(sides),)),
        ],
        compiler_params=pltpu.CompilerParams(vmem_limit_bytes=18 << 20),
        cost_estimate=LIGHT,
    )(weight, *sides, *ready)


def sum_kernel(*refs):
    sources, outs, held, sems = refs[:8], refs[-17:-9], refs[-9:-1], refs[-1]
    copies = fetched(sources, held, sems)
    for part in range(2):
        blocks = held[4 * part : 4 * part + 4]
        for copy in copies[4 * part : 4 * part + 4]:
            copy.wait()
        rows = outs[4 * part].shape[0]
        for k in range(4):
            here = pl.ds(k * rows, rows)
            total = blocks[0][here, :].astype(jnp.float32)
            for ref in blocks[1:]:
                total = total + ref[here, :].astype(jnp.float32)
            outs[4 * part + k][...] = total.astype(jnp.bfloat16)


def sum_blocks(parts, grant, ready=()):
    blocks = [block for part in parts for block in part]
    out = pl.pallas_call(
        sum_kernel,
        out_shape=[
            jax.ShapeDtypeStruct((block.shape[0] // 4, block.shape[1]), jnp.bfloat16)
            for block in blocks
        ],
        in_specs=[UNREAD] * (8 + len(ready)),
        out_specs=[WHOLE] * 8,
        scratch_shapes=[pltpu.VMEM(block.shape, block.dtype) for block in blocks]
        + [pltpu.SemaphoreType.DMA((8,))],
        compiler_params=pltpu.CompilerParams(vmem_limit_bytes=grant),
        cost_estimate=LIGHT,
    )(*blocks, *ready)
    return [out[:4], out[4:]]


def copy_kernel(source, out, sem):
    copy = pltpu.make_async_copy(source, out, sem)
    copy.start()
    copy.wait()


def copied(block):
    return pl.pallas_call(
        copy_kernel,
        out_shape=jax.ShapeDtypeStruct(block.shape, block.dtype),
        in_specs=[UNREAD],
        out_specs=UNREAD,
        scratch_shapes=[pltpu.SemaphoreType.DMA],
        compiler_params=pltpu.CompilerParams(vmem_limit_bytes=1 << 20),
        cost_estimate=LIGHT,
    )(block)


def last_kernel(*refs):
    down, up = refs[-2:]
    sums = []
    for part in range(2):
        total = refs[4 * part][...].astype(jnp.float32)
        for ref in refs[4 * part + 1 : 4 * part + 4]:
            total = total + ref[...].astype(jnp.float32)
        sums.append(total)
    width = down.shape[1]
    cut = sums[0].shape[1] - width
    down[...] = sums[0][:, :width]
    up[:, :cut] = sums[0][:, width:]
    up[:, cut:] = sums[1]


def last_sum(parts, ready, width):
    return pl.pallas_call(
        last_kernel,
        out_shape=[jax.ShapeDtypeStruct((16, width), jnp.float32)] * 2,
        in_specs=[WHOLE] * 8 + [UNREAD] * len(ready),
        out_specs=[WHOLE] * 2,
        compiler_params=pltpu.CompilerParams(vmem_limit_bytes=4 << 20),
        cost_estimate=LIGHT,
    )(*[block for part in parts for block in part], *ready)


def exchanged(parts, step):
    first, second = parts
    axes = (ORDER["x"][step], ORDER["y"][step])
    return [
        [first[0]] + [shift_each(first[by], axes, by) for by in (1, 3, 2)],
        [second[0]] + [shift(second[by], ORDER["z"][step], by) for by in (1, 3, 2)],
    ]


def local(
    ref_image,
    ref_text,
    learner_image,
    learner_text,
    patches,
    cotangent,
    w_up,
    w_down,
    counts,
    sel_index,
    sel_dest,
):
    core = lax.axis_index("core")
    at = jnp.stack([lax.axis_index(name) for name in ("y", "x", "zl", "core", "zh")]).astype(
        jnp.int32
    )
    slots = sel_index.shape[0]
    patch_rows, size = patches.shape[1:]
    count, width, rows = slots * patch_rows, w_up.shape[1], ref_image.shape[0]

    learner = lax.axis_index("zh") == 1
    pad = ((0, 0), (0, learner_image.shape[1] - ref_image.shape[1]))
    x_mine = patches[sel_index].reshape(count, size)
    cot_mine = cotangent[sel_index].reshape(count, size)
    learner_image, learner_text, x_mine, cot_mine = lax.optimization_barrier(
        (learner_image, learner_text, x_mine, cot_mine)
    )
    image = jnp.where(learner, learner_image, jnp.pad(ref_image, pad))
    text = jnp.where(learner, learner_text, jnp.pad(ref_text, pad))
    other_image = lax.ppermute(image, "zl", SWAP)
    x_other = lax.ppermute(x_mine, "core", SWAP)
    cot_other = lax.ppermute(cot_mine, "core", SWAP)
    texts = around(text, "y")
    joined = join_rows(texts, [other_image, x_other, cot_mine])
    texts_other = lax.ppermute(joined, "core", SWAP)
    pair = pair_rows(at, image, other_image, [joined])
    images = around(pair, "x")

    act, slope = up(at, x_mine, x_other, w_up)
    x_first, x_second = turn(at, x_mine, x_other, ("xy", "z"), [])

    parts = partial_losses(at, images, texts, texts_other, [act, x_first])
    grad_pre = back(at, cot_mine, cot_other, w_down, slope, [parts])
    (cot_first,) = turn(at, cot_mine, cot_other, ("xy",), [parts])
    parts = lax.all_to_all(
        parts, ("y", "x", "zl", "core", "zh"), split_axis=0, concat_axis=0, tiled=True
    )
    scores, weight = weights(counts, sel_index, parts, [grad_pre, cot_first])
    learnability = lax.dynamic_slice_in_dim(scores[0], core * rows, rows)

    cut = 640
    second = products(weight, [x_second], [grad_pre], ((0, 0, cut, width),))
    first = products(
        weight,
        [cot_first, x_first],
        [act, grad_pre],
        ((0, 0, 0, width), (1, 1, 0, cut)),
        second[:1],
    )
    blocks = exchanged([first, second], 0)
    keep, give = down(at, act, w_down, [first[0], second[0]])
    got = lax.ppermute(give, "core", SWAP)
    boxed = place(counts, sel_dest.reshape(slots), x_mine, keep, got, [])
    boxed = boxed.reshape(32, 4, patch_rows, size)
    routed = lax.all_to_all(boxed, DP, split_axis=0, concat_axis=0, tiled=True)
    routed = copied(routed.reshape(128, patch_rows, size))
    blocks = sum_blocks(blocks, 56 << 20)
    blocks = sum_blocks(exchanged(blocks, 1), 6 << 20)
    grad_down_t, grad_up = last_sum(exchanged(blocks, 2), [routed], width)
    return (learnability, routed, grad_up, grad_down_t)


def solution(mesh):
    mesh = Mesh(mesh.devices.reshape(4, 4, 2, 2, 2), ("y", "x", "zl", "core", "zh"))
    pairs = P(("y", "x", "zl", "core"), None)
    patch = P(DP, "zh", "core")
    return jax.shard_map(
        local,
        mesh=mesh,
        in_specs=(
            pairs,
            pairs,
            pairs,
            pairs,
            patch,
            patch,
            P(None, "core"),
            P("core", None),
            P(DP),
            P(DP),
            P(DP, None),
        ),
        out_specs=(
            P(("y", "x", "zl", "core")),
            patch,
            P(CHIPS, "core"),
            P(CHIPS, "core"),
        ),
        check_vma=False,
    )
```

```python
import functools
import math

import jax
import jax.numpy as jnp
from jax import lax
from jax.experimental import pallas as pl
from jax.experimental.pallas import tpu as pltpu
from jax.sharding import Mesh, PartitionSpec as P

DP = ("y", "x", "zl")
CHIPS = ("y", "x", "zl", "zh")
SWAP = [(0, 1), (1, 0)]
ORDER = {"x": "xyz", "y": "yzx", "z": "zxy"}
WHOLE = pl.BlockSpec(memory_space=pltpu.VMEM)
SCALARS = pl.BlockSpec(memory_space=pltpu.SMEM)
UNREAD = pl.BlockSpec(memory_space=pl.ANY)
LIGHT = pl.CostEstimate(flops=1 << 20, bytes_accessed=1 << 16, transcendentals=0)


def unit(rows):
    wide = rows.astype(jnp.float32)
    norm = lax.rsqrt(jnp.sum(wide * wide, axis=1, keepdims=True) + 1e-06)
    return (wide * norm).astype(jnp.bfloat16)


def softplus(value):
    return jnp.maximum(value, 0.0) + jnp.log1p(jnp.exp(-jnp.abs(value)))


def loss_kernel(at, *refs):
    img_refs, txt_refs, txt_other, (out, img, txt) = refs[:4], refs[4:8], refs[8], refs[-3:]
    here_y, here_x, here_zl, here_core, learner = (at[k] for k in range(5))
    for k in range(4):
        img[pl.ds(128 * k, 128), :] = unit(img_refs[k][...])
        own = pl.multiple_of(128 * k + 64 * here_core, 64)
        txt[pl.ds(own, 64), :] = unit(txt_refs[k][...])
        other = pl.multiple_of(128 * k + 64 * (1 - here_core), 64)
        txt[pl.ds(other, 64), :] = unit(txt_other[pl.ds(64 * k, 64), :])
    contract = (((1,), (1,)), ((), ()))
    col_sum = jnp.zeros((1, 512), jnp.float32)
    row_sums = []
    for k in range(4):
        scores = (
            10.0
            * lax.dot_general(
                img[pl.ds(128 * k, 128), :], txt[...], contract, preferred_element_type=jnp.float32
            )
            - 5.0
        )
        if k == 0:
            row = lax.broadcasted_iota(jnp.int32, scores.shape, 0) - 64 * here_zl
            col = lax.broadcasted_iota(jnp.int32, scores.shape, 1) - 64 * here_core
            same = (row == col) & (row >= 0) & (row < 64)
            scores = jnp.where(same, -scores, scores)
        terms = softplus(scores)
        col_sum = col_sum + jnp.sum(terms, axis=0, keepdims=True)
        folded = terms[:, :128] + terms[:, 128:256] + terms[:, 256:384] + terms[:, 384:]
        row_sums.append(jnp.sum(folded.T, axis=0, keepdims=True))
    dest = lax.broadcasted_iota(jnp.int32, (128, 128), 0)
    lane = lax.broadcasted_iota(jnp.int32, (1, 128), 1)
    dest_y, dest_x, dest_zl = dest >> 5, (dest >> 3) & 3, (dest >> 2) & 1
    own_half = (lane >> 6) == here_core
    total = jnp.zeros((128, 128), jnp.float32)
    for k in range(4):
        straight = row_sums[k]
        crossed = pltpu.roll(straight, 64, 1)
        for zl in range(2):
            placed = jnp.where(own_half, jnp.where(here_core == zl, straight, crossed), 0.0)
            mine = (dest_y == here_y) & (dest_x == ((here_x + k) & 3)) & (dest_zl == zl)
            total = total + jnp.where(mine, placed, 0.0)
        mine = (dest_y == ((here_y + k) & 3)) & (dest_x == here_x) & (dest_zl == here_zl)
        total = total + jnp.where(mine, col_sum[:, 128 * k : 128 * (k + 1)], 0.0)
    out[...] = jnp.where(learner == 1, 0.5, -0.5) * total


def partial_losses(at, images, texts, texts_other, ready):
    return pl.pallas_call(
        loss_kernel,
        out_shape=jax.ShapeDtypeStruct((128, 128), jnp.float32),
        in_specs=[SCALARS] + [WHOLE] * 9 + [UNREAD] * len(ready),
        out_specs=WHOLE,
        scratch_shapes=[pltpu.VMEM((512, 1024), jnp.bfloat16)] * 2,
        compiler_params=pltpu.CompilerParams(vmem_limit_bytes=8 << 20),
        cost_estimate=LIGHT,
    )(at, *images, *texts, texts_other, *ready)


def listed(values, axis, shape):
    at = lax.broadcasted_iota(jnp.int32, shape, axis)
    out = jnp.zeros(shape, jnp.int32)
    for k in range(shape[axis]):
        out = jnp.where(at == k, values[k], out)
    return out


def weight_kernel(count, index, parts, *refs):
    learn, weight = refs[-2:]
    score = jnp.sum(parts[...], axis=0, keepdims=True)
    learn[...] = jnp.broadcast_to(score, (8, 128))
    slots = index.shape[0]
    picked = listed(index, 0, (slots, 128)) == lax.broadcasted_iota(jnp.int32, (slots, 128), 1)
    chosen = jnp.sum(jnp.where(picked, score, 0.0), axis=1, keepdims=True)
    live = lax.broadcasted_iota(jnp.int32, (slots, 128), 0) < count[0]
    value = jnp.where(live, 1.0 / (1.0 + jnp.exp(-chosen)), 0.0)
    weight[...] = jnp.broadcast_to(value[:, None, :], (slots, 8, 128)).reshape(8 * slots, 128)


def weights(counts, index, parts, ready):
    slots = index.shape[0]
    return pl.pallas_call(
        weight_kernel,
        out_shape=(
            jax.ShapeDtypeStruct((8, 128), jnp.float32),
            jax.ShapeDtypeStruct((8 * slots, 128), jnp.float32),
        ),
        in_specs=[SCALARS, SCALARS, WHOLE] + [UNREAD] * len(ready),
        out_specs=(WHOLE, WHOLE),
        compiler_params=pltpu.CompilerParams(vmem_limit_bytes=2 << 20),
        cost_estimate=LIGHT,
    )(counts, index, parts, *ready)


def pair_kernel(at, own, other, *refs):
    pair = refs[-1]
    pair[pl.ds(pl.multiple_of(64 * at[2], 64), 64), :] = own[...]
    pair[pl.ds(pl.multiple_of(64 * (1 - at[2]), 64), 64), :] = other[...]


def pair_rows(at, own, other, ready):
    rows, width = own.shape
    return pl.pallas_call(
        pair_kernel,
        out_shape=jax.ShapeDtypeStruct((2 * rows, width), own.dtype),
        in_specs=[SCALARS, WHOLE, WHOLE] + [UNREAD] * len(ready),
        out_specs=WHOLE,
        compiler_params=pltpu.CompilerParams(vmem_limit_bytes=2 << 20),
        cost_estimate=LIGHT,
    )(at, own, other, *ready)


def join_kernel(*refs):
    out = refs[-1]
    rows = refs[0].shape[0]
    for k, block in enumerate(refs[: out.shape[0] // rows]):
        out[k * rows : (k + 1) * rows, :] = block[...]


def join_rows(blocks, ready):
    rows, width = blocks[0].shape
    return pl.pallas_call(
        join_kernel,
        out_shape=jax.ShapeDtypeStruct((len(blocks) * rows, width), blocks[0].dtype),
        in_specs=[WHOLE] * len(blocks) + [UNREAD] * len(ready),
        out_specs=WHOLE,
        compiler_params=pltpu.CompilerParams(vmem_limit_bytes=2 << 20),
        cost_estimate=LIGHT,
    )(*blocks, *ready)


def half(ref, axis, which, size):
    start = pl.multiple_of(which * size, size)
    return ref[pl.ds(start, size), :] if axis == 0 else ref[:, pl.ds(start, size)]


def up_kernel(at, mine, other, w_up, *refs):
    act, slope, held, sems = refs[-4:]
    size = mine.shape[1]
    steps, _, tile = held.shape
    columns = [pl.ds(n * tile, tile) for n in range(steps)]
    copies = fetched([w_up.at[:, cols] for cols in columns], [held.at[n] for n in range(steps)], sems)
    scale = math.sqrt(2.0 / math.pi)
    for n, cols in enumerate(columns):
        copies[n].wait()
        near, far = half(held.at[n], 0, at[3], size), half(held.at[n], 0, 1 - at[3], size)
        for row in range(0, mine.shape[0], 256):
            rows = pl.ds(row, 256)
            pre = jnp.dot(mine[rows, :], near, preferred_element_type=jnp.float32)
            pre = pre + jnp.dot(other[rows, :], far, preferred_element_type=jnp.float32)
            square = pre * pre
            tanh = jnp.tanh(pre * (scale + (scale * 0.044715) * square))
            gate = 0.5 + 0.5 * tanh
            act[rows, cols] = (pre * gate).astype(jnp.bfloat16)
            bend = pre * (0.5 - 0.5 * tanh * tanh) * (scale + (scale * 3 * 0.044715) * square)
            slope[rows, cols] = (gate + bend).astype(jnp.bfloat16)


def up(at, mine, other, w_up, ready):
    rows, size = mine.shape
    width, tile = w_up.shape[1], 512
    return pl.pallas_call(
        up_kernel,
        out_shape=[jax.ShapeDtypeStruct((rows, width), jnp.bfloat16)] * 2,
        in_specs=[SCALARS, WHOLE, WHOLE, UNREAD] + [UNREAD] * len(ready),
        out_specs=[WHOLE, WHOLE],
        scratch_shapes=[
            pltpu.VMEM((width // tile, 2 * size, tile), w_up.dtype),
            pltpu.SemaphoreType.DMA((width // tile,)),
        ],
        compiler_params=pltpu.CompilerParams(vmem_limit_bytes=16 << 20),
        cost_estimate=LIGHT,
    )(at, mine, other, w_up, *ready)


def back_kernel(at, mine, other, w_down, slope, *refs):
    out, held, sems = refs[-3:]
    size = mine.shape[1]
    steps, tile, _ = held.shape
    columns = [pl.ds(n * tile, tile) for n in range(steps)]
    copies = fetched([w_down.at[cols] for cols in columns], [held.at[n] for n in range(steps)], sems)
    contract = (((1,), (1,)), ((), ()))
    for n, cols in enumerate(columns):
        copies[n].wait()
        near, far = half(held.at[n], 1, at[3], size), half(held.at[n], 1, 1 - at[3], size)
        back = lax.dot_general(mine[...], near, contract, preferred_element_type=jnp.float32)
        back = back + lax.dot_general(other[...], far, contract, preferred_element_type=jnp.float32)
        out[:, cols] = (back * slope[:, cols].astype(jnp.float32)).astype(jnp.bfloat16)


def back(at, mine, other, w_down, slope, ready):
    rows, size = mine.shape
    width, tile = w_down.shape[0], 512
    return pl.pallas_call(
        back_kernel,
        out_shape=jax.ShapeDtypeStruct((rows, width), jnp.bfloat16),
        in_specs=[SCALARS, WHOLE, WHOLE, UNREAD, WHOLE] + [UNREAD] * len(ready),
        out_specs=WHOLE,
        scratch_shapes=[
            pltpu.VMEM((width // tile, tile, 2 * size), w_down.dtype),
            pltpu.SemaphoreType.DMA((width // tile,)),
        ],
        compiler_params=pltpu.CompilerParams(vmem_limit_bytes=56 << 20),
        cost_estimate=LIGHT,
    )(at, mine, other, w_down, slope, *ready)


def turn_kernel(starts, at, mine, other, *refs):
    outs, turned = refs[len(refs) - 1 - len(starts) : -1], refs[-1]
    blocks = turned.shape[0] // 2
    turned[pl.ds(at[3] * blocks, blocks)] = mine[...].T.reshape((blocks,) + turned.shape[1:])
    turned[pl.ds((1 - at[3]) * blocks, blocks)] = other[...].T.reshape(
        (blocks,) + turned.shape[1:]
    )
    here = {"x": at[1], "y": at[0], "z": 2 * at[4] + at[2]}
    for start, out in zip(starts, outs):
        for k in range(2 * blocks):
            steps = (k >> 4, (k >> 2) & 3, k & 3)
            spot = {}
            for axis in "xyz":
                by = [steps[ORDER[one].index(axis)] for one in start]
                by = by[0] + at[3] * (by[-1] - by[0])
                spot[axis] = (here[axis] + by) & 3
            block = 16 * spot["y"] + 4 * spot["x"] + 2 * (spot["z"] & 1) + (spot["z"] >> 1)
            out[16 * k : 16 * (k + 1), :] = turned[block]


def turn(at, mine, other, starts, ready):
    rows, size = mine.shape
    return pl.pallas_call(
        functools.partial(turn_kernel, starts),
        out_shape=[jax.ShapeDtypeStruct((2 * size, rows), mine.dtype)] * len(starts),
        in_specs=[SCALARS, WHOLE, WHOLE] + [UNREAD] * len(ready),
        out_specs=[WHOLE] * len(starts),
        scratch_shapes=[pltpu.VMEM((2 * size // 16, 16, rows), mine.dtype)],
        compiler_params=pltpu.CompilerParams(vmem_limit_bytes=8 << 20),
        cost_estimate=LIGHT,
    )(at, mine, other, *ready)


def down_kernel(at, act, w_down, *refs):
    keep, give = refs[-2:]
    size = keep.shape[1]
    keep[...] = jnp.dot(
        act[...], half(w_down, 1, at[3], size), preferred_element_type=jnp.float32
    )
    give[...] = jnp.dot(
        act[...], half(w_down, 1, 1 - at[3], size), preferred_element_type=jnp.float32
    )


def down(at, act, w_down, ready):
    rows, size = act.shape[0], w_down.shape[1] // 2
    return pl.pallas_call(
        down_kernel,
        out_shape=[jax.ShapeDtypeStruct((rows, size), jnp.float32)] * 2,
        in_specs=[SCALARS, WHOLE, WHOLE] + [UNREAD] * len(ready),
        out_specs=[WHOLE, WHOLE],
        compiler_params=pltpu.CompilerParams(vmem_limit_bytes=14 << 20),
        cost_estimate=LIGHT,
    )(at, act, w_down, *ready)


def place_kernel(count, target, own, keep, got, *refs):
    out = refs[-1]
    slots, rows = target.shape[0], own.shape[0]
    each = rows // slots
    out_rows = (own[...].astype(jnp.float32) + keep[...] + got[...]).astype(jnp.bfloat16)
    slot = lax.broadcasted_iota(jnp.int32, (slots, slots), 0)
    before = lax.broadcasted_iota(jnp.int32, (slots, slots), 1)
    to = listed(target, 0, (slots, slots))
    same = (listed(target, 1, (1, slots)) == to) & (before < slot)
    rank = jnp.sum(same.astype(jnp.int32), axis=1, keepdims=True)
    live = slot[:, :1] < count[0]
    first = jnp.where(live, each * (4 * to[:, :1] + rank), -each)
    lane = lax.broadcasted_iota(jnp.int32, (slots, rows), 1)
    mine = (lane // each) == lax.broadcasted_iota(jnp.int32, (slots, rows), 0)
    goes = jnp.sum(jnp.where(mine, first + lane % each, 0), axis=0, keepdims=True)
    step = 256
    for at in range(0, out.shape[0], step):
        here = lax.broadcasted_iota(jnp.int32, (step, rows), 0) + at == goes
        out[at : at + step, :] = jnp.dot(
            jnp.where(here, 1.0, 0.0).astype(jnp.bfloat16),
            out_rows,
            preferred_element_type=jnp.float32,
        ).astype(jnp.bfloat16)


def place(counts, target, own, keep, got, ready):
    rows, size = own.shape
    return pl.pallas_call(
        place_kernel,
        out_shape=jax.ShapeDtypeStruct((2 * rows, size), jnp.bfloat16),
        in_specs=[SCALARS, SCALARS] + [WHOLE] * 3 + [UNREAD] * len(ready),
        out_specs=WHOLE,
        compiler_params=pltpu.CompilerParams(vmem_limit_bytes=8 << 20),
        cost_estimate=LIGHT,
    )(counts, target, own, keep, got, *ready)


def around(block, axis):
    return [block] + [shift(block, axis, 4 - by) for by in (1, 2, 3)]


def shift(block, axis, by):
    if axis == "z":
        at = [(z % 2) * 2 + z // 2 for z in range(4)]
        return lax.ppermute(block, ("zl", "zh"), [(at[z], at[(z + by) % 4]) for z in range(4)])
    return lax.ppermute(block, axis, [(k, (k + by) % 4) for k in range(4)])


def number(spot, core):
    return 8 * (4 * spot["y"] + spot["x"]) + 4 * (spot["z"] % 2) + 2 * core + spot["z"] // 2


def shift_each(block, axes, by):
    route = []
    for chip in range(64):
        spot = {"x": chip % 4, "y": chip // 4 % 4, "z": chip // 16}
        for core in range(2):
            axis = axes[core]
            there = {**spot, axis: (spot[axis] + by) % 4}
            route.append((number(spot, core), number(there, core)))
    return lax.ppermute(block, ("y", "x", "zl", "core", "zh"), route)


def fetched(sources, targets, sems):
    copies = [
        pltpu.make_async_copy(source, target, sems.at[k])
        for k, (source, target) in enumerate(zip(sources, targets))
    ]
    for copy in copies:
        copy.start()
    return copies


def product_kernel(pieces, weight, *refs):
    lefts = 1 + max(piece[0] for piece in pieces)
    count = lefts + 1 + max(piece[1] for piece in pieces)
    sources, rest = refs[:count], refs[len(refs) - count - 6 :]
    outs, held, scaled, sems = rest[:4], rest[4 : 4 + count], rest[-2], rest[-1]
    sides, steps = [], []
    for left, right, first, last in pieces:
        sides.append((sources[left], held[left]))
        for start in range(first, last, 512):
            cols = pl.ds(start, min(512, last - start))
            sides.append((sources[lefts + right].at[:, cols], held[lefts + right].at[:, cols]))
    copies = fetched(*zip(*sides), sems)
    rows = weight[...]
    depth = outs[0].shape[0]
    done = number = 0
    for left, right, first, last in pieces:
        copies[number].wait()
        number += 1
        for start in range(first, last, 256):
            if (start - first) % 512 == 0:
                copies[number].wait()
                number += 1
            size = min(256, last - start)
            for col in range(0, size, 128):
                piece = held[lefts + right][:, start + col : start + col + 128]
                piece = piece.astype(jnp.float32) * rows
                scaled[:, done + col : done + col + 128] = piece.astype(jnp.bfloat16)
            for k in range(4):
                outs[k][:, done : done + size] = jnp.dot(
                    held[left][depth * k : depth * (k + 1), :],
                    scaled[:, done : done + size],
                    preferred_element_type=jnp.float32,
                ).astype(jnp.bfloat16)
            done += size


def products(weight, lefts, rights, pieces, ready=()):
    width = sum(last - first for _, _, first, last in pieces)
    sides = [*lefts, *rights]
    depth = weight.shape[0]
    copies = sum(1 + pl.cdiv(last - first, 512) for _, _, first, last in pieces)
    return pl.pallas_call(
        functools.partial(product_kernel, pieces),
        out_shape=[jax.ShapeDtypeStruct((256, width), jnp.bfloat16)] * 4,
        in_specs=[WHOLE] + [UNREAD] * (len(sides) + len(ready)),
        out_specs=[WHOLE] * 4,
        scratch_shapes=[pltpu.VMEM(side.shape, side.dtype) for side in sides]
        + [pltpu.VMEM((depth, width), jnp.bfloat16), pltpu.SemaphoreType.DMA((copies,))],
        compiler_params=pltpu.CompilerParams(vmem_limit_bytes=20 << 20),
        cost_estimate=LIGHT,
    )(weight, *sides, *ready)


def sum_kernel(*refs):
    sources, outs, held, sems = refs[:8], refs[-17:-9], refs[-9:-1], refs[-1]
    chunks = []
    for part in range(2):
        rows = outs[4 * part].shape[0]
        for k in range(4):
            for block in range(4 * part, 4 * part + 4):
                here = pl.ds(k * rows, rows)
                chunks.append((sources[block].at[here], held[block].at[here]))
    copies = fetched(*zip(*chunks), sems)
    for part in range(2):
        rows = outs[4 * part].shape[0]
        for k in range(4):
            for copy in copies[16 * part + 4 * k : 16 * part + 4 * k + 4]:
                copy.wait()
            here = pl.ds(k * rows, rows)
            total = held[4 * part][here, :].astype(jnp.float32)
            for ref in held[4 * part + 1 : 4 * part + 4]:
                total = total + ref[here, :].astype(jnp.float32)
            outs[4 * part + k][...] = total.astype(jnp.bfloat16)


def sum_blocks(parts, grant):
    blocks = [block for part in parts for block in part]
    out = pl.pallas_call(
        sum_kernel,
        out_shape=[
            jax.ShapeDtypeStruct((block.shape[0] // 4, block.shape[1]), jnp.bfloat16)
            for block in blocks
        ],
        in_specs=[UNREAD] * 8,
        out_specs=[WHOLE] * 8,
        scratch_shapes=[pltpu.VMEM(block.shape, block.dtype) for block in blocks]
        + [pltpu.SemaphoreType.DMA((32,))],
        compiler_params=pltpu.CompilerParams(vmem_limit_bytes=grant),
        cost_estimate=LIGHT,
    )(*blocks)
    return [out[:4], out[4:]]


def copy_kernel(source, out, sem):
    copy = pltpu.make_async_copy(source, out, sem)
    copy.start()
    copy.wait()


def copied(block):
    return pl.pallas_call(
        copy_kernel,
        out_shape=jax.ShapeDtypeStruct(block.shape, block.dtype),
        in_specs=[UNREAD],
        out_specs=UNREAD,
        scratch_shapes=[pltpu.SemaphoreType.DMA],
        compiler_params=pltpu.CompilerParams(vmem_limit_bytes=56 << 20),
        cost_estimate=LIGHT,
    )(block)


def last_kernel(*refs):
    down, up = refs[-2:]
    sums = []
    for part in range(2):
        total = refs[4 * part][...].astype(jnp.float32)
        for ref in refs[4 * part + 1 : 4 * part + 4]:
            total = total + ref[...].astype(jnp.float32)
        sums.append(total)
    width = down.shape[1]
    cut = sums[0].shape[1] - width
    down[...] = sums[0][:, :width]
    up[:, :cut] = sums[0][:, width:]
    up[:, cut:] = sums[1]


def last_sum(parts, ready, width):
    return pl.pallas_call(
        last_kernel,
        out_shape=[jax.ShapeDtypeStruct((16, width), jnp.float32)] * 2,
        in_specs=[WHOLE] * 8 + [UNREAD] * len(ready),
        out_specs=[WHOLE] * 2,
        compiler_params=pltpu.CompilerParams(vmem_limit_bytes=4 << 20),
        cost_estimate=LIGHT,
    )(*[block for part in parts for block in part], *ready)


def exchanged(parts, step):
    first, second = parts
    axes = (ORDER["x"][step], ORDER["y"][step])
    return [
        [first[0]] + [shift_each(first[by], axes, by) for by in (1, 3, 2)],
        [second[0]] + [shift(second[by], ORDER["z"][step], by) for by in (1, 3, 2)],
    ]


def local(
    ref_image,
    ref_text,
    learner_image,
    learner_text,
    patches,
    cotangent,
    w_up,
    w_down,
    counts,
    sel_index,
    sel_dest,
):
    core = lax.axis_index("core")
    at = jnp.stack([lax.axis_index(name) for name in ("y", "x", "zl", "core", "zh")]).astype(
        jnp.int32
    )
    slots = sel_index.shape[0]
    patch_rows, size = patches.shape[1:]
    count, width, rows = slots * patch_rows, w_up.shape[1], ref_image.shape[0]

    learner = lax.axis_index("zh") == 1
    pad = ((0, 0), (0, learner_image.shape[1] - ref_image.shape[1]))
    x_mine = patches[sel_index].reshape(count, size)
    cot_mine = cotangent[sel_index].reshape(count, size)
    learner_image, learner_text, x_mine, cot_mine = lax.optimization_barrier(
        (learner_image, learner_text, x_mine, cot_mine)
    )
    image = jnp.where(learner, learner_image, jnp.pad(ref_image, pad))
    text = jnp.where(learner, learner_text, jnp.pad(ref_text, pad))
    other_image = lax.ppermute(image, "zl", SWAP)
    x_other = lax.ppermute(x_mine, "core", SWAP)
    cot_other = lax.ppermute(cot_mine, "core", SWAP)
    texts = around(text, "y")
    joined = join_rows(texts, [other_image, x_other, cot_mine])
    texts_other = lax.ppermute(joined, "core", SWAP)
    pair = pair_rows(at, image, other_image, [joined])
    images = around(pair, "x")

    act, slope = up(at, x_mine, x_other, w_up, [pair])
    x_first, x_second = turn(at, x_mine, x_other, ("xy", "z"), [pair])

    parts = partial_losses(at, images, texts, texts_other, [act, x_first, cot_other])
    keep, give = down(at, act, w_down, [parts])
    got = lax.ppermute(give, "core", SWAP)
    grad_pre = back(at, cot_mine, cot_other, w_down, slope, [parts])
    (cot_first,) = turn(at, cot_mine, cot_other, ("xy",), [parts])
    parts = lax.all_to_all(
        parts, ("y", "x", "zl", "core", "zh"), split_axis=0, concat_axis=0, tiled=True
    )
    scores, weight = weights(counts, sel_index, parts, [grad_pre, cot_first, got])
    learnability = lax.dynamic_slice_in_dim(scores[0], core * rows, rows)

    cut = 640
    second = products(weight, [x_second], [grad_pre], ((0, 0, cut, width),))
    first = products(
        weight,
        [cot_first, x_first],
        [act, grad_pre],
        ((0, 0, 0, width), (1, 1, 0, cut)),
        second[:1],
    )
    blocks = exchanged([first, second], 0)
    boxed = place(counts, sel_dest.reshape(slots), x_mine, keep, got, [first[0]])
    boxed = boxed.reshape(32, 4, patch_rows, size)
    routed = lax.all_to_all(boxed, DP, split_axis=0, concat_axis=0, tiled=True)
    routed = copied(routed.reshape(128, patch_rows, size))
    blocks = sum_blocks(blocks, 56 << 20)
    blocks = sum_blocks(exchanged(blocks, 1), 6 << 20)
    grad_down_t, grad_up = last_sum(exchanged(blocks, 2), [routed], width)
    return (learnability, routed, grad_up, grad_down_t)


def solution(mesh):
    mesh = Mesh(mesh.devices.reshape(4, 4, 2, 2, 2), ("y", "x", "zl", "core", "zh"))
    pairs = P(("y", "x", "zl", "core"), None)
    patch = P(DP, "zh", "core")
    return jax.shard_map(
        local,
        mesh=mesh,
        in_specs=(
            pairs,
            pairs,
            pairs,
            pairs,
            patch,
            patch,
            P(None, "core"),
            P("core", None),
            P(DP),
            P(DP),
            P(DP, None),
        ),
        out_specs=(
            P(("y", "x", "zl", "core")),
            patch,
            P(CHIPS, "core"),
            P(CHIPS, "core"),
        ),
        check_vma=False,
    )
```

```python
import functools
import math

import jax
import jax.numpy as jnp
from jax import lax
from jax.experimental import pallas as pl
from jax.experimental.pallas import tpu as pltpu
from jax.sharding import Mesh, PartitionSpec as P

DP = ("y", "x", "zl")
CHIPS = ("y", "x", "zl", "zh")
SWAP = [(0, 1), (1, 0)]
ORDER = {"x": "xyz", "y": "yzx", "z": "zxy"}
WHOLE = pl.BlockSpec(memory_space=pltpu.VMEM)
SCALARS = pl.BlockSpec(memory_space=pltpu.SMEM)
UNREAD = pl.BlockSpec(memory_space=pl.ANY)
LIGHT = pl.CostEstimate(flops=1 << 20, bytes_accessed=1 << 16, transcendentals=0)


def unit(rows):
    wide = rows.astype(jnp.float32)
    norm = lax.rsqrt(jnp.sum(wide * wide, axis=1, keepdims=True) + 1e-06)
    return (wide * norm).astype(jnp.bfloat16)


def softplus(value):
    return jnp.maximum(value, 0.0) + jnp.log1p(jnp.exp(-jnp.abs(value)))


def loss_kernel(at, *refs):
    img_refs, txt_refs, txt_other, (out, img, txt) = refs[:4], refs[4:8], refs[8], refs[-3:]
    here_y, here_x, here_zl, here_core, learner = (at[k] for k in range(5))
    for k in range(4):
        img[pl.ds(128 * k, 128), :] = unit(img_refs[k][...])
        own = pl.multiple_of(128 * k + 64 * here_core, 64)
        txt[pl.ds(own, 64), :] = unit(txt_refs[k][...])
        other = pl.multiple_of(128 * k + 64 * (1 - here_core), 64)
        txt[pl.ds(other, 64), :] = unit(txt_other[pl.ds(64 * k, 64), :])
    contract = (((1,), (1,)), ((), ()))
    col_sum = jnp.zeros((1, 512), jnp.float32)
    row_sums = []
    for k in range(4):
        scores = (
            10.0
            * lax.dot_general(
                img[pl.ds(128 * k, 128), :], txt[...], contract, preferred_element_type=jnp.float32
            )
            - 5.0
        )
        if k == 0:
            row = lax.broadcasted_iota(jnp.int32, scores.shape, 0) - 64 * here_zl
            col = lax.broadcasted_iota(jnp.int32, scores.shape, 1) - 64 * here_core
            same = (row == col) & (row >= 0) & (row < 64)
            scores = jnp.where(same, -scores, scores)
        terms = softplus(scores)
        col_sum = col_sum + jnp.sum(terms, axis=0, keepdims=True)
        folded = terms[:, :128] + terms[:, 128:256] + terms[:, 256:384] + terms[:, 384:]
        row_sums.append(jnp.sum(folded.T, axis=0, keepdims=True))
    dest = lax.broadcasted_iota(jnp.int32, (128, 128), 0)
    lane = lax.broadcasted_iota(jnp.int32, (1, 128), 1)
    dest_y, dest_x, dest_zl = dest >> 5, (dest >> 3) & 3, (dest >> 2) & 1
    own_half = (lane >> 6) == here_core
    total = jnp.zeros((128, 128), jnp.float32)
    for k in range(4):
        straight = row_sums[k]
        crossed = pltpu.roll(straight, 64, 1)
        for zl in range(2):
            placed = jnp.where(own_half, jnp.where(here_core == zl, straight, crossed), 0.0)
            mine = (dest_y == here_y) & (dest_x == ((here_x + k) & 3)) & (dest_zl == zl)
            total = total + jnp.where(mine, placed, 0.0)
        mine = (dest_y == ((here_y + k) & 3)) & (dest_x == here_x) & (dest_zl == here_zl)
        total = total + jnp.where(mine, col_sum[:, 128 * k : 128 * (k + 1)], 0.0)
    out[...] = jnp.where(learner == 1, 0.5, -0.5) * total


def partial_losses(at, images, texts, texts_other, ready):
    return pl.pallas_call(
        loss_kernel,
        out_shape=jax.ShapeDtypeStruct((128, 128), jnp.float32),
        in_specs=[SCALARS] + [WHOLE] * 9 + [UNREAD] * len(ready),
        out_specs=WHOLE,
        scratch_shapes=[pltpu.VMEM((512, 1024), jnp.bfloat16)] * 2,
        compiler_params=pltpu.CompilerParams(vmem_limit_bytes=8 << 20),
        cost_estimate=LIGHT,
    )(at, *images, *texts, texts_other, *ready)


def listed(values, axis, shape):
    at = lax.broadcasted_iota(jnp.int32, shape, axis)
    out = jnp.zeros(shape, jnp.int32)
    for k in range(shape[axis]):
        out = jnp.where(at == k, values[k], out)
    return out


def weight_kernel(count, index, parts, *refs):
    learn, weight = refs[-2:]
    score = jnp.sum(parts[...], axis=0, keepdims=True)
    learn[...] = jnp.broadcast_to(score, (8, 128))
    slots = index.shape[0]
    picked = listed(index, 0, (slots, 128)) == lax.broadcasted_iota(jnp.int32, (slots, 128), 1)
    chosen = jnp.sum(jnp.where(picked, score, 0.0), axis=1, keepdims=True)
    live = lax.broadcasted_iota(jnp.int32, (slots, 128), 0) < count[0]
    value = jnp.where(live, 1.0 / (1.0 + jnp.exp(-chosen)), 0.0)
    weight[...] = jnp.broadcast_to(value[:, None, :], (slots, 8, 128)).reshape(8 * slots, 128)


def weights(counts, index, parts, ready):
    slots = index.shape[0]
    return pl.pallas_call(
        weight_kernel,
        out_shape=(
            jax.ShapeDtypeStruct((8, 128), jnp.float32),
            jax.ShapeDtypeStruct((8 * slots, 128), jnp.float32),
        ),
        in_specs=[SCALARS, SCALARS, WHOLE] + [UNREAD] * len(ready),
        out_specs=(WHOLE, WHOLE),
        compiler_params=pltpu.CompilerParams(vmem_limit_bytes=2 << 20),
        cost_estimate=LIGHT,
    )(counts, index, parts, *ready)


def pair_kernel(at, own, other, *refs):
    pair = refs[-1]
    pair[pl.ds(pl.multiple_of(64 * at[2], 64), 64), :] = own[...]
    pair[pl.ds(pl.multiple_of(64 * (1 - at[2]), 64), 64), :] = other[...]


def pair_rows(at, own, other, ready):
    rows, width = own.shape
    return pl.pallas_call(
        pair_kernel,
        out_shape=jax.ShapeDtypeStruct((2 * rows, width), own.dtype),
        in_specs=[SCALARS, WHOLE, WHOLE] + [UNREAD] * len(ready),
        out_specs=WHOLE,
        compiler_params=pltpu.CompilerParams(vmem_limit_bytes=2 << 20),
        cost_estimate=LIGHT,
    )(at, own, other, *ready)


def join_kernel(*refs):
    out = refs[-1]
    rows = refs[0].shape[0]
    for k, block in enumerate(refs[: out.shape[0] // rows]):
        out[k * rows : (k + 1) * rows, :] = block[...]


def join_rows(blocks, ready):
    rows, width = blocks[0].shape
    return pl.pallas_call(
        join_kernel,
        out_shape=jax.ShapeDtypeStruct((len(blocks) * rows, width), blocks[0].dtype),
        in_specs=[WHOLE] * len(blocks) + [UNREAD] * len(ready),
        out_specs=WHOLE,
        compiler_params=pltpu.CompilerParams(vmem_limit_bytes=2 << 20),
        cost_estimate=LIGHT,
    )(*blocks, *ready)


def half(ref, axis, which, size):
    start = pl.multiple_of(which * size, size)
    return ref[pl.ds(start, size), :] if axis == 0 else ref[:, pl.ds(start, size)]


def up_kernel(at, mine, other, w_up, *refs):
    act, slope, held, sems = refs[-4:]
    size = mine.shape[1]
    steps, _, tile = held.shape
    columns = [pl.ds(n * tile, tile) for n in range(steps)]
    copies = fetched([w_up.at[:, cols] for cols in columns], [held.at[n] for n in range(steps)], sems)
    scale = math.sqrt(2.0 / math.pi)
    for n, cols in enumerate(columns):
        copies[n].wait()
        near, far = half(held.at[n], 0, at[3], size), half(held.at[n], 0, 1 - at[3], size)
        for row in range(0, mine.shape[0], 256):
            rows = pl.ds(row, 256)
            pre = jnp.dot(mine[rows, :], near, preferred_element_type=jnp.float32)
            pre = pre + jnp.dot(other[rows, :], far, preferred_element_type=jnp.float32)
            square = pre * pre
            tanh = jnp.tanh(pre * (scale + (scale * 0.044715) * square))
            gate = 0.5 + 0.5 * tanh
            act[rows, cols] = (pre * gate).astype(jnp.bfloat16)
            bend = pre * (0.5 - 0.5 * tanh * tanh) * (scale + (scale * 3 * 0.044715) * square)
            slope[rows, cols] = (gate + bend).astype(jnp.bfloat16)


def up(at, mine, other, w_up, ready):
    rows, size = mine.shape
    width, tile = w_up.shape[1], 512
    return pl.pallas_call(
        up_kernel,
        out_shape=[jax.ShapeDtypeStruct((rows, width), jnp.bfloat16)] * 2,
        in_specs=[SCALARS, WHOLE, WHOLE, UNREAD] + [UNREAD] * len(ready),
        out_specs=[WHOLE, WHOLE],
        scratch_shapes=[
            pltpu.VMEM((width // tile, 2 * size, tile), w_up.dtype),
            pltpu.SemaphoreType.DMA((width // tile,)),
        ],
        compiler_params=pltpu.CompilerParams(vmem_limit_bytes=16 << 20),
        cost_estimate=LIGHT,
    )(at, mine, other, w_up, *ready)


def back_kernel(at, mine, other, w_down, slope, *refs):
    out, held, sems = refs[-3:]
    size = mine.shape[1]
    steps, tile, _ = held.shape
    columns = [pl.ds(n * tile, tile) for n in range(steps)]
    copies = fetched([w_down.at[cols] for cols in columns], [held.at[n] for n in range(steps)], sems)
    contract = (((1,), (1,)), ((), ()))
    for n, cols in enumerate(columns):
        copies[n].wait()
        near, far = half(held.at[n], 1, at[3], size), half(held.at[n], 1, 1 - at[3], size)
        back = lax.dot_general(mine[...], near, contract, preferred_element_type=jnp.float32)
        back = back + lax.dot_general(other[...], far, contract, preferred_element_type=jnp.float32)
        out[:, cols] = (back * slope[:, cols].astype(jnp.float32)).astype(jnp.bfloat16)


def back(at, mine, other, w_down, slope, ready):
    rows, size = mine.shape
    width, tile = w_down.shape[0], 512
    return pl.pallas_call(
        back_kernel,
        out_shape=jax.ShapeDtypeStruct((rows, width), jnp.bfloat16),
        in_specs=[SCALARS, WHOLE, WHOLE, UNREAD, WHOLE] + [UNREAD] * len(ready),
        out_specs=WHOLE,
        scratch_shapes=[
            pltpu.VMEM((width // tile, tile, 2 * size), w_down.dtype),
            pltpu.SemaphoreType.DMA((width // tile,)),
        ],
        compiler_params=pltpu.CompilerParams(vmem_limit_bytes=14 << 20),
        cost_estimate=LIGHT,
    )(at, mine, other, w_down, slope, *ready)


def turn_kernel(starts, at, mine, other, *refs):
    outs, turned = refs[len(refs) - 1 - len(starts) : -1], refs[-1]
    blocks = turned.shape[0] // 2
    turned[pl.ds(at[3] * blocks, blocks)] = mine[...].T.reshape((blocks,) + turned.shape[1:])
    turned[pl.ds((1 - at[3]) * blocks, blocks)] = other[...].T.reshape(
        (blocks,) + turned.shape[1:]
    )
    here = {"x": at[1], "y": at[0], "z": 2 * at[4] + at[2]}
    for start, out in zip(starts, outs):
        for k in range(2 * blocks):
            steps = (k >> 4, (k >> 2) & 3, k & 3)
            spot = {}
            for axis in "xyz":
                by = [steps[ORDER[one].index(axis)] for one in start]
                by = by[0] + at[3] * (by[-1] - by[0])
                spot[axis] = (here[axis] + by) & 3
            block = 16 * spot["y"] + 4 * spot["x"] + 2 * (spot["z"] & 1) + (spot["z"] >> 1)
            out[16 * k : 16 * (k + 1), :] = turned[block]


def turn(at, mine, other, starts, ready):
    rows, size = mine.shape
    return pl.pallas_call(
        functools.partial(turn_kernel, starts),
        out_shape=[jax.ShapeDtypeStruct((2 * size, rows), mine.dtype)] * len(starts),
        in_specs=[SCALARS, WHOLE, WHOLE] + [UNREAD] * len(ready),
        out_specs=[WHOLE] * len(starts),
        scratch_shapes=[pltpu.VMEM((2 * size // 16, 16, rows), mine.dtype)],
        compiler_params=pltpu.CompilerParams(vmem_limit_bytes=8 << 20),
        cost_estimate=LIGHT,
    )(at, mine, other, *ready)


def down_kernel(at, act, w_down, *refs):
    keep, give = refs[-2:]
    size = keep.shape[1]
    keep[...] = jnp.dot(
        act[...], half(w_down, 1, at[3], size), preferred_element_type=jnp.float32
    )
    give[...] = jnp.dot(
        act[...], half(w_down, 1, 1 - at[3], size), preferred_element_type=jnp.float32
    )


def down(at, act, w_down, ready):
    rows, size = act.shape[0], w_down.shape[1] // 2
    return pl.pallas_call(
        down_kernel,
        out_shape=[jax.ShapeDtypeStruct((rows, size), jnp.float32)] * 2,
        in_specs=[SCALARS, WHOLE, WHOLE] + [UNREAD] * len(ready),
        out_specs=[WHOLE, WHOLE],
        compiler_params=pltpu.CompilerParams(vmem_limit_bytes=14 << 20),
        cost_estimate=LIGHT,
    )(at, act, w_down, *ready)


def place_kernel(count, target, own, keep, got, *refs):
    out = refs[-1]
    slots, rows = target.shape[0], own.shape[0]
    each = rows // slots
    out_rows = (own[...].astype(jnp.float32) + keep[...] + got[...]).astype(jnp.bfloat16)
    slot = lax.broadcasted_iota(jnp.int32, (slots, slots), 0)
    before = lax.broadcasted_iota(jnp.int32, (slots, slots), 1)
    to = listed(target, 0, (slots, slots))
    same = (listed(target, 1, (1, slots)) == to) & (before < slot)
    rank = jnp.sum(same.astype(jnp.int32), axis=1, keepdims=True)
    live = slot[:, :1] < count[0]
    first = jnp.where(live, each * (4 * to[:, :1] + rank), -each)
    lane = lax.broadcasted_iota(jnp.int32, (slots, rows), 1)
    mine = (lane // each) == lax.broadcasted_iota(jnp.int32, (slots, rows), 0)
    goes = jnp.sum(jnp.where(mine, first + lane % each, 0), axis=0, keepdims=True)
    step = 256
    for at in range(0, out.shape[0], step):
        here = lax.broadcasted_iota(jnp.int32, (step, rows), 0) + at == goes
        out[at : at + step, :] = jnp.dot(
            jnp.where(here, 1.0, 0.0).astype(jnp.bfloat16),
            out_rows,
            preferred_element_type=jnp.float32,
        ).astype(jnp.bfloat16)


def place(counts, target, own, keep, got, ready):
    rows, size = own.shape
    return pl.pallas_call(
        place_kernel,
        out_shape=jax.ShapeDtypeStruct((2 * rows, size), jnp.bfloat16),
        in_specs=[SCALARS, SCALARS] + [WHOLE] * 3 + [UNREAD] * len(ready),
        out_specs=WHOLE,
        compiler_params=pltpu.CompilerParams(vmem_limit_bytes=8 << 20),
        cost_estimate=LIGHT,
    )(counts, target, own, keep, got, *ready)


def around(block, axis):
    return [block] + [shift(block, axis, 4 - by) for by in (1, 2, 3)]


def shift(block, axis, by):
    if axis == "z":
        at = [(z % 2) * 2 + z // 2 for z in range(4)]
        return lax.ppermute(block, ("zl", "zh"), [(at[z], at[(z + by) % 4]) for z in range(4)])
    return lax.ppermute(block, axis, [(k, (k + by) % 4) for k in range(4)])


def number(spot, core):
    return 8 * (4 * spot["y"] + spot["x"]) + 4 * (spot["z"] % 2) + 2 * core + spot["z"] // 2


def shift_each(block, axes, by):
    route = []
    for chip in range(64):
        spot = {"x": chip % 4, "y": chip // 4 % 4, "z": chip // 16}
        for core in range(2):
            axis = axes[core]
            there = {**spot, axis: (spot[axis] + by) % 4}
            route.append((number(spot, core), number(there, core)))
    return lax.ppermute(block, ("y", "x", "zl", "core", "zh"), route)


def fetched(sources, targets, sems):
    copies = [
        pltpu.make_async_copy(source, target, sems.at[k])
        for k, (source, target) in enumerate(zip(sources, targets))
    ]
    for copy in copies:
        copy.start()
    return copies


def product_kernel(pieces, weight, *refs):
    lefts = 1 + max(piece[0] for piece in pieces)
    rights = 1 + max(piece[1] for piece in pieces)
    count = lefts + rights
    sources, rest = refs[:count], refs[len(refs) - count - 6 :]
    outs, held, scaled, sems = rest[:4], rest[4 : 4 + count], rest[-2], rest[-1]
    copies = fetched(sources, held, sems)
    rows = weight[...]
    depth = outs[0].shape[0]
    done = 0
    seen = set()
    for left, right, first, last in pieces:
        for k in (lefts + right, left):
            if k not in seen:
                copies[k].wait()
                seen.add(k)
        for col in range(first, last, 128):
            piece = held[lefts + right][:, col : col + 128].astype(jnp.float32) * rows
            scaled[:, col - first : col - first + 128] = piece.astype(jnp.bfloat16)
        for k in range(4):
            for col in range(0, last - first, 256):
                end = min(col + 256, last - first)
                outs[k][:, done + col : done + end] = jnp.dot(
                    held[left][depth * k : depth * (k + 1), :],
                    scaled[:, col:end],
                    preferred_element_type=jnp.float32,
                ).astype(jnp.bfloat16)
        done += last - first


def products(weight, lefts, rights, pieces, ready=()):
    width = sum(last - first for _, _, first, last in pieces)
    sides = [*lefts, *rights]
    depth = weight.shape[0]
    return pl.pallas_call(
        functools.partial(product_kernel, pieces),
        out_shape=[jax.ShapeDtypeStruct((256, width), jnp.bfloat16)] * 4,
        in_specs=[WHOLE] + [UNREAD] * len(sides) + [UNREAD] * len(ready),
        out_specs=[WHOLE] * 4,
        scratch_shapes=[pltpu.VMEM(side.shape, side.dtype) for side in sides]
        + [
            pltpu.VMEM((depth, max(piece[3] - piece[2] for piece in pieces)), jnp.bfloat16),
            pltpu.SemaphoreType.DMA((len(sides),)),
        ],
        compiler_params=pltpu.CompilerParams(vmem_limit_bytes=20 << 20),
        cost_estimate=LIGHT,
    )(weight, *sides, *ready)


def sum_kernel(*refs):
    sources, outs, held, sems = refs[:8], refs[-17:-9], refs[-9:-1], refs[-1]
    copies = fetched(sources, held, sems)
    for part in range(2):
        blocks = held[4 * part : 4 * part + 4]
        for copy in copies[4 * part : 4 * part + 4]:
            copy.wait()
        rows = outs[4 * part].shape[0]
        for k in range(4):
            here = pl.ds(k * rows, rows)
            total = blocks[0][here, :].astype(jnp.float32)
            for ref in blocks[1:]:
                total = total + ref[here, :].astype(jnp.float32)
            outs[4 * part + k][...] = total.astype(jnp.bfloat16)


def sum_blocks(parts, grant, ready=()):
    blocks = [block for part in parts for block in part]
    out = pl.pallas_call(
        sum_kernel,
        out_shape=[
            jax.ShapeDtypeStruct((block.shape[0] // 4, block.shape[1]), jnp.bfloat16)
            for block in blocks
        ],
        in_specs=[UNREAD] * (8 + len(ready)),
        out_specs=[WHOLE] * 8,
        scratch_shapes=[pltpu.VMEM(block.shape, block.dtype) for block in blocks]
        + [pltpu.SemaphoreType.DMA((8,))],
        compiler_params=pltpu.CompilerParams(vmem_limit_bytes=grant),
        cost_estimate=LIGHT,
    )(*blocks, *ready)
    return [out[:4], out[4:]]


def copy_kernel(source, out):
    out[...] = source[...]


def copied(block):
    return pl.pallas_call(
        copy_kernel,
        out_shape=jax.ShapeDtypeStruct(block.shape, block.dtype),
        in_specs=[WHOLE],
        out_specs=WHOLE,
        compiler_params=pltpu.CompilerParams(vmem_limit_bytes=4 << 20),
        cost_estimate=LIGHT,
    )(block)


def last_kernel(*refs):
    down, up = refs[-2:]
    sums = []
    for part in range(2):
        total = refs[4 * part][...].astype(jnp.float32)
        for ref in refs[4 * part + 1 : 4 * part + 4]:
            total = total + ref[...].astype(jnp.float32)
        sums.append(total)
    width = down.shape[1]
    cut = sums[0].shape[1] - width
    down[...] = sums[0][:, :width]
    up[:, :cut] = sums[0][:, width:]
    up[:, cut:] = sums[1]


def last_sum(parts, ready, width):
    return pl.pallas_call(
        last_kernel,
        out_shape=[jax.ShapeDtypeStruct((16, width), jnp.float32)] * 2,
        in_specs=[WHOLE] * 8 + [UNREAD] * len(ready),
        out_specs=[WHOLE] * 2,
        compiler_params=pltpu.CompilerParams(vmem_limit_bytes=4 << 20),
        cost_estimate=LIGHT,
    )(*[block for part in parts for block in part], *ready)


def exchanged(parts, step):
    first, second = parts
    axes = (ORDER["x"][step], ORDER["y"][step])
    return [
        [first[0]] + [shift_each(first[by], axes, by) for by in (1, 3, 2)],
        [second[0]] + [shift(second[by], ORDER["z"][step], by) for by in (1, 3, 2)],
    ]


def local(
    ref_image,
    ref_text,
    learner_image,
    learner_text,
    patches,
    cotangent,
    w_up,
    w_down,
    counts,
    sel_index,
    sel_dest,
):
    core = lax.axis_index("core")
    at = jnp.stack([lax.axis_index(name) for name in ("y", "x", "zl", "core", "zh")]).astype(
        jnp.int32
    )
    slots = sel_index.shape[0]
    patch_rows, size = patches.shape[1:]
    count, width, rows = slots * patch_rows, w_up.shape[1], ref_image.shape[0]

    learner = lax.axis_index("zh") == 1
    pad = ((0, 0), (0, learner_image.shape[1] - ref_image.shape[1]))
    x_mine = patches[sel_index].reshape(count, size)
    cot_mine = cotangent[sel_index].reshape(count, size)
    learner_image, learner_text, x_mine, cot_mine = lax.optimization_barrier(
        (learner_image, learner_text, x_mine, cot_mine)
    )
    image = jnp.where(learner, learner_image, jnp.pad(ref_image, pad))
    text = jnp.where(learner, learner_text, jnp.pad(ref_text, pad))
    other_image = lax.ppermute(image, "zl", SWAP)
    x_other = lax.ppermute(x_mine, "core", SWAP)
    cot_other = lax.ppermute(cot_mine, "core", SWAP)
    texts = around(text, "y")
    joined = join_rows(texts, [other_image, x_other, cot_mine])
    texts_other = lax.ppermute(joined, "core", SWAP)
    pair = pair_rows(at, image, other_image, [joined])
    images = around(pair, "x")

    act, slope = up(at, x_mine, x_other, w_up, [pair])
    x_first, x_second = turn(at, x_mine, x_other, ("xy", "z"), [pair])

    grad_pre = back(at, cot_mine, cot_other, w_down, slope, [])

    parts = partial_losses(at, images, texts, texts_other, [x_first, grad_pre])
    keep, give = down(at, act, w_down, [parts])
    got = lax.ppermute(give, "core", SWAP)
    (cot_first,) = turn(at, cot_mine, cot_other, ("xy",), [parts])
    parts = lax.all_to_all(
        parts, ("y", "x", "zl", "core", "zh"), split_axis=0, concat_axis=0, tiled=True
    )
    scores, weight = weights(counts, sel_index, parts, [cot_first, got])
    learnability = lax.dynamic_slice_in_dim(scores[0], core * rows, rows)

    cut = 384
    second = products(weight, [x_second], [grad_pre], ((0, 0, cut, width),))
    first = products(
        weight,
        [cot_first, x_first],
        [act, grad_pre],
        ((0, 0, 0, width), (1, 1, 0, cut)),
        second[:1],
    )
    blocks = exchanged([first, second], 0)
    boxed = place(counts, sel_dest.reshape(slots), x_mine, keep, got, [first[0]])
    boxed = boxed.reshape(32, 4, patch_rows, size)
    routed = lax.all_to_all(boxed, DP, split_axis=0, concat_axis=0, tiled=True)
    routed = copied(routed.reshape(128, patch_rows, size))
    blocks = sum_blocks(blocks, 56 << 20)
    blocks = sum_blocks(exchanged(blocks, 1), 6 << 20, [routed])
    grad_down_t, grad_up = last_sum(exchanged(blocks, 2), [], width)
    return (learnability, routed, grad_up, grad_down_t)


def solution(mesh):
    mesh = Mesh(mesh.devices.reshape(4, 4, 2, 2, 2), ("y", "x", "zl", "core", "zh"))
    pairs = P(("y", "x", "zl", "core"), None)
    patch = P(DP, "zh", "core")
    return jax.shard_map(
        local,
        mesh=mesh,
        in_specs=(
            pairs,
            pairs,
            pairs,
            pairs,
            patch,
            patch,
            P(None, "core"),
            P("core", None),
            P(DP),
            P(DP),
            P(DP, None),
        ),
        out_specs=(
            P(("y", "x", "zl", "core")),
            patch,
            P(CHIPS, "core"),
            P(CHIPS, "core"),
        ),
        check_vma=False,
    )
```

```python
import functools
import math

import jax
import jax.numpy as jnp
from jax import lax
from jax.experimental import pallas as pl
from jax.experimental.pallas import tpu as pltpu
from jax.sharding import Mesh, PartitionSpec as P

DP = ("y", "x", "zl")
CHIPS = ("y", "x", "zl", "zh")
SWAP = [(0, 1), (1, 0)]
ORDER = {"x": "xyz", "y": "yzx", "z": "zxy"}
WHOLE = pl.BlockSpec(memory_space=pltpu.VMEM)
SCALARS = pl.BlockSpec(memory_space=pltpu.SMEM)
UNREAD = pl.BlockSpec(memory_space=pl.ANY)
LIGHT = pl.CostEstimate(flops=1 << 20, bytes_accessed=1 << 16, transcendentals=0)


def unit(rows):
    wide = rows.astype(jnp.float32)
    norm = lax.rsqrt(jnp.sum(wide * wide, axis=1, keepdims=True) + 1e-06)
    return (wide * norm).astype(jnp.bfloat16)


def softplus(value):
    return jnp.maximum(value, 0.0) + jnp.log1p(jnp.exp(-jnp.abs(value)))


def loss_kernel(at, *refs):
    img_refs, txt_refs, txt_other, (out, img, txt) = refs[:4], refs[4:8], refs[8], refs[-3:]
    here_y, here_x, here_zl, here_core, learner = (at[k] for k in range(5))
    for k in range(4):
        img[pl.ds(128 * k, 128), :] = unit(img_refs[k][...])
        own = pl.multiple_of(128 * k + 64 * here_core, 64)
        txt[pl.ds(own, 64), :] = unit(txt_refs[k][...])
        other = pl.multiple_of(128 * k + 64 * (1 - here_core), 64)
        txt[pl.ds(other, 64), :] = unit(txt_other[pl.ds(64 * k, 64), :])
    contract = (((1,), (1,)), ((), ()))
    col_sum = jnp.zeros((1, 512), jnp.float32)
    row_sums = []
    for k in range(4):
        scores = (
            10.0
            * lax.dot_general(
                img[pl.ds(128 * k, 128), :], txt[...], contract, preferred_element_type=jnp.float32
            )
            - 5.0
        )
        if k == 0:
            row = lax.broadcasted_iota(jnp.int32, scores.shape, 0) - 64 * here_zl
            col = lax.broadcasted_iota(jnp.int32, scores.shape, 1) - 64 * here_core
            same = (row == col) & (row >= 0) & (row < 64)
            scores = jnp.where(same, -scores, scores)
        terms = softplus(scores)
        col_sum = col_sum + jnp.sum(terms, axis=0, keepdims=True)
        folded = terms[:, :128] + terms[:, 128:256] + terms[:, 256:384] + terms[:, 384:]
        row_sums.append(jnp.sum(folded.T, axis=0, keepdims=True))
    dest = lax.broadcasted_iota(jnp.int32, (128, 128), 0)
    lane = lax.broadcasted_iota(jnp.int32, (1, 128), 1)
    dest_y, dest_x, dest_zl = dest >> 5, (dest >> 3) & 3, (dest >> 2) & 1
    own_half = (lane >> 6) == here_core
    total = jnp.zeros((128, 128), jnp.float32)
    for k in range(4):
        straight = row_sums[k]
        crossed = pltpu.roll(straight, 64, 1)
        for zl in range(2):
            placed = jnp.where(own_half, jnp.where(here_core == zl, straight, crossed), 0.0)
            mine = (dest_y == here_y) & (dest_x == ((here_x + k) & 3)) & (dest_zl == zl)
            total = total + jnp.where(mine, placed, 0.0)
        mine = (dest_y == ((here_y + k) & 3)) & (dest_x == here_x) & (dest_zl == here_zl)
        total = total + jnp.where(mine, col_sum[:, 128 * k : 128 * (k + 1)], 0.0)
    out[...] = jnp.where(learner == 1, 0.5, -0.5) * total


def partial_losses(at, images, texts, texts_other, ready):
    return pl.pallas_call(
        loss_kernel,
        out_shape=jax.ShapeDtypeStruct((128, 128), jnp.float32),
        in_specs=[SCALARS] + [WHOLE] * 9 + [UNREAD] * len(ready),
        out_specs=WHOLE,
        scratch_shapes=[pltpu.VMEM((512, 1024), jnp.bfloat16)] * 2,
        compiler_params=pltpu.CompilerParams(vmem_limit_bytes=8 << 20),
        cost_estimate=LIGHT,
    )(at, *images, *texts, texts_other, *ready)


def listed(values, axis, shape):
    at = lax.broadcasted_iota(jnp.int32, shape, axis)
    out = jnp.zeros(shape, jnp.int32)
    for k in range(shape[axis]):
        out = jnp.where(at == k, values[k], out)
    return out


def weight_kernel(count, index, parts, *refs):
    learn, weight = refs[-2:]
    score = jnp.sum(parts[...], axis=0, keepdims=True)
    learn[...] = jnp.broadcast_to(score, (8, 128))
    slots = index.shape[0]
    picked = listed(index, 0, (slots, 128)) == lax.broadcasted_iota(jnp.int32, (slots, 128), 1)
    chosen = jnp.sum(jnp.where(picked, score, 0.0), axis=1, keepdims=True)
    live = lax.broadcasted_iota(jnp.int32, (slots, 128), 0) < count[0]
    value = jnp.where(live, 1.0 / (1.0 + jnp.exp(-chosen)), 0.0)
    weight[...] = jnp.broadcast_to(value[:, None, :], (slots, 8, 128)).reshape(8 * slots, 128)


def weights(counts, index, parts, ready):
    slots = index.shape[0]
    return pl.pallas_call(
        weight_kernel,
        out_shape=(
            jax.ShapeDtypeStruct((8, 128), jnp.float32),
            jax.ShapeDtypeStruct((8 * slots, 128), jnp.float32),
        ),
        in_specs=[SCALARS, SCALARS, WHOLE] + [UNREAD] * len(ready),
        out_specs=(WHOLE, WHOLE),
        compiler_params=pltpu.CompilerParams(vmem_limit_bytes=2 << 20),
        cost_estimate=LIGHT,
    )(counts, index, parts, *ready)


def pair_kernel(at, own, other, *refs):
    pair = refs[-1]
    pair[pl.ds(pl.multiple_of(64 * at[2], 64), 64), :] = own[...]
    pair[pl.ds(pl.multiple_of(64 * (1 - at[2]), 64), 64), :] = other[...]


def pair_rows(at, own, other, ready):
    rows, width = own.shape
    return pl.pallas_call(
        pair_kernel,
        out_shape=jax.ShapeDtypeStruct((2 * rows, width), own.dtype),
        in_specs=[SCALARS, WHOLE, WHOLE] + [UNREAD] * len(ready),
        out_specs=WHOLE,
        compiler_params=pltpu.CompilerParams(vmem_limit_bytes=2 << 20),
        cost_estimate=LIGHT,
    )(at, own, other, *ready)


def join_kernel(*refs):
    out = refs[-1]
    rows = refs[0].shape[0]
    for k, block in enumerate(refs[: out.shape[0] // rows]):
        out[k * rows : (k + 1) * rows, :] = block[...]


def join_rows(blocks, ready):
    rows, width = blocks[0].shape
    return pl.pallas_call(
        join_kernel,
        out_shape=jax.ShapeDtypeStruct((len(blocks) * rows, width), blocks[0].dtype),
        in_specs=[WHOLE] * len(blocks) + [UNREAD] * len(ready),
        out_specs=WHOLE,
        compiler_params=pltpu.CompilerParams(vmem_limit_bytes=2 << 20),
        cost_estimate=LIGHT,
    )(*blocks, *ready)


def half(ref, axis, which, size):
    start = pl.multiple_of(which * size, size)
    return ref[pl.ds(start, size), :] if axis == 0 else ref[:, pl.ds(start, size)]


def up_kernel(at, mine, other, w_up, *refs):
    act, slope, held, sems = refs[-4:]
    size = mine.shape[1]
    steps, _, tile = held.shape
    columns = [pl.ds(n * tile, tile) for n in range(steps)]
    copies = fetched([w_up.at[:, cols] for cols in columns], [held.at[n] for n in range(steps)], sems)
    scale = math.sqrt(2.0 / math.pi)
    for n, cols in enumerate(columns):
        copies[n].wait()
        near, far = half(held.at[n], 0, at[3], size), half(held.at[n], 0, 1 - at[3], size)
        for row in range(0, mine.shape[0], 256):
            rows = pl.ds(row, 256)
            pre = jnp.dot(mine[rows, :], near, preferred_element_type=jnp.float32)
            pre = pre + jnp.dot(other[rows, :], far, preferred_element_type=jnp.float32)
            square = pre * pre
            tanh = jnp.tanh(pre * (scale + (scale * 0.044715) * square))
            gate = 0.5 + 0.5 * tanh
            act[rows, cols] = (pre * gate).astype(jnp.bfloat16)
            bend = pre * (0.5 - 0.5 * tanh * tanh) * (scale + (scale * 3 * 0.044715) * square)
            slope[rows, cols] = (gate + bend).astype(jnp.bfloat16)


def up(at, mine, other, w_up, ready):
    rows, size = mine.shape
    width, tile = w_up.shape[1], 512
    return pl.pallas_call(
        up_kernel,
        out_shape=[jax.ShapeDtypeStruct((rows, width), jnp.bfloat16)] * 2,
        in_specs=[SCALARS, WHOLE, WHOLE, UNREAD] + [UNREAD] * len(ready),
        out_specs=[WHOLE, WHOLE],
        scratch_shapes=[
            pltpu.VMEM((width // tile, 2 * size, tile), w_up.dtype),
            pltpu.SemaphoreType.DMA((width // tile,)),
        ],
        compiler_params=pltpu.CompilerParams(vmem_limit_bytes=16 << 20),
        cost_estimate=LIGHT,
    )(at, mine, other, w_up, *ready)


def back_kernel(at, mine, other, w_down, slope, *refs):
    out, held, sems = refs[-3:]
    size = mine.shape[1]
    steps, tile, _ = held.shape
    columns = [pl.ds(n * tile, tile) for n in range(steps)]
    copies = fetched([w_down.at[cols] for cols in columns], [held.at[n] for n in range(steps)], sems)
    contract = (((1,), (1,)), ((), ()))
    for n, cols in enumerate(columns):
        copies[n].wait()
        near, far = half(held.at[n], 1, at[3], size), half(held.at[n], 1, 1 - at[3], size)
        back = lax.dot_general(mine[...], near, contract, preferred_element_type=jnp.float32)
        back = back + lax.dot_general(other[...], far, contract, preferred_element_type=jnp.float32)
        out[:, cols] = (back * slope[:, cols].astype(jnp.float32)).astype(jnp.bfloat16)


def back(at, mine, other, w_down, slope, ready):
    rows, size = mine.shape
    width, tile = w_down.shape[0], 512
    return pl.pallas_call(
        back_kernel,
        out_shape=jax.ShapeDtypeStruct((rows, width), jnp.bfloat16),
        in_specs=[SCALARS, WHOLE, WHOLE, UNREAD, WHOLE] + [UNREAD] * len(ready),
        out_specs=WHOLE,
        scratch_shapes=[
            pltpu.VMEM((width // tile, tile, 2 * size), w_down.dtype),
            pltpu.SemaphoreType.DMA((width // tile,)),
        ],
        compiler_params=pltpu.CompilerParams(vmem_limit_bytes=14 << 20),
        cost_estimate=LIGHT,
    )(at, mine, other, w_down, slope, *ready)


def turn_kernel(starts, at, mine, other, *refs):
    outs, turned = refs[len(refs) - 1 - len(starts) : -1], refs[-1]
    blocks = turned.shape[0] // 2
    turned[pl.ds(at[3] * blocks, blocks)] = mine[...].T.reshape((blocks,) + turned.shape[1:])
    turned[pl.ds((1 - at[3]) * blocks, blocks)] = other[...].T.reshape(
        (blocks,) + turned.shape[1:]
    )
    here = {"x": at[1], "y": at[0], "z": 2 * at[4] + at[2]}
    for start, out in zip(starts, outs):
        for k in range(2 * blocks):
            steps = (k >> 4, (k >> 2) & 3, k & 3)
            spot = {}
            for axis in "xyz":
                by = [steps[ORDER[one].index(axis)] for one in start]
                by = by[0] + at[3] * (by[-1] - by[0])
                spot[axis] = (here[axis] + by) & 3
            block = 16 * spot["y"] + 4 * spot["x"] + 2 * (spot["z"] & 1) + (spot["z"] >> 1)
            out[16 * k : 16 * (k + 1), :] = turned[block]


def turn(at, mine, other, starts, ready):
    rows, size = mine.shape
    return pl.pallas_call(
        functools.partial(turn_kernel, starts),
        out_shape=[jax.ShapeDtypeStruct((2 * size, rows), mine.dtype)] * len(starts),
        in_specs=[SCALARS, WHOLE, WHOLE] + [UNREAD] * len(ready),
        out_specs=[WHOLE] * len(starts),
        scratch_shapes=[pltpu.VMEM((2 * size // 16, 16, rows), mine.dtype)],
        compiler_params=pltpu.CompilerParams(vmem_limit_bytes=8 << 20),
        cost_estimate=LIGHT,
    )(at, mine, other, *ready)


def down_kernel(at, act, w_down, *refs):
    keep, give = refs[-2:]
    size = keep.shape[1]
    keep[...] = jnp.dot(
        act[...], half(w_down, 1, at[3], size), preferred_element_type=jnp.float32
    )
    give[...] = jnp.dot(
        act[...], half(w_down, 1, 1 - at[3], size), preferred_element_type=jnp.float32
    ).astype(jnp.bfloat16)


def down(at, act, w_down, ready):
    rows, size = act.shape[0], w_down.shape[1] // 2
    return pl.pallas_call(
        down_kernel,
        out_shape=[
            jax.ShapeDtypeStruct((rows, size), jnp.float32),
            jax.ShapeDtypeStruct((rows, size), jnp.bfloat16),
        ],
        in_specs=[SCALARS, WHOLE, WHOLE] + [UNREAD] * len(ready),
        out_specs=[WHOLE, WHOLE],
        compiler_params=pltpu.CompilerParams(vmem_limit_bytes=14 << 20),
        cost_estimate=LIGHT,
    )(at, act, w_down, *ready)


def place_kernel(count, target, own, keep, got, *refs):
    out = refs[-1]
    slots, rows = target.shape[0], own.shape[0]
    each = rows // slots
    out_rows = own[...].astype(jnp.float32) + keep[...] + got[...].astype(jnp.float32)
    out_rows = out_rows.astype(jnp.bfloat16)
    slot = lax.broadcasted_iota(jnp.int32, (slots, slots), 0)
    before = lax.broadcasted_iota(jnp.int32, (slots, slots), 1)
    to = listed(target, 0, (slots, slots))
    same = (listed(target, 1, (1, slots)) == to) & (before < slot)
    rank = jnp.sum(same.astype(jnp.int32), axis=1, keepdims=True)
    live = slot[:, :1] < count[0]
    first = jnp.where(live, each * (4 * to[:, :1] + rank), -each)
    lane = lax.broadcasted_iota(jnp.int32, (slots, rows), 1)
    mine = (lane // each) == lax.broadcasted_iota(jnp.int32, (slots, rows), 0)
    goes = jnp.sum(jnp.where(mine, first + lane % each, 0), axis=0, keepdims=True)
    step = 256
    for at in range(0, out.shape[0], step):
        here = lax.broadcasted_iota(jnp.int32, (step, rows), 0) + at == goes
        out[at : at + step, :] = jnp.dot(
            jnp.where(here, 1.0, 0.0).astype(jnp.bfloat16),
            out_rows,
            preferred_element_type=jnp.float32,
        ).astype(jnp.bfloat16)


def place(counts, target, own, keep, got, ready):
    rows, size = own.shape
    return pl.pallas_call(
        place_kernel,
        out_shape=jax.ShapeDtypeStruct((2 * rows, size), jnp.bfloat16),
        in_specs=[SCALARS, SCALARS] + [WHOLE] * 3 + [UNREAD] * len(ready),
        out_specs=WHOLE,
        compiler_params=pltpu.CompilerParams(vmem_limit_bytes=8 << 20),
        cost_estimate=LIGHT,
    )(counts, target, own, keep, got, *ready)


def around(block, axis):
    return [block] + [shift(block, axis, 4 - by) for by in (1, 2, 3)]


def shift(block, axis, by):
    if axis == "z":
        at = [(z % 2) * 2 + z // 2 for z in range(4)]
        return lax.ppermute(block, ("zl", "zh"), [(at[z], at[(z + by) % 4]) for z in range(4)])
    return lax.ppermute(block, axis, [(k, (k + by) % 4) for k in range(4)])


def number(spot, core):
    return 8 * (4 * spot["y"] + spot["x"]) + 4 * (spot["z"] % 2) + 2 * core + spot["z"] // 2


def shift_each(block, axes, by):
    route = []
    for chip in range(64):
        spot = {"x": chip % 4, "y": chip // 4 % 4, "z": chip // 16}
        for core in range(2):
            axis = axes[core]
            there = {**spot, axis: (spot[axis] + by) % 4}
            route.append((number(spot, core), number(there, core)))
    return lax.ppermute(block, ("y", "x", "zl", "core", "zh"), route)


def fetched(sources, targets, sems):
    copies = [
        pltpu.make_async_copy(source, target, sems.at[k])
        for k, (source, target) in enumerate(zip(sources, targets))
    ]
    for copy in copies:
        copy.start()
    return copies


def product_kernel(pieces, weight, *refs):
    lefts = 1 + max(piece[0] for piece in pieces)
    rights = 1 + max(piece[1] for piece in pieces)
    count = lefts + rights
    sources, rest = refs[:count], refs[len(refs) - count - 6 :]
    outs, held, scaled, sems = rest[:4], rest[4 : 4 + count], rest[-2], rest[-1]
    copies = fetched(sources, held, sems)
    rows = weight[...]
    depth = outs[0].shape[0]
    done = 0
    seen = set()
    for left, right, first, last in pieces:
        for k in (lefts + right, left):
            if k not in seen:
                copies[k].wait()
                seen.add(k)
        for col in range(first, last, 128):
            piece = held[lefts + right][:, col : col + 128].astype(jnp.float32) * rows
            scaled[:, col - first : col - first + 128] = piece.astype(jnp.bfloat16)
        for k in range(4):
            for col in range(0, last - first, 256):
                end = min(col + 256, last - first)
                outs[k][:, done + col : done + end] = jnp.dot(
                    held[left][depth * k : depth * (k + 1), :],
                    scaled[:, col:end],
                    preferred_element_type=jnp.float32,
                ).astype(jnp.bfloat16)
        done += last - first


def products(weight, lefts, rights, pieces, ready=()):
    width = sum(last - first for _, _, first, last in pieces)
    sides = [*lefts, *rights]
    depth = weight.shape[0]
    return pl.pallas_call(
        functools.partial(product_kernel, pieces),
        out_shape=[jax.ShapeDtypeStruct((256, width), jnp.bfloat16)] * 4,
        in_specs=[WHOLE] + [UNREAD] * len(sides) + [UNREAD] * len(ready),
        out_specs=[WHOLE] * 4,
        scratch_shapes=[pltpu.VMEM(side.shape, side.dtype) for side in sides]
        + [
            pltpu.VMEM((depth, max(piece[3] - piece[2] for piece in pieces)), jnp.bfloat16),
            pltpu.SemaphoreType.DMA((len(sides),)),
        ],
        compiler_params=pltpu.CompilerParams(vmem_limit_bytes=20 << 20),
        cost_estimate=LIGHT,
    )(weight, *sides, *ready)


def sum_kernel(*refs):
    sources, outs, held, sems = refs[:8], refs[-17:-9], refs[-9:-1], refs[-1]
    copies = fetched(sources, held, sems)
    for part in range(2):
        blocks = held[4 * part : 4 * part + 4]
        for copy in copies[4 * part : 4 * part + 4]:
            copy.wait()
        rows = outs[4 * part].shape[0]
        for k in range(4):
            here = pl.ds(k * rows, rows)
            total = blocks[0][here, :].astype(jnp.float32)
            for ref in blocks[1:]:
                total = total + ref[here, :].astype(jnp.float32)
            outs[4 * part + k][...] = total.astype(jnp.bfloat16)


def sum_blocks(parts, grant, ready=()):
    blocks = [block for part in parts for block in part]
    out = pl.pallas_call(
        sum_kernel,
        out_shape=[
            jax.ShapeDtypeStruct((block.shape[0] // 4, block.shape[1]), jnp.bfloat16)
            for block in blocks
        ],
        in_specs=[UNREAD] * (8 + len(ready)),
        out_specs=[WHOLE] * 8,
        scratch_shapes=[pltpu.VMEM(block.shape, block.dtype) for block in blocks]
        + [pltpu.SemaphoreType.DMA((8,))],
        compiler_params=pltpu.CompilerParams(vmem_limit_bytes=grant),
        cost_estimate=LIGHT,
    )(*blocks, *ready)
    return [out[:4], out[4:]]


def copy_kernel(source, out):
    out[...] = source[...]


def copied(block):
    return pl.pallas_call(
        copy_kernel,
        out_shape=jax.ShapeDtypeStruct(block.shape, block.dtype),
        in_specs=[WHOLE],
        out_specs=WHOLE,
        compiler_params=pltpu.CompilerParams(vmem_limit_bytes=4 << 20),
        cost_estimate=LIGHT,
    )(block)


def last_kernel(*refs):
    down, up = refs[-2:]
    sums = []
    for part in range(2):
        total = refs[4 * part][...].astype(jnp.float32)
        for ref in refs[4 * part + 1 : 4 * part + 4]:
            total = total + ref[...].astype(jnp.float32)
        sums.append(total)
    width = down.shape[1]
    cut = sums[0].shape[1] - width
    down[...] = sums[0][:, :width]
    up[:, :cut] = sums[0][:, width:]
    up[:, cut:] = sums[1]


def last_sum(parts, ready, width):
    return pl.pallas_call(
        last_kernel,
        out_shape=[jax.ShapeDtypeStruct((16, width), jnp.float32)] * 2,
        in_specs=[WHOLE] * 8 + [UNREAD] * len(ready),
        out_specs=[WHOLE] * 2,
        compiler_params=pltpu.CompilerParams(vmem_limit_bytes=4 << 20),
        cost_estimate=LIGHT,
    )(*[block for part in parts for block in part], *ready)


def exchanged(parts, step):
    first, second = parts
    axes = (ORDER["x"][step], ORDER["y"][step])
    return [
        [first[0]] + [shift_each(first[by], axes, by) for by in (2, 1, 3)],
        [second[0]] + [shift(second[by], ORDER["z"][step], by) for by in (2, 1, 3)],
    ]


def local(
    ref_image,
    ref_text,
    learner_image,
    learner_text,
    patches,
    cotangent,
    w_up,
    w_down,
    counts,
    sel_index,
    sel_dest,
):
    core = lax.axis_index("core")
    at = jnp.stack([lax.axis_index(name) for name in ("y", "x", "zl", "core", "zh")]).astype(
        jnp.int32
    )
    slots = sel_index.shape[0]
    patch_rows, size = patches.shape[1:]
    count, width, rows = slots * patch_rows, w_up.shape[1], ref_image.shape[0]

    learner = lax.axis_index("zh") == 1
    pad = ((0, 0), (0, learner_image.shape[1] - ref_image.shape[1]))
    x_mine = patches[sel_index].reshape(count, size)
    cot_mine = cotangent[sel_index].reshape(count, size)
    learner_image, learner_text, x_mine, cot_mine = lax.optimization_barrier(
        (learner_image, learner_text, x_mine, cot_mine)
    )
    image = jnp.where(learner, learner_image, jnp.pad(ref_image, pad))
    text = jnp.where(learner, learner_text, jnp.pad(ref_text, pad))
    other_image = lax.ppermute(image, "zl", SWAP)
    x_other = lax.ppermute(x_mine, "core", SWAP)
    cot_other = lax.ppermute(cot_mine, "core", SWAP)
    texts = around(text, "y")
    joined = join_rows(texts, [other_image, x_other, cot_mine])
    texts_other = lax.ppermute(joined, "core", SWAP)
    pair = pair_rows(at, image, other_image, [joined])
    images = around(pair, "x")

    act, slope = up(at, x_mine, x_other, w_up, [pair])
    x_first, x_second = turn(at, x_mine, x_other, ("xy", "z"), [pair])

    grad_pre = back(at, cot_mine, cot_other, w_down, slope, [])
    (cot_first,) = turn(at, cot_mine, cot_other, ("xy",), [])

    parts = partial_losses(at, images, texts, texts_other, [x_first, grad_pre, cot_first])
    parts = lax.all_to_all(
        parts, ("y", "x", "zl", "core", "zh"), split_axis=0, concat_axis=0, tiled=True
    )
    scores, weight = weights(counts, sel_index, parts, [])
    learnability = lax.dynamic_slice_in_dim(scores[0], core * rows, rows)

    cut = 384
    second = products(weight, [x_second], [grad_pre], ((0, 0, cut, width),))
    first = products(
        weight,
        [cot_first, x_first],
        [act, grad_pre],
        ((0, 0, 0, width), (1, 1, 0, cut)),
        second[:1],
    )
    blocks = exchanged([first, second], 0)
    keep, give = down(at, act, w_down, [first[0], second[0]])
    got = lax.ppermute(give, "core", SWAP)
    boxed = place(counts, sel_dest.reshape(slots), x_mine, keep, got, [blocks[1][1]])
    boxed = boxed.reshape(32, 4, patch_rows, size)
    routed = lax.all_to_all(boxed, DP, split_axis=0, concat_axis=0, tiled=True)
    routed = copied(routed.reshape(128, patch_rows, size))
    blocks = sum_blocks(blocks, 56 << 20)
    blocks = sum_blocks(exchanged(blocks, 1), 6 << 20, [routed])
    grad_down_t, grad_up = last_sum(exchanged(blocks, 2), [], width)
    return (learnability, routed, grad_up, grad_down_t)


def solution(mesh):
    mesh = Mesh(mesh.devices.reshape(4, 4, 2, 2, 2), ("y", "x", "zl", "core", "zh"))
    pairs = P(("y", "x", "zl", "core"), None)
    patch = P(DP, "zh", "core")
    return jax.shard_map(
        local,
        mesh=mesh,
        in_specs=(
            pairs,
            pairs,
            pairs,
            pairs,
            patch,
            patch,
            P(None, "core"),
            P("core", None),
            P(DP),
            P(DP),
            P(DP, None),
        ),
        out_specs=(
            P(("y", "x", "zl", "core")),
            patch,
            P(CHIPS, "core"),
            P(CHIPS, "core"),
        ),
        check_vma=False,
    )
```

```python
import functools
import math

import jax
import jax.numpy as jnp
from jax import lax
from jax.experimental import pallas as pl
from jax.experimental.pallas import tpu as pltpu
from jax.sharding import Mesh, PartitionSpec as P

DP = ("y", "x", "zl")
CHIPS = ("y", "x", "zl", "zh")
SWAP = [(0, 1), (1, 0)]
ORDER = {"x": "xyz", "y": "yzx", "z": "zxy"}
WHOLE = pl.BlockSpec(memory_space=pltpu.VMEM)
SCALARS = pl.BlockSpec(memory_space=pltpu.SMEM)
UNREAD = pl.BlockSpec(memory_space=pl.ANY)
LIGHT = pl.CostEstimate(flops=1 << 20, bytes_accessed=1 << 16, transcendentals=0)


def unit(rows):
    wide = rows.astype(jnp.float32)
    norm = lax.rsqrt(jnp.sum(wide * wide, axis=1, keepdims=True) + 1e-06)
    return (wide * norm).astype(jnp.bfloat16)


def softplus(value):
    return jnp.maximum(value, 0.0) + jnp.log1p(jnp.exp(-jnp.abs(value)))


def loss_kernel(at, *refs):
    img_refs, txt_refs, txt_other, (out, img, txt) = refs[:4], refs[4:8], refs[8], refs[-3:]
    here_y, here_x, here_zl, here_core, learner = (at[k] for k in range(5))
    for k in range(4):
        img[pl.ds(128 * k, 128), :] = unit(img_refs[k][...])
        own = pl.multiple_of(128 * k + 64 * here_core, 64)
        txt[pl.ds(own, 64), :] = unit(txt_refs[k][...])
        other = pl.multiple_of(128 * k + 64 * (1 - here_core), 64)
        txt[pl.ds(other, 64), :] = unit(txt_other[pl.ds(64 * k, 64), :])
    contract = (((1,), (1,)), ((), ()))
    col_sum = jnp.zeros((1, 512), jnp.float32)
    row_sums = []
    for k in range(4):
        scores = (
            10.0
            * lax.dot_general(
                img[pl.ds(128 * k, 128), :], txt[...], contract, preferred_element_type=jnp.float32
            )
            - 5.0
        )
        if k == 0:
            row = lax.broadcasted_iota(jnp.int32, scores.shape, 0) - 64 * here_zl
            col = lax.broadcasted_iota(jnp.int32, scores.shape, 1) - 64 * here_core
            same = (row == col) & (row >= 0) & (row < 64)
            scores = jnp.where(same, -scores, scores)
        terms = softplus(scores)
        col_sum = col_sum + jnp.sum(terms, axis=0, keepdims=True)
        folded = terms[:, :128] + terms[:, 128:256] + terms[:, 256:384] + terms[:, 384:]
        row_sums.append(jnp.sum(folded.T, axis=0, keepdims=True))
    dest = lax.broadcasted_iota(jnp.int32, (128, 128), 0)
    lane = lax.broadcasted_iota(jnp.int32, (1, 128), 1)
    dest_y, dest_x, dest_zl = dest >> 5, (dest >> 3) & 3, (dest >> 2) & 1
    own_half = (lane >> 6) == here_core
    total = jnp.zeros((128, 128), jnp.float32)
    for k in range(4):
        straight = row_sums[k]
        crossed = pltpu.roll(straight, 64, 1)
        for zl in range(2):
            placed = jnp.where(own_half, jnp.where(here_core == zl, straight, crossed), 0.0)
            mine = (dest_y == here_y) & (dest_x == ((here_x + k) & 3)) & (dest_zl == zl)
            total = total + jnp.where(mine, placed, 0.0)
        mine = (dest_y == ((here_y + k) & 3)) & (dest_x == here_x) & (dest_zl == here_zl)
        total = total + jnp.where(mine, col_sum[:, 128 * k : 128 * (k + 1)], 0.0)
    out[...] = jnp.where(learner == 1, 0.5, -0.5) * total


def partial_losses(at, images, texts, texts_other, ready):
    return pl.pallas_call(
        loss_kernel,
        out_shape=jax.ShapeDtypeStruct((128, 128), jnp.float32),
        in_specs=[SCALARS] + [WHOLE] * 9 + [UNREAD] * len(ready),
        out_specs=WHOLE,
        scratch_shapes=[pltpu.VMEM((512, 1024), jnp.bfloat16)] * 2,
        compiler_params=pltpu.CompilerParams(vmem_limit_bytes=8 << 20),
        cost_estimate=LIGHT,
    )(at, *images, *texts, texts_other, *ready)


def listed(values, axis, shape):
    at = lax.broadcasted_iota(jnp.int32, shape, axis)
    out = jnp.zeros(shape, jnp.int32)
    for k in range(shape[axis]):
        out = jnp.where(at == k, values[k], out)
    return out


def weight_kernel(count, index, parts, *refs):
    learn, weight = refs[-2:]
    score = jnp.sum(parts[...], axis=0, keepdims=True)
    learn[...] = jnp.broadcast_to(score, (8, 128))
    slots = index.shape[0]
    picked = listed(index, 0, (slots, 128)) == lax.broadcasted_iota(jnp.int32, (slots, 128), 1)
    chosen = jnp.sum(jnp.where(picked, score, 0.0), axis=1, keepdims=True)
    live = lax.broadcasted_iota(jnp.int32, (slots, 128), 0) < count[0]
    value = jnp.where(live, 1.0 / (1.0 + jnp.exp(-chosen)), 0.0)
    weight[...] = jnp.broadcast_to(value[:, None, :], (slots, 8, 128)).reshape(8 * slots, 128)


def weights(counts, index, parts, ready):
    slots = index.shape[0]
    return pl.pallas_call(
        weight_kernel,
        out_shape=(
            jax.ShapeDtypeStruct((8, 128), jnp.float32),
            jax.ShapeDtypeStruct((8 * slots, 128), jnp.float32),
        ),
        in_specs=[SCALARS, SCALARS, WHOLE] + [UNREAD] * len(ready),
        out_specs=(WHOLE, WHOLE),
        compiler_params=pltpu.CompilerParams(vmem_limit_bytes=2 << 20),
        cost_estimate=LIGHT,
    )(counts, index, parts, *ready)


def pair_kernel(at, own, other, *refs):
    pair = refs[-1]
    pair[pl.ds(pl.multiple_of(64 * at[2], 64), 64), :] = own[...]
    pair[pl.ds(pl.multiple_of(64 * (1 - at[2]), 64), 64), :] = other[...]


def pair_rows(at, own, other, ready):
    rows, width = own.shape
    return pl.pallas_call(
        pair_kernel,
        out_shape=jax.ShapeDtypeStruct((2 * rows, width), own.dtype),
        in_specs=[SCALARS, WHOLE, WHOLE] + [UNREAD] * len(ready),
        out_specs=WHOLE,
        compiler_params=pltpu.CompilerParams(vmem_limit_bytes=2 << 20),
        cost_estimate=LIGHT,
    )(at, own, other, *ready)


def join_kernel(*refs):
    out = refs[-1]
    rows = refs[0].shape[0]
    for k, block in enumerate(refs[: out.shape[0] // rows]):
        out[k * rows : (k + 1) * rows, :] = block[...]


def join_rows(blocks, ready):
    rows, width = blocks[0].shape
    return pl.pallas_call(
        join_kernel,
        out_shape=jax.ShapeDtypeStruct((len(blocks) * rows, width), blocks[0].dtype),
        in_specs=[WHOLE] * len(blocks) + [UNREAD] * len(ready),
        out_specs=WHOLE,
        compiler_params=pltpu.CompilerParams(vmem_limit_bytes=2 << 20),
        cost_estimate=LIGHT,
    )(*blocks, *ready)


def half(ref, axis, which, size):
    start = pl.multiple_of(which * size, size)
    return ref[pl.ds(start, size), :] if axis == 0 else ref[:, pl.ds(start, size)]


def up_kernel(at, mine, other, w_up, *refs):
    act, slope, held, sems = refs[-4:]
    size = mine.shape[1]
    steps, _, tile = held.shape
    columns = [pl.ds(n * tile, tile) for n in range(steps)]
    copies = fetched([w_up.at[:, cols] for cols in columns], [held.at[n] for n in range(steps)], sems)
    scale = math.sqrt(2.0 / math.pi)
    for n, cols in enumerate(columns):
        copies[n].wait()
        near, far = half(held.at[n], 0, at[3], size), half(held.at[n], 0, 1 - at[3], size)
        for row in range(0, mine.shape[0], 256):
            rows = pl.ds(row, 256)
            pre = jnp.dot(mine[rows, :], near, preferred_element_type=jnp.float32)
            pre = pre + jnp.dot(other[rows, :], far, preferred_element_type=jnp.float32)
            square = pre * pre
            tanh = jnp.tanh(pre * (scale + (scale * 0.044715) * square))
            gate = 0.5 + 0.5 * tanh
            value = pre * gate
            act[rows, cols] = value.astype(jnp.bfloat16)
            bend = value * (1.0 - gate) * (2 * scale + (6 * scale * 0.044715) * square)
            slope[rows, cols] = (gate + bend).astype(jnp.bfloat16)


def up(at, mine, other, w_up, ready):
    rows, size = mine.shape
    width, tile = w_up.shape[1], 512
    return pl.pallas_call(
        up_kernel,
        out_shape=[jax.ShapeDtypeStruct((rows, width), jnp.bfloat16)] * 2,
        in_specs=[SCALARS, WHOLE, WHOLE, UNREAD] + [UNREAD] * len(ready),
        out_specs=[WHOLE, WHOLE],
        scratch_shapes=[
            pltpu.VMEM((width // tile, 2 * size, tile), w_up.dtype),
            pltpu.SemaphoreType.DMA((width // tile,)),
        ],
        compiler_params=pltpu.CompilerParams(vmem_limit_bytes=16 << 20),
        cost_estimate=LIGHT,
    )(at, mine, other, w_up, *ready)


def back_kernel(at, mine, other, w_down, slope, *refs):
    out, held, sems = refs[-3:]
    size = mine.shape[1]
    steps, tile, _ = held.shape
    columns = [pl.ds(n * tile, tile) for n in range(steps)]
    copies = fetched([w_down.at[cols] for cols in columns], [held.at[n] for n in range(steps)], sems)
    contract = (((1,), (1,)), ((), ()))
    for n, cols in enumerate(columns):
        copies[n].wait()
        near, far = half(held.at[n], 1, at[3], size), half(held.at[n], 1, 1 - at[3], size)
        back = lax.dot_general(mine[...], near, contract, preferred_element_type=jnp.float32)
        back = back + lax.dot_general(other[...], far, contract, preferred_element_type=jnp.float32)
        out[:, cols] = (back * slope[:, cols].astype(jnp.float32)).astype(jnp.bfloat16)


def back(at, mine, other, w_down, slope, ready):
    rows, size = mine.shape
    width, tile = w_down.shape[0], 512
    return pl.pallas_call(
        back_kernel,
        out_shape=jax.ShapeDtypeStruct((rows, width), jnp.bfloat16),
        in_specs=[SCALARS, WHOLE, WHOLE, UNREAD, WHOLE] + [UNREAD] * len(ready),
        out_specs=WHOLE,
        scratch_shapes=[
            pltpu.VMEM((width // tile, tile, 2 * size), w_down.dtype),
            pltpu.SemaphoreType.DMA((width // tile,)),
        ],
        compiler_params=pltpu.CompilerParams(vmem_limit_bytes=14 << 20),
        cost_estimate=LIGHT,
    )(at, mine, other, w_down, slope, *ready)


def turn_kernel(starts, at, mine, other, *refs):
    outs, turned = refs[len(refs) - 1 - len(starts) : -1], refs[-1]
    blocks = turned.shape[0] // 2
    turned[pl.ds(at[3] * blocks, blocks)] = mine[...].T.reshape((blocks,) + turned.shape[1:])
    turned[pl.ds((1 - at[3]) * blocks, blocks)] = other[...].T.reshape(
        (blocks,) + turned.shape[1:]
    )
    here = {"x": at[1], "y": at[0], "z": 2 * at[4] + at[2]}
    for start, out in zip(starts, outs):
        for k in range(2 * blocks):
            steps = (k >> 4, (k >> 2) & 3, k & 3)
            spot = {}
            for axis in "xyz":
                by = [steps[ORDER[one].index(axis)] for one in start]
                by = by[0] + at[3] * (by[-1] - by[0])
                spot[axis] = (here[axis] + by) & 3
            block = 16 * spot["y"] + 4 * spot["x"] + 2 * (spot["z"] & 1) + (spot["z"] >> 1)
            out[16 * k : 16 * (k + 1), :] = turned[block]


def turn(at, mine, other, starts, ready):
    rows, size = mine.shape
    return pl.pallas_call(
        functools.partial(turn_kernel, starts),
        out_shape=[jax.ShapeDtypeStruct((2 * size, rows), mine.dtype)] * len(starts),
        in_specs=[SCALARS, WHOLE, WHOLE] + [UNREAD] * len(ready),
        out_specs=[WHOLE] * len(starts),
        scratch_shapes=[pltpu.VMEM((2 * size // 16, 16, rows), mine.dtype)],
        compiler_params=pltpu.CompilerParams(vmem_limit_bytes=8 << 20),
        cost_estimate=LIGHT,
    )(at, mine, other, *ready)


def down_kernel(at, act, w_down, *refs):
    keep, give = refs[-2:]
    size = keep.shape[1]
    keep[...] = jnp.dot(
        act[...], half(w_down, 1, at[3], size), preferred_element_type=jnp.float32
    )
    give[...] = jnp.dot(
        act[...], half(w_down, 1, 1 - at[3], size), preferred_element_type=jnp.float32
    ).astype(jnp.bfloat16)


def down(at, act, w_down, ready):
    rows, size = act.shape[0], w_down.shape[1] // 2
    return pl.pallas_call(
        down_kernel,
        out_shape=[
            jax.ShapeDtypeStruct((rows, size), jnp.float32),
            jax.ShapeDtypeStruct((rows, size), jnp.bfloat16),
        ],
        in_specs=[SCALARS, WHOLE, WHOLE] + [UNREAD] * len(ready),
        out_specs=[WHOLE, WHOLE],
        compiler_params=pltpu.CompilerParams(vmem_limit_bytes=14 << 20),
        cost_estimate=LIGHT,
    )(at, act, w_down, *ready)


def place_kernel(count, target, own, keep, got, *refs):
    out = refs[-1]
    slots, rows = target.shape[0], own.shape[0]
    each = rows // slots
    out_rows = own[...].astype(jnp.float32) + keep[...] + got[...].astype(jnp.float32)
    out_rows = out_rows.astype(jnp.bfloat16)
    slot = lax.broadcasted_iota(jnp.int32, (slots, slots), 0)
    before = lax.broadcasted_iota(jnp.int32, (slots, slots), 1)
    to = listed(target, 0, (slots, slots))
    same = (listed(target, 1, (1, slots)) == to) & (before < slot)
    rank = jnp.sum(same.astype(jnp.int32), axis=1, keepdims=True)
    live = slot[:, :1] < count[0]
    first = jnp.where(live, each * (4 * to[:, :1] + rank), -each)
    lane = lax.broadcasted_iota(jnp.int32, (slots, rows), 1)
    mine = (lane // each) == lax.broadcasted_iota(jnp.int32, (slots, rows), 0)
    goes = jnp.sum(jnp.where(mine, first + lane % each, 0), axis=0, keepdims=True)
    step = 256
    for at in range(0, out.shape[0], step):
        here = lax.broadcasted_iota(jnp.int32, (step, rows), 0) + at == goes
        out[at : at + step, :] = jnp.dot(
            jnp.where(here, 1.0, 0.0).astype(jnp.bfloat16),
            out_rows,
            preferred_element_type=jnp.float32,
        ).astype(jnp.bfloat16)


def place(counts, target, own, keep, got, ready):
    rows, size = own.shape
    return pl.pallas_call(
        place_kernel,
        out_shape=jax.ShapeDtypeStruct((2 * rows, size), jnp.bfloat16),
        in_specs=[SCALARS, SCALARS] + [WHOLE] * 3 + [UNREAD] * len(ready),
        out_specs=WHOLE,
        compiler_params=pltpu.CompilerParams(vmem_limit_bytes=8 << 20),
        cost_estimate=LIGHT,
    )(counts, target, own, keep, got, *ready)


def around(block, axis):
    return [block] + [shift(block, axis, 4 - by) for by in (1, 2, 3)]


def shift(block, axis, by):
    if axis == "z":
        at = [(z % 2) * 2 + z // 2 for z in range(4)]
        return lax.ppermute(block, ("zl", "zh"), [(at[z], at[(z + by) % 4]) for z in range(4)])
    return lax.ppermute(block, axis, [(k, (k + by) % 4) for k in range(4)])


def number(spot, core):
    return 8 * (4 * spot["y"] + spot["x"]) + 4 * (spot["z"] % 2) + 2 * core + spot["z"] // 2


def shift_each(block, axes, by):
    route = []
    for chip in range(64):
        spot = {"x": chip % 4, "y": chip // 4 % 4, "z": chip // 16}
        for core in range(2):
            axis = axes[core]
            there = {**spot, axis: (spot[axis] + by) % 4}
            route.append((number(spot, core), number(there, core)))
    return lax.ppermute(block, ("y", "x", "zl", "core", "zh"), route)


def fetched(sources, targets, sems):
    copies = [
        pltpu.make_async_copy(source, target, sems.at[k])
        for k, (source, target) in enumerate(zip(sources, targets))
    ]
    for copy in copies:
        copy.start()
    return copies


def product_kernel(pieces, weight, *refs):
    lefts = 1 + max(piece[0] for piece in pieces)
    rights = 1 + max(piece[1] for piece in pieces)
    count = lefts + rights
    sources, rest = refs[:count], refs[len(refs) - count - 6 :]
    outs, held, scaled, sems = rest[:4], rest[4 : 4 + count], rest[-2], rest[-1]
    copies = fetched(sources, held, sems)
    rows = weight[...]
    depth = outs[0].shape[0]
    done = 0
    seen = set()
    for left, right, first, last in pieces:
        for k in (lefts + right, left):
            if k not in seen:
                copies[k].wait()
                seen.add(k)
        for col in range(first, last, 128):
            piece = held[lefts + right][:, col : col + 128].astype(jnp.float32) * rows
            scaled[:, col - first : col - first + 128] = piece.astype(jnp.bfloat16)
        for col in range(0, last - first, 256):
            end = min(col + 256, last - first)
            product = jnp.dot(held[left][...], scaled[:, col:end], preferred_element_type=jnp.float32)
            for k in range(4):
                outs[k][:, done + col : done + end] = product[depth * k : depth * (k + 1)].astype(
                    jnp.bfloat16
                )
        done += last - first


def products(weight, lefts, rights, pieces, ready=()):
    width = sum(last - first for _, _, first, last in pieces)
    sides = [*lefts, *rights]
    depth = weight.shape[0]
    return pl.pallas_call(
        functools.partial(product_kernel, pieces),
        out_shape=[jax.ShapeDtypeStruct((256, width), jnp.bfloat16)] * 4,
        in_specs=[WHOLE] + [UNREAD] * len(sides) + [UNREAD] * len(ready),
        out_specs=[WHOLE] * 4,
        scratch_shapes=[pltpu.VMEM(side.shape, side.dtype) for side in sides]
        + [
            pltpu.VMEM((depth, max(piece[3] - piece[2] for piece in pieces)), jnp.bfloat16),
            pltpu.SemaphoreType.DMA((len(sides),)),
        ],
        compiler_params=pltpu.CompilerParams(vmem_limit_bytes=20 << 20),
        cost_estimate=LIGHT,
    )(weight, *sides, *ready)


def sum_kernel(*refs):
    sources, outs, held, sems = refs[:4], refs[-9:-5], refs[-5:-1], refs[-1]
    copies = fetched(sources, held, sems)
    for copy in copies:
        copy.wait()
    rows = outs[0].shape[0]
    for k in range(4):
        here = pl.ds(k * rows, rows)
        total = held[0][here, :].astype(jnp.float32)
        for ref in held[1:]:
            total = total + ref[here, :].astype(jnp.float32)
        outs[k][...] = total.astype(jnp.bfloat16)


def sum_blocks(blocks, grant, ready=()):
    rows, width = blocks[0].shape
    return pl.pallas_call(
        sum_kernel,
        out_shape=[jax.ShapeDtypeStruct((rows // 4, width), jnp.bfloat16)] * 4,
        in_specs=[UNREAD] * (4 + len(ready)),
        out_specs=[WHOLE] * 4,
        scratch_shapes=[pltpu.VMEM(block.shape, block.dtype) for block in blocks]
        + [pltpu.SemaphoreType.DMA((4,))],
        compiler_params=pltpu.CompilerParams(vmem_limit_bytes=grant),
        cost_estimate=LIGHT,
    )(*blocks, *ready)


def copy_kernel(source, out):
    out[...] = source[...]


def copied(block):
    return pl.pallas_call(
        copy_kernel,
        out_shape=jax.ShapeDtypeStruct(block.shape, block.dtype),
        in_specs=[WHOLE],
        out_specs=WHOLE,
        compiler_params=pltpu.CompilerParams(vmem_limit_bytes=56 << 20),
        cost_estimate=LIGHT,
    )(block)


def last_kernel(*refs):
    down, up = refs[-2:]
    sums = []
    for part in range(2):
        total = refs[4 * part][...].astype(jnp.float32)
        for ref in refs[4 * part + 1 : 4 * part + 4]:
            total = total + ref[...].astype(jnp.float32)
        sums.append(total)
    width = down.shape[1]
    cut = sums[0].shape[1] - width
    down[...] = sums[0][:, :width]
    up[:, :cut] = sums[0][:, width:]
    up[:, cut:] = sums[1]


def last_sum(parts, ready, width):
    return pl.pallas_call(
        last_kernel,
        out_shape=[jax.ShapeDtypeStruct((16, width), jnp.float32)] * 2,
        in_specs=[WHOLE] * 8 + [UNREAD] * len(ready),
        out_specs=[WHOLE] * 2,
        compiler_params=pltpu.CompilerParams(vmem_limit_bytes=4 << 20),
        cost_estimate=LIGHT,
    )(*[block for part in parts for block in part], *ready)


def exchanged(parts, step):
    first, second = parts
    axes = (ORDER["x"][step], ORDER["y"][step])
    return [
        [first[0]] + [shift_each(first[by], axes, by) for by in (2, 1, 3)],
        [second[0]] + [shift(second[by], ORDER["z"][step], by) for by in (2, 1, 3)],
    ]


def local(
    ref_image,
    ref_text,
    learner_image,
    learner_text,
    patches,
    cotangent,
    w_up,
    w_down,
    counts,
    sel_index,
    sel_dest,
):
    core = lax.axis_index("core")
    at = jnp.stack([lax.axis_index(name) for name in ("y", "x", "zl", "core", "zh")]).astype(
        jnp.int32
    )
    slots = sel_index.shape[0]
    patch_rows, size = patches.shape[1:]
    count, width, rows = slots * patch_rows, w_up.shape[1], ref_image.shape[0]

    learner = lax.axis_index("zh") == 1
    pad = ((0, 0), (0, learner_image.shape[1] - ref_image.shape[1]))
    x_mine = patches[sel_index].reshape(count, size)
    cot_mine = cotangent[sel_index].reshape(count, size)
    learner_image, learner_text, x_mine, cot_mine = lax.optimization_barrier(
        (learner_image, learner_text, x_mine, cot_mine)
    )
    image = jnp.where(learner, learner_image, jnp.pad(ref_image, pad))
    text = jnp.where(learner, learner_text, jnp.pad(ref_text, pad))
    other_image = lax.ppermute(image, "zl", SWAP)
    x_other = lax.ppermute(x_mine, "core", SWAP)
    cot_other = lax.ppermute(cot_mine, "core", SWAP)
    texts = around(text, "y")
    joined = join_rows(texts, [other_image, x_other, cot_mine])
    texts_other = lax.ppermute(joined, "core", SWAP)
    pair = pair_rows(at, image, other_image, [joined])
    images = around(pair, "x")

    act, slope = up(at, x_mine, x_other, w_up, [pair])
    x_first, x_second = turn(at, x_mine, x_other, ("xy", "z"), [pair])

    grad_pre = back(at, cot_mine, cot_other, w_down, slope, [])
    (cot_first,) = turn(at, cot_mine, cot_other, ("xy",), [])

    parts = partial_losses(at, images, texts, texts_other, [x_first, grad_pre, cot_first])
    parts = lax.all_to_all(
        parts, ("y", "x", "zl", "core", "zh"), split_axis=0, concat_axis=0, tiled=True
    )
    scores, weight = weights(counts, sel_index, parts, [])
    learnability = lax.dynamic_slice_in_dim(scores[0], core * rows, rows)

    cut = 384
    second = products(weight, [x_second], [grad_pre], ((0, 0, cut, width),))
    first = products(
        weight,
        [cot_first, x_first],
        [act, grad_pre],
        ((0, 0, 0, width), (1, 1, 0, cut)),
        second[:1],
    )
    blocks = exchanged([first, second], 0)
    keep, give = down(at, act, w_down, [first[0], second[0]])
    got = lax.ppermute(give, "core", SWAP)
    boxed = place(counts, sel_dest.reshape(slots), x_mine, keep, got, [blocks[1][1]])
    boxed = boxed.reshape(32, 4, patch_rows, size)
    routed = lax.all_to_all(boxed, DP, split_axis=0, concat_axis=0, tiled=True)
    routed = copied(routed.reshape(128, patch_rows, size))
    blocks = [sum_blocks(part, 56 << 20) for part in blocks]
    blocks = [sum_blocks(part, 6 << 20) for part in exchanged(blocks, 1)]
    grad_down_t, grad_up = last_sum(exchanged(blocks, 2), [routed], width)
    return (learnability, routed, grad_up, grad_down_t)


def solution(mesh):
    mesh = Mesh(mesh.devices.reshape(4, 4, 2, 2, 2), ("y", "x", "zl", "core", "zh"))
    pairs = P(("y", "x", "zl", "core"), None)
    patch = P(DP, "zh", "core")
    return jax.shard_map(
        local,
        mesh=mesh,
        in_specs=(
            pairs,
            pairs,
            pairs,
            pairs,
            patch,
            patch,
            P(None, "core"),
            P("core", None),
            P(DP),
            P(DP),
            P(DP, None),
        ),
        out_specs=(
            P(("y", "x", "zl", "core")),
            patch,
            P(CHIPS, "core"),
            P(CHIPS, "core"),
        ),
        check_vma=False,
    )
```

```python
import functools
import math

import jax
import jax.numpy as jnp
from jax import lax
from jax.experimental import pallas as pl
from jax.experimental.pallas import tpu as pltpu
from jax.sharding import Mesh, PartitionSpec as P

DP = ("y", "x", "zl")
CHIPS = ("y", "x", "zl", "zh")
SWAP = [(0, 1), (1, 0)]
ORDER = {"x": "xyz", "y": "yzx", "z": "zxy"}
WHOLE = pl.BlockSpec(memory_space=pltpu.VMEM)
SCALARS = pl.BlockSpec(memory_space=pltpu.SMEM)
UNREAD = pl.BlockSpec(memory_space=pl.ANY)
LIGHT = pl.CostEstimate(flops=1 << 20, bytes_accessed=1 << 16, transcendentals=0)


def unit(rows):
    wide = rows.astype(jnp.float32)
    norm = lax.rsqrt(jnp.sum(wide * wide, axis=1, keepdims=True) + 1e-06)
    return (wide * norm).astype(jnp.bfloat16)


def softplus(value):
    return jnp.maximum(value, 0.0) + jnp.log1p(jnp.exp(-jnp.abs(value)))


def loss_kernel(at, *refs):
    img_refs, txt_refs, txt_other, (out, img, txt) = refs[:4], refs[4:8], refs[8], refs[-3:]
    here_y, here_x, here_zl, here_core, learner = (at[k] for k in range(5))
    for k in range(4):
        img[pl.ds(128 * k, 128), :] = unit(img_refs[k][...])
        own = pl.multiple_of(128 * k + 64 * here_core, 64)
        txt[pl.ds(own, 64), :] = unit(txt_refs[k][...])
        other = pl.multiple_of(128 * k + 64 * (1 - here_core), 64)
        txt[pl.ds(other, 64), :] = unit(txt_other[pl.ds(64 * k, 64), :])
    contract = (((1,), (1,)), ((), ()))
    col_sum = jnp.zeros((1, 512), jnp.float32)
    row_sums = []
    for k in range(4):
        scores = (
            10.0
            * lax.dot_general(
                img[pl.ds(128 * k, 128), :], txt[...], contract, preferred_element_type=jnp.float32
            )
            - 5.0
        )
        if k == 0:
            row = lax.broadcasted_iota(jnp.int32, scores.shape, 0) - 64 * here_zl
            col = lax.broadcasted_iota(jnp.int32, scores.shape, 1) - 64 * here_core
            same = (row == col) & (row >= 0) & (row < 64)
            scores = jnp.where(same, -scores, scores)
        terms = softplus(scores)
        col_sum = col_sum + jnp.sum(terms, axis=0, keepdims=True)
        folded = terms[:, :128] + terms[:, 128:256] + terms[:, 256:384] + terms[:, 384:]
        row_sums.append(jnp.sum(folded.T, axis=0, keepdims=True))
    dest = lax.broadcasted_iota(jnp.int32, (128, 128), 0)
    lane = lax.broadcasted_iota(jnp.int32, (1, 128), 1)
    dest_y, dest_x, dest_zl = dest >> 5, (dest >> 3) & 3, (dest >> 2) & 1
    own_half = (lane >> 6) == here_core
    total = jnp.zeros((128, 128), jnp.float32)
    for k in range(4):
        straight = row_sums[k]
        crossed = pltpu.roll(straight, 64, 1)
        for zl in range(2):
            placed = jnp.where(own_half, jnp.where(here_core == zl, straight, crossed), 0.0)
            mine = (dest_y == here_y) & (dest_x == ((here_x + k) & 3)) & (dest_zl == zl)
            total = total + jnp.where(mine, placed, 0.0)
        mine = (dest_y == ((here_y + k) & 3)) & (dest_x == here_x) & (dest_zl == here_zl)
        total = total + jnp.where(mine, col_sum[:, 128 * k : 128 * (k + 1)], 0.0)
    out[...] = jnp.where(learner == 1, 0.5, -0.5) * total


def partial_losses(at, images, texts, texts_other, ready):
    return pl.pallas_call(
        loss_kernel,
        out_shape=jax.ShapeDtypeStruct((128, 128), jnp.float32),
        in_specs=[SCALARS] + [WHOLE] * 9 + [UNREAD] * len(ready),
        out_specs=WHOLE,
        scratch_shapes=[pltpu.VMEM((512, 1024), jnp.bfloat16)] * 2,
        compiler_params=pltpu.CompilerParams(vmem_limit_bytes=8 << 20),
        cost_estimate=LIGHT,
    )(at, *images, *texts, texts_other, *ready)


def listed(values, axis, shape):
    at = lax.broadcasted_iota(jnp.int32, shape, axis)
    out = jnp.zeros(shape, jnp.int32)
    for k in range(shape[axis]):
        out = jnp.where(at == k, values[k], out)
    return out


def weight_kernel(at, index, parts, *refs):
    learn, weight = refs[-2:]
    score = jnp.sum(parts[...], axis=0, keepdims=True)
    learn[...] = jnp.broadcast_to(score, (8, 128))
    slots = index.shape[0]
    picked = listed(index, 0, (slots, 128)) == lax.broadcasted_iota(jnp.int32, (slots, 128), 1)
    chosen = jnp.sum(jnp.where(picked, score, 0.0), axis=1, keepdims=True)
    live = lax.broadcasted_iota(jnp.int32, (slots, 128), 0) < at[5]
    value = jnp.where(live, 1.0 / (1.0 + jnp.exp(-chosen)), 0.0)
    weight[...] = jnp.broadcast_to(value[:, None, :], (slots, 8, 128)).reshape(8 * slots, 128)


def weights(at, index, parts, ready):
    slots = index.shape[0]
    return pl.pallas_call(
        weight_kernel,
        out_shape=(
            jax.ShapeDtypeStruct((8, 128), jnp.float32),
            jax.ShapeDtypeStruct((8 * slots, 128), jnp.float32),
        ),
        in_specs=[SCALARS, SCALARS, WHOLE] + [UNREAD] * len(ready),
        out_specs=(WHOLE, WHOLE),
        compiler_params=pltpu.CompilerParams(vmem_limit_bytes=2 << 20),
        cost_estimate=LIGHT,
    )(at, index, parts, *ready)


def pair_kernel(at, own, other, *refs):
    pair = refs[-1]
    pair[pl.ds(pl.multiple_of(64 * at[2], 64), 64), :] = own[...]
    pair[pl.ds(pl.multiple_of(64 * (1 - at[2]), 64), 64), :] = other[...]


def pair_rows(at, own, other, ready):
    rows, width = own.shape
    return pl.pallas_call(
        pair_kernel,
        out_shape=jax.ShapeDtypeStruct((2 * rows, width), own.dtype),
        in_specs=[SCALARS, WHOLE, WHOLE] + [UNREAD] * len(ready),
        out_specs=WHOLE,
        compiler_params=pltpu.CompilerParams(vmem_limit_bytes=2 << 20),
        cost_estimate=LIGHT,
    )(at, own, other, *ready)


def join_kernel(*refs):
    out = refs[-1]
    rows = refs[0].shape[0]
    for k, block in enumerate(refs[: out.shape[0] // rows]):
        out[k * rows : (k + 1) * rows, :] = block[...]


def join_rows(blocks, ready):
    rows, width = blocks[0].shape
    return pl.pallas_call(
        join_kernel,
        out_shape=jax.ShapeDtypeStruct((len(blocks) * rows, width), blocks[0].dtype),
        in_specs=[WHOLE] * len(blocks) + [UNREAD] * len(ready),
        out_specs=WHOLE,
        compiler_params=pltpu.CompilerParams(vmem_limit_bytes=2 << 20),
        cost_estimate=LIGHT,
    )(*blocks, *ready)


def half(ref, axis, which, size):
    start = pl.multiple_of(which * size, size)
    return ref[pl.ds(start, size), :] if axis == 0 else ref[:, pl.ds(start, size)]


def up_kernel(at, mine, other, w_up, *refs):
    act, slope, held, sems = refs[-4:]
    size = mine.shape[1]
    steps, _, tile = held.shape
    columns = [pl.ds(n * tile, tile) for n in range(steps)]
    copies = fetched([w_up.at[:, cols] for cols in columns], [held.at[n] for n in range(steps)], sems)
    scale = math.sqrt(2.0 / math.pi)
    for n, cols in enumerate(columns):
        copies[n].wait()
        near, far = half(held.at[n], 0, at[3], size), half(held.at[n], 0, 1 - at[3], size)
        for row in range(0, mine.shape[0], 256):
            rows = pl.ds(row, 256)
            pre = jnp.dot(mine[rows, :], near, preferred_element_type=jnp.float32)
            pre = pre + jnp.dot(other[rows, :], far, preferred_element_type=jnp.float32)
            square = pre * pre
            tanh = jnp.tanh(pre * (scale + (scale * 0.044715) * square))
            gate = 0.5 + 0.5 * tanh
            value = pre * gate
            act[rows, cols] = value.astype(jnp.bfloat16)
            bend = value * (1.0 - gate) * (2 * scale + (6 * scale * 0.044715) * square)
            slope[rows, cols] = (gate + bend).astype(jnp.bfloat16)


def up(at, mine, other, w_up, ready):
    rows, size = mine.shape
    width, tile = w_up.shape[1], 512
    return pl.pallas_call(
        up_kernel,
        out_shape=[jax.ShapeDtypeStruct((rows, width), jnp.bfloat16)] * 2,
        in_specs=[SCALARS, WHOLE, WHOLE, UNREAD] + [UNREAD] * len(ready),
        out_specs=[WHOLE, WHOLE],
        scratch_shapes=[
            pltpu.VMEM((width // tile, 2 * size, tile), w_up.dtype),
            pltpu.SemaphoreType.DMA((width // tile,)),
        ],
        compiler_params=pltpu.CompilerParams(vmem_limit_bytes=16 << 20),
        cost_estimate=LIGHT,
    )(at, mine, other, w_up, *ready)


def back_kernel(at, mine, other, w_down, slope, *refs):
    out, held, sems = refs[-3:]
    size = mine.shape[1]
    steps, tile, _ = held.shape
    columns = [pl.ds(n * tile, tile) for n in range(steps)]
    copies = fetched([w_down.at[cols] for cols in columns], [held.at[n] for n in range(steps)], sems)
    contract = (((1,), (1,)), ((), ()))
    for n, cols in enumerate(columns):
        copies[n].wait()
        near, far = half(held.at[n], 1, at[3], size), half(held.at[n], 1, 1 - at[3], size)
        back = lax.dot_general(mine[...], near, contract, preferred_element_type=jnp.float32)
        back = back + lax.dot_general(other[...], far, contract, preferred_element_type=jnp.float32)
        out[:, cols] = (back * slope[:, cols].astype(jnp.float32)).astype(jnp.bfloat16)


def back(at, mine, other, w_down, slope, ready):
    rows, size = mine.shape
    width, tile = w_down.shape[0], 512
    return pl.pallas_call(
        back_kernel,
        out_shape=jax.ShapeDtypeStruct((rows, width), jnp.bfloat16),
        in_specs=[SCALARS, WHOLE, WHOLE, UNREAD, WHOLE] + [UNREAD] * len(ready),
        out_specs=WHOLE,
        scratch_shapes=[
            pltpu.VMEM((width // tile, tile, 2 * size), w_down.dtype),
            pltpu.SemaphoreType.DMA((width // tile,)),
        ],
        compiler_params=pltpu.CompilerParams(vmem_limit_bytes=14 << 20),
        cost_estimate=LIGHT,
    )(at, mine, other, w_down, slope, *ready)


def turn_kernel(starts, at, mine, other, *refs):
    outs, turned = refs[len(refs) - 1 - len(starts) : -1], refs[-1]
    blocks = turned.shape[0] // 2
    turned[pl.ds(at[3] * blocks, blocks)] = mine[...].T.reshape((blocks,) + turned.shape[1:])
    turned[pl.ds((1 - at[3]) * blocks, blocks)] = other[...].T.reshape(
        (blocks,) + turned.shape[1:]
    )
    here = {"x": at[1], "y": at[0], "z": 2 * at[4] + at[2]}
    for start, out in zip(starts, outs):
        for k in range(2 * blocks):
            steps = (k >> 4, (k >> 2) & 3, k & 3)
            spot = {}
            for axis in "xyz":
                by = [steps[ORDER[one].index(axis)] for one in start]
                by = by[0] + at[3] * (by[-1] - by[0])
                spot[axis] = (here[axis] + by) & 3
            block = 16 * spot["y"] + 4 * spot["x"] + 2 * (spot["z"] & 1) + (spot["z"] >> 1)
            out[16 * k : 16 * (k + 1), :] = turned[block]


def turn(at, mine, other, starts, ready):
    rows, size = mine.shape
    return pl.pallas_call(
        functools.partial(turn_kernel, starts),
        out_shape=[jax.ShapeDtypeStruct((2 * size, rows), mine.dtype)] * len(starts),
        in_specs=[SCALARS, WHOLE, WHOLE] + [UNREAD] * len(ready),
        out_specs=[WHOLE] * len(starts),
        scratch_shapes=[pltpu.VMEM((2 * size // 16, 16, rows), mine.dtype)],
        compiler_params=pltpu.CompilerParams(vmem_limit_bytes=8 << 20),
        cost_estimate=LIGHT,
    )(at, mine, other, *ready)


def down_kernel(at, act, w_down, *refs):
    keep, give = refs[-2:]
    size = keep.shape[1]
    keep[...] = jnp.dot(
        act[...], half(w_down, 1, at[3], size), preferred_element_type=jnp.float32
    )
    give[...] = jnp.dot(
        act[...], half(w_down, 1, 1 - at[3], size), preferred_element_type=jnp.float32
    ).astype(jnp.bfloat16)


def down(at, act, w_down, ready):
    rows, size = act.shape[0], w_down.shape[1] // 2
    return pl.pallas_call(
        down_kernel,
        out_shape=[
            jax.ShapeDtypeStruct((rows, size), jnp.float32),
            jax.ShapeDtypeStruct((rows, size), jnp.bfloat16),
        ],
        in_specs=[SCALARS, WHOLE, WHOLE] + [UNREAD] * len(ready),
        out_specs=[WHOLE, WHOLE],
        compiler_params=pltpu.CompilerParams(vmem_limit_bytes=14 << 20),
        cost_estimate=LIGHT,
    )(at, act, w_down, *ready)


def place_kernel(here, target, own, keep, got, *refs):
    out = refs[-1]
    slots, rows = target.shape[0], own.shape[0]
    each = rows // slots
    out_rows = own[...].astype(jnp.float32) + keep[...] + got[...].astype(jnp.float32)
    out_rows = out_rows.astype(jnp.bfloat16)
    slot = lax.broadcasted_iota(jnp.int32, (slots, slots), 0)
    before = lax.broadcasted_iota(jnp.int32, (slots, slots), 1)
    to = listed(target, 0, (slots, slots))
    same = (listed(target, 1, (1, slots)) == to) & (before < slot)
    rank = jnp.sum(same.astype(jnp.int32), axis=1, keepdims=True)
    live = slot[:, :1] < here[5]
    first = jnp.where(live, each * (4 * to[:, :1] + rank), -each)
    lane = lax.broadcasted_iota(jnp.int32, (slots, rows), 1)
    mine = (lane // each) == lax.broadcasted_iota(jnp.int32, (slots, rows), 0)
    goes = jnp.sum(jnp.where(mine, first + lane % each, 0), axis=0, keepdims=True)
    step = 256
    for at in range(0, out.shape[0], step):
        reached = lax.broadcasted_iota(jnp.int32, (step, rows), 0) + at == goes
        out[at : at + step, :] = jnp.dot(
            jnp.where(reached, 1.0, 0.0).astype(jnp.bfloat16),
            out_rows,
            preferred_element_type=jnp.float32,
        ).astype(jnp.bfloat16)


def place(at, target, own, keep, got, ready):
    rows, size = own.shape
    return pl.pallas_call(
        place_kernel,
        out_shape=jax.ShapeDtypeStruct((2 * rows, size), jnp.bfloat16),
        in_specs=[SCALARS, SCALARS] + [WHOLE] * 3 + [UNREAD] * len(ready),
        out_specs=WHOLE,
        compiler_params=pltpu.CompilerParams(vmem_limit_bytes=8 << 20),
        cost_estimate=LIGHT,
    )(at, target, own, keep, got, *ready)


def around(block, axis):
    return [block] + [shift(block, axis, 4 - by) for by in (1, 2, 3)]


def shift(block, axis, by):
    if axis == "z":
        at = [(z % 2) * 2 + z // 2 for z in range(4)]
        return lax.ppermute(block, ("zl", "zh"), [(at[z], at[(z + by) % 4]) for z in range(4)])
    return lax.ppermute(block, axis, [(k, (k + by) % 4) for k in range(4)])


def number(spot, core):
    return 8 * (4 * spot["y"] + spot["x"]) + 4 * (spot["z"] % 2) + 2 * core + spot["z"] // 2


def shift_each(block, axes, by):
    route = []
    for chip in range(64):
        spot = {"x": chip % 4, "y": chip // 4 % 4, "z": chip // 16}
        for core in range(2):
            axis = axes[core]
            there = {**spot, axis: (spot[axis] + by) % 4}
            route.append((number(spot, core), number(there, core)))
    return lax.ppermute(block, ("y", "x", "zl", "core", "zh"), route)


def fetched(sources, targets, sems):
    copies = [
        pltpu.make_async_copy(source, target, sems.at[k])
        for k, (source, target) in enumerate(zip(sources, targets))
    ]
    for copy in copies:
        copy.start()
    return copies


def product_kernel(pieces, weight, *refs):
    lefts = 1 + max(piece[0] for piece in pieces)
    rights = 1 + max(piece[1] for piece in pieces)
    count = lefts + rights
    sources, rest = refs[:count], refs[len(refs) - count - 6 :]
    outs, held, scaled, sems = rest[:4], rest[4 : 4 + count], rest[-2], rest[-1]
    copies = fetched(sources, held, sems)
    rows = weight[...]
    depth = outs[0].shape[0]
    done = 0
    seen = set()
    for left, right, first, last in pieces:
        for k in (lefts + right, left):
            if k not in seen:
                copies[k].wait()
                seen.add(k)
        for col in range(first, last, 128):
            piece = held[lefts + right][:, col : col + 128].astype(jnp.float32) * rows
            scaled[:, col - first : col - first + 128] = piece.astype(jnp.bfloat16)
        for col in range(0, last - first, 256):
            end = min(col + 256, last - first)
            product = jnp.dot(held[left][...], scaled[:, col:end], preferred_element_type=jnp.float32)
            for k in range(4):
                outs[k][:, done + col : done + end] = product[depth * k : depth * (k + 1)].astype(
                    jnp.bfloat16
                )
        done += last - first


def products(weight, lefts, rights, pieces, ready=()):
    width = sum(last - first for _, _, first, last in pieces)
    sides = [*lefts, *rights]
    depth = weight.shape[0]
    return pl.pallas_call(
        functools.partial(product_kernel, pieces),
        out_shape=[jax.ShapeDtypeStruct((256, width), jnp.bfloat16)] * 4,
        in_specs=[WHOLE] + [UNREAD] * len(sides) + [UNREAD] * len(ready),
        out_specs=[WHOLE] * 4,
        scratch_shapes=[pltpu.VMEM(side.shape, side.dtype) for side in sides]
        + [
            pltpu.VMEM((depth, max(piece[3] - piece[2] for piece in pieces)), jnp.bfloat16),
            pltpu.SemaphoreType.DMA((len(sides),)),
        ],
        compiler_params=pltpu.CompilerParams(vmem_limit_bytes=20 << 20),
        cost_estimate=LIGHT,
    )(weight, *sides, *ready)


def sum_kernel(*refs):
    sources, outs, held, sems = refs[:4], refs[-9:-5], refs[-5:-1], refs[-1]
    copies = fetched(sources, held, sems)
    for copy in copies:
        copy.wait()
    rows = outs[0].shape[0]
    for k in range(4):
        here = pl.ds(k * rows, rows)
        total = held[0][here, :].astype(jnp.float32)
        for ref in held[1:]:
            total = total + ref[here, :].astype(jnp.float32)
        outs[k][...] = total.astype(jnp.bfloat16)


def sum_blocks(blocks, grant, ready=()):
    rows, width = blocks[0].shape
    return pl.pallas_call(
        sum_kernel,
        out_shape=[jax.ShapeDtypeStruct((rows // 4, width), jnp.bfloat16)] * 4,
        in_specs=[UNREAD] * (4 + len(ready)),
        out_specs=[WHOLE] * 4,
        scratch_shapes=[pltpu.VMEM(block.shape, block.dtype) for block in blocks]
        + [pltpu.SemaphoreType.DMA((4,))],
        compiler_params=pltpu.CompilerParams(vmem_limit_bytes=grant),
        cost_estimate=LIGHT,
    )(*blocks, *ready)


def copy_kernel(source, out, token):
    out[...] = source[...]
    token[...] = jnp.zeros(token.shape, token.dtype)


def copied(block):
    return pl.pallas_call(
        copy_kernel,
        out_shape=(
            jax.ShapeDtypeStruct(block.shape, block.dtype),
            jax.ShapeDtypeStruct((8, 128), jnp.float32),
        ),
        in_specs=[WHOLE],
        out_specs=(WHOLE, WHOLE),
        compiler_params=pltpu.CompilerParams(vmem_limit_bytes=4 << 20),
        cost_estimate=LIGHT,
    )(block)


def last_kernel(*refs):
    down, up = refs[-2:]
    sums = []
    for part in range(2):
        total = refs[4 * part][...].astype(jnp.float32)
        for ref in refs[4 * part + 1 : 4 * part + 4]:
            total = total + ref[...].astype(jnp.float32)
        sums.append(total)
    width = down.shape[1]
    cut = sums[0].shape[1] - width
    down[...] = sums[0][:, :width]
    up[:, :cut] = sums[0][:, width:]
    up[:, cut:] = sums[1]


def last_sum(parts, ready, width):
    return pl.pallas_call(
        last_kernel,
        out_shape=[jax.ShapeDtypeStruct((16, width), jnp.float32)] * 2,
        in_specs=[WHOLE] * 8 + [UNREAD] * len(ready),
        out_specs=[WHOLE] * 2,
        compiler_params=pltpu.CompilerParams(vmem_limit_bytes=4 << 20),
        cost_estimate=LIGHT,
    )(*[block for part in parts for block in part], *ready)


def exchanged(parts, step):
    first, second = parts
    axes = (ORDER["x"][step], ORDER["y"][step])
    return [
        [first[0]] + [shift_each(first[by], axes, by) for by in (2, 1, 3)],
        [second[0]] + [shift(second[by], ORDER["z"][step], by) for by in (2, 1, 3)],
    ]


def local(
    ref_image,
    ref_text,
    learner_image,
    learner_text,
    patches,
    cotangent,
    w_up,
    w_down,
    counts,
    sel_index,
    sel_dest,
):
    core = lax.axis_index("core")
    at = [lax.axis_index(name) for name in ("y", "x", "zl", "core", "zh")]
    at = jnp.stack([*at, counts[0]]).astype(jnp.int32)
    slots = sel_index.shape[0]
    patch_rows, size = patches.shape[1:]
    count, width, rows = slots * patch_rows, w_up.shape[1], ref_image.shape[0]

    learner = lax.axis_index("zh") == 1
    pad = ((0, 0), (0, learner_image.shape[1] - ref_image.shape[1]))
    x_mine = patches[sel_index].reshape(count, size)
    cot_mine = cotangent[sel_index].reshape(count, size)
    learner_image, learner_text, x_mine, cot_mine, at = lax.optimization_barrier(
        (learner_image, learner_text, x_mine, cot_mine, at)
    )
    image = jnp.where(learner, learner_image, jnp.pad(ref_image, pad))
    text = jnp.where(learner, learner_text, jnp.pad(ref_text, pad))
    other_image = lax.ppermute(image, "zl", SWAP)
    x_other = lax.ppermute(x_mine, "core", SWAP)
    cot_other = lax.ppermute(cot_mine, "core", SWAP)
    texts = around(text, "y")
    joined = join_rows(texts, [other_image, x_other, cot_mine])
    texts_other = lax.ppermute(joined, "core", SWAP)
    pair = pair_rows(at, image, other_image, [joined])
    images = around(pair, "x")

    act, slope = up(at, x_mine, x_other, w_up, [pair])
    x_first, x_second = turn(at, x_mine, x_other, ("xy", "z"), [pair])

    grad_pre = back(at, cot_mine, cot_other, w_down, slope, [])
    (cot_first,) = turn(at, cot_mine, cot_other, ("xy",), [])

    parts = partial_losses(at, images, texts, texts_other, [x_first, grad_pre, cot_first])
    parts = lax.all_to_all(
        parts, ("y", "x", "zl", "core", "zh"), split_axis=0, concat_axis=0, tiled=True
    )
    scores, weight = weights(at, sel_index, parts, [])
    learnability = lax.dynamic_slice_in_dim(scores[0], core * rows, rows)

    cut = 384
    second = products(weight, [x_second], [grad_pre], ((0, 0, cut, width),))
    first = products(
        weight,
        [cot_first, x_first],
        [act, grad_pre],
        ((0, 0, 0, width), (1, 1, 0, cut)),
        second[:1],
    )
    blocks = exchanged([first, second], 0)
    keep, give = down(at, act, w_down, [blocks[0][1]])
    got = lax.ppermute(give, "core", SWAP)
    boxed = place(at, sel_dest.reshape(slots), x_mine, keep, got, [])
    boxed = boxed.reshape(32, 4, patch_rows, size)
    routed = lax.all_to_all(boxed, DP, split_axis=0, concat_axis=0, tiled=True)
    routed, token = copied(routed.reshape(128, patch_rows, size))
    blocks = [sum_blocks(part, 56 << 20) for part in blocks]
    blocks = [sum_blocks(part, 6 << 20) for part in exchanged(blocks, 1)]
    grad_down_t, grad_up = last_sum(exchanged(blocks, 2), [token], width)
    return (learnability, routed, grad_up, grad_down_t)


def solution(mesh):
    mesh = Mesh(mesh.devices.reshape(4, 4, 2, 2, 2), ("y", "x", "zl", "core", "zh"))
    pairs = P(("y", "x", "zl", "core"), None)
    patch = P(DP, "zh", "core")
    return jax.shard_map(
        local,
        mesh=mesh,
        in_specs=(
            pairs,
            pairs,
            pairs,
            pairs,
            patch,
            patch,
            P(None, "core"),
            P("core", None),
            P(DP),
            P(DP),
            P(DP, None),
        ),
        out_specs=(
            P(("y", "x", "zl", "core")),
            patch,
            P(CHIPS, "core"),
            P(CHIPS, "core"),
        ),
        check_vma=False,
    )
```

```python
import functools
import math

import jax
import jax.numpy as jnp
from jax import lax
from jax.experimental import pallas as pl
from jax.experimental.pallas import tpu as pltpu
from jax.sharding import Mesh, PartitionSpec as P

DP = ("y", "x", "zl")
CHIPS = ("y", "x", "zl", "zh")
SWAP = [(0, 1), (1, 0)]
ORDER = {"x": "xyz", "y": "yzx", "z": "zxy"}
WHOLE = pl.BlockSpec(memory_space=pltpu.VMEM)
SCALARS = pl.BlockSpec(memory_space=pltpu.SMEM)
UNREAD = pl.BlockSpec(memory_space=pl.ANY)
LIGHT = pl.CostEstimate(flops=1 << 20, bytes_accessed=1 << 16, transcendentals=0)


def unit(rows):
    wide = rows.astype(jnp.float32)
    norm = lax.rsqrt(jnp.sum(wide * wide, axis=1, keepdims=True) + 1e-06)
    return (wide * norm).astype(jnp.bfloat16)


def softplus(value):
    return jnp.maximum(value, 0.0) + jnp.log1p(jnp.exp(-jnp.abs(value)))


def loss_kernel(at, *refs):
    img_refs, txt_refs, txt_other, (out, img, txt) = refs[:4], refs[4:8], refs[8], refs[-3:]
    here_y, here_x, here_zl, here_core, learner = (at[k] for k in range(5))
    for k in range(4):
        img[pl.ds(128 * k, 128), :] = unit(img_refs[k][...])
        own = pl.multiple_of(128 * k + 64 * here_core, 64)
        txt[pl.ds(own, 64), :] = unit(txt_refs[k][...])
        other = pl.multiple_of(128 * k + 64 * (1 - here_core), 64)
        txt[pl.ds(other, 64), :] = unit(txt_other[pl.ds(64 * k, 64), :])
    contract = (((1,), (1,)), ((), ()))
    col_sum = jnp.zeros((1, 512), jnp.float32)
    row_sums = []
    for k in range(4):
        scores = (
            10.0
            * lax.dot_general(
                img[pl.ds(128 * k, 128), :], txt[...], contract, preferred_element_type=jnp.float32
            )
            - 5.0
        )
        if k == 0:
            row = lax.broadcasted_iota(jnp.int32, scores.shape, 0) - 64 * here_zl
            col = lax.broadcasted_iota(jnp.int32, scores.shape, 1) - 64 * here_core
            same = (row == col) & (row >= 0) & (row < 64)
            scores = jnp.where(same, -scores, scores)
        terms = softplus(scores)
        col_sum = col_sum + jnp.sum(terms, axis=0, keepdims=True)
        folded = terms[:, :128] + terms[:, 128:256] + terms[:, 256:384] + terms[:, 384:]
        row_sums.append(jnp.sum(folded.T, axis=0, keepdims=True))
    dest = lax.broadcasted_iota(jnp.int32, (128, 128), 0)
    lane = lax.broadcasted_iota(jnp.int32, (1, 128), 1)
    dest_y, dest_x, dest_zl = dest >> 5, (dest >> 3) & 3, (dest >> 2) & 1
    own_half = (lane >> 6) == here_core
    total = jnp.zeros((128, 128), jnp.float32)
    for k in range(4):
        straight = row_sums[k]
        crossed = pltpu.roll(straight, 64, 1)
        for zl in range(2):
            placed = jnp.where(own_half, jnp.where(here_core == zl, straight, crossed), 0.0)
            mine = (dest_y == here_y) & (dest_x == ((here_x + k) & 3)) & (dest_zl == zl)
            total = total + jnp.where(mine, placed, 0.0)
        mine = (dest_y == ((here_y + k) & 3)) & (dest_x == here_x) & (dest_zl == here_zl)
        total = total + jnp.where(mine, col_sum[:, 128 * k : 128 * (k + 1)], 0.0)
    out[...] = jnp.where(learner == 1, 0.5, -0.5) * total


def partial_losses(at, images, texts, texts_other, ready):
    return pl.pallas_call(
        loss_kernel,
        out_shape=jax.ShapeDtypeStruct((128, 128), jnp.float32),
        in_specs=[SCALARS] + [WHOLE] * 9 + [UNREAD] * len(ready),
        out_specs=WHOLE,
        scratch_shapes=[pltpu.VMEM((512, 1024), jnp.bfloat16)] * 2,
        compiler_params=pltpu.CompilerParams(vmem_limit_bytes=8 << 20),
        cost_estimate=LIGHT,
    )(at, *images, *texts, texts_other, *ready)


def listed(values, axis, shape):
    at = lax.broadcasted_iota(jnp.int32, shape, axis)
    out = jnp.zeros(shape, jnp.int32)
    for k in range(shape[axis]):
        out = jnp.where(at == k, values[k], out)
    return out


def weight_kernel(at, index, parts, *refs):
    learn, weight = refs[-2:]
    score = jnp.sum(parts[...], axis=0, keepdims=True)
    learn[...] = jnp.broadcast_to(score, (8, 128))
    slots = index.shape[0]
    picked = listed(index, 0, (slots, 128)) == lax.broadcasted_iota(jnp.int32, (slots, 128), 1)
    chosen = jnp.sum(jnp.where(picked, score, 0.0), axis=1, keepdims=True)
    live = lax.broadcasted_iota(jnp.int32, (slots, 128), 0) < at[5]
    value = jnp.where(live, 1.0 / (1.0 + jnp.exp(-chosen)), 0.0)
    weight[...] = jnp.broadcast_to(value[:, None, :], (slots, 8, 128)).reshape(8 * slots, 128)


def weights(at, index, parts, ready):
    slots = index.shape[0]
    return pl.pallas_call(
        weight_kernel,
        out_shape=(
            jax.ShapeDtypeStruct((8, 128), jnp.float32),
            jax.ShapeDtypeStruct((8 * slots, 128), jnp.float32),
        ),
        in_specs=[SCALARS, SCALARS, WHOLE] + [UNREAD] * len(ready),
        out_specs=(WHOLE, WHOLE),
        compiler_params=pltpu.CompilerParams(vmem_limit_bytes=2 << 20),
        cost_estimate=LIGHT,
    )(at, index, parts, *ready)


def pair_kernel(at, own, other, *refs):
    pair = refs[-1]
    pair[pl.ds(pl.multiple_of(64 * at[2], 64), 64), :] = own[...]
    pair[pl.ds(pl.multiple_of(64 * (1 - at[2]), 64), 64), :] = other[...]


def pair_rows(at, own, other, ready):
    rows, width = own.shape
    return pl.pallas_call(
        pair_kernel,
        out_shape=jax.ShapeDtypeStruct((2 * rows, width), own.dtype),
        in_specs=[SCALARS, WHOLE, WHOLE] + [UNREAD] * len(ready),
        out_specs=WHOLE,
        compiler_params=pltpu.CompilerParams(vmem_limit_bytes=2 << 20),
        cost_estimate=LIGHT,
    )(at, own, other, *ready)


def join_kernel(*refs):
    out = refs[-1]
    rows = refs[0].shape[0]
    for k, block in enumerate(refs[: out.shape[0] // rows]):
        out[k * rows : (k + 1) * rows, :] = block[...]


def join_rows(blocks, ready):
    rows, width = blocks[0].shape
    return pl.pallas_call(
        join_kernel,
        out_shape=jax.ShapeDtypeStruct((len(blocks) * rows, width), blocks[0].dtype),
        in_specs=[WHOLE] * len(blocks) + [UNREAD] * len(ready),
        out_specs=WHOLE,
        compiler_params=pltpu.CompilerParams(vmem_limit_bytes=2 << 20),
        cost_estimate=LIGHT,
    )(*blocks, *ready)


def half(ref, axis, which, size):
    start = pl.multiple_of(which * size, size)
    return ref[pl.ds(start, size), :] if axis == 0 else ref[:, pl.ds(start, size)]


def up_kernel(at, mine, other, w_up, *refs):
    act, slope, held, sems = refs[-4:]
    size = mine.shape[1]
    steps, _, tile = held.shape
    columns = [pl.ds(n * tile, tile) for n in range(steps)]
    copies = fetched([w_up.at[:, cols] for cols in columns], [held.at[n] for n in range(steps)], sems)
    scale = math.sqrt(2.0 / math.pi)
    for n, cols in enumerate(columns):
        copies[n].wait()
        near, far = half(held.at[n], 0, at[3], size), half(held.at[n], 0, 1 - at[3], size)
        for row in range(0, mine.shape[0], 256):
            rows = pl.ds(row, 256)
            pre = jnp.dot(mine[rows, :], near, preferred_element_type=jnp.float32)
            pre = pre + jnp.dot(other[rows, :], far, preferred_element_type=jnp.float32)
            square = pre * pre
            tanh = jnp.tanh(pre * (scale + (scale * 0.044715) * square))
            gate = 0.5 + 0.5 * tanh
            value = pre * gate
            act[rows, cols] = value.astype(jnp.bfloat16)
            bend = value * (1.0 - gate) * (2 * scale + (6 * scale * 0.044715) * square)
            slope[rows, cols] = (gate + bend).astype(jnp.bfloat16)


def up(at, mine, other, w_up, ready):
    rows, size = mine.shape
    width, tile = w_up.shape[1], 512
    return pl.pallas_call(
        up_kernel,
        out_shape=[jax.ShapeDtypeStruct((rows, width), jnp.bfloat16)] * 2,
        in_specs=[SCALARS, WHOLE, WHOLE, UNREAD] + [UNREAD] * len(ready),
        out_specs=[WHOLE, WHOLE],
        scratch_shapes=[
            pltpu.VMEM((width // tile, 2 * size, tile), w_up.dtype),
            pltpu.SemaphoreType.DMA((width // tile,)),
        ],
        compiler_params=pltpu.CompilerParams(vmem_limit_bytes=16 << 20),
        cost_estimate=LIGHT,
    )(at, mine, other, w_up, *ready)


def back_kernel(at, mine, other, w_down, slope, *refs):
    out, held, sems = refs[-3:]
    size = mine.shape[1]
    steps, tile, _ = held.shape
    columns = [pl.ds(n * tile, tile) for n in range(steps)]
    copies = fetched([w_down.at[cols] for cols in columns], [held.at[n] for n in range(steps)], sems)
    contract = (((1,), (1,)), ((), ()))
    for n, cols in enumerate(columns):
        copies[n].wait()
        near, far = half(held.at[n], 1, at[3], size), half(held.at[n], 1, 1 - at[3], size)
        back = lax.dot_general(mine[...], near, contract, preferred_element_type=jnp.float32)
        back = back + lax.dot_general(other[...], far, contract, preferred_element_type=jnp.float32)
        out[:, cols] = (back * slope[:, cols].astype(jnp.float32)).astype(jnp.bfloat16)


def back(at, mine, other, w_down, slope, ready):
    rows, size = mine.shape
    width, tile = w_down.shape[0], 512
    return pl.pallas_call(
        back_kernel,
        out_shape=jax.ShapeDtypeStruct((rows, width), jnp.bfloat16),
        in_specs=[SCALARS, WHOLE, WHOLE, UNREAD, WHOLE] + [UNREAD] * len(ready),
        out_specs=WHOLE,
        scratch_shapes=[
            pltpu.VMEM((width // tile, tile, 2 * size), w_down.dtype),
            pltpu.SemaphoreType.DMA((width // tile,)),
        ],
        compiler_params=pltpu.CompilerParams(vmem_limit_bytes=14 << 20),
        cost_estimate=LIGHT,
    )(at, mine, other, w_down, slope, *ready)


def turn_kernel(starts, at, mine, other, *refs):
    outs, turned = refs[len(refs) - 1 - len(starts) : -1], refs[-1]
    blocks = turned.shape[0] // 2
    turned[pl.ds(at[3] * blocks, blocks)] = mine[...].T.reshape((blocks,) + turned.shape[1:])
    turned[pl.ds((1 - at[3]) * blocks, blocks)] = other[...].T.reshape(
        (blocks,) + turned.shape[1:]
    )
    here = {"x": at[1], "y": at[0], "z": 2 * at[4] + at[2]}
    for start, out in zip(starts, outs):
        for k in range(2 * blocks):
            steps = (k >> 4, (k >> 2) & 3, k & 3)
            spot = {}
            for axis in "xyz":
                by = [steps[ORDER[one].index(axis)] for one in start]
                by = by[0] + at[3] * (by[-1] - by[0])
                spot[axis] = (here[axis] + by) & 3
            block = 16 * spot["y"] + 4 * spot["x"] + 2 * (spot["z"] & 1) + (spot["z"] >> 1)
            out[16 * k : 16 * (k + 1), :] = turned[block]


def turn(at, mine, other, starts, ready):
    rows, size = mine.shape
    return pl.pallas_call(
        functools.partial(turn_kernel, starts),
        out_shape=[jax.ShapeDtypeStruct((2 * size, rows), mine.dtype)] * len(starts),
        in_specs=[SCALARS, WHOLE, WHOLE] + [UNREAD] * len(ready),
        out_specs=[WHOLE] * len(starts),
        scratch_shapes=[pltpu.VMEM((2 * size // 16, 16, rows), mine.dtype)],
        compiler_params=pltpu.CompilerParams(vmem_limit_bytes=8 << 20),
        cost_estimate=LIGHT,
    )(at, mine, other, *ready)


def down_kernel(at, act, w_down, *refs):
    keep, give = refs[-2:]
    size = keep.shape[1]
    keep[...] = jnp.dot(
        act[...], half(w_down, 1, at[3], size), preferred_element_type=jnp.float32
    )
    give[...] = jnp.dot(
        act[...], half(w_down, 1, 1 - at[3], size), preferred_element_type=jnp.float32
    ).astype(jnp.bfloat16)


def down(at, act, w_down, ready):
    rows, size = act.shape[0], w_down.shape[1] // 2
    return pl.pallas_call(
        down_kernel,
        out_shape=[
            jax.ShapeDtypeStruct((rows, size), jnp.float32),
            jax.ShapeDtypeStruct((rows, size), jnp.bfloat16),
        ],
        in_specs=[SCALARS, WHOLE, WHOLE] + [UNREAD] * len(ready),
        out_specs=[WHOLE, WHOLE],
        compiler_params=pltpu.CompilerParams(vmem_limit_bytes=14 << 20),
        cost_estimate=LIGHT,
    )(at, act, w_down, *ready)


def place_kernel(here, target, own, keep, got, *refs):
    out = refs[-1]
    slots, rows = target.shape[0], own.shape[0]
    each = rows // slots
    out_rows = own[...].astype(jnp.float32) + keep[...] + got[...].astype(jnp.float32)
    out_rows = out_rows.astype(jnp.bfloat16)
    slot = lax.broadcasted_iota(jnp.int32, (slots, slots), 0)
    before = lax.broadcasted_iota(jnp.int32, (slots, slots), 1)
    to = listed(target, 0, (slots, slots))
    same = (listed(target, 1, (1, slots)) == to) & (before < slot)
    rank = jnp.sum(same.astype(jnp.int32), axis=1, keepdims=True)
    live = slot[:, :1] < here[5]
    first = jnp.where(live, each * (4 * to[:, :1] + rank), -each)
    lane = lax.broadcasted_iota(jnp.int32, (slots, rows), 1)
    mine = (lane // each) == lax.broadcasted_iota(jnp.int32, (slots, rows), 0)
    goes = jnp.sum(jnp.where(mine, first + lane % each, 0), axis=0, keepdims=True)
    step = 256
    for at in range(0, out.shape[0], step):
        reached = lax.broadcasted_iota(jnp.int32, (step, rows), 0) + at == goes
        out[at : at + step, :] = jnp.dot(
            jnp.where(reached, 1.0, 0.0).astype(jnp.bfloat16),
            out_rows,
            preferred_element_type=jnp.float32,
        ).astype(jnp.bfloat16)


def place(at, target, own, keep, got, ready):
    rows, size = own.shape
    return pl.pallas_call(
        place_kernel,
        out_shape=jax.ShapeDtypeStruct((2 * rows, size), jnp.bfloat16),
        in_specs=[SCALARS, SCALARS] + [WHOLE] * 3 + [UNREAD] * len(ready),
        out_specs=WHOLE,
        compiler_params=pltpu.CompilerParams(vmem_limit_bytes=8 << 20),
        cost_estimate=LIGHT,
    )(at, target, own, keep, got, *ready)


def around(block, axis):
    return [block] + [shift(block, axis, 4 - by) for by in (1, 2, 3)]


def shift(block, axis, by):
    if axis == "z":
        at = [(z % 2) * 2 + z // 2 for z in range(4)]
        return lax.ppermute(block, ("zl", "zh"), [(at[z], at[(z + by) % 4]) for z in range(4)])
    return lax.ppermute(block, axis, [(k, (k + by) % 4) for k in range(4)])


def number(spot, core):
    return 8 * (4 * spot["y"] + spot["x"]) + 4 * (spot["z"] % 2) + 2 * core + spot["z"] // 2


def shift_each(block, axes, by):
    route = []
    for chip in range(64):
        spot = {"x": chip % 4, "y": chip // 4 % 4, "z": chip // 16}
        for core in range(2):
            axis = axes[core]
            there = {**spot, axis: (spot[axis] + by) % 4}
            route.append((number(spot, core), number(there, core)))
    return lax.ppermute(block, ("y", "x", "zl", "core", "zh"), route)


def fetched(sources, targets, sems):
    copies = [
        pltpu.make_async_copy(source, target, sems.at[k])
        for k, (source, target) in enumerate(zip(sources, targets))
    ]
    for copy in copies:
        copy.start()
    return copies


def product_kernel(pieces, weight, *refs):
    lefts = 1 + max(piece[0] for piece in pieces)
    rights = 1 + max(piece[1] for piece in pieces)
    count = lefts + rights
    sources, rest = refs[:count], refs[len(refs) - count - 6 :]
    outs, held, scaled, sems = rest[:4], rest[4 : 4 + count], rest[-2], rest[-1]
    copies = fetched(sources, held, sems)
    rows = weight[...]
    depth = outs[0].shape[0]
    done = 0
    seen = set()
    for left, right, first, last in pieces:
        for k in (lefts + right, left):
            if k not in seen:
                copies[k].wait()
                seen.add(k)
        for col in range(first, last, 128):
            piece = held[lefts + right][:, col : col + 128].astype(jnp.float32) * rows
            scaled[:, col - first : col - first + 128] = piece.astype(jnp.bfloat16)
        for col in range(0, last - first, 256):
            end = min(col + 256, last - first)
            product = jnp.dot(held[left][...], scaled[:, col:end], preferred_element_type=jnp.float32)
            for k in range(4):
                outs[k][:, done + col : done + end] = product[depth * k : depth * (k + 1)].astype(
                    jnp.bfloat16
                )
        done += last - first


def products(weight, lefts, rights, pieces, ready=()):
    width = sum(last - first for _, _, first, last in pieces)
    sides = [*lefts, *rights]
    depth = weight.shape[0]
    return pl.pallas_call(
        functools.partial(product_kernel, pieces),
        out_shape=[jax.ShapeDtypeStruct((256, width), jnp.bfloat16)] * 4,
        in_specs=[WHOLE] + [UNREAD] * len(sides) + [UNREAD] * len(ready),
        out_specs=[WHOLE] * 4,
        scratch_shapes=[pltpu.VMEM(side.shape, side.dtype) for side in sides]
        + [
            pltpu.VMEM((depth, max(piece[3] - piece[2] for piece in pieces)), jnp.bfloat16),
            pltpu.SemaphoreType.DMA((len(sides),)),
        ],
        compiler_params=pltpu.CompilerParams(vmem_limit_bytes=20 << 20),
        cost_estimate=LIGHT,
    )(weight, *sides, *ready)


def sum_kernel(*refs):
    sources, outs, held, sems = refs[:4], refs[-9:-5], refs[-5:-1], refs[-1]
    copies = fetched(sources, held, sems)
    for copy in copies:
        copy.wait()
    rows = outs[0].shape[0]
    for k in range(4):
        here = pl.ds(k * rows, rows)
        total = held[0][here, :].astype(jnp.float32)
        for ref in held[1:]:
            total = total + ref[here, :].astype(jnp.float32)
        outs[k][...] = total.astype(jnp.bfloat16)


def sum_blocks(blocks, grant, ready=()):
    rows, width = blocks[0].shape
    return pl.pallas_call(
        sum_kernel,
        out_shape=[jax.ShapeDtypeStruct((rows // 4, width), jnp.bfloat16)] * 4,
        in_specs=[UNREAD] * (4 + len(ready)),
        out_specs=[WHOLE] * 4,
        scratch_shapes=[pltpu.VMEM(block.shape, block.dtype) for block in blocks]
        + [pltpu.SemaphoreType.DMA((4,))],
        compiler_params=pltpu.CompilerParams(vmem_limit_bytes=grant),
        cost_estimate=LIGHT,
    )(*blocks, *ready)


def copy_kernel(source, out, token):
    out[...] = source[...]
    token[...] = jnp.zeros(token.shape, token.dtype)


def copied(block):
    return pl.pallas_call(
        copy_kernel,
        out_shape=(
            jax.ShapeDtypeStruct(block.shape, block.dtype),
            jax.ShapeDtypeStruct((8, 128), jnp.float32),
        ),
        in_specs=[WHOLE],
        out_specs=(WHOLE, WHOLE),
        compiler_params=pltpu.CompilerParams(vmem_limit_bytes=4 << 20),
        cost_estimate=LIGHT,
    )(block)


def last_kernel(*refs):
    down, up = refs[-2:]
    sums = []
    for part in range(2):
        total = refs[4 * part][...].astype(jnp.float32)
        for ref in refs[4 * part + 1 : 4 * part + 4]:
            total = total + ref[...].astype(jnp.float32)
        sums.append(total)
    width = down.shape[1]
    cut = sums[0].shape[1] - width
    down[...] = sums[0][:, :width]
    up[:, :cut] = sums[0][:, width:]
    up[:, cut:] = sums[1]


def last_sum(parts, ready, width):
    return pl.pallas_call(
        last_kernel,
        out_shape=[jax.ShapeDtypeStruct((16, width), jnp.float32)] * 2,
        in_specs=[WHOLE] * 8 + [UNREAD] * len(ready),
        out_specs=[WHOLE] * 2,
        compiler_params=pltpu.CompilerParams(vmem_limit_bytes=4 << 20),
        cost_estimate=LIGHT,
    )(*[block for part in parts for block in part], *ready)


def exchanged(parts, step):
    first, second = parts
    axes = (ORDER["x"][step], ORDER["y"][step])
    return [
        [first[0]] + [shift_each(first[by], axes, by) for by in (2, 1, 3)],
        [second[0]] + [shift(second[by], ORDER["z"][step], by) for by in (2, 1, 3)],
    ]


def local(
    ref_image,
    ref_text,
    learner_image,
    learner_text,
    patches,
    cotangent,
    w_up,
    w_down,
    counts,
    sel_index,
    sel_dest,
):
    core = lax.axis_index("core")
    at = [lax.axis_index(name) for name in ("y", "x", "zl", "core", "zh")]
    at = jnp.stack([*at, counts[0]]).astype(jnp.int32)
    slots = sel_index.shape[0]
    patch_rows, size = patches.shape[1:]
    count, width, rows = slots * patch_rows, w_up.shape[1], ref_image.shape[0]

    learner = lax.axis_index("zh") == 1
    pad = ((0, 0), (0, learner_image.shape[1] - ref_image.shape[1]))
    x_mine = patches[sel_index].reshape(count, size)
    cot_mine = cotangent[sel_index].reshape(count, size)
    learner_image, learner_text, x_mine, cot_mine, at = lax.optimization_barrier(
        (learner_image, learner_text, x_mine, cot_mine, at)
    )
    image = jnp.where(learner, learner_image, jnp.pad(ref_image, pad))
    text = jnp.where(learner, learner_text, jnp.pad(ref_text, pad))
    other_image = lax.ppermute(image, "zl", SWAP)
    x_other = lax.ppermute(x_mine, "core", SWAP)
    cot_other = lax.ppermute(cot_mine, "core", SWAP)
    texts = around(text, "y")
    joined = join_rows(texts, [other_image, x_other, cot_mine])
    texts_other = lax.ppermute(joined, "core", SWAP)
    pair = pair_rows(at, image, other_image, [joined])
    images = around(pair, "x")

    act, slope = up(at, x_mine, x_other, w_up, [pair])
    x_first, x_second = turn(at, x_mine, x_other, ("xy", "z"), [pair])

    grad_pre = back(at, cot_mine, cot_other, w_down, slope, [])
    (cot_first,) = turn(at, cot_mine, cot_other, ("xy",), [])

    parts = partial_losses(at, images, texts, texts_other, [x_first, grad_pre, cot_first])
    parts = lax.all_to_all(
        parts, ("y", "x", "zl", "core", "zh"), split_axis=0, concat_axis=0, tiled=True
    )
    scores, weight = weights(at, sel_index, parts, [])
    learnability = lax.dynamic_slice_in_dim(scores[0], core * rows, rows)

    cut = 384
    second = products(weight, [x_second], [grad_pre], ((0, 0, cut, width),))
    first = products(
        weight,
        [cot_first, x_first],
        [act, grad_pre],
        ((0, 0, 0, width), (1, 1, 0, cut)),
        second[:1],
    )
    blocks = exchanged([first, second], 0)
    keep, give = down(at, act, w_down, [first[0], second[0]])
    got = lax.ppermute(give, "core", SWAP)
    boxed = place(at, sel_dest.reshape(slots), x_mine, keep, got, [blocks[1][1]])
    boxed = boxed.reshape(32, 4, patch_rows, size)
    routed = lax.all_to_all(boxed, DP, split_axis=0, concat_axis=0, tiled=True)
    routed, token = copied(routed.reshape(128, patch_rows, size))
    blocks = [sum_blocks(part, 56 << 20) for part in blocks]
    blocks = [sum_blocks(part, 6 << 20) for part in exchanged(blocks, 1)]
    grad_down_t, grad_up = last_sum(exchanged(blocks, 2), [token], width)
    return (learnability, routed, grad_up, grad_down_t)


def solution(mesh):
    mesh = Mesh(mesh.devices.reshape(4, 4, 2, 2, 2), ("y", "x", "zl", "core", "zh"))
    pairs = P(("y", "x", "zl", "core"), None)
    patch = P(DP, "zh", "core")
    return jax.shard_map(
        local,
        mesh=mesh,
        in_specs=(
            pairs,
            pairs,
            pairs,
            pairs,
            patch,
            patch,
            P(None, "core"),
            P("core", None),
            P(DP),
            P(DP),
            P(DP, None),
        ),
        out_specs=(
            P(("y", "x", "zl", "core")),
            patch,
            P(CHIPS, "core"),
            P(CHIPS, "core"),
        ),
        check_vma=False,
    )
```

```python
import functools
import math

import jax
import jax.numpy as jnp
from jax import lax
from jax.experimental import pallas as pl
from jax.experimental.pallas import tpu as pltpu
from jax.sharding import Mesh, PartitionSpec as P

DP = ("y", "x", "zl")
CHIPS = ("y", "x", "zl", "zh")
SWAP = [(0, 1), (1, 0)]
ORDER = {"x": "xyz", "y": "yzx", "z": "zxy"}
WHOLE = pl.BlockSpec(memory_space=pltpu.VMEM)
SCALARS = pl.BlockSpec(memory_space=pltpu.SMEM)
UNREAD = pl.BlockSpec(memory_space=pl.ANY)
LIGHT = pl.CostEstimate(flops=1 << 20, bytes_accessed=1 << 16, transcendentals=0)


def unit(rows):
    wide = rows.astype(jnp.float32)
    norm = lax.rsqrt(jnp.sum(wide * wide, axis=1, keepdims=True) + 1e-06)
    return (wide * norm).astype(jnp.bfloat16)


def softplus(value):
    return jnp.maximum(value, 0.0) + jnp.log1p(jnp.exp(-jnp.abs(value)))


def loss_kernel(at, *refs):
    img_refs, txt_refs, txt_other, (out, img, txt) = refs[:4], refs[4:8], refs[8], refs[-3:]
    here_y, here_x, here_zl, here_core, learner = (at[k] for k in range(5))
    for k in range(4):
        img[pl.ds(128 * k, 128), :] = unit(img_refs[k][...])
        own = pl.multiple_of(128 * k + 64 * here_core, 64)
        txt[pl.ds(own, 64), :] = unit(txt_refs[k][...])
        other = pl.multiple_of(128 * k + 64 * (1 - here_core), 64)
        txt[pl.ds(other, 64), :] = unit(txt_other[pl.ds(64 * k, 64), :])
    contract = (((1,), (1,)), ((), ()))
    col_sum = jnp.zeros((1, 512), jnp.float32)
    row_sums = []
    for k in range(4):
        scores = (
            10.0
            * lax.dot_general(
                img[pl.ds(128 * k, 128), :], txt[...], contract, preferred_element_type=jnp.float32
            )
            - 5.0
        )
        if k == 0:
            row = lax.broadcasted_iota(jnp.int32, scores.shape, 0) - 64 * here_zl
            col = lax.broadcasted_iota(jnp.int32, scores.shape, 1) - 64 * here_core
            same = (row == col) & (row >= 0) & (row < 64)
            scores = jnp.where(same, -scores, scores)
        terms = softplus(scores)
        col_sum = col_sum + jnp.sum(terms, axis=0, keepdims=True)
        folded = terms[:, :128] + terms[:, 128:256] + terms[:, 256:384] + terms[:, 384:]
        row_sums.append(jnp.sum(folded.T, axis=0, keepdims=True))
    dest = lax.broadcasted_iota(jnp.int32, (128, 128), 0)
    lane = lax.broadcasted_iota(jnp.int32, (1, 128), 1)
    dest_y, dest_x, dest_zl = dest >> 5, (dest >> 3) & 3, (dest >> 2) & 1
    own_half = (lane >> 6) == here_core
    total = jnp.zeros((128, 128), jnp.float32)
    for k in range(4):
        straight = row_sums[k]
        crossed = pltpu.roll(straight, 64, 1)
        for zl in range(2):
            placed = jnp.where(own_half, jnp.where(here_core == zl, straight, crossed), 0.0)
            mine = (dest_y == here_y) & (dest_x == ((here_x + k) & 3)) & (dest_zl == zl)
            total = total + jnp.where(mine, placed, 0.0)
        mine = (dest_y == ((here_y + k) & 3)) & (dest_x == here_x) & (dest_zl == here_zl)
        total = total + jnp.where(mine, col_sum[:, 128 * k : 128 * (k + 1)], 0.0)
    out[...] = jnp.where(learner == 1, 0.5, -0.5) * total


def partial_losses(at, images, texts, texts_other, ready):
    return pl.pallas_call(
        loss_kernel,
        out_shape=jax.ShapeDtypeStruct((128, 128), jnp.float32),
        in_specs=[SCALARS] + [WHOLE] * 9 + [UNREAD] * len(ready),
        out_specs=WHOLE,
        scratch_shapes=[pltpu.VMEM((512, 1024), jnp.bfloat16)] * 2,
        compiler_params=pltpu.CompilerParams(vmem_limit_bytes=8 << 20),
        cost_estimate=LIGHT,
    )(at, *images, *texts, texts_other, *ready)


def listed(values, axis, shape):
    at = lax.broadcasted_iota(jnp.int32, shape, axis)
    out = jnp.zeros(shape, jnp.int32)
    for k in range(shape[axis]):
        out = jnp.where(at == k, values[k], out)
    return out


def weight_kernel(at, index, parts, *refs):
    learn, weight = refs[-2:]
    score = jnp.sum(parts[...], axis=0, keepdims=True)
    learn[...] = jnp.broadcast_to(score, (8, 128))
    slots = index.shape[0]
    picked = listed(index, 0, (slots, 128)) == lax.broadcasted_iota(jnp.int32, (slots, 128), 1)
    chosen = jnp.sum(jnp.where(picked, score, 0.0), axis=1, keepdims=True)
    live = lax.broadcasted_iota(jnp.int32, (slots, 128), 0) < at[5]
    value = jnp.where(live, 1.0 / (1.0 + jnp.exp(-chosen)), 0.0)
    weight[...] = jnp.broadcast_to(value[:, None, :], (slots, 8, 128)).reshape(8 * slots, 128)


def weights(at, index, parts, ready):
    slots = index.shape[0]
    return pl.pallas_call(
        weight_kernel,
        out_shape=(
            jax.ShapeDtypeStruct((8, 128), jnp.float32),
            jax.ShapeDtypeStruct((8 * slots, 128), jnp.float32),
        ),
        in_specs=[SCALARS, SCALARS, WHOLE] + [UNREAD] * len(ready),
        out_specs=(WHOLE, WHOLE),
        compiler_params=pltpu.CompilerParams(vmem_limit_bytes=2 << 20),
        cost_estimate=LIGHT,
    )(at, index, parts, *ready)


def pair_kernel(at, own, other, *refs):
    pair = refs[-1]
    pair[pl.ds(pl.multiple_of(64 * at[2], 64), 64), :] = own[...]
    pair[pl.ds(pl.multiple_of(64 * (1 - at[2]), 64), 64), :] = other[...]


def pair_rows(at, own, other, ready):
    rows, width = own.shape
    return pl.pallas_call(
        pair_kernel,
        out_shape=jax.ShapeDtypeStruct((2 * rows, width), own.dtype),
        in_specs=[SCALARS, WHOLE, WHOLE] + [UNREAD] * len(ready),
        out_specs=WHOLE,
        compiler_params=pltpu.CompilerParams(vmem_limit_bytes=2 << 20),
        cost_estimate=LIGHT,
    )(at, own, other, *ready)


def join_kernel(*refs):
    out = refs[-1]
    rows = refs[0].shape[0]
    for k, block in enumerate(refs[: out.shape[0] // rows]):
        out[k * rows : (k + 1) * rows, :] = block[...]


def join_rows(blocks, ready):
    rows, width = blocks[0].shape
    return pl.pallas_call(
        join_kernel,
        out_shape=jax.ShapeDtypeStruct((len(blocks) * rows, width), blocks[0].dtype),
        in_specs=[WHOLE] * len(blocks) + [UNREAD] * len(ready),
        out_specs=WHOLE,
        compiler_params=pltpu.CompilerParams(vmem_limit_bytes=2 << 20),
        cost_estimate=LIGHT,
    )(*blocks, *ready)


def half(ref, axis, which, size):
    start = pl.multiple_of(which * size, size)
    return ref[pl.ds(start, size), :] if axis == 0 else ref[:, pl.ds(start, size)]


def up_kernel(at, mine, other, w_up, *refs):
    act, slope, held, sems = refs[-4:]
    size = mine.shape[1]
    steps, _, tile = held.shape
    columns = [pl.ds(n * tile, tile) for n in range(steps)]
    copies = fetched([w_up.at[:, cols] for cols in columns], [held.at[n] for n in range(steps)], sems)
    scale = math.sqrt(2.0 / math.pi)
    for n, cols in enumerate(columns):
        copies[n].wait()
        near, far = half(held.at[n], 0, at[3], size), half(held.at[n], 0, 1 - at[3], size)
        for row in range(0, mine.shape[0], 256):
            rows = pl.ds(row, 256)
            pre = jnp.dot(mine[rows, :], near, preferred_element_type=jnp.float32)
            pre = pre + jnp.dot(other[rows, :], far, preferred_element_type=jnp.float32)
            square = pre * pre
            tanh = jnp.tanh(pre * (scale + (scale * 0.044715) * square))
            gate = 0.5 + 0.5 * tanh
            value = pre * gate
            act[rows, cols] = value.astype(jnp.bfloat16)
            bend = value * (1.0 - gate) * (2 * scale + (6 * scale * 0.044715) * square)
            slope[rows, cols] = (gate + bend).astype(jnp.bfloat16)


def up(at, mine, other, w_up, ready):
    rows, size = mine.shape
    width, tile = w_up.shape[1], 512
    return pl.pallas_call(
        up_kernel,
        out_shape=[jax.ShapeDtypeStruct((rows, width), jnp.bfloat16)] * 2,
        in_specs=[SCALARS, WHOLE, WHOLE, UNREAD] + [UNREAD] * len(ready),
        out_specs=[WHOLE, WHOLE],
        scratch_shapes=[
            pltpu.VMEM((width // tile, 2 * size, tile), w_up.dtype),
            pltpu.SemaphoreType.DMA((width // tile,)),
        ],
        compiler_params=pltpu.CompilerParams(vmem_limit_bytes=16 << 20),
        cost_estimate=LIGHT,
    )(at, mine, other, w_up, *ready)


def back_kernel(at, mine, other, w_down, slope, *refs):
    out, held, sems = refs[-3:]
    size = mine.shape[1]
    steps, tile, _ = held.shape
    columns = [pl.ds(n * tile, tile) for n in range(steps)]
    copies = fetched([w_down.at[cols] for cols in columns], [held.at[n] for n in range(steps)], sems)
    contract = (((1,), (1,)), ((), ()))
    for n, cols in enumerate(columns):
        copies[n].wait()
        near, far = half(held.at[n], 1, at[3], size), half(held.at[n], 1, 1 - at[3], size)
        back = lax.dot_general(mine[...], near, contract, preferred_element_type=jnp.float32)
        back = back + lax.dot_general(other[...], far, contract, preferred_element_type=jnp.float32)
        out[:, cols] = (back * slope[:, cols].astype(jnp.float32)).astype(jnp.bfloat16)


def back(at, mine, other, w_down, slope, ready):
    rows, size = mine.shape
    width, tile = w_down.shape[0], 512
    return pl.pallas_call(
        back_kernel,
        out_shape=jax.ShapeDtypeStruct((rows, width), jnp.bfloat16),
        in_specs=[SCALARS, WHOLE, WHOLE, UNREAD, WHOLE] + [UNREAD] * len(ready),
        out_specs=WHOLE,
        scratch_shapes=[
            pltpu.VMEM((width // tile, tile, 2 * size), w_down.dtype),
            pltpu.SemaphoreType.DMA((width // tile,)),
        ],
        compiler_params=pltpu.CompilerParams(vmem_limit_bytes=14 << 20),
        cost_estimate=LIGHT,
    )(at, mine, other, w_down, slope, *ready)


def turn_kernel(starts, at, mine, other, *refs):
    outs, turned = refs[len(refs) - 1 - len(starts) : -1], refs[-1]
    blocks = turned.shape[0] // 2
    turned[pl.ds(at[3] * blocks, blocks)] = mine[...].T.reshape((blocks,) + turned.shape[1:])
    turned[pl.ds((1 - at[3]) * blocks, blocks)] = other[...].T.reshape(
        (blocks,) + turned.shape[1:]
    )
    here = {"x": at[1], "y": at[0], "z": 2 * at[4] + at[2]}
    for start, out in zip(starts, outs):
        for k in range(2 * blocks):
            steps = (k >> 4, (k >> 2) & 3, k & 3)
            spot = {}
            for axis in "xyz":
                by = [steps[ORDER[one].index(axis)] for one in start]
                by = by[0] + at[3] * (by[-1] - by[0])
                spot[axis] = (here[axis] + by) & 3
            block = 16 * spot["y"] + 4 * spot["x"] + 2 * (spot["z"] & 1) + (spot["z"] >> 1)
            out[16 * k : 16 * (k + 1), :] = turned[block]


def turn(at, mine, other, starts, ready):
    rows, size = mine.shape
    return pl.pallas_call(
        functools.partial(turn_kernel, starts),
        out_shape=[jax.ShapeDtypeStruct((2 * size, rows), mine.dtype)] * len(starts),
        in_specs=[SCALARS, WHOLE, WHOLE] + [UNREAD] * len(ready),
        out_specs=[WHOLE] * len(starts),
        scratch_shapes=[pltpu.VMEM((2 * size // 16, 16, rows), mine.dtype)],
        compiler_params=pltpu.CompilerParams(vmem_limit_bytes=8 << 20),
        cost_estimate=LIGHT,
    )(at, mine, other, *ready)


def down_kernel(at, act, w_down, *refs):
    keep, give = refs[-2:]
    size = keep.shape[1]
    keep[...] = jnp.dot(
        act[...], half(w_down, 1, at[3], size), preferred_element_type=jnp.float32
    )
    give[...] = jnp.dot(
        act[...], half(w_down, 1, 1 - at[3], size), preferred_element_type=jnp.float32
    ).astype(jnp.bfloat16)


def down(at, act, w_down, ready):
    rows, size = act.shape[0], w_down.shape[1] // 2
    return pl.pallas_call(
        down_kernel,
        out_shape=[
            jax.ShapeDtypeStruct((rows, size), jnp.float32),
            jax.ShapeDtypeStruct((rows, size), jnp.bfloat16),
        ],
        in_specs=[SCALARS, WHOLE, WHOLE] + [UNREAD] * len(ready),
        out_specs=[WHOLE, WHOLE],
        compiler_params=pltpu.CompilerParams(vmem_limit_bytes=14 << 20),
        cost_estimate=LIGHT,
    )(at, act, w_down, *ready)


def place_kernel(here, target, own, keep, got, *refs):
    out = refs[-1]
    slots, rows = target.shape[0], own.shape[0]
    each = rows // slots
    out_rows = own[...].astype(jnp.float32) + keep[...] + got[...].astype(jnp.float32)
    out_rows = out_rows.astype(jnp.bfloat16)
    slot = lax.broadcasted_iota(jnp.int32, (slots, slots), 0)
    before = lax.broadcasted_iota(jnp.int32, (slots, slots), 1)
    to = listed(target, 0, (slots, slots))
    same = (listed(target, 1, (1, slots)) == to) & (before < slot)
    rank = jnp.sum(same.astype(jnp.int32), axis=1, keepdims=True)
    live = slot[:, :1] < here[5]
    first = jnp.where(live, each * (4 * to[:, :1] + rank), -each)
    lane = lax.broadcasted_iota(jnp.int32, (slots, rows), 1)
    mine = (lane // each) == lax.broadcasted_iota(jnp.int32, (slots, rows), 0)
    goes = jnp.sum(jnp.where(mine, first + lane % each, 0), axis=0, keepdims=True)
    step = 256
    for at in range(0, out.shape[0], step):
        reached = lax.broadcasted_iota(jnp.int32, (step, rows), 0) + at == goes
        out[at : at + step, :] = jnp.dot(
            jnp.where(reached, 1.0, 0.0).astype(jnp.bfloat16),
            out_rows,
            preferred_element_type=jnp.float32,
        ).astype(jnp.bfloat16)


def place(at, target, own, keep, got, ready):
    rows, size = own.shape
    return pl.pallas_call(
        place_kernel,
        out_shape=jax.ShapeDtypeStruct((2 * rows, size), jnp.bfloat16),
        in_specs=[SCALARS, SCALARS] + [WHOLE] * 3 + [UNREAD] * len(ready),
        out_specs=WHOLE,
        compiler_params=pltpu.CompilerParams(vmem_limit_bytes=8 << 20),
        cost_estimate=LIGHT,
    )(at, target, own, keep, got, *ready)


def around(block, axis):
    return [block] + [shift(block, axis, 4 - by) for by in (1, 2, 3)]


def shift(block, axis, by):
    if axis == "z":
        at = [(z % 2) * 2 + z // 2 for z in range(4)]
        return lax.ppermute(block, ("zl", "zh"), [(at[z], at[(z + by) % 4]) for z in range(4)])
    return lax.ppermute(block, axis, [(k, (k + by) % 4) for k in range(4)])


def number(spot, core):
    return 8 * (4 * spot["y"] + spot["x"]) + 4 * (spot["z"] % 2) + 2 * core + spot["z"] // 2


def shift_each(block, axes, by):
    route = []
    for chip in range(64):
        spot = {"x": chip % 4, "y": chip // 4 % 4, "z": chip // 16}
        for core in range(2):
            axis = axes[core]
            there = {**spot, axis: (spot[axis] + by) % 4}
            route.append((number(spot, core), number(there, core)))
    return lax.ppermute(block, ("y", "x", "zl", "core", "zh"), route)


def fetched(sources, targets, sems):
    copies = [
        pltpu.make_async_copy(source, target, sems.at[k])
        for k, (source, target) in enumerate(zip(sources, targets))
    ]
    for copy in copies:
        copy.start()
    return copies


def product_kernel(pieces, weight, *refs):
    lefts = 1 + max(piece[0] for piece in pieces)
    rights = 1 + max(piece[1] for piece in pieces)
    count = lefts + rights
    sources, rest = refs[:count], refs[len(refs) - count - 6 :]
    outs, held, scaled, sems = rest[:4], rest[4 : 4 + count], rest[-2], rest[-1]
    copies = []
    for left, right, first, last in pieces:
        cols = pl.ds(first, last - first)
        right = lefts + right
        copies.append(
            [
                pltpu.make_async_copy(
                    sources[right].at[:, cols], held[right].at[:, cols], sems.at[right]
                ),
                pltpu.make_async_copy(sources[left], held[left], sems.at[left]),
            ]
        )
    for copy in copies[0]:
        copy.start()
    rows = weight[...]
    depth = outs[0].shape[0]
    done = 0
    for number, (left, right, first, last) in enumerate(pieces):
        copies[number][0].wait()
        if number + 1 < len(pieces):
            for copy in copies[number + 1]:
                copy.start()
        for col in range(first, last, 128):
            piece = held[lefts + right][:, col : col + 128].astype(jnp.float32) * rows
            scaled[:, col - first : col - first + 128] = piece.astype(jnp.bfloat16)
        copies[number][1].wait()
        for col in range(0, last - first, 256):
            end = min(col + 256, last - first)
            product = jnp.dot(held[left][...], scaled[:, col:end], preferred_element_type=jnp.float32)
            for k in range(4):
                outs[k][:, done + col : done + end] = product[depth * k : depth * (k + 1)].astype(
                    jnp.bfloat16
                )
        done += last - first


def products(weight, lefts, rights, pieces, ready=()):
    width = sum(last - first for _, _, first, last in pieces)
    sides = [*lefts, *rights]
    depth = weight.shape[0]
    return pl.pallas_call(
        functools.partial(product_kernel, pieces),
        out_shape=[jax.ShapeDtypeStruct((256, width), jnp.bfloat16)] * 4,
        in_specs=[WHOLE] + [UNREAD] * len(sides) + [UNREAD] * len(ready),
        out_specs=[WHOLE] * 4,
        scratch_shapes=[pltpu.VMEM(side.shape, side.dtype) for side in sides]
        + [
            pltpu.VMEM((depth, max(piece[3] - piece[2] for piece in pieces)), jnp.bfloat16),
            pltpu.SemaphoreType.DMA((len(sides),)),
        ],
        compiler_params=pltpu.CompilerParams(vmem_limit_bytes=20 << 20),
        cost_estimate=LIGHT,
    )(weight, *sides, *ready)


def sum_kernel(*refs):
    sources, outs, held, sems = refs[:4], refs[-9:-5], refs[-5:-1], refs[-1]
    copies = fetched(sources, held, sems)
    for copy in copies:
        copy.wait()
    rows = outs[0].shape[0]
    for k in range(4):
        here = pl.ds(k * rows, rows)
        total = held[0][here, :].astype(jnp.float32)
        for ref in held[1:]:
            total = total + ref[here, :].astype(jnp.float32)
        outs[k][...] = total.astype(jnp.bfloat16)


def sum_blocks(blocks, grant, ready=()):
    rows, width = blocks[0].shape
    return pl.pallas_call(
        sum_kernel,
        out_shape=[jax.ShapeDtypeStruct((rows // 4, width), jnp.bfloat16)] * 4,
        in_specs=[UNREAD] * (4 + len(ready)),
        out_specs=[WHOLE] * 4,
        scratch_shapes=[pltpu.VMEM(block.shape, block.dtype) for block in blocks]
        + [pltpu.SemaphoreType.DMA((4,))],
        compiler_params=pltpu.CompilerParams(vmem_limit_bytes=grant),
        cost_estimate=LIGHT,
    )(*blocks, *ready)


def copy_kernel(source, out, token):
    out[...] = source[...]
    token[...] = jnp.zeros(token.shape, token.dtype)


def copied(block):
    return pl.pallas_call(
        copy_kernel,
        out_shape=(
            jax.ShapeDtypeStruct(block.shape, block.dtype),
            jax.ShapeDtypeStruct((8, 128), jnp.float32),
        ),
        in_specs=[WHOLE],
        out_specs=(WHOLE, WHOLE),
        compiler_params=pltpu.CompilerParams(vmem_limit_bytes=4 << 20),
        cost_estimate=LIGHT,
    )(block)


def last_kernel(*refs):
    down, up = refs[-2:]
    sums = []
    for part in range(2):
        total = refs[4 * part][...].astype(jnp.float32)
        for ref in refs[4 * part + 1 : 4 * part + 4]:
            total = total + ref[...].astype(jnp.float32)
        sums.append(total)
    width = down.shape[1]
    cut = sums[0].shape[1] - width
    down[...] = sums[0][:, :width]
    up[:, :cut] = sums[0][:, width:]
    up[:, cut:] = sums[1]


def last_sum(parts, ready, width):
    return pl.pallas_call(
        last_kernel,
        out_shape=[jax.ShapeDtypeStruct((16, width), jnp.float32)] * 2,
        in_specs=[WHOLE] * 8 + [UNREAD] * len(ready),
        out_specs=[WHOLE] * 2,
        compiler_params=pltpu.CompilerParams(vmem_limit_bytes=4 << 20),
        cost_estimate=LIGHT,
    )(*[block for part in parts for block in part], *ready)


def exchanged(parts, step):
    first, second = parts
    axes = (ORDER["x"][step], ORDER["y"][step])
    return [
        [first[0]] + [shift_each(first[by], axes, by) for by in (2, 1, 3)],
        [second[0]] + [shift(second[by], ORDER["z"][step], by) for by in (2, 1, 3)],
    ]


def local(
    ref_image,
    ref_text,
    learner_image,
    learner_text,
    patches,
    cotangent,
    w_up,
    w_down,
    counts,
    sel_index,
    sel_dest,
):
    core = lax.axis_index("core")
    at = [lax.axis_index(name) for name in ("y", "x", "zl", "core", "zh")]
    at = jnp.stack([*at, counts[0]]).astype(jnp.int32)
    slots = sel_index.shape[0]
    patch_rows, size = patches.shape[1:]
    count, width, rows = slots * patch_rows, w_up.shape[1], ref_image.shape[0]

    learner = lax.axis_index("zh") == 1
    pad = ((0, 0), (0, learner_image.shape[1] - ref_image.shape[1]))
    x_mine = patches[sel_index].reshape(count, size)
    cot_mine = cotangent[sel_index].reshape(count, size)
    learner_image, learner_text, x_mine, cot_mine, at = lax.optimization_barrier(
        (learner_image, learner_text, x_mine, cot_mine, at)
    )
    image = jnp.where(learner, learner_image, jnp.pad(ref_image, pad))
    text = jnp.where(learner, learner_text, jnp.pad(ref_text, pad))
    other_image = lax.ppermute(image, "zl", SWAP)
    x_other = lax.ppermute(x_mine, "core", SWAP)
    cot_other = lax.ppermute(cot_mine, "core", SWAP)
    texts = around(text, "y")
    joined = join_rows(texts, [other_image, x_other, cot_mine])
    texts_other = lax.ppermute(joined, "core", SWAP)
    pair = pair_rows(at, image, other_image, [joined])
    images = around(pair, "x")

    act, slope = up(at, x_mine, x_other, w_up, [pair])
    x_first, x_second = turn(at, x_mine, x_other, ("xy", "z"), [pair])

    grad_pre = back(at, cot_mine, cot_other, w_down, slope, [])
    (cot_first,) = turn(at, cot_mine, cot_other, ("xy",), [])

    parts = partial_losses(at, images, texts, texts_other, [x_first, grad_pre, cot_first])
    parts = lax.all_to_all(
        parts, ("y", "x", "zl", "core", "zh"), split_axis=0, concat_axis=0, tiled=True
    )
    scores, weight = weights(at, sel_index, parts, [])
    learnability = lax.dynamic_slice_in_dim(scores[0], core * rows, rows)

    cut = 384
    second = products(weight, [x_second], [grad_pre], ((0, 0, cut, width),))
    first = products(
        weight,
        [cot_first, x_first],
        [act, grad_pre],
        ((0, 0, 0, width), (1, 1, 0, cut)),
        second[:1],
    )
    blocks = exchanged([first, second], 0)
    keep, give = down(at, act, w_down, [first[0], second[0]])
    got = lax.ppermute(give, "core", SWAP)
    boxed = place(at, sel_dest.reshape(slots), x_mine, keep, got, [blocks[1][1]])
    boxed = boxed.reshape(32, 4, patch_rows, size)
    routed = lax.all_to_all(boxed, DP, split_axis=0, concat_axis=0, tiled=True)
    routed, token = copied(routed.reshape(128, patch_rows, size))
    blocks = [sum_blocks(part, 56 << 20) for part in blocks]
    blocks = [sum_blocks(part, 6 << 20) for part in exchanged(blocks, 1)]
    grad_down_t, grad_up = last_sum(exchanged(blocks, 2), [token], width)
    return (learnability, routed, grad_up, grad_down_t)


def solution(mesh):
    mesh = Mesh(mesh.devices.reshape(4, 4, 2, 2, 2), ("y", "x", "zl", "core", "zh"))
    pairs = P(("y", "x", "zl", "core"), None)
    patch = P(DP, "zh", "core")
    return jax.shard_map(
        local,
        mesh=mesh,
        in_specs=(
            pairs,
            pairs,
            pairs,
            pairs,
            patch,
            patch,
            P(None, "core"),
            P("core", None),
            P(DP),
            P(DP),
            P(DP, None),
        ),
        out_specs=(
            P(("y", "x", "zl", "core")),
            patch,
            P(CHIPS, "core"),
            P(CHIPS, "core"),
        ),
        check_vma=False,
    )
```

```python
import functools
import math

import jax
import jax.numpy as jnp
from jax import lax
from jax.experimental import pallas as pl
from jax.experimental.pallas import tpu as pltpu
from jax.sharding import Mesh, PartitionSpec as P

DP = ("y", "x", "zl")
CHIPS = ("y", "x", "zl", "zh")
SWAP = [(0, 1), (1, 0)]
ORDER = {"x": "xyz", "y": "yzx", "z": "zxy"}
WHOLE = pl.BlockSpec(memory_space=pltpu.VMEM)
SCALARS = pl.BlockSpec(memory_space=pltpu.SMEM)
UNREAD = pl.BlockSpec(memory_space=pl.ANY)
LIGHT = pl.CostEstimate(flops=1 << 20, bytes_accessed=1 << 16, transcendentals=0)


def unit(rows):
    wide = rows.astype(jnp.float32)
    norm = lax.rsqrt(jnp.sum(wide * wide, axis=1, keepdims=True) + 1e-06)
    return (wide * norm).astype(jnp.bfloat16)


def softplus(value):
    return jnp.maximum(value, 0.0) + jnp.log1p(jnp.exp(-jnp.abs(value)))


def loss_kernel(at, *refs):
    img_refs, txt_refs, txt_other, (out, img, txt) = refs[:4], refs[4:8], refs[8], refs[-3:]
    here_y, here_x, here_zl, here_core, learner = (at[k] for k in range(5))
    for k in range(4):
        img[pl.ds(128 * k, 128), :] = unit(img_refs[k][...])
        own = pl.multiple_of(128 * k + 64 * here_core, 64)
        txt[pl.ds(own, 64), :] = unit(txt_refs[k][...])
        other = pl.multiple_of(128 * k + 64 * (1 - here_core), 64)
        txt[pl.ds(other, 64), :] = unit(txt_other[pl.ds(64 * k, 64), :])
    contract = (((1,), (1,)), ((), ()))
    col_sum = jnp.zeros((1, 512), jnp.float32)
    row_sums = []
    for k in range(4):
        scores = (
            10.0
            * lax.dot_general(
                img[pl.ds(128 * k, 128), :], txt[...], contract, preferred_element_type=jnp.float32
            )
            - 5.0
        )
        if k == 0:
            row = lax.broadcasted_iota(jnp.int32, scores.shape, 0) - 64 * here_zl
            col = lax.broadcasted_iota(jnp.int32, scores.shape, 1) - 64 * here_core
            same = (row == col) & (row >= 0) & (row < 64)
            scores = jnp.where(same, -scores, scores)
        terms = softplus(scores)
        col_sum = col_sum + jnp.sum(terms, axis=0, keepdims=True)
        folded = terms[:, :128] + terms[:, 128:256] + terms[:, 256:384] + terms[:, 384:]
        row_sums.append(jnp.sum(folded.T, axis=0, keepdims=True))
    dest = lax.broadcasted_iota(jnp.int32, (128, 128), 0)
    lane = lax.broadcasted_iota(jnp.int32, (1, 128), 1)
    dest_y, dest_x, dest_zl = dest >> 5, (dest >> 3) & 3, (dest >> 2) & 1
    own_half = (lane >> 6) == here_core
    total = jnp.zeros((128, 128), jnp.float32)
    for k in range(4):
        straight = row_sums[k]
        crossed = pltpu.roll(straight, 64, 1)
        for zl in range(2):
            placed = jnp.where(own_half, jnp.where(here_core == zl, straight, crossed), 0.0)
            mine = (dest_y == here_y) & (dest_x == ((here_x + k) & 3)) & (dest_zl == zl)
            total = total + jnp.where(mine, placed, 0.0)
        mine = (dest_y == ((here_y + k) & 3)) & (dest_x == here_x) & (dest_zl == here_zl)
        total = total + jnp.where(mine, col_sum[:, 128 * k : 128 * (k + 1)], 0.0)
    out[...] = jnp.where(learner == 1, 0.5, -0.5) * total


def partial_losses(at, images, texts, texts_other, ready):
    return pl.pallas_call(
        loss_kernel,
        out_shape=jax.ShapeDtypeStruct((128, 128), jnp.float32),
        in_specs=[SCALARS] + [WHOLE] * 9 + [UNREAD] * len(ready),
        out_specs=WHOLE,
        scratch_shapes=[pltpu.VMEM((512, 1024), jnp.bfloat16)] * 2,
        compiler_params=pltpu.CompilerParams(vmem_limit_bytes=8 << 20),
        cost_estimate=LIGHT,
    )(at, *images, *texts, texts_other, *ready)


def listed(values, axis, shape):
    at = lax.broadcasted_iota(jnp.int32, shape, axis)
    out = jnp.zeros(shape, jnp.int32)
    for k in range(shape[axis]):
        out = jnp.where(at == k, values[k], out)
    return out


def weight_kernel(at, index, parts, *refs):
    learn, weight = refs[-2:]
    score = jnp.sum(parts[...], axis=0, keepdims=True)
    learn[...] = jnp.broadcast_to(score, (8, 128))
    slots = index.shape[0]
    picked = listed(index, 0, (slots, 128)) == lax.broadcasted_iota(jnp.int32, (slots, 128), 1)
    chosen = jnp.sum(jnp.where(picked, score, 0.0), axis=1, keepdims=True)
    live = lax.broadcasted_iota(jnp.int32, (slots, 128), 0) < at[5]
    value = jnp.where(live, 1.0 / (1.0 + jnp.exp(-chosen)), 0.0)
    weight[...] = jnp.broadcast_to(value[:, None, :], (slots, 8, 128)).reshape(8 * slots, 128)


def weights(at, index, parts, ready):
    slots = index.shape[0]
    return pl.pallas_call(
        weight_kernel,
        out_shape=(
            jax.ShapeDtypeStruct((8, 128), jnp.float32),
            jax.ShapeDtypeStruct((8 * slots, 128), jnp.float32),
        ),
        in_specs=[SCALARS, SCALARS, WHOLE] + [UNREAD] * len(ready),
        out_specs=(WHOLE, WHOLE),
        compiler_params=pltpu.CompilerParams(vmem_limit_bytes=2 << 20),
        cost_estimate=LIGHT,
    )(at, index, parts, *ready)


def pair_kernel(at, own, other, *refs):
    pair = refs[-1]
    pair[pl.ds(pl.multiple_of(64 * at[2], 64), 64), :] = own[...]
    pair[pl.ds(pl.multiple_of(64 * (1 - at[2]), 64), 64), :] = other[...]


def pair_rows(at, own, other, ready):
    rows, width = own.shape
    return pl.pallas_call(
        pair_kernel,
        out_shape=jax.ShapeDtypeStruct((2 * rows, width), own.dtype),
        in_specs=[SCALARS, WHOLE, WHOLE] + [UNREAD] * len(ready),
        out_specs=WHOLE,
        compiler_params=pltpu.CompilerParams(vmem_limit_bytes=2 << 20),
        cost_estimate=LIGHT,
    )(at, own, other, *ready)


def join_kernel(*refs):
    out = refs[-1]
    rows = refs[0].shape[0]
    for k, block in enumerate(refs[: out.shape[0] // rows]):
        out[k * rows : (k + 1) * rows, :] = block[...]


def join_rows(blocks, ready):
    rows, width = blocks[0].shape
    return pl.pallas_call(
        join_kernel,
        out_shape=jax.ShapeDtypeStruct((len(blocks) * rows, width), blocks[0].dtype),
        in_specs=[WHOLE] * len(blocks) + [UNREAD] * len(ready),
        out_specs=WHOLE,
        compiler_params=pltpu.CompilerParams(vmem_limit_bytes=2 << 20),
        cost_estimate=LIGHT,
    )(*blocks, *ready)


def half(ref, axis, which, size):
    start = pl.multiple_of(which * size, size)
    return ref[pl.ds(start, size), :] if axis == 0 else ref[:, pl.ds(start, size)]


def up_kernel(at, mine, other, w_up, *refs):
    act, slope, held, sems = refs[-4:]
    size = mine.shape[1]
    steps, _, tile = held.shape
    columns = [pl.ds(n * tile, tile) for n in range(steps)]
    copies = fetched([w_up.at[:, cols] for cols in columns], [held.at[n] for n in range(steps)], sems)
    scale = math.sqrt(2.0 / math.pi)
    for n, cols in enumerate(columns):
        copies[n].wait()
        near, far = half(held.at[n], 0, at[3], size), half(held.at[n], 0, 1 - at[3], size)
        for row in range(0, mine.shape[0], 256):
            rows = pl.ds(row, 256)
            pre = jnp.dot(mine[rows, :], near, preferred_element_type=jnp.float32)
            pre = pre + jnp.dot(other[rows, :], far, preferred_element_type=jnp.float32)
            square = pre * pre
            tanh = jnp.tanh(pre * (scale + (scale * 0.044715) * square))
            gate = 0.5 + 0.5 * tanh
            value = pre * gate
            act[rows, cols] = value.astype(jnp.bfloat16)
            bend = value * (1.0 - gate) * (2 * scale + (6 * scale * 0.044715) * square)
            slope[rows, cols] = (gate + bend).astype(jnp.bfloat16)


def up(at, mine, other, w_up, ready):
    rows, size = mine.shape
    width, tile = w_up.shape[1], 512
    return pl.pallas_call(
        up_kernel,
        out_shape=[jax.ShapeDtypeStruct((rows, width), jnp.bfloat16)] * 2,
        in_specs=[SCALARS, WHOLE, WHOLE, UNREAD] + [UNREAD] * len(ready),
        out_specs=[WHOLE, WHOLE],
        scratch_shapes=[
            pltpu.VMEM((width // tile, 2 * size, tile), w_up.dtype),
            pltpu.SemaphoreType.DMA((width // tile,)),
        ],
        compiler_params=pltpu.CompilerParams(vmem_limit_bytes=16 << 20),
        cost_estimate=LIGHT,
    )(at, mine, other, w_up, *ready)


def back_kernel(at, mine, other, w_down, slope, *refs):
    out, held, sems = refs[-3:]
    size = mine.shape[1]
    steps, tile, _ = held.shape
    columns = [pl.ds(n * tile, tile) for n in range(steps)]
    copies = fetched([w_down.at[cols] for cols in columns], [held.at[n] for n in range(steps)], sems)
    contract = (((1,), (1,)), ((), ()))
    for n, cols in enumerate(columns):
        copies[n].wait()
        near, far = half(held.at[n], 1, at[3], size), half(held.at[n], 1, 1 - at[3], size)
        back = lax.dot_general(mine[...], near, contract, preferred_element_type=jnp.float32)
        back = back + lax.dot_general(other[...], far, contract, preferred_element_type=jnp.float32)
        out[:, cols] = (back * slope[:, cols].astype(jnp.float32)).astype(jnp.bfloat16)


def back(at, mine, other, w_down, slope, ready):
    rows, size = mine.shape
    width, tile = w_down.shape[0], 512
    return pl.pallas_call(
        back_kernel,
        out_shape=jax.ShapeDtypeStruct((rows, width), jnp.bfloat16),
        in_specs=[SCALARS, WHOLE, WHOLE, UNREAD, WHOLE] + [UNREAD] * len(ready),
        out_specs=WHOLE,
        scratch_shapes=[
            pltpu.VMEM((width // tile, tile, 2 * size), w_down.dtype),
            pltpu.SemaphoreType.DMA((width // tile,)),
        ],
        compiler_params=pltpu.CompilerParams(vmem_limit_bytes=14 << 20),
        cost_estimate=LIGHT,
    )(at, mine, other, w_down, slope, *ready)


def turn_kernel(starts, at, mine, other, *refs):
    outs, turned = refs[len(refs) - 1 - len(starts) : -1], refs[-1]
    blocks = turned.shape[0] // 2
    turned[pl.ds(at[3] * blocks, blocks)] = mine[...].T.reshape((blocks,) + turned.shape[1:])
    turned[pl.ds((1 - at[3]) * blocks, blocks)] = other[...].T.reshape(
        (blocks,) + turned.shape[1:]
    )
    here = {"x": at[1], "y": at[0], "z": 2 * at[4] + at[2]}
    for start, out in zip(starts, outs):
        for k in range(2 * blocks):
            steps = (k >> 4, (k >> 2) & 3, k & 3)
            spot = {}
            for axis in "xyz":
                by = [steps[ORDER[one].index(axis)] for one in start]
                by = by[0] + at[3] * (by[-1] - by[0])
                spot[axis] = (here[axis] + by) & 3
            block = 16 * spot["y"] + 4 * spot["x"] + 2 * (spot["z"] & 1) + (spot["z"] >> 1)
            out[16 * k : 16 * (k + 1), :] = turned[block]


def turn(at, mine, other, starts, ready):
    rows, size = mine.shape
    return pl.pallas_call(
        functools.partial(turn_kernel, starts),
        out_shape=[jax.ShapeDtypeStruct((2 * size, rows), mine.dtype)] * len(starts),
        in_specs=[SCALARS, WHOLE, WHOLE] + [UNREAD] * len(ready),
        out_specs=[WHOLE] * len(starts),
        scratch_shapes=[pltpu.VMEM((2 * size // 16, 16, rows), mine.dtype)],
        compiler_params=pltpu.CompilerParams(vmem_limit_bytes=8 << 20),
        cost_estimate=LIGHT,
    )(at, mine, other, *ready)


def down_kernel(at, act, w_down, *refs):
    keep, give = refs[-2:]
    size = keep.shape[1]
    keep[...] = jnp.dot(
        act[...], half(w_down, 1, at[3], size), preferred_element_type=jnp.float32
    )
    give[...] = jnp.dot(
        act[...], half(w_down, 1, 1 - at[3], size), preferred_element_type=jnp.float32
    ).astype(jnp.bfloat16)


def down(at, act, w_down, ready):
    rows, size = act.shape[0], w_down.shape[1] // 2
    return pl.pallas_call(
        down_kernel,
        out_shape=[
            jax.ShapeDtypeStruct((rows, size), jnp.float32),
            jax.ShapeDtypeStruct((rows, size), jnp.bfloat16),
        ],
        in_specs=[SCALARS, WHOLE, WHOLE] + [UNREAD] * len(ready),
        out_specs=[WHOLE, WHOLE],
        compiler_params=pltpu.CompilerParams(vmem_limit_bytes=14 << 20),
        cost_estimate=LIGHT,
    )(at, act, w_down, *ready)


def place_kernel(here, target, own, keep, got, *refs):
    out = refs[-1]
    slots, rows = target.shape[0], own.shape[0]
    each = rows // slots
    out_rows = own[...].astype(jnp.float32) + keep[...] + got[...].astype(jnp.float32)
    out_rows = out_rows.astype(jnp.bfloat16)
    slot = lax.broadcasted_iota(jnp.int32, (slots, slots), 0)
    before = lax.broadcasted_iota(jnp.int32, (slots, slots), 1)
    to = listed(target, 0, (slots, slots))
    same = (listed(target, 1, (1, slots)) == to) & (before < slot)
    rank = jnp.sum(same.astype(jnp.int32), axis=1, keepdims=True)
    live = slot[:, :1] < here[5]
    first = jnp.where(live, each * (4 * to[:, :1] + rank), -each)
    lane = lax.broadcasted_iota(jnp.int32, (slots, rows), 1)
    mine = (lane // each) == lax.broadcasted_iota(jnp.int32, (slots, rows), 0)
    goes = jnp.sum(jnp.where(mine, first + lane % each, 0), axis=0, keepdims=True)
    step = 256
    for at in range(0, out.shape[0], step):
        reached = lax.broadcasted_iota(jnp.int32, (step, rows), 0) + at == goes
        out[at : at + step, :] = jnp.dot(
            jnp.where(reached, 1.0, 0.0).astype(jnp.bfloat16),
            out_rows,
            preferred_element_type=jnp.float32,
        ).astype(jnp.bfloat16)


def place(at, target, own, keep, got, ready):
    rows, size = own.shape
    return pl.pallas_call(
        place_kernel,
        out_shape=jax.ShapeDtypeStruct((2 * rows, size), jnp.bfloat16),
        in_specs=[SCALARS, SCALARS] + [WHOLE] * 3 + [UNREAD] * len(ready),
        out_specs=WHOLE,
        compiler_params=pltpu.CompilerParams(vmem_limit_bytes=8 << 20),
        cost_estimate=LIGHT,
    )(at, target, own, keep, got, *ready)


def around(block, axis):
    return [block] + [shift(block, axis, 4 - by) for by in (1, 2, 3)]


def shift(block, axis, by):
    if axis == "z":
        at = [(z % 2) * 2 + z // 2 for z in range(4)]
        return lax.ppermute(block, ("zl", "zh"), [(at[z], at[(z + by) % 4]) for z in range(4)])
    return lax.ppermute(block, axis, [(k, (k + by) % 4) for k in range(4)])


def number(spot, core):
    return 8 * (4 * spot["y"] + spot["x"]) + 4 * (spot["z"] % 2) + 2 * core + spot["z"] // 2


def shift_each(block, axes, by):
    route = []
    for chip in range(64):
        spot = {"x": chip % 4, "y": chip // 4 % 4, "z": chip // 16}
        for core in range(2):
            axis = axes[core]
            there = {**spot, axis: (spot[axis] + by) % 4}
            route.append((number(spot, core), number(there, core)))
    return lax.ppermute(block, ("y", "x", "zl", "core", "zh"), route)


def fetched(sources, targets, sems):
    copies = [
        pltpu.make_async_copy(source, target, sems.at[k])
        for k, (source, target) in enumerate(zip(sources, targets))
    ]
    for copy in copies:
        copy.start()
    return copies


def product_kernel(pieces, weight, *refs):
    lefts = 1 + max(piece[0] for piece in pieces)
    rights = 1 + max(piece[1] for piece in pieces)
    count = lefts + rights
    sources, rest = refs[:count], refs[len(refs) - count - 6 :]
    outs, held, scaled, sems = rest[:4], rest[4 : 4 + count], rest[-2], rest[-1]
    copies = fetched(sources, held, sems)
    rows = weight[...]
    depth = outs[0].shape[0]
    done = 0
    seen = set()
    for left, right, first, last in pieces:
        for k in (lefts + right, left):
            if k not in seen:
                copies[k].wait()
                seen.add(k)
        for col in range(first, last, 128):
            piece = held[lefts + right][:, col : col + 128].astype(jnp.float32) * rows
            scaled[:, col - first : col - first + 128] = piece.astype(jnp.bfloat16)
        for col in range(0, last - first, 256):
            end = min(col + 256, last - first)
            product = jnp.dot(held[left][...], scaled[:, col:end], preferred_element_type=jnp.float32)
            for k in range(4):
                outs[k][:, done + col : done + end] = product[depth * k : depth * (k + 1)].astype(
                    jnp.bfloat16
                )
        done += last - first


def products(weight, lefts, rights, pieces, ready=()):
    width = sum(last - first for _, _, first, last in pieces)
    sides = [*lefts, *rights]
    depth = weight.shape[0]
    return pl.pallas_call(
        functools.partial(product_kernel, pieces),
        out_shape=[jax.ShapeDtypeStruct((256, width), jnp.bfloat16)] * 4,
        in_specs=[WHOLE] + [UNREAD] * len(sides) + [UNREAD] * len(ready),
        out_specs=[WHOLE] * 4,
        scratch_shapes=[pltpu.VMEM(side.shape, side.dtype) for side in sides]
        + [
            pltpu.VMEM((depth, max(piece[3] - piece[2] for piece in pieces)), jnp.bfloat16),
            pltpu.SemaphoreType.DMA((len(sides),)),
        ],
        compiler_params=pltpu.CompilerParams(vmem_limit_bytes=20 << 20),
        cost_estimate=LIGHT,
    )(weight, *sides, *ready)


def sum_kernel(*refs):
    sources, outs, held, sems = refs[:4], refs[-9:-5], refs[-5:-1], refs[-1]
    copies = fetched(sources, held, sems)
    for copy in copies:
        copy.wait()
    rows = outs[0].shape[0]
    for k in range(4):
        here = pl.ds(k * rows, rows)
        total = held[0][here, :].astype(jnp.float32)
        for ref in held[1:]:
            total = total + ref[here, :].astype(jnp.float32)
        outs[k][...] = total.astype(jnp.bfloat16)


def sum_blocks(blocks, grant, ready=()):
    rows, width = blocks[0].shape
    return pl.pallas_call(
        sum_kernel,
        out_shape=[jax.ShapeDtypeStruct((rows // 4, width), jnp.bfloat16)] * 4,
        in_specs=[UNREAD] * (4 + len(ready)),
        out_specs=[WHOLE] * 4,
        scratch_shapes=[pltpu.VMEM(block.shape, block.dtype) for block in blocks]
        + [pltpu.SemaphoreType.DMA((4,))],
        compiler_params=pltpu.CompilerParams(vmem_limit_bytes=grant),
        cost_estimate=LIGHT,
    )(*blocks, *ready)


def copy_kernel(source, out, token):
    out[...] = source[...]
    token[...] = jnp.zeros(token.shape, token.dtype)


def copied(block):
    return pl.pallas_call(
        copy_kernel,
        out_shape=(
            jax.ShapeDtypeStruct(block.shape, block.dtype),
            jax.ShapeDtypeStruct((8, 128), jnp.float32),
        ),
        in_specs=[WHOLE],
        out_specs=(WHOLE, WHOLE),
        compiler_params=pltpu.CompilerParams(vmem_limit_bytes=4 << 20),
        cost_estimate=LIGHT,
    )(block)


def last_kernel(*refs):
    down, up = refs[-2:]
    sums = []
    for part in range(2):
        total = refs[4 * part][...].astype(jnp.float32)
        for ref in refs[4 * part + 1 : 4 * part + 4]:
            total = total + ref[...].astype(jnp.float32)
        sums.append(total)
    width = down.shape[1]
    cut = sums[0].shape[1] - width
    down[...] = sums[0][:, :width]
    up[:, :cut] = sums[0][:, width:]
    up[:, cut:] = sums[1]


def last_sum(parts, ready, width):
    return pl.pallas_call(
        last_kernel,
        out_shape=[jax.ShapeDtypeStruct((16, width), jnp.float32)] * 2,
        in_specs=[WHOLE] * 8 + [UNREAD] * len(ready),
        out_specs=[WHOLE] * 2,
        compiler_params=pltpu.CompilerParams(vmem_limit_bytes=4 << 20),
        cost_estimate=LIGHT,
    )(*[block for part in parts for block in part], *ready)


def exchanged(parts, step):
    first, second = parts
    axes = (ORDER["x"][step], ORDER["y"][step])
    return [
        [first[0]] + [shift_each(first[by], axes, by) for by in (2, 1, 3)],
        [second[0]] + [shift(second[by], ORDER["z"][step], by) for by in (2, 1, 3)],
    ]


def local(
    ref_image,
    ref_text,
    learner_image,
    learner_text,
    patches,
    cotangent,
    w_up,
    w_down,
    counts,
    sel_index,
    sel_dest,
):
    core = lax.axis_index("core")
    at = [lax.axis_index(name) for name in ("y", "x", "zl", "core", "zh")]
    at = jnp.stack([*at, counts[0]]).astype(jnp.int32)
    slots = sel_index.shape[0]
    patch_rows, size = patches.shape[1:]
    count, width, rows = slots * patch_rows, w_up.shape[1], ref_image.shape[0]

    learner = lax.axis_index("zh") == 1
    pad = ((0, 0), (0, learner_image.shape[1] - ref_image.shape[1]))
    x_mine = patches[sel_index].reshape(count, size)
    cot_mine = cotangent[sel_index].reshape(count, size)
    learner_image, learner_text, x_mine, cot_mine, at = lax.optimization_barrier(
        (learner_image, learner_text, x_mine, cot_mine, at)
    )
    image = jnp.where(learner, learner_image, jnp.pad(ref_image, pad))
    text = jnp.where(learner, learner_text, jnp.pad(ref_text, pad))
    other_image = lax.ppermute(image, "zl", SWAP)
    x_other = lax.ppermute(x_mine, "core", SWAP)
    cot_other = lax.ppermute(cot_mine, "core", SWAP)
    texts = around(text, "y")
    joined = join_rows(texts, [other_image, x_other, cot_mine])
    texts_other = lax.ppermute(joined, "core", SWAP)
    pair = pair_rows(at, image, other_image, [joined])
    images = around(pair, "x")

    act, slope = up(at, x_mine, x_other, w_up, [pair])
    x_first, x_second = turn(at, x_mine, x_other, ("xy", "z"), [pair])

    grad_pre = back(at, cot_mine, cot_other, w_down, slope, [])
    (cot_first,) = turn(at, cot_mine, cot_other, ("xy",), [])

    keep, give = down(at, act, w_down, [grad_pre])
    parts = partial_losses(at, images, texts, texts_other, [x_first, grad_pre, cot_first, keep])
    parts = lax.all_to_all(
        parts, ("y", "x", "zl", "core", "zh"), split_axis=0, concat_axis=0, tiled=True
    )
    scores, weight = weights(at, sel_index, parts, [])
    learnability = lax.dynamic_slice_in_dim(scores[0], core * rows, rows)

    cut = 384
    second = products(weight, [x_second], [grad_pre], ((0, 0, cut, width),))
    first = products(
        weight,
        [cot_first, x_first],
        [act, grad_pre],
        ((0, 0, 0, width), (1, 1, 0, cut)),
        second[:1],
    )
    blocks = exchanged([first, second], 0)
    got = lax.ppermute(give, "core", SWAP)
    boxed = place(at, sel_dest.reshape(slots), x_mine, keep, got, [blocks[1][1]])
    boxed = boxed.reshape(32, 4, patch_rows, size)
    routed = lax.all_to_all(boxed, DP, split_axis=0, concat_axis=0, tiled=True)
    routed, token = copied(routed.reshape(128, patch_rows, size))
    blocks = [sum_blocks(part, 56 << 20) for part in blocks]
    blocks = [sum_blocks(part, 6 << 20) for part in exchanged(blocks, 1)]
    grad_down_t, grad_up = last_sum(exchanged(blocks, 2), [token], width)
    return (learnability, routed, grad_up, grad_down_t)


def solution(mesh):
    mesh = Mesh(mesh.devices.reshape(4, 4, 2, 2, 2), ("y", "x", "zl", "core", "zh"))
    pairs = P(("y", "x", "zl", "core"), None)
    patch = P(DP, "zh", "core")
    return jax.shard_map(
        local,
        mesh=mesh,
        in_specs=(
            pairs,
            pairs,
            pairs,
            pairs,
            patch,
            patch,
            P(None, "core"),
            P("core", None),
            P(DP),
            P(DP),
            P(DP, None),
        ),
        out_specs=(
            P(("y", "x", "zl", "core")),
            patch,
            P(CHIPS, "core"),
            P(CHIPS, "core"),
        ),
        check_vma=False,
    )
```
